32 devices in a mesh: pts: 16 (over z, y, x), tp: 2 (over core).
Axes of the slice: x: 2, y: 2, z: 4, core: 2. Of those that a mesh axis runs over, the one named last changes fastest.
Arguments:
- points: bfloat16 [16384, 512], P(('pts', 'tp')), may hold values from -6 to 6
- neighbours: int32 [16384, 27], P('pts'), may hold values from 0 to 1280, as said below
- valid_count: int32 [16], P('pts'), may hold values from 640 to 1024, as said below
- conv_weight: bfloat16 [27, 512, 512], P(None, None, 'tp'), may hold values from -0.0546875 to 0.0546875
- encode_weight: bfloat16 [512, 512], P('tp'), may hold values from -0.25 to 0.25
- encode_gain: float32 [512], replicated, may hold values from 0.25 to 1.75
- encode_shift: float32 [512], replicated, may hold values from -3 to 3
- attend_gain: float32 [512], replicated, may hold values from 0.25 to 1.75
- attend_shift: float32 [512], replicated, may hold values from -3 to 3
- heads_weight: bfloat16 [3, 512, 512], P(None, None, 'tp'), may hold values from -0.25 to 0.25
- output_weight: bfloat16 [512, 512], P('tp'), may hold values from -1.5 to 1.5
- output_bias: float32 [512], replicated, may hold values from -3 to 3
- feed_gain: float32 [512], replicated, may hold values from 0.25 to 1.75
- feed_shift: float32 [512], replicated, may hold values from -3 to 3
- expand_weight: bfloat16 [512, 2048], P(None, 'tp'), may hold values from -0.25 to 0.25
- expand_bias: float32 [2048], P('tp'), may hold values from -3 to 3
- reduce_weight: bfloat16 [2048, 512], P('tp'), may hold values from -0.125 to 0.125
- reduce_bias: float32 [512], replicated, may hold values from -3 to 3
- cotangent: bfloat16 [16384, 512], P(('pts', 'tp')), may hold values from -6 to 6
Outputs:
- out: bfloat16 [16384, 512], P(('pts', 'tp'))
- points_gradient: float32 [16384, 512], P(('pts', 'tp'))
- conv_gradient: float32 [27, 512, 512], P(None, 'pts', 'tp')
- encode_gradient: float32 [512, 512], P('tp', 'pts')
- encode_gain_gradient: float32 [512], replicated
- encode_shift_gradient: float32 [512], replicated
- attend_gain_gradient: float32 [512], replicated
- attend_shift_gradient: float32 [512], replicated
- heads_gradient: float32 [3, 512, 512], P(None, 'pts', 'tp')
- output_gradient: float32 [512, 512], P('tp', 'pts')
- output_bias_gradient: float32 [512], replicated
- feed_gain_gradient: float32 [512], replicated
- feed_shift_gradient: float32 [512], replicated
- expand_gradient: float32 [512, 2048], P('pts', 'tp')
- expand_bias_gradient: float32 [2048], replicated
- reduce_gradient: float32 [2048, 512], P('tp', 'pts')
- reduce_bias_gradient: float32 [512], replicated
The draws below stay inside these ranges and needn't reach their ends.
Inputs may be any that keep to these rules, and one draw needn't show every extreme that they name: `neighbours`: entry k of point i names a row of a window of 1280 rows that begins 128 rows before the first point of i's patch; the value 1024 + 2 * 128 means that the neighbour is absent, and window rows outside the whole array are absent too. A present entry lies at most 128 rows from the point's own window row 128 + (i mod 1024). Entry 13 names the point itself. Points of a patch at position valid_count or later are padding and are never keys.
All inputs are finite; a program needn't handle non-finite values.
Results may differ from the reference program's by a relative error of at most 0.014.
Values may be sent and summed in bfloat16 or wider, within the bound.
A program may use at most 192 MiB of HBM per device.

```python
from functools import partial
import jax
import jax.numpy as jnp
from jax import lax

C = 512
HEADS = 32
HEAD_DIM = 16
HID = 2048
PATCH = 1024
HALO = 128
NEIGH = 27
PATCHES = 16
TOKENS = 16384


def draw_neighbours(key, part):
    key = jax.random.fold_in(key, 11)
    first_key, second_key = jax.random.split(key)
    spread_rows = jax.random.randint(first_key, (TOKENS, NEIGH), -HALO, HALO + 1)
    absent = jax.random.randint(second_key, (TOKENS, NEIGH), 0, 4) == 0
    centre_row = jnp.arange(TOKENS, dtype=jnp.int32) % PATCH + HALO
    column = jnp.clip(centre_row[:, None] + spread_rows, 0, PATCH + 2 * HALO - 1)
    column = jnp.where(absent, PATCH + 2 * HALO, column)
    centre = jnp.arange(NEIGH, dtype=jnp.int32) == NEIGH // 2
    column = jnp.where(centre[None, :], centre_row[:, None], column)
    column = column.at[0, 0].set(PATCH + 2 * HALO)
    column = column.at[0, NEIGH - 1].set(0)
    return column.astype(jnp.int32)


def draw_valid_count(key, part):
    key = jax.random.fold_in(key, 23)
    count_key, chosen_key = jax.random.split(key)
    lowest = 5 * PATCH // 8
    counts = jax.random.randint(count_key, (PATCHES,), lowest, PATCH + 1)
    chosen = jax.random.randint(chosen_key, (), 0, PATCHES)
    counts = counts.at[chosen].set(PATCH)
    counts = counts.at[(chosen + 1) % PATCHES].set(lowest)
    return counts.astype(jnp.int32)


def spiked(array, rng, source, target, parts, factor):
    def block_of(position):
        return (jnp.arange(array.shape[position]) // (array.shape[position] // parts)).reshape((-1,) + (1,) * (array.ndim - 1 - position))

    one_side = jax.random.permutation(rng, parts)[block_of(target)]
    other_side = (block_of(target) + parts // 2) % parts
    return jnp.where((block_of(source) == one_side) | (block_of(source) == other_side), factor * array, array)


def block_scale(stream_key, extent, shards, smallest, high):
    loudness = 1.0
    for position, shards_of in shards:
        draws = jax.random.uniform(jax.random.fold_in(jax.random.fold_in(stream_key, 6), position), (shards_of,), jnp.float32, smallest / len(shards), high / len(shards))
        loudness = loudness * jnp.repeat(jnp.exp(draws), extent[position] // shards_of).reshape((-1,) + (1,) * (len(extent) - 1 - position))
    return loudness


def bell_draw(own_key, shape, scale, reach, cuts=(), kind=jnp.bfloat16):
    entries = jax.random.normal(own_key, shape, jnp.float32) * scale
    if len(cuts) > 0:
        entries = block_scale(own_key, shape, cuts, -0.22, 0.18) * entries
    return jnp.clip(entries, min=-reach, max=reach).astype(kind)


def bell_draw_with(key, dims, deviation, reach, pieces, heavy, kind=jnp.bfloat16):
    drawn = deviation * jax.random.normal(key, dims, jnp.float32)
    if pieces:
        drawn = drawn * block_scale(key, dims, pieces, -0.22, 0.18)
    return jnp.clip(spiked(drawn, jax.random.fold_in(key, 3), *heavy), -reach, reach).astype(kind)


def setup_inputs(seed: int = 0) -> dict:
    splits = jax.random.split(jax.random.key(seed), 20)
    points = bell_draw(splits[0], (TOKENS, C), 1.0, 6.0, ((0, 32),))
    neighbours = draw_neighbours(jax.random.fold_in(splits[19], 71), 0)
    valid_count = draw_valid_count(jax.random.fold_in(splits[19], 71), 0)
    conv_weight = bell_draw(splits[3], (NEIGH, C, C), (NEIGH * C) ** -0.5, 0.0546875, ((2, 2),))
    encode_weight = bell_draw(splits[4], (C, C), C ** -0.5, 0.25, ((0, 2),))
    encode_gain = jnp.clip(1.0 + 0.15 * jax.random.normal(splits[5], (C,), jnp.float32), 0.25, 1.75)
    encode_shift = bell_draw(splits[6], (C,), 0.5, 3.0, (), jnp.float32)
    attend_gain = jnp.clip(1.0 + 0.15 * jax.random.normal(splits[7], (C,), jnp.float32), 0.25, 1.75)
    attend_shift = bell_draw(splits[8], (C,), 0.5, 3.0, (), jnp.float32)
    heads_weight = bell_draw(splits[9], (3, C, C), C ** -0.5, 0.25, ((2, 2),))
    output_weight = bell_draw(splits[10], (C, C), (C // 32) ** -0.5, 1.5, ((0, 2),))
    output_bias = bell_draw(splits[11], (C,), 0.5, 3.0, (), jnp.float32)
    feed_gain = jnp.clip(1.0 + 0.15 * jax.random.normal(splits[12], (C,), jnp.float32), 0.25, 1.75)
    feed_shift = bell_draw(splits[13], (C,), 0.5, 3.0, (), jnp.float32)
    expand_weight = bell_draw(splits[14], (C, HID), C ** -0.5, 0.25, ((1, 2),))
    expand_bias = bell_draw(splits[15], (HID,), 0.5, 3.0, ((0, 2),), jnp.float32)
    reduce_weight = bell_draw(splits[16], (HID, C), HID ** -0.5, 0.125, ((0, 2),))
    reduce_bias = bell_draw(splits[17], (C,), 0.5, 3.0, (), jnp.float32)
    cotangent = bell_draw_with(splits[18], (TOKENS, C), 1.0, 6.0, ((0, 32),), (0, 1, 32, 2.75))
    return dict(points=points, neighbours=neighbours, valid_count=valid_count, conv_weight=conv_weight, encode_weight=encode_weight, encode_gain=encode_gain, encode_shift=encode_shift, attend_gain=attend_gain, attend_shift=attend_shift, heads_weight=heads_weight, output_weight=output_weight, output_bias=output_bias, feed_gain=feed_gain, feed_shift=feed_shift, expand_weight=expand_weight, expand_bias=expand_bias, reduce_weight=reduce_weight, reduce_bias=reduce_bias, cotangent=cotangent)


@jax.custom_vjp
def low(v):
    return lax.optimization_barrier(v.astype(jnp.bfloat16)).astype(jnp.float32)

@jax.custom_vjp
def low_back(v):
    return v

def low_keep(v):
    return (low(v), None)

def low_pass(kept, grad):
    return (grad,)

def back_keep(v):
    return (v, None)

def back_low(kept, grad):
    return (low(grad),)
low.defvjp(low_keep, low_pass)
low_back.defvjp(back_keep, back_low)
EPSILON = 1e-05
MASKED = -1e+30
HIGH = lax.Precision.HIGHEST

def layer_norm(values, norm_gain, norm_shift):
    row_mean = lax.optimization_barrier(jnp.mean(values, axis=-1, keepdims=True))
    centred = values - row_mean
    inverse = lax.rsqrt(lax.optimization_barrier(jnp.mean(centred * centred, axis=-1, keepdims=True)) + EPSILON)
    return centred * inverse * norm_gain + norm_shift

def conv_rows(field, neighbours, conv_weight):
    starts = jnp.arange(TOKENS, dtype=jnp.int32) // PATCH * PATCH - HALO

    def one_offset(running, inputs):
        column, weight = inputs
        source = starts + column
        usable = (column < PATCH + 2 * HALO) & (source >= 0) & (source < TOKENS)
        rows = jnp.take(field, jnp.clip(source, 0, TOKENS - 1).astype(jnp.int32), axis=0)
        rows = jnp.where(usable[:, None], rows, 0.0)
        return (running + jnp.dot(rows, weight, precision=HIGH), None)
    running, unused = lax.scan(jax.checkpoint(one_offset), jnp.zeros((TOKENS, C), jnp.float32), (neighbours.T, conv_weight))
    return running

def patch_attention(heads_weight, inputs):
    patch_in, count = inputs
    scale = HEAD_DIM ** (-0.5)
    projected = low(low_back(jnp.einsum('tc,jcm->jtm', patch_in, heads_weight, precision=HIGH)))
    queries = projected[0].reshape(PATCH, HEADS, HEAD_DIM)
    keys = projected[1].reshape(PATCH, HEADS, HEAD_DIM)
    values = projected[2].reshape(PATCH, HEADS, HEAD_DIM)
    scores = low_back(jnp.einsum('qhd,khd->hqk', queries, keys, precision=HIGH) * scale)
    key_valid = jnp.arange(PATCH, dtype=jnp.int32) < count
    scores = jnp.where(key_valid[None, None, :], scores, MASKED)
    probs = low(jax.nn.softmax(scores, axis=-1))
    mixed = jnp.einsum('hqk,khd->qhd', probs, values, precision=HIGH)
    return low(low_back(mixed.reshape(PATCH, HEADS * HEAD_DIM)))

def block_forward(points, conv_weight, encode_weight, encode_gain, encode_shift, attend_gain, attend_shift, heads_weight, output_weight, output_bias, feed_gain, feed_shift, expand_weight, expand_bias, reduce_weight, reduce_bias, neighbours, valid_count):
    conved = low(low_back(conv_rows(points, neighbours, conv_weight)))
    linear = low_back(jnp.dot(conved, encode_weight, precision=HIGH))
    first = points + layer_norm(linear, encode_gain, encode_shift)
    attend_in = low(layer_norm(first, attend_gain, attend_shift))
    mixed = lax.map(jax.checkpoint(partial(patch_attention, heads_weight)), (attend_in.reshape(PATCHES, PATCH, C), valid_count))
    mixed = mixed.reshape(TOKENS, C)
    second = first + low_back(jnp.dot(mixed, output_weight, precision=HIGH)) + output_bias
    feed_in = low(layer_norm(second, feed_gain, feed_shift))
    hidden = low_back(jnp.dot(feed_in, expand_weight, precision=HIGH) + expand_bias)
    active = low(jax.nn.gelu(hidden, approximate=False))
    return second + low_back(jnp.dot(active, reduce_weight, precision=HIGH)) + reduce_bias

def reference(points, neighbours, valid_count, conv_weight, encode_weight, encode_gain, encode_shift, attend_gain, attend_shift, heads_weight, output_weight, output_bias, feed_gain, feed_shift, expand_weight, expand_bias, reduce_weight, reduce_bias, cotangent):

    def forward(points_in, conv_in, encode_in, encode_gain_in, encode_shift_in, attend_gain_in, attend_shift_in, heads_in, output_in, output_bias_in, feed_gain_in, feed_shift_in, expand_in, expand_bias_in, reduce_in, reduce_bias_in):
        return block_forward(points_in, conv_in, encode_in, encode_gain_in, encode_shift_in, attend_gain_in, attend_shift_in, heads_in, output_in, output_bias_in, feed_gain_in, feed_shift_in, expand_in, expand_bias_in, reduce_in, reduce_bias_in, neighbours, valid_count)
    result, backward = jax.vjp(forward, points.astype(jnp.float32), conv_weight.astype(jnp.float32), encode_weight.astype(jnp.float32), encode_gain.astype(jnp.float32), encode_shift.astype(jnp.float32), attend_gain.astype(jnp.float32), attend_shift.astype(jnp.float32), heads_weight.astype(jnp.float32), output_weight.astype(jnp.float32), output_bias.astype(jnp.float32), feed_gain.astype(jnp.float32), feed_shift.astype(jnp.float32), expand_weight.astype(jnp.float32), expand_bias.astype(jnp.float32), reduce_weight.astype(jnp.float32), reduce_bias.astype(jnp.float32))
    points_gradient, conv_gradient, encode_gradient, encode_gain_gradient, encode_shift_gradient, attend_gain_gradient, attend_shift_gradient, heads_gradient, output_gradient, output_bias_gradient, feed_gain_gradient, feed_shift_gradient, expand_gradient, expand_bias_gradient, reduce_gradient, reduce_bias_gradient = backward(cotangent.astype(jnp.float32))
    return (result.astype(jnp.bfloat16), points_gradient, conv_gradient, encode_gradient, encode_gain_gradient, encode_shift_gradient, attend_gain_gradient, attend_shift_gradient, heads_gradient, output_gradient, output_bias_gradient, feed_gain_gradient, feed_shift_gradient, expand_gradient, expand_bias_gradient, reduce_gradient, reduce_bias_gradient)
```

```python
import functools

import jax
import jax.numpy as jnp
from jax import lax
from jax.experimental import pallas as pl
from jax.experimental.pallas import tpu as pltpu
from jax.sharding import PartitionSpec as P

HEAD_DIM = 16
HALO = 128
BLOCK = 256
GROUP = 3
EPSILON = 1e-05
MASKED = -1e30
SWAP = ((0, 1), (1, 0))
KERNEL_BITS = 4
ORDERS = ((0, 1, 2, 3), (1, 0, 2, 3), (2, 3, 0, 1), (2, 3, 1, 0))
SUM_STEPS = (6, 9, 11, 13)
CONV_LAGS = (2, 4, 5, 6)
EXTRA_STEPS = (4, 6, 8, 10)


def to_low(values):
    return values.astype(jnp.bfloat16)


def to_wide(values):
    return values.astype(jnp.float32)


def product(left, right, left_dim, right_dim):
    dims = (((left_dim,), (right_dim,)), ((), ()))
    return lax.dot_general(left, right, dims, preferred_element_type=jnp.float32)


def swap(values):
    return lax.ppermute(values, "tp", SWAP)


def conv_forward_kernel(near_ref, window_ref, weight_ref, out_ref, total, rows):
    step = pl.program_id(0)
    blocks = near_ref.shape[0] // BLOCK
    channels = window_ref.shape[1]

    @pl.when(step == 0)
    def _():
        total[...] = jnp.zeros_like(total)

    lane = lax.broadcasted_iota(jnp.int32, (BLOCK, near_ref.shape[1]), 1)
    slots = to_wide(lax.broadcasted_iota(jnp.int32, (BLOCK, 2 * BLOCK), 1))
    for block in range(blocks):
        window = window_ref[block * BLOCK : (block + 2) * BLOCK, :]
        near = near_ref[block * BLOCK : (block + 1) * BLOCK, :]
        for offset in range(GROUP):
            chosen = jnp.where(lane == step * GROUP + offset, near, 0.0)
            column = jnp.sum(chosen, axis=1, keepdims=True) - float(block * BLOCK)
            select = to_low(jnp.where(column == slots, 1.0, 0.0))
            rows[
                block * BLOCK : (block + 1) * BLOCK,
                offset * channels : (offset + 1) * channels,
            ] = to_low(product(select, window, 1, 0))
    weight = weight_ref[...].reshape(GROUP * channels, weight_ref.shape[2])
    total[...] += product(rows[...], weight, 1, 0)

    @pl.when(step == pl.num_programs(0) - 1)
    def _():
        out_ref[...] = to_low(total[...])


def conv_forward(near, window, weight):
    offsets, channels, width = weight.shape
    rows = near.shape[0]
    return pl.pallas_call(
        conv_forward_kernel,
        grid=(offsets // GROUP,),
        in_specs=[
            pl.BlockSpec(near.shape, lambda i: (0, 0)),
            pl.BlockSpec(window.shape, lambda i: (0, 0)),
            pl.BlockSpec((GROUP, channels, width), lambda i: (i, 0, 0)),
        ],
        out_specs=pl.BlockSpec((rows, width), lambda i: (0, 0)),
        out_shape=jax.ShapeDtypeStruct((rows, width), jnp.bfloat16),
        scratch_shapes=[
            pltpu.VMEM((rows, width), jnp.float32),
            pltpu.VMEM((rows, GROUP * channels), jnp.bfloat16),
        ],
        compiler_params=pltpu.CompilerParams(vmem_limit_bytes=40 << 20),
        cost_estimate=pl.CostEstimate(
            flops=30 * 10**9, bytes_accessed=12 * 10**6, transcendentals=0
        ),
    )(near, window, weight)


def partner_of(bit):
    me = lax.axis_index("pts")
    return me + (1 - 2 * ((me // (1 << bit)) % 2)) * (1 << bit)


def greet_partners():
    barrier = pltpu.get_barrier_semaphore()
    for bit in range(KERNEL_BITS):
        pl.semaphore_signal(
            barrier, inc=1, device_id={"pts": partner_of(bit)}, device_id_type=pl.DeviceIdType.MESH
        )
    pl.semaphore_wait(barrier, KERNEL_BITS)


class PairSums:
    def __init__(self, keep, sends, arrivals, send_sem, arrive_sem):
        self.keep, self.sends, self.arrivals = keep, sends, arrivals
        self.send_sem, self.arrive_sem = send_sem, arrive_sem

    def copy(self, stage, chunk, bit):
        return pltpu.make_async_remote_copy(
            src_ref=self.sends[stage].at[chunk],
            dst_ref=self.arrivals[stage].at[chunk],
            send_sem=self.send_sem.at[stage, chunk],
            recv_sem=self.arrive_sem.at[stage, chunk],
            device_id={"pts": partner_of(bit)},
            device_id_type=pl.DeviceIdType.MESH,
        )

    def start(self, stage, chunk, kinds):
        for holds, order in kinds:
            if holds is True:
                self.copy(stage, chunk, order[stage]).start()
            else:

                @pl.when(holds)
                def _(order=order):
                    self.copy(stage, chunk, order[stage]).start()

    def advance(self, stage, chunk, kinds, out_ref):
        self.copy(stage, chunk, 0).wait()
        rows = self.keep.shape[2]
        low = rows - (rows >> stage)
        half = (rows - low) // 2
        arrived = self.arrivals[stage]
        if stage == KERNEL_BITS - 1:
            out_ref[chunk] = self.keep[chunk, :, low:] + to_wide(arrived[chunk])
            return
        self.sends[stage + 1][chunk] = to_low(
            self.keep[chunk, :, low : low + half] + to_wide(arrived[chunk, :, :half])
        )
        self.start(stage + 1, chunk, kinds)
        self.keep[chunk, :, low + half :] += to_wide(arrived[chunk, :, half:])


def pair_scratch(chunks, lead, rows, width):
    halves = [(chunks, lead, rows >> (stage + 1), width) for stage in range(KERNEL_BITS)]
    return (
        [pltpu.VMEM(halves[0], jnp.float32)]
        + [pltpu.VMEM(shape, jnp.bfloat16) for shape in halves]
        + [pltpu.VMEM(shape, jnp.bfloat16) for shape in halves]
        + [pltpu.SemaphoreType.DMA((KERNEL_BITS, chunks))] * 2
    )


def pair_sums(scratch):
    keep, rest = scratch[0], scratch[1:]
    return PairSums(keep, rest[:KERNEL_BITS], rest[KERNEL_BITS : 2 * KERNEL_BITS], *rest[-2:])


def conv_backward_kernel(
    near_ref, window_ref, grad_ref, weight_ref, extra_ref, sum_ref, input_ref, spread, *scratch
):
    rows, width = grad_ref.shape
    blocks = rows // BLOCK
    extras = extra_ref.shape[0]
    chunks = sum_ref.shape[0]
    step = pl.program_id(0)
    sums = pair_sums(scratch)
    half = sums.keep.shape[2]

    def kinds(chunk):
        return ((chunk % 2 == 0, ORDERS[0]), (chunk % 2 == 1, ORDERS[1]))

    @pl.when(step == 0)
    def _():
        input_ref[...] = jnp.zeros_like(input_ref)
        greet_partners()
        for chunk in range(extras):
            sums.sends[0][chunk] = to_low(extra_ref[chunk, :, :half])
            sums.start(0, chunk, ((True, ORDERS[2 + chunk]),))
            sums.keep[chunk] = extra_ref[chunk, :, half:]

    @pl.when(step < chunks - extras)
    def _():
        slots = to_wide(lax.broadcasted_iota(jnp.int32, (BLOCK, 1), 0))
        chunk = step + extras
        for offset in range(GROUP):
            near = near_ref[offset]
            for part in range(blocks + 1):
                low = max(part - 1, 0) * BLOCK
                high = min(part + 1, blocks) * BLOCK
                select = to_low(
                    jnp.where(near[:, low:high] - float(part * BLOCK) == slots, 1.0, 0.0)
                )
                spread[
                    part * BLOCK : (part + 1) * BLOCK, offset * width : (offset + 1) * width
                ] = to_low(product(select, grad_ref[low:high, :], 1, 0))
        for offset in range(GROUP):
            weight_grad = product(
                window_ref[chunk % 2], spread[:, offset * width : (offset + 1) * width], 1, 0
            )
            sums.sends[0][chunk, offset] = to_low(weight_grad[:half])
            sums.keep[chunk, offset] = weight_grad[half:]
        sums.start(0, chunk, kinds(chunk))
        for offset in range(GROUP):
            input_ref[...] += product(
                spread[:, offset * width : (offset + 1) * width], weight_ref[offset], 1, 1
            )

    for stage in range(KERNEL_BITS):
        chunk = step + extras - CONV_LAGS[stage]

        @pl.when((chunk >= extras) & (chunk < chunks))
        def _(stage=stage, chunk=chunk):
            sums.advance(stage, chunk, kinds(chunk), sum_ref)

        @pl.when(step == EXTRA_STEPS[stage])
        def _(stage=stage):
            for chunk in range(extras):
                sums.advance(stage, chunk, ((True, ORDERS[2 + chunk]),), sum_ref)


def conv_backward(near, window, grad, weight, extra):
    offsets, channels, width = weight.shape
    rows = grad.shape[0]
    wide = window.shape[2]
    extras = extra.shape[0]
    steps = offsets // GROUP
    chunks = steps + extras
    kept = channels >> KERNEL_BITS
    once = pl.Buffered(1)
    return pl.pallas_call(
        conv_backward_kernel,
        grid=(steps + CONV_LAGS[-1],),
        in_specs=[
            pl.BlockSpec((GROUP, 1, rows), lambda i: (jnp.minimum(i, steps - 1), 0, 0)),
            pl.BlockSpec(window.shape, lambda i: (0, 0, 0), pipeline_mode=once),
            pl.BlockSpec((rows, width), lambda i: (0, 0), pipeline_mode=once),
            pl.BlockSpec((GROUP, channels, width), lambda i: (jnp.minimum(i, steps - 1), 0, 0)),
            pl.BlockSpec(extra.shape, lambda i: (0, 0, 0, 0), pipeline_mode=once),
        ],
        out_specs=[
            pl.BlockSpec(
                (chunks, GROUP, kept, width), lambda i: (0, 0, 0, 0), pipeline_mode=once
            ),
            pl.BlockSpec((wide, channels), lambda i: (0, 0), pipeline_mode=once),
        ],
        out_shape=[
            jax.ShapeDtypeStruct((chunks, GROUP, kept, width), jnp.float32),
            jax.ShapeDtypeStruct((wide, channels), jnp.float32),
        ],
        scratch_shapes=[pltpu.VMEM((wide, GROUP * width), jnp.bfloat16)]
        + pair_scratch(chunks, GROUP, channels, width),
        compiler_params=pltpu.CompilerParams(
            vmem_limit_bytes=56 << 20, collective_id=1, has_side_effects=True
        ),
        cost_estimate=pl.CostEstimate(
            flops=80 * 10**9, bytes_accessed=16 * 10**6, transcendentals=0
        ),
    )(near, window, grad, weight, extra)


def attend_kernel(chunk, query_ref, key_ref, value_ref, bias_ref, out_ref, log_ref):
    depth, points = query_ref.shape
    row = lax.broadcasted_iota(jnp.int32, (depth, points), 0)
    ones = to_low(jnp.where(row == 0, 1.0, 0.0))
    keys = jnp.concatenate([key_ref[...], bias_ref[...]], axis=0)
    queries = jnp.concatenate([to_low(to_wide(query_ref[...]) * depth**-0.5), ones], axis=0)
    values = jnp.concatenate([value_ref[...], ones], axis=0)
    for start in range(0, points, chunk):
        scores = product(keys, queries[:, start : start + chunk], 0, 0)
        top = jnp.max(scores, axis=0, keepdims=True)
        mixed = product(values, to_low(jnp.exp(scores - top)), 1, 0)
        total = mixed[depth : depth + 1, :]
        out_ref[:, start : start + chunk] = to_low(mixed[:depth] / total)
        log_ref[0, :, start : start + chunk] = top + jnp.log(total)


def attend(queries, keys, values, bias):
    width, points = queries.shape
    heads = width // HEAD_DIM
    block = pl.BlockSpec((HEAD_DIM, points), lambda i: (i, 0))
    return pl.pallas_call(
        functools.partial(attend_kernel, 512),
        grid=(heads,),
        in_specs=[block, block, block, pl.BlockSpec(bias.shape, lambda i: (0, 0))],
        out_specs=[block, pl.BlockSpec((1, 1, points), lambda i: (i, 0, 0))],
        out_shape=[
            jax.ShapeDtypeStruct((width, points), jnp.bfloat16),
            jax.ShapeDtypeStruct((heads, 1, points), jnp.float32),
        ],
        compiler_params=pltpu.CompilerParams(vmem_limit_bytes=40 << 20),
        cost_estimate=pl.CostEstimate(
            flops=36 * 10**9, bytes_accessed=3 * 10**6, transcendentals=0
        ),
    )(queries, keys, values, bias)


def attend_back_kernel(
    chunk,
    query_ref,
    key_ref,
    value_ref,
    bias_ref,
    mixed_ref,
    log_ref,
    grad_ref,
    extra_ref,
    query_grad_ref,
    key_grad_ref,
    value_grad_ref,
    sum_ref,
    key_total,
    value_total,
    *scratch,
):
    depth, points = query_ref.shape
    scale = depth**-0.5
    sums = pair_sums(scratch)
    half = sums.keep.shape[2]
    head = pl.program_id(0)

    @pl.when(head == 0)
    def _():
        greet_partners()
        for chunk in range(extra_ref.shape[0]):
            sums.sends[0][chunk] = to_low(extra_ref[chunk, :, :half])
            sums.start(0, chunk, ((True, ORDERS[chunk]),))
            sums.keep[chunk] = extra_ref[chunk, :, half:]

    for stage, due in enumerate(SUM_STEPS):

        @pl.when(head == due)
        def _(stage=stage):
            for chunk in range(extra_ref.shape[0]):
                sums.advance(stage, chunk, ((True, ORDERS[chunk]),), sum_ref)

    row = lax.broadcasted_iota(jnp.int32, (depth, points), 0)
    query, key, value, grad = query_ref[...], key_ref[...], value_ref[...], grad_ref[...]
    row_dot = jnp.sum(to_wide(grad) * to_wide(mixed_ref[...]), axis=0, keepdims=True)

    def three_parts(values, lead):
        upper = to_wide(to_low(values))
        middle = to_wide(to_low(values - upper))
        lower = values - upper - middle
        tail = jnp.where(row == 1, -upper, jnp.where(row == 2, -middle, 0.0))
        tail = jnp.where(row == 3, -lower, tail)
        return to_low(jnp.where(row == 0, lead, tail))

    ones = to_low(jnp.where((row > 0) & (row < 4), 1.0, 0.0))
    keys = jnp.concatenate([key, bias_ref[...] + ones], axis=0)
    queries = jnp.concatenate(
        [to_low(to_wide(query) * scale), three_parts(log_ref[0], 1.0)], axis=0
    )
    values = jnp.concatenate([value, ones], axis=0)
    grads = jnp.concatenate([grad, three_parts(row_dot, 0.0)], axis=0)
    query_rows, grad_rows = query.T, grad.T
    for start in range(0, points, chunk):
        part = slice(start, start + chunk)
        probs = jnp.exp(product(keys, queries[:, part], 0, 0))
        score_grad = to_low(probs * product(values, grads[:, part], 0, 0))
        value_part = product(to_low(probs), grad_rows[part], 1, 0)
        key_part = product(score_grad, query_rows[part], 1, 0)
        if start == 0:
            value_total[...] = value_part
            key_total[...] = key_part
        else:
            value_total[...] += value_part
            key_total[...] += key_part
        query_grad_ref[:, part] = to_low(product(key, score_grad, 1, 0) * scale)
    key_grad_ref[...] = to_low((key_total[...] * scale).T)
    value_grad_ref[...] = to_low(value_total[...].T)


def attend_back(queries, keys, values, bias, mixed, logs, grads, extra):
    width, points = queries.shape
    heads = width // HEAD_DIM
    block = pl.BlockSpec((HEAD_DIM, points), lambda i: (i, 0))
    summed = (*extra.shape[:2], extra.shape[2] >> KERNEL_BITS, extra.shape[3])
    return pl.pallas_call(
        functools.partial(attend_back_kernel, 512),
        grid=(heads,),
        in_specs=[
            block,
            block,
            block,
            pl.BlockSpec(bias.shape, lambda i: (0, 0)),
            block,
            pl.BlockSpec((1, 1, points), lambda i: (i, 0, 0)),
            block,
            pl.BlockSpec(extra.shape, lambda i: (0, 0, 0, 0), pipeline_mode=pl.Buffered(1)),
        ],
        out_specs=[
            block,
            block,
            block,
            pl.BlockSpec(summed, lambda i: (0, 0, 0, 0), pipeline_mode=pl.Buffered(1)),
        ],
        out_shape=[jax.ShapeDtypeStruct((width, points), jnp.bfloat16)] * 3
        + [jax.ShapeDtypeStruct(summed, jnp.float32)],
        scratch_shapes=[pltpu.VMEM((points, HEAD_DIM), jnp.float32)] * 2
        + pair_scratch(*extra.shape),
        compiler_params=pltpu.CompilerParams(
            vmem_limit_bytes=40 << 20, collective_id=0, has_side_effects=True
        ),
        cost_estimate=pl.CostEstimate(
            flops=50 * 10**9, bytes_accessed=5 * 10**6, transcendentals=0
        ),
    )(queries, keys, values, bias, mixed, logs, grads, extra)


def exchange(values, bit):
    count = lax.axis_size("pts")
    return lax.ppermute(values, "pts", [(i, i ^ (1 << bit)) for i in range(count)])


def patch_bits():
    return lax.axis_size("pts").bit_length() - 1


def nested_picks(channels, order):
    me = lax.axis_index("pts")
    order = order + tuple(range(KERNEL_BITS, patch_bits()))
    depth = channels >> len(order)
    place = jnp.arange(channels, dtype=jnp.int32)
    slot = jnp.zeros_like(place)
    for stage, bit in enumerate(order):
        kept = (place // (channels >> (stage + 1))) % 2
        slot = slot + (1 << bit) * (1 - (kept + (me >> bit)) % 2)
    picked = slot * depth + place % depth
    return to_low(picked[:, None] == jnp.arange(channels)[None, :])


def sum_rest(keep):
    for bit in range(KERNEL_BITS, patch_bits()):
        half = keep.shape[-2] // 2
        keep = keep[..., half:, :] + to_wide(exchange(to_low(keep[..., :half, :]), bit))
    return keep


def sum_all(values):
    values = values + swap(values)
    for bit in range(patch_bits()):
        values = values + exchange(values, bit)
    return values


def layer_norm(values, norm_gain, norm_shift):
    row_mean = jnp.mean(values, axis=-1, keepdims=True)
    centred = values - row_mean
    inverse = lax.rsqrt(jnp.mean(centred * centred, axis=-1, keepdims=True) + EPSILON)
    normal_part = centred * inverse
    return (normal_part * norm_gain + norm_shift, normal_part, inverse)


def norm_back(upstream, normal_part, inverse, norm_gain):
    scaled = upstream * norm_gain
    across = (
        scaled
        - jnp.mean(scaled, axis=-1, keepdims=True)
        - normal_part * jnp.mean(scaled * normal_part, axis=-1, keepdims=True)
    )
    return (across * inverse, jnp.sum(upstream * normal_part, axis=0), jnp.sum(upstream, axis=0))


def exact_gelu(values):
    return jax.nn.gelu(values, approximate=False)


def per_device(
    points,
    neighbours,
    valid_count,
    conv_weight,
    encode_weight,
    encode_gain,
    encode_shift,
    attend_gain,
    attend_shift,
    heads_weight,
    output_weight,
    output_bias,
    feed_gain,
    feed_shift,
    expand_weight,
    expand_bias,
    reduce_weight,
    reduce_bias,
    cotangent,
):
    local, channels = points.shape
    rows = 2 * local
    patches = lax.axis_size("pts")
    side = lax.axis_index("tp")
    is_first = side == 0
    picks = [nested_picks(channels, order) for order in ORDERS]

    def in_order(own, other):
        return jnp.concatenate(
            [jnp.where(is_first, own, other), jnp.where(is_first, other, own)], axis=0
        )

    edge = jnp.where(is_first, points[:HALO], points[local - HALO :])
    straight = [(2 * i + 1, 2 * i + 3) for i in range(patches - 1)]
    straight += [(2 * i + 2, 2 * i) for i in range(patches - 1)]
    across = [(2 * i + 1, 2 * i + 2) for i in range(patches - 1)]
    across += [(2 * i + 2, 2 * i + 1) for i in range(patches - 1)]
    edge_straight = lax.ppermute(edge, ("pts", "tp"), straight)
    edge_across = lax.ppermute(edge, ("pts", "tp"), across)
    points_other = swap(points)
    low_rim = jnp.where(is_first, edge_across, edge_straight)
    high_rim = jnp.where(is_first, edge_straight, edge_across)
    window = jnp.concatenate([low_rim, in_order(points, points_other), high_rim], axis=0)

    encode_other = swap(encode_weight)
    output_other = swap(output_weight)
    expand_other = swap(expand_weight)
    reduce_other = swap(reduce_weight)
    expand_bias_other = swap(expand_bias)

    near = to_wide(neighbours)
    near_columns = near.T.reshape(near.shape[1], 1, rows)
    window_turned = jnp.stack([to_low(product(picks[i], window, 1, 1)) for i in range(2)])

    conved = conv_forward(near, window, conv_weight)
    conved_own = lax.dynamic_slice_in_dim(conved, side * local, local, 0)
    conved_other = swap(lax.dynamic_slice_in_dim(conved, (1 - side) * local, local, 0))
    linear = product(conved_own, encode_weight, 1, 0) + product(conved_other, encode_other, 1, 0)
    encoded, encode_normal, encode_inverse = layer_norm(linear, encode_gain, encode_shift)
    first = to_wide(points) + encoded

    attend_out, attend_normal, attend_inverse = layer_norm(first, attend_gain, attend_shift)
    attend_low = to_low(attend_out)
    attend_whole = jnp.concatenate([attend_low, swap(attend_low)], axis=0)
    projected = to_low(
        jnp.einsum("jcm,tc->jmt", heads_weight, attend_whole, preferred_element_type=jnp.float32)
    )
    place = jnp.arange(rows, dtype=jnp.int32)
    place = jnp.where(is_first, place, (place + local) % rows)
    bias = jnp.where(place < valid_count[0], 0.0, MASKED)
    bias = jnp.where(jnp.arange(HEAD_DIM)[:, None] == 0, bias[None, :], 0.0)
    bias = to_low(bias)
    mixed, logs = attend(projected[0], projected[1], projected[2], bias)
    mixed_other = swap(mixed[:, local:])
    attended = product(mixed[:, :local], output_weight, 0, 0)
    attended += product(mixed_other, output_other, 0, 0)
    second = first + attended + output_bias

    feed_out, feed_normal, feed_inverse = layer_norm(second, feed_gain, feed_shift)
    feed_low = to_low(feed_out)
    upstream = to_wide(cotangent)
    result = second + reduce_bias
    feed_grad = 0.0
    reduce_parts, expand_parts, bias_parts = [], [], []
    cotangent_nested = to_low(product(cotangent, picks[0], 1, 1))
    feed_nested = to_low(product(feed_low, picks[1], 1, 1))
    for up, up_bias, down in (
        (expand_weight, expand_bias, reduce_weight),
        (expand_other, expand_bias_other, reduce_other),
    ):
        hidden = product(feed_low, up, 1, 0) + up_bias
        gelu_value, gelu_back = jax.vjp(exact_gelu, hidden)
        active = to_low(gelu_value)
        hidden_grad = to_low(gelu_back(product(cotangent, down, 1, 1))[0])
        result += product(active, down, 1, 0)
        feed_grad += product(hidden_grad, up, 1, 1)
        reduce_parts.append(product(cotangent_nested, active, 0, 0))
        expand_parts.append(product(feed_nested, hidden_grad, 0, 0))
        bias_parts.append(jnp.sum(to_wide(hidden_grad), axis=0))
    expand_bias_grad = jnp.concatenate(
        [
            jnp.where(is_first, bias_parts[0], bias_parts[1]),
            jnp.where(is_first, bias_parts[1], bias_parts[0]),
        ]
    )
    feed_grads = jnp.stack(
        [reduce_parts[0] + swap(reduce_parts[1]), expand_parts[0] + swap(expand_parts[1])]
    )
    feed_back, feed_gain_grad, feed_shift_grad = norm_back(
        feed_grad, feed_normal, feed_inverse, feed_gain
    )
    second_grad = upstream + feed_back

    second_low = to_low(second_grad)
    second_whole = jnp.concatenate([second_low, swap(second_low)], axis=0)
    mixed_grad = to_low(product(output_weight, second_whole, 1, 1))
    *projected_grad, feed_sums = attend_back(
        projected[0], projected[1], projected[2], bias, mixed, logs, mixed_grad, feed_grads[:, None]
    )
    feed_sums = sum_rest(feed_sums)[:, 0]
    attend_nested = to_low(product(attend_whole, picks[2], 1, 1))
    heads_grad = jnp.stack([product(attend_nested, part, 0, 1) for part in projected_grad])
    attend_grad = sum(
        product(part, heads_weight[index], 0, 1) for index, part in enumerate(projected_grad)
    )
    attend_grad = attend_grad[:local] + swap(attend_grad[local:])
    attend_back_grad, attend_gain_grad, attend_shift_grad = norm_back(
        attend_grad, attend_normal, attend_inverse, attend_gain
    )
    first_grad = second_grad + attend_back_grad

    linear_full, encode_gain_grad, encode_shift_grad = norm_back(
        first_grad, encode_normal, encode_inverse, encode_gain
    )
    linear_low = to_low(linear_full)
    linear_whole = in_order(linear_low, swap(linear_low))
    conved_grad = to_low(product(linear_whole, encode_weight, 1, 1))
    output_grad = product(to_low(product(second_whole, picks[3], 1, 1)), mixed, 0, 1)
    encode_grad = product(to_low(product(linear_whole, picks[3], 1, 1)), conved, 0, 0)
    extra = jnp.stack([heads_grad, jnp.stack([output_grad, encode_grad, 0.0 * encode_grad])])
    weight_sums, window_grad = conv_backward(
        near_columns, window_turned, conved_grad, conv_weight, extra
    )
    weight_sums = sum_rest(weight_sums)
    conv_out = weight_sums[2:].reshape(-1, *weight_sums.shape[2:])

    half = local + HALO
    window_own = lax.dynamic_slice_in_dim(window_grad, side * half, half, 0)
    window_own += swap(lax.dynamic_slice_in_dim(window_grad, (1 - side) * half, half, 0))
    rim = jnp.where(is_first, window_own[:HALO], window_own[local:])
    arrived = to_wide(lax.ppermute(to_low(rim), ("pts", "tp"), across))
    points_gradient = first_grad + lax.dynamic_slice_in_dim(
        window_own, (1 - side) * HALO, local, 0
    )
    rest = jnp.zeros((local - HALO, channels), jnp.float32)
    points_gradient += jnp.where(
        is_first,
        jnp.concatenate([arrived, rest], axis=0),
        jnp.concatenate([rest, arrived], axis=0),
    )

    vectors = sum_all(
        jnp.concatenate(
            [
                encode_gain_grad,
                encode_shift_grad,
                attend_gain_grad,
                attend_shift_grad,
                jnp.sum(second_grad, axis=0),
                feed_gain_grad,
                feed_shift_grad,
                jnp.sum(upstream, axis=0),
                expand_bias_grad,
            ]
        )
    )
    vectors = jnp.split(vectors, [channels * i for i in range(1, 9)])
    return (
        to_low(result),
        points_gradient,
        conv_out,
        weight_sums[1, 1].T,
        vectors[0],
        vectors[1],
        vectors[2],
        vectors[3],
        weight_sums[0],
        weight_sums[1, 0].T,
        vectors[4],
        vectors[5],
        vectors[6],
        feed_sums[1],
        vectors[8],
        feed_sums[0].T,
        vectors[7],
    )


def solution(mesh):
    placed = (
        P(("pts", "tp"), None),
        P("pts", None),
        P("pts"),
        P(None, None, "tp"),
        P("tp", None),
        P(),
        P(),
        P(),
        P(),
        P(None, None, "tp"),
        P("tp", None),
        P(),
        P(),
        P(),
        P(None, "tp"),
        P("tp"),
        P("tp", None),
        P(),
        P(("pts", "tp"), None),
    )
    return jax.shard_map(
        per_device,
        mesh=mesh,
        in_specs=placed,
        out_specs=(
            P(("pts", "tp"), None),
            P(("pts", "tp"), None),
            P(None, "pts", "tp"),
            P("tp", "pts"),
            P(),
            P(),
            P(),
            P(),
            P(None, "pts", "tp"),
            P("tp", "pts"),
            P(),
            P(),
            P(),
            P("pts", "tp"),
            P(),
            P("tp", "pts"),
            P(),
        ),
        check_vma=False,
    )
```

```python
import functools

import jax
import jax.numpy as jnp
from jax import lax
from jax.experimental import pallas as pl
from jax.experimental.pallas import tpu as pltpu
from jax.sharding import PartitionSpec as P

MESH = pl.DeviceIdType.MESH
HEAD_DIM = 16
HALO = 128
BLOCK = 256
GROUP = 3
EPSILON = 1e-05
MASKED = -1e30
SWAP = ((0, 1), (1, 0))
KERNEL_BITS = 4
ORDERS = ((0, 1, 2, 3), (1, 0, 2, 3), (2, 3, 0, 1), (2, 3, 1, 0))
HEADS_STEP = 4
HEADS_BACK_STEP = 2
SUM_STEPS = (3, 5, 6, 7)
CONV_LAGS = (2, 4, 5, 6)
EXTRA_STEPS = (4, 6, 8, 10)
VECTOR_STEPS = (1, 2, 3, 4, 5)
INPUT_STEPS = (9, 11, 13)


def to_low(values):
    return values.astype(jnp.bfloat16)


def to_wide(values):
    return values.astype(jnp.float32)


def product(left, right, left_dim, right_dim):
    dims = (((left_dim,), (right_dim,)), ((), ()))
    return lax.dot_general(left, right, dims, preferred_element_type=jnp.float32)


def layer_norm(values):
    row_mean = jnp.mean(values, axis=-1, keepdims=True)
    centred = values - row_mean
    inverse = lax.rsqrt(jnp.mean(centred * centred, axis=-1, keepdims=True) + EPSILON)
    return centred * inverse, inverse


def norm_back(upstream, normal_part, inverse, norm_gain):
    scaled = upstream * norm_gain
    across = (
        scaled
        - jnp.mean(scaled, axis=-1, keepdims=True)
        - normal_part * jnp.mean(scaled * normal_part, axis=-1, keepdims=True)
    )
    return across * inverse


def column_sum(values):
    return jnp.sum(values, axis=0, keepdims=True)


def nested_picks(channels, order):
    me = lax.axis_index("pts")
    order = order + tuple(range(KERNEL_BITS, patch_bits()))
    depth = channels >> len(order)
    place = lax.broadcasted_iota(jnp.int32, (channels, channels), 0)
    picked = place & (depth - 1)
    for stage, bit in enumerate(order):
        kept = (place >> (channels.bit_length() - 2 - stage)) & 1
        picked = picked + (1 - ((kept + me // (1 << bit)) & 1)) * (depth << bit)
    column = lax.broadcasted_iota(jnp.int32, (channels, channels), 1)
    return to_low(jnp.where(picked == column, 1.0, 0.0))


class Copies:
    def __init__(self, send_sem, arrive_sem):
        self.send_sem, self.arrive_sem = send_sem, arrive_sem

    def to(self, device, source, target, send, arrive=None):
        return pltpu.make_async_remote_copy(
            src_ref=source,
            dst_ref=target,
            send_sem=self.send_sem.at[send],
            recv_sem=self.arrive_sem.at[send if arrive is None else arrive],
            device_id=device,
            device_id_type=MESH,
        )


def copy_sems(count):
    return [pltpu.SemaphoreType.DMA((count,))] * 2


def patch_bits():
    return lax.axis_size("pts").bit_length() - 1


def sibling():
    return {"tp": 1 - lax.axis_index("tp")}


def greet_sibling():
    barrier = pltpu.get_barrier_semaphore()
    pl.semaphore_signal(barrier, inc=1, device_id=sibling(), device_id_type=MESH)
    pl.semaphore_wait(barrier, 1)


def vmem():
    return pl.BlockSpec(memory_space=pltpu.VMEM)


def whole(array):
    zeros = (0,) * array.ndim
    return pl.BlockSpec(array.shape, lambda i: zeros, pipeline_mode=pl.Buffered(1))


def forward_kernel(
    near_ref,
    points_ref,
    weight_ref,
    encode_ref,
    encode_gain_ref,
    encode_shift_ref,
    attend_gain_ref,
    attend_shift_ref,
    heads_ref,
    output_ref,
    expand_ref,
    reduce_ref,
    bias_ref,
    window_out,
    conved_ref,
    linear_ref,
    first_ref,
    attend_ref,
    projected_ref,
    output_other,
    expand_other,
    reduce_other,
    bias_other,
    window,
    total,
    rows,
    encode_other,
    conved_other,
    attend_other,
    send_sem,
    arrive_sem,
):
    step = pl.program_id(0)
    local, channels = points_ref.shape
    blocks = near_ref.shape[0] // BLOCK
    patches = lax.axis_size("pts")
    me, side = lax.axis_index("pts"), lax.axis_index("tp")
    copies = Copies(send_sem, arrive_sem)
    own_rows = window.at[pl.ds(pl.multiple_of(HALO + side * local, HALO), local)]
    points_copy = copies.to(sibling(), points_ref, own_rows, 0)
    low_rim, high_rim = window.at[0:HALO], window.at[HALO + 2 * local :]
    low_copies = [
        copies.to({"pts": me + 1, "tp": core}, points_ref.at[local - HALO :], low_rim, 3 + core, 1)
        for core in range(2)
    ]
    high_copies = [
        copies.to({"pts": me - 1, "tp": core}, points_ref.at[0:HALO], high_rim, 3 + core, 2)
        for core in range(2)
    ]
    weight_copies = [
        copies.to(sibling(), encode_ref, encode_other, 5),
        copies.to(sibling(), output_ref, output_other, 6),
        copies.to(sibling(), expand_ref, expand_other, 7),
        copies.to(sibling(), reduce_ref, reduce_other, 8),
        copies.to(sibling(), bias_ref, bias_other, 9),
    ]

    @pl.when(step == 0)
    def _():
        barrier = pltpu.get_barrier_semaphore()
        pl.semaphore_signal(barrier, inc=1, device_id=sibling(), device_id_type=MESH)

        @pl.when(me > 0)
        def _():
            pl.semaphore_signal(
                barrier, inc=1, device_id={"pts": me - 1, "tp": 1}, device_id_type=MESH
            )

        @pl.when(me < patches - 1)
        def _():
            pl.semaphore_signal(
                barrier, inc=1, device_id={"pts": me + 1, "tp": 0}, device_id_type=MESH
            )

        up = (side == 1) & (me < patches - 1)
        down = (side == 0) & (me > 0)
        pl.semaphore_wait(barrier, jnp.where(up | down, 3, 1))
        points_copy.start()

        @pl.when(up)
        def _():
            for copy in low_copies:
                copy.start()

        @pl.when(down)
        def _():
            for copy in high_copies:
                copy.start()

        for copy in weight_copies:
            copy.start()
        own_rows[...] = points_ref[...]
        total[...] = jnp.zeros_like(total)

        @pl.when(me == 0)
        def _():
            low_rim[...] = jnp.zeros_like(low_rim)

        @pl.when(me == patches - 1)
        def _():
            high_rim[...] = jnp.zeros_like(high_rim)

        points_copy.wait()

        @pl.when(me > 0)
        def _():
            low_copies[0].wait_recv()

        @pl.when(me < patches - 1)
        def _():
            high_copies[0].wait_recv()

        @pl.when(up)
        def _():
            for copy in low_copies:
                copy.wait_send()

        @pl.when(down)
        def _():
            for copy in high_copies:
                copy.wait_send()

        window_out[...] = window[...]

    lane = lax.broadcasted_iota(jnp.int32, (BLOCK, near_ref.shape[1]), 1)
    slots = to_wide(lax.broadcasted_iota(jnp.int32, (BLOCK, 2 * BLOCK), 1))
    for block in range(blocks):
        part = window[block * BLOCK : (block + 2) * BLOCK, :]
        near = near_ref[block * BLOCK : (block + 1) * BLOCK, :]
        for offset in range(GROUP):
            chosen = jnp.where(lane == step * GROUP + offset, near, 0.0)
            column = jnp.sum(chosen, axis=1, keepdims=True) - float(block * BLOCK)
            select = to_low(jnp.where(column == slots, 1.0, 0.0))
            rows[
                block * BLOCK : (block + 1) * BLOCK,
                offset * channels : (offset + 1) * channels,
            ] = to_low(product(select, part, 1, 0))
    weight = weight_ref[...].reshape(GROUP * channels, weight_ref.shape[2])
    total[...] += product(rows[...], weight, 1, 0)

    @pl.when(step == pl.num_programs(0) - 1)
    def _():
        conved_ref[...] = to_low(total[...])
        mine = pl.ds(pl.multiple_of(side * local, local), local)
        theirs = pl.ds(pl.multiple_of((1 - side) * local, local), local)
        conved_copy = copies.to(sibling(), conved_ref.at[theirs], conved_other, 10)
        conved_copy.start()
        weight_copies[0].wait()
        linear = product(conved_ref[mine], encode_ref[...], 1, 0)
        conved_copy.wait()
        linear += product(conved_other[...], encode_other[...], 1, 0)
        linear_ref[...] = linear
        first = layer_norm(linear)[0] * encode_gain_ref[...] + encode_shift_ref[...]
        first += to_wide(points_ref[...])
        first_ref[...] = first
        attend_out = layer_norm(first)[0] * attend_gain_ref[...] + attend_shift_ref[...]
        attend_ref[0] = to_low(attend_out)
        attend_copy = copies.to(sibling(), attend_ref.at[0], attend_other, 11)
        attend_copy.start()
        turned = [heads_ref[index].T for index in range(3)]
        for index in range(3):
            projected_ref[index, :, :local] = to_low(product(turned[index], attend_ref[0], 1, 1))
        attend_copy.wait()
        attend_ref[1] = attend_other[...]
        for index in range(3):
            projected_ref[index, :, local:] = to_low(
                product(turned[index], attend_other[...], 1, 1)
            )
        for copy in weight_copies[1:]:
            copy.wait()


def forward_start(
    near, points, conv_weight, encode_weight, norms, heads_weight, output_weight, expand_weight,
    reduce_weight, expand_bias
):
    offsets, channels, width = conv_weight.shape
    local = points.shape[0]
    rows = 2 * local
    wide = rows + 2 * HALO
    low, full = jnp.bfloat16, jnp.float32
    shape = jax.ShapeDtypeStruct
    anywhere = pl.BlockSpec(memory_space=pl.ANY)
    outs = [
        shape((wide, channels), low),
        shape((rows, width), low),
        shape((local, channels), full),
        shape((local, channels), full),
        shape((2, local, channels), low),
        shape((3, width, rows), low),
    ]
    away = [
        shape(array.shape, array.dtype)
        for array in (output_weight, expand_weight, reduce_weight, expand_bias)
    ]
    return pl.pallas_call(
        forward_kernel,
        grid=(offsets // GROUP,),
        in_specs=[
            whole(near),
            whole(points),
            pl.BlockSpec((GROUP, channels, width), lambda i: (i, 0, 0)),
            whole(encode_weight),
            *[whole(norm) for norm in norms],
            whole(heads_weight),
            anywhere,
            anywhere,
            anywhere,
            anywhere,
        ],
        out_specs=[whole(out) for out in outs] + [anywhere] * 4,
        out_shape=outs + away,
        scratch_shapes=[
            pltpu.VMEM((wide, channels), low),
            pltpu.VMEM((rows, width), full),
            pltpu.VMEM((rows, GROUP * channels), low),
            pltpu.VMEM(encode_weight.shape, low),
            pltpu.VMEM((local, width), low),
            pltpu.VMEM((local, channels), low),
            *copy_sems(12),
        ],
        compiler_params=pltpu.CompilerParams(
            vmem_limit_bytes=48 << 20, collective_id=2, has_side_effects=True
        ),
        cost_estimate=pl.CostEstimate(
            flops=30 * 10**9, bytes_accessed=16 * 10**6, transcendentals=0
        ),
    )(
        near, points, conv_weight, encode_weight, *norms, heads_weight, output_weight,
        expand_weight, reduce_weight, expand_bias
    )


def staged(units, begin, finish):
    ready = begin(units[0])
    for index, unit in enumerate(units):
        later = begin(units[index + 1]) if index + 1 < len(units) else None
        finish(unit, ready)
        ready = later


def attend_kernel(chunk, query_ref, key_ref, value_ref, bias_ref, out_ref, log_ref):
    points = query_ref.shape[1]
    heads = query_ref.shape[0] // HEAD_DIM
    row = lax.broadcasted_iota(jnp.int32, (HEAD_DIM, points), 0)
    ones = to_low(jnp.where(row == 0, 1.0, 0.0))
    operands = []
    for head in range(heads):
        part = slice(head * HEAD_DIM, (head + 1) * HEAD_DIM)
        scaled = to_low(to_wide(query_ref[part]) * HEAD_DIM**-0.5)
        operands.append(
            (
                jnp.concatenate([scaled, ones], axis=0),
                jnp.concatenate([key_ref[part], bias_ref[...]], axis=0),
                jnp.concatenate([value_ref[part], ones], axis=0),
            )
        )

    def begin(unit):
        head, start = unit
        queries, keys, _ = operands[head]
        return product(keys, queries[:, start : start + chunk], 0, 0)

    def finish(unit, scores):
        head, start = unit
        top = jnp.max(scores, axis=0, keepdims=True)
        mixed = product(operands[head][2], to_low(jnp.exp(scores - top)), 1, 0)
        total = mixed[HEAD_DIM : HEAD_DIM + 1, :]
        out_ref[head * HEAD_DIM : (head + 1) * HEAD_DIM, start : start + chunk] = to_low(
            mixed[:HEAD_DIM] / total
        )
        log_ref[head, :, start : start + chunk] = top + jnp.log(total)

    staged([(h, c) for c in range(0, points, chunk) for h in range(heads)], begin, finish)


def attend(projected, bias):
    width, points = projected.shape[1:]
    heads = width // HEAD_DIM
    height = HEAD_DIM * HEADS_STEP
    return pl.pallas_call(
        functools.partial(attend_kernel, 512),
        grid=(heads // HEADS_STEP,),
        in_specs=[
            *[pl.BlockSpec((None, height, points), lambda i, j=j: (j, i, 0)) for j in range(3)],
            pl.BlockSpec(bias.shape, lambda i: (0, 0)),
        ],
        out_specs=[
            pl.BlockSpec((height, points), lambda i: (i, 0)),
            pl.BlockSpec((HEADS_STEP, 1, points), lambda i: (i, 0, 0)),
        ],
        out_shape=[
            jax.ShapeDtypeStruct((width, points), jnp.bfloat16),
            jax.ShapeDtypeStruct((heads, 1, points), jnp.float32),
        ],
        compiler_params=pltpu.CompilerParams(vmem_limit_bytes=48 << 20),
        cost_estimate=pl.CostEstimate(
            flops=36 * 10**9, bytes_accessed=3 * 10**6, transcendentals=0
        ),
    )(projected, projected, projected, bias)


def attend_back_kernel(
    chunk,
    query_ref,
    key_ref,
    value_ref,
    bias_ref,
    mixed_ref,
    log_ref,
    grad_ref,
    extra_ref,
    out_ref,
    sum_ref,
    key_total,
    value_total,
    *scratch,
):
    points = query_ref.shape[1]
    heads = query_ref.shape[0] // HEAD_DIM
    scale = HEAD_DIM**-0.5
    sums = pair_sums(scratch)
    half = sums.keep.shape[2]
    step = pl.program_id(0)

    @pl.when(step == 0)
    def _():
        pl.semaphore_wait(greet_partners(), KERNEL_BITS)
        for index in range(extra_ref.shape[0]):
            sums.sends[0][index] = to_low(extra_ref[index, :, :half])
            sums.start(0, index, ((True, ORDERS[index]),))
            sums.keep[index] = extra_ref[index, :, half:]

    for stage, due in enumerate(SUM_STEPS):

        @pl.when(step == due)
        def _(stage=stage):
            for index in range(extra_ref.shape[0]):
                sums.advance(stage, index, ((True, ORDERS[index]),), sum_ref)

    row = lax.broadcasted_iota(jnp.int32, (HEAD_DIM, points), 0)
    ones = to_low(jnp.where((row > 0) & (row < 4), 1.0, 0.0))

    def three_parts(values, lead):
        upper = to_wide(to_low(values))
        middle = to_wide(to_low(values - upper))
        lower = values - upper - middle
        tail = jnp.where(row == 1, -upper, jnp.where(row == 2, -middle, 0.0))
        tail = jnp.where(row == 3, -lower, tail)
        return to_low(jnp.where(row == 0, lead, tail))

    operands = []
    for head in range(heads):
        part = slice(head * HEAD_DIM, (head + 1) * HEAD_DIM)
        query, key, value, grad = query_ref[part], key_ref[part], value_ref[part], grad_ref[part]
        row_dot = column_sum(to_wide(grad) * to_wide(mixed_ref[part]))
        scaled = to_low(to_wide(query) * scale)
        operands.append(
            (
                jnp.concatenate([scaled, three_parts(log_ref[head], 1.0)], axis=0),
                jnp.concatenate([key, bias_ref[...] + ones], axis=0),
                jnp.concatenate([value, ones], axis=0),
                jnp.concatenate([grad, three_parts(row_dot, 0.0)], axis=0),
            )
        )

    def begin(unit):
        head, start = unit
        queries, keys, values, grads = operands[head]
        return (
            product(keys, queries[:, start : start + chunk], 0, 0),
            product(values, grads[:, start : start + chunk], 0, 0),
        )

    def finish(unit, ready):
        head, start = unit
        scores, prob_grad = ready
        part = slice(head * HEAD_DIM, (head + 1) * HEAD_DIM)
        now = slice(start, start + chunk)
        probs = jnp.exp(scores)
        score_grad = to_low(probs * prob_grad)
        out_ref[0, part, now] = to_low(product(key_ref[part], score_grad, 1, 0) * scale)
        value_part = product(grad_ref[part, now], to_low(probs), 1, 1)
        key_part = product(query_ref[part, now], score_grad, 1, 1)
        if start == 0:
            value_total[head] = value_part
            key_total[head] = key_part
        else:
            value_total[head] += value_part
            key_total[head] += key_part

    staged([(h, c) for c in range(0, points, chunk) for h in range(heads)], begin, finish)
    for head in range(heads):
        part = slice(head * HEAD_DIM, (head + 1) * HEAD_DIM)
        out_ref[1, part] = to_low(key_total[head] * scale)
        out_ref[2, part] = to_low(value_total[head])


def attend_back(projected, bias, mixed, logs, grads, extra):
    width, points = projected.shape[1:]
    heads = width // HEAD_DIM
    height = HEAD_DIM * HEADS_BACK_STEP
    block = pl.BlockSpec((height, points), lambda i: (i, 0))
    summed = (*extra.shape[:2], extra.shape[2] >> KERNEL_BITS, extra.shape[3])
    outs = [
        jax.ShapeDtypeStruct((3, width, points), jnp.bfloat16),
        jax.ShapeDtypeStruct(summed, jnp.float32),
    ]
    return pl.pallas_call(
        functools.partial(attend_back_kernel, 512),
        grid=(heads // HEADS_BACK_STEP,),
        in_specs=[
            *[pl.BlockSpec((None, height, points), lambda i, j=j: (j, i, 0)) for j in range(3)],
            pl.BlockSpec(bias.shape, lambda i: (0, 0)),
            block,
            pl.BlockSpec((HEADS_BACK_STEP, 1, points), lambda i: (i, 0, 0)),
            block,
            whole(extra),
        ],
        out_specs=[pl.BlockSpec((3, height, points), lambda i: (0, i, 0)), whole(outs[1])],
        out_shape=outs,
        scratch_shapes=[pltpu.VMEM((HEADS_BACK_STEP, HEAD_DIM, points), jnp.float32)] * 2
        + pair_scratch(*extra.shape),
        compiler_params=pltpu.CompilerParams(
            vmem_limit_bytes=48 << 20, collective_id=0, has_side_effects=True
        ),
        cost_estimate=pl.CostEstimate(
            flops=50 * 10**9, bytes_accessed=5 * 10**6, transcendentals=0
        ),
    )(projected, projected, projected, bias, mixed, logs, grads, extra)


def feed_kernel(
    mixed_ref,
    first_ref,
    output_ref,
    output_other_ref,
    output_bias_ref,
    gain_ref,
    shift_ref,
    cotangent_ref,
    expand_ref,
    expand_other_ref,
    bias_ref,
    bias_other_ref,
    reduce_ref,
    reduce_other_ref,
    reduce_bias_ref,
    result_ref,
    second_grad_ref,
    mixed_grad_ref,
    sums_ref,
    vectors_ref,
    bias_grad_ref,
    mixed_other,
    second_own,
    second_other,
    away,
    arrived,
    send_sem,
    arrive_sem,
):
    local, channels = first_ref.shape
    width = output_ref.shape[0]
    hidden_width = bias_ref.shape[1]
    columns = hidden_width // 2
    copies = Copies(send_sem, arrive_sem)
    greet_sibling()
    mixed_copy = copies.to(sibling(), mixed_ref.at[:, local:], mixed_other, 0)
    mixed_copy.start()
    cotangent = cotangent_ref[...]
    cotangent_turned = to_low(product(nested_picks(channels, ORDERS[0]), cotangent, 1, 1))
    second = first_ref[...] + output_bias_ref[...]
    second += product(mixed_ref[:, :local], output_ref[...], 0, 0)
    mixed_copy.wait()
    second += product(mixed_other[...], output_other_ref[...], 0, 0)
    normal, inverse = layer_norm(second)
    feed_low = to_low(normal * gain_ref[...] + shift_ref[...])
    feed_turned = to_low(product(nested_picks(channels, ORDERS[1]), feed_low, 1, 1))
    result = second + reduce_bias_ref[...]
    feed_grad = jnp.zeros_like(second)
    weight_copies = []
    for index, (up_ref, up_bias_ref, down_ref) in enumerate(
        (
            (expand_other_ref, bias_other_ref, reduce_other_ref),
            (expand_ref, bias_ref, reduce_ref),
        )
    ):
        for start in range(0, hidden_width, columns):
            now = slice(start, start + columns)
            hidden = product(feed_low, up_ref[:, now], 1, 0) + up_bias_ref[:, now]
            below = 0.5 + 0.5 * lax.erf(hidden * 0.5**0.5)
            slope = below + hidden * (jnp.exp(-0.5 * hidden * hidden) * (0.5 / jnp.pi) ** 0.5)
            active = to_low(hidden * below)
            hidden_grad = to_low(product(cotangent, down_ref[now, :], 1, 1) * slope)
            result += product(active, down_ref[now, :], 1, 0)
            feed_grad += product(hidden_grad, up_ref[:, now], 1, 1)
            bias_grad_ref[index : index + 1, now] = column_sum(to_wide(hidden_grad))
            reduce_grad = product(cotangent_turned, active, 1, 0)
            expand_grad = product(feed_turned, hidden_grad, 1, 0)
            if index == 0:
                away[0, :, now] = reduce_grad
                away[1, :, now] = expand_grad
                for kind in range(2):
                    copy = copies.to(
                        sibling(),
                        away.at[kind, :, now],
                        arrived.at[kind, :, now],
                        2 + len(weight_copies),
                    )
                    copy.start()
                    weight_copies.append(copy)
            else:
                sums_ref[0, :, now] = reduce_grad
                sums_ref[1, :, now] = expand_grad
    result_ref[...] = to_low(result)
    upstream = to_wide(cotangent)
    second_grad = upstream + norm_back(feed_grad, normal, inverse, gain_ref[...])
    second_grad_ref[...] = second_grad
    second_own[...] = to_low(second_grad)
    second_copy = copies.to(sibling(), second_own, second_other, 1)
    second_copy.start()
    vectors_ref[0:1] = column_sum(second_grad)
    vectors_ref[1:2] = column_sum(feed_grad * normal)
    vectors_ref[2:3] = column_sum(feed_grad)
    vectors_ref[3:4] = column_sum(upstream)
    mixed_grad_ref[:, :local] = to_low(product(output_ref[...], second_own[...], 1, 1))
    picks = [nested_picks(channels, order) for order in ORDERS[:2]]
    part = width // 2
    for kind in range(2):
        turned = to_low(product(picks[kind], second_own[...], 1, 1))
        sums_ref[kind, :, hidden_width:] = product(
            turned, mixed_ref[kind * part : (kind + 1) * part, :local], 1, 1
        )
    second_copy.wait()
    mixed_grad_ref[:, local:] = to_low(product(output_ref[...], second_other[...], 1, 1))
    for kind in range(2):
        turned = to_low(product(picks[kind], second_other[...], 1, 1))
        sums_ref[kind, :, hidden_width:] += product(
            turned, mixed_ref[kind * part : (kind + 1) * part, local:], 1, 1
        )
    for copy in weight_copies:
        copy.wait()
    sums_ref[:, :, :hidden_width] += arrived[...]


def feed(operands):
    local, channels = operands[1].shape
    width, rows = operands[0].shape
    hidden = operands[10].shape[1]
    low, full = jnp.bfloat16, jnp.float32
    shape = jax.ShapeDtypeStruct
    return pl.pallas_call(
        feed_kernel,
        in_specs=[vmem()] * len(operands),
        out_specs=[vmem()] * 6,
        out_shape=[
            shape((local, channels), low),
            shape((local, channels), full),
            shape((width, rows), low),
            shape((2, channels, hidden + width // 2), full),
            shape((4, channels), full),
            shape((2, hidden), full),
        ],
        scratch_shapes=[
            pltpu.VMEM((width, local), low),
            pltpu.VMEM((local, channels), low),
            pltpu.VMEM((local, channels), low),
            pltpu.VMEM((2, channels, hidden), full),
            pltpu.VMEM((2, channels, hidden), full),
            *copy_sems(6),
        ],
        compiler_params=pltpu.CompilerParams(
            vmem_limit_bytes=56 << 20, collective_id=3, has_side_effects=True
        ),
        cost_estimate=pl.CostEstimate(
            flops=10 * 10**9, bytes_accessed=16 * 10**6, transcendentals=0
        ),
    )(*operands)


def return_kernel(
    grad_ref,
    heads_ref,
    attend_ref,
    second_grad_ref,
    first_ref,
    linear_ref,
    attend_gain_ref,
    encode_gain_ref,
    encode_ref,
    conved_ref,
    first_grad_ref,
    conved_grad_ref,
    extra_ref,
    vectors_ref,
    attend_away,
    attend_arrived,
    linear_own,
    linear_other,
    send_sem,
    arrive_sem,
):
    local, channels = first_ref.shape
    side = lax.axis_index("tp")
    mine = pl.ds(pl.multiple_of(side * local, local), local)
    theirs = pl.ds(pl.multiple_of((1 - side) * local, local), local)
    copies = Copies(send_sem, arrive_sem)

    def attend_grad(start):
        return sum(
            product(grad_ref[index, :, start : start + local].T, heads_ref[index], 1, 1)
            for index in range(3)
        )

    attend_away[...] = attend_grad(local)
    greet_sibling()
    attend_copy = copies.to(sibling(), attend_away, attend_arrived, 0)
    attend_copy.start()
    upstream = attend_grad(0)
    picks = [nested_picks(channels, order) for order in ORDERS[2:]]
    for kind in range(2):
        turned = [to_low(product(picks[kind], attend_ref[i], 1, 1)) for i in range(2)]
        for index in (0, 1) if kind == 0 else (2,):
            extra_ref[kind, index % 2] = product(
                turned[0], grad_ref[index, :, :local], 1, 1
            ) + product(turned[1], grad_ref[index, :, local:], 1, 1)
    normal, inverse = layer_norm(first_ref[...])
    attend_copy.wait()
    upstream += attend_arrived[...]
    first_grad = second_grad_ref[...] + norm_back(upstream, normal, inverse, attend_gain_ref[...])
    first_grad_ref[...] = first_grad
    vectors_ref[0:1] = column_sum(upstream * normal)
    vectors_ref[1:2] = column_sum(upstream)
    normal, inverse = layer_norm(linear_ref[...])
    linear_own[...] = to_low(norm_back(first_grad, normal, inverse, encode_gain_ref[...]))
    linear_copy = copies.to(sibling(), linear_own, linear_other, 1)
    linear_copy.start()
    vectors_ref[2:3] = column_sum(first_grad * normal)
    vectors_ref[3:4] = column_sum(first_grad)
    conved_grad_ref[mine] = to_low(product(linear_own[...], encode_ref[...], 1, 1))
    turned = to_low(product(picks[1], linear_own[...], 1, 1))
    extra_ref[1, 1] = product(turned, conved_ref[mine], 1, 0)
    linear_copy.wait()
    conved_grad_ref[theirs] = to_low(product(linear_other[...], encode_ref[...], 1, 1))
    turned = to_low(product(picks[1], linear_other[...], 1, 1))
    extra_ref[1, 1] += product(turned, conved_ref[theirs], 1, 0)


def return_to_conv(operands):
    local, channels = operands[4].shape
    rows, width = operands[9].shape
    low, full = jnp.bfloat16, jnp.float32
    shape = jax.ShapeDtypeStruct
    return pl.pallas_call(
        return_kernel,
        in_specs=[vmem()] * len(operands),
        out_specs=[vmem()] * 4,
        out_shape=[
            shape((local, channels), full),
            shape((rows, width), low),
            shape((2, 2, channels, width), full),
            shape((4, channels), full),
        ],
        scratch_shapes=[
            pltpu.VMEM((local, channels), full),
            pltpu.VMEM((local, channels), full),
            pltpu.VMEM((local, channels), low),
            pltpu.VMEM((local, channels), low),
            *copy_sems(2),
        ],
        compiler_params=pltpu.CompilerParams(
            vmem_limit_bytes=48 << 20, collective_id=4, has_side_effects=True
        ),
        cost_estimate=pl.CostEstimate(
            flops=6 * 10**9, bytes_accessed=12 * 10**6, transcendentals=0
        ),
    )(*operands)


def partner_of(bit):
    me = lax.axis_index("pts")
    return me + (1 - 2 * ((me // (1 << bit)) % 2)) * (1 << bit)


def greet_partners():
    barrier = pltpu.get_barrier_semaphore()
    for bit in range(KERNEL_BITS):
        pl.semaphore_signal(
            barrier, inc=1, device_id={"pts": partner_of(bit)}, device_id_type=MESH
        )
    return barrier


class PairSums:
    def __init__(self, keep, sends, arrivals, send_sem, arrive_sem):
        self.keep, self.sends, self.arrivals = keep, sends, arrivals
        self.send_sem, self.arrive_sem = send_sem, arrive_sem

    def copy(self, stage, chunk, bit):
        return pltpu.make_async_remote_copy(
            src_ref=self.sends[stage].at[chunk],
            dst_ref=self.arrivals[stage].at[chunk],
            send_sem=self.send_sem.at[stage, chunk],
            recv_sem=self.arrive_sem.at[stage, chunk],
            device_id={"pts": partner_of(bit)},
            device_id_type=MESH,
        )

    def start(self, stage, chunk, kinds):
        for holds, order in kinds:
            if holds is True:
                self.copy(stage, chunk, order[stage]).start()
            else:

                @pl.when(holds)
                def _(order=order):
                    self.copy(stage, chunk, order[stage]).start()

    def advance(self, stage, chunk, kinds, out_ref):
        self.copy(stage, chunk, 0).wait()
        rows = self.keep.shape[2]
        low = rows - (rows >> stage)
        half = (rows - low) // 2
        arrived = self.arrivals[stage]
        if stage == KERNEL_BITS - 1:
            out_ref[chunk] = self.keep[chunk, :, low:] + to_wide(arrived[chunk])
            return
        self.sends[stage + 1][chunk] = to_low(
            self.keep[chunk, :, low : low + half] + to_wide(arrived[chunk, :, :half])
        )
        self.start(stage + 1, chunk, kinds)
        self.keep[chunk, :, low + half :] += to_wide(arrived[chunk, :, half:])


def pair_scratch(chunks, lead, rows, width):
    halves = [(chunks, lead, rows >> (stage + 1), width) for stage in range(KERNEL_BITS)]
    return (
        [pltpu.VMEM(halves[0], jnp.float32)]
        + [pltpu.VMEM(shape, jnp.bfloat16) for shape in halves]
        + [pltpu.VMEM(shape, jnp.bfloat16) for shape in halves]
        + [pltpu.SemaphoreType.DMA((KERNEL_BITS, chunks))] * 2
    )


def pair_sums(scratch):
    keep, rest = scratch[0], scratch[1:]
    return PairSums(keep, rest[:KERNEL_BITS], rest[KERNEL_BITS : 2 * KERNEL_BITS], *rest[-2:])


def conv_backward_kernel(
    near_ref,
    window_ref,
    grad_ref,
    weight_ref,
    extra_ref,
    vector_ref,
    first_grad_ref,
    sum_ref,
    extra_sum_ref,
    vector_out_ref,
    points_grad_ref,
    spread,
    window_turned,
    input_grad,
    input_away,
    input_arrived,
    rim_away,
    rim_arrived,
    vector_away,
    vector_arrived,
    send_sem,
    arrive_sem,
    *scratch,
):
    rows, width = grad_ref.shape
    local, channels = first_grad_ref.shape
    blocks = rows // BLOCK
    extras = extra_ref.shape[0]
    chunks = sum_ref.shape[0]
    patches = lax.axis_size("pts")
    me, side = lax.axis_index("pts"), lax.axis_index("tp")
    step = pl.program_id(0)
    middle = len(scratch) // 2
    sums, extra_sums = pair_sums(scratch[:middle]), pair_sums(scratch[middle:])
    half = channels // 2
    copies = Copies(send_sem, arrive_sem)
    share = local + HALO
    input_copy = copies.to(sibling(), input_away, input_arrived, 0)
    rim_copies = [
        copies.to({"pts": me - 1, "tp": 1}, rim_away, rim_arrived, 1),
        copies.to({"pts": me + 1, "tp": 0}, rim_away, rim_arrived, 1),
    ]
    has_rim = [(side == 0) & (me > 0), (side == 1) & (me < patches - 1)]

    def vector_copy(stage):
        device = sibling() if stage == 0 else {"pts": partner_of(stage - 1)}
        return copies.to(device, vector_away.at[stage], vector_arrived.at[stage], 2 + stage)

    def kinds(chunk):
        return ((chunk % 2 == 0, ORDERS[0]), (chunk % 2 == 1, ORDERS[1]))

    @pl.when(step == 0)
    def _():
        barrier = greet_partners()
        pl.semaphore_signal(barrier, inc=1, device_id=sibling(), device_id_type=MESH)
        for has, device in zip(has_rim, ({"pts": me - 1, "tp": 1}, {"pts": me + 1, "tp": 0})):

            @pl.when(has)
            def _(device=device):
                pl.semaphore_signal(barrier, inc=1, device_id=device, device_id_type=MESH)

        rims = jnp.where(has_rim[0] | has_rim[1], 1, 0)
        pl.semaphore_wait(barrier, KERNEL_BITS + 1 + rims)
        for index in range(extras):
            extra_sums.sends[0][index] = to_low(extra_ref[index, :, :half])
            extra_sums.start(0, index, ((True, ORDERS[2 + index]),))
            extra_sums.keep[index] = extra_ref[index, :, half:]
        vector_away[0] = vector_ref[...]
        vector_copy(0).start()
        for index in range(2):
            window_turned[index] = to_low(
                product(nested_picks(channels, ORDERS[index]), window_ref[...], 1, 1)
            )
        input_grad[...] = jnp.zeros_like(input_grad)

    @pl.when(step < chunks)
    def _():
        slots = to_wide(lax.broadcasted_iota(jnp.int32, (BLOCK, 1), 0))
        for offset in range(GROUP):
            near = near_ref[pl.ds(step * GROUP + offset, 1), :]
            for part in range(blocks + 1):
                low = max(part - 1, 0) * BLOCK
                high = min(part + 1, blocks) * BLOCK
                select = to_low(
                    jnp.where(near[:, low:high] - float(part * BLOCK) == slots, 1.0, 0.0)
                )
                spread[
                    part * BLOCK : (part + 1) * BLOCK, offset * width : (offset + 1) * width
                ] = to_low(product(select, grad_ref[low:high, :], 1, 0))
        for offset in range(GROUP):
            weight_grad = product(
                window_turned[step % 2], spread[:, offset * width : (offset + 1) * width], 1, 0
            )
            sums.sends[0][step, offset] = to_low(weight_grad[:half])
            sums.keep[step, offset] = weight_grad[half:]
        sums.start(0, step, kinds(step))
        for offset in range(GROUP):
            input_grad[...] += product(
                spread[:, offset * width : (offset + 1) * width], weight_ref[offset], 1, 1
            )

    for stage, due in enumerate(VECTOR_STEPS):

        @pl.when(step == due)
        def _(stage=stage):
            vector_copy(stage).wait()
            summed = vector_away[stage] + vector_arrived[stage]
            if stage < KERNEL_BITS:
                vector_away[stage + 1] = summed
                vector_copy(stage + 1).start()
            else:
                vector_out_ref[...] = summed

    @pl.when(step == INPUT_STEPS[0])
    def _():
        theirs = pl.ds(pl.multiple_of((1 - side) * share, HALO), share)
        input_away[...] = input_grad[theirs, :]
        input_copy.start()

    @pl.when(step == INPUT_STEPS[1])
    def _():
        input_copy.wait()
        mine = pl.ds(pl.multiple_of(side * share, HALO), share)
        input_arrived[...] += input_grad[mine, :]
        rim_away[...] = to_low(
            input_arrived[pl.ds(pl.multiple_of(side * local, HALO), HALO), :]
        )
        for has, copy in zip(has_rim, rim_copies):

            @pl.when(has)
            def _(copy=copy):
                copy.start()

    @pl.when(step == INPUT_STEPS[2])
    def _():
        inner = pl.ds(pl.multiple_of((1 - side) * HALO, HALO), local)
        points_grad_ref[...] = first_grad_ref[...] + input_arrived[inner, :]
        edge = pl.ds(pl.multiple_of(side * (local - HALO), HALO), HALO)
        for has, copy in zip(has_rim, rim_copies):

            @pl.when(has)
            def _(copy=copy):
                copy.wait()
                points_grad_ref[edge, :] += to_wide(rim_arrived[...])

    for stage in range(KERNEL_BITS):
        chunk = step - CONV_LAGS[stage]

        @pl.when((chunk >= 0) & (chunk < chunks))
        def _(stage=stage, chunk=chunk):
            sums.advance(stage, chunk, kinds(chunk), sum_ref)

        @pl.when(step == EXTRA_STEPS[stage])
        def _(stage=stage):
            for index in range(extras):
                extra_sums.advance(stage, index, ((True, ORDERS[2 + index]),), extra_sum_ref)


def conv_backward(near, window, grad, weight, extra, vector, first_grad):
    offsets, channels, width = weight.shape
    wide = window.shape[0]
    local = first_grad.shape[0]
    chunks = offsets // GROUP
    low, full = jnp.bfloat16, jnp.float32
    outs = [
        jax.ShapeDtypeStruct((chunks, GROUP, channels >> KERNEL_BITS, width), full),
        jax.ShapeDtypeStruct((*extra.shape[:2], channels >> KERNEL_BITS, width), full),
        jax.ShapeDtypeStruct(vector.shape, full),
        jax.ShapeDtypeStruct(first_grad.shape, full),
    ]
    return pl.pallas_call(
        conv_backward_kernel,
        grid=(chunks + CONV_LAGS[-1],),
        in_specs=[
            whole(near),
            whole(window),
            whole(grad),
            pl.BlockSpec((GROUP, channels, width), lambda i: (jnp.minimum(i, chunks - 1), 0, 0)),
            whole(extra),
            whole(vector),
            whole(first_grad),
        ],
        out_specs=[whole(out) for out in outs],
        out_shape=outs,
        scratch_shapes=[
            pltpu.VMEM((wide, GROUP * width), low),
            pltpu.VMEM((2, channels, wide), low),
            pltpu.VMEM((wide, channels), full),
            pltpu.VMEM((local + HALO, channels), full),
            pltpu.VMEM((local + HALO, channels), full),
            pltpu.VMEM((HALO, channels), low),
            pltpu.VMEM((HALO, channels), low),
            pltpu.VMEM((KERNEL_BITS + 1, *vector.shape), full),
            pltpu.VMEM((KERNEL_BITS + 1, *vector.shape), full),
            *copy_sems(3 + KERNEL_BITS),
            *pair_scratch(chunks, GROUP, channels, width),
            *pair_scratch(*extra.shape),
        ],
        compiler_params=pltpu.CompilerParams(
            vmem_limit_bytes=58 << 20, collective_id=1, has_side_effects=True
        ),
        cost_estimate=pl.CostEstimate(
            flops=80 * 10**9, bytes_accessed=16 * 10**6, transcendentals=0
        ),
    )(near, window, grad, weight, extra, vector, first_grad)


def exchange(values, bit):
    count = lax.axis_size("pts")
    return lax.ppermute(values, "pts", [(i, i ^ (1 << bit)) for i in range(count)])


def sum_rest(keep):
    for bit in range(KERNEL_BITS, patch_bits()):
        half = keep.shape[-2] // 2
        keep = keep[..., half:, :] + to_wide(exchange(to_low(keep[..., :half, :]), bit))
    return keep


def per_device(
    points,
    neighbours,
    valid_count,
    conv_weight,
    encode_weight,
    encode_gain,
    encode_shift,
    attend_gain,
    attend_shift,
    heads_weight,
    output_weight,
    output_bias,
    feed_gain,
    feed_shift,
    expand_weight,
    expand_bias,
    reduce_weight,
    reduce_bias,
    cotangent,
):
    local, channels = points.shape
    rows = 2 * local
    is_first = lax.axis_index("tp") == 0
    near = to_wide(neighbours)
    norms = [v[None, :] for v in (encode_gain, encode_shift, attend_gain, attend_shift)]
    (
        window, conved, linear, first, attend_in, projected,
        output_other, expand_other, reduce_other, bias_other,
    ) = forward_start(
        near, points, conv_weight, encode_weight, norms, heads_weight, output_weight,
        expand_weight, reduce_weight, expand_bias[None, :]
    )

    place = jnp.arange(rows, dtype=jnp.int32)
    place = jnp.where(is_first, place, (place + local) % rows)
    bias = jnp.where(place < valid_count[0], 0.0, MASKED)
    bias = to_low(jnp.where(jnp.arange(HEAD_DIM)[:, None] == 0, bias[None, :], 0.0))
    mixed, logs = attend(projected, bias)
    result, second_grad, mixed_grad, feed_grads, feed_vectors, bias_grads = feed(
        [
            mixed, first, output_weight, output_other, output_bias[None, :], feed_gain[None, :],
            feed_shift[None, :], cotangent, expand_weight, expand_other, expand_bias[None, :],
            bias_other, reduce_weight, reduce_other, reduce_bias[None, :],
        ]
    )
    projected_grad, feed_sums = attend_back(
        projected, bias, mixed, logs, mixed_grad, feed_grads[:, None]
    )
    first_grad, conved_grad, extra, return_vectors = return_to_conv(
        [
            projected_grad, heads_weight, attend_in, second_grad, first, linear, norms[2],
            norms[0], encode_weight, conved,
        ]
    )
    own, other = bias_grads[1], bias_grads[0]
    vector = jnp.concatenate(
        [
            feed_vectors.reshape(-1),
            return_vectors.reshape(-1),
            jnp.where(is_first, own, other),
            jnp.where(is_first, other, own),
        ]
    ).reshape(-1, 128)
    weight_sums, extra_sums, vector, points_gradient = conv_backward(
        near.T, window, conved_grad, conv_weight, extra, vector, first_grad
    )
    for bit in range(KERNEL_BITS, patch_bits()):
        vector = vector + exchange(vector, bit)
    vectors = jnp.split(vector.reshape(-1), [channels * i for i in range(1, 9)])
    feed_sums = sum_rest(feed_sums)[:, 0]
    weight_sums = sum_rest(weight_sums)
    extra_sums = sum_rest(extra_sums)
    hidden = expand_weight.shape[1]
    output_sums = jnp.concatenate([feed_sums[0, :, hidden:], feed_sums[1, :, hidden:]], axis=1)
    return (
        result,
        points_gradient,
        weight_sums.reshape(-1, *weight_sums.shape[2:]),
        extra_sums[1, 1].T,
        vectors[6],
        vectors[7],
        vectors[4],
        vectors[5],
        extra_sums.reshape(-1, *extra_sums.shape[2:])[:3],
        output_sums.T,
        vectors[0],
        vectors[1],
        vectors[2],
        feed_sums[1, :, :hidden],
        vectors[8],
        feed_sums[0, :, :hidden].T,
        vectors[3],
    )


def solution(mesh):
    placed = (
        P(("pts", "tp"), None),
        P("pts", None),
        P("pts"),
        P(None, None, "tp"),
        P("tp", None),
        P(),
        P(),
        P(),
        P(),
        P(None, None, "tp"),
        P("tp", None),
        P(),
        P(),
        P(),
        P(None, "tp"),
        P("tp"),
        P("tp", None),
        P(),
        P(("pts", "tp"), None),
    )
    return jax.shard_map(
        per_device,
        mesh=mesh,
        in_specs=placed,
        out_specs=(
            P(("pts", "tp"), None),
            P(("pts", "tp"), None),
            P(None, "pts", "tp"),
            P("tp", "pts"),
            P(),
            P(),
            P(),
            P(),
            P(None, "pts", "tp"),
            P("tp", "pts"),
            P(),
            P(),
            P(),
            P("pts", "tp"),
            P(),
            P("tp", "pts"),
            P(),
        ),
        check_vma=False,
    )
```

```python
import functools

import jax
import jax.numpy as jnp
from jax import lax
from jax.experimental import pallas as pl
from jax.experimental.pallas import tpu as pltpu
from jax.sharding import PartitionSpec as P

MESH = pl.DeviceIdType.MESH
HEAD_DIM = 16
HALO = 128
BLOCK = 256
GROUP = 3
EPSILON = 1e-05
MASKED = -1e30
KERNEL_BITS = 4
ORDERS = ((0, 1, 2, 3), (1, 0, 2, 3))
VMEM_BYTES = 60 << 20
HEADS_STEP = 4
HEADS_BACK_STEP = 2
SUM_STEPS = (3, 5, 6, 7)
SHARE_BIT = 2
CONV_ORDERS = ((0, 1, 3), (1, 0, 3))
EXTRA_ORDERS = ((2, 0, 1, 3), (2, 1, 0, 3))
CONV_LAGS = (2, 4, 6)
EXTRA_STEPS = (3, 4, 5, 6)
VECTOR_STEPS = (1, 2, 3, 4, 5)
WIDE_GROUP = 9


def to_low(values):
    return values.astype(jnp.bfloat16)


def to_wide(values):
    return values.astype(jnp.float32)


def product(left, right, left_dim, right_dim):
    dims = (((left_dim,), (right_dim,)), ((), ()))
    return lax.dot_general(left, right, dims, preferred_element_type=jnp.float32)


def layer_norm(values):
    row_mean = jnp.mean(values, axis=-1, keepdims=True)
    centred = values - row_mean
    inverse = lax.rsqrt(jnp.mean(centred * centred, axis=-1, keepdims=True) + EPSILON)
    return centred * inverse, inverse


def norm_back(upstream, normal_part, inverse, norm_gain):
    scaled = upstream * norm_gain
    across = (
        scaled
        - jnp.mean(scaled, axis=-1, keepdims=True)
        - normal_part * jnp.mean(scaled * normal_part, axis=-1, keepdims=True)
    )
    return across * inverse


def column_sum(values):
    return jnp.sum(values, axis=0, keepdims=True)


def nested_picks(channels, order):
    me = lax.axis_index("pts")
    order = order + tuple(range(KERNEL_BITS, patch_bits()))
    depth = channels >> len(order)
    place = lax.broadcasted_iota(jnp.int32, (channels, channels), 0)
    picked = place & (depth - 1)
    for stage, bit in enumerate(order):
        kept = (place >> (channels.bit_length() - 2 - stage)) & 1
        picked = picked + (1 - ((kept + me // (1 << bit)) & 1)) * (depth << bit)
    column = lax.broadcasted_iota(jnp.int32, (channels, channels), 1)
    return to_low(jnp.where(picked == column, 1.0, 0.0))


class Copies:
    def __init__(self, send_sem, arrive_sem):
        self.send_sem, self.arrive_sem = send_sem, arrive_sem

    def to(self, device, source, target, send, arrive=None):
        return pltpu.make_async_remote_copy(
            src_ref=source,
            dst_ref=target,
            send_sem=self.send_sem.at[send],
            recv_sem=self.arrive_sem.at[send if arrive is None else arrive],
            device_id=device,
            device_id_type=MESH,
        )


def copy_sems(count):
    return [pltpu.SemaphoreType.DMA((count,))] * 2


def patch_bits():
    return lax.axis_size("pts").bit_length() - 1


def sibling():
    return {"tp": 1 - lax.axis_index("tp")}


def greet_sibling():
    barrier = pltpu.get_barrier_semaphore()
    pl.semaphore_signal(barrier, inc=1, device_id=sibling(), device_id_type=MESH)
    pl.semaphore_wait(barrier, 1)


def vmem():
    return pl.BlockSpec(memory_space=pltpu.VMEM)


def whole(array):
    zeros = (0,) * array.ndim
    return pl.BlockSpec(array.shape, lambda i: zeros, pipeline_mode=pl.Buffered(1))


def forward_kernel(
    near_ref,
    points_ref,
    weight_ref,
    encode_ref,
    encode_gain_ref,
    encode_shift_ref,
    attend_gain_ref,
    attend_shift_ref,
    heads_ref,
    output_ref,
    expand_ref,
    reduce_ref,
    bias_ref,
    turned_ref,
    conved_ref,
    linear_ref,
    first_ref,
    attend_ref,
    projected_ref,
    output_other,
    expand_other,
    reduce_other,
    bias_other,
    window,
    total,
    rows,
    encode_other,
    conved_other,
    attend_other,
    send_sem,
    arrive_sem,
):
    step = pl.program_id(0)
    local, channels = points_ref.shape
    blocks = near_ref.shape[0] // BLOCK
    patches = lax.axis_size("pts")
    me, side = lax.axis_index("pts"), lax.axis_index("tp")
    copies = Copies(send_sem, arrive_sem)
    own_rows = window.at[pl.ds(pl.multiple_of(HALO + side * local, HALO), local)]
    points_copy = copies.to(sibling(), points_ref, own_rows, 0)
    low_rim, high_rim = window.at[0:HALO], window.at[HALO + 2 * local :]
    low_copies = [
        copies.to({"pts": me + 1, "tp": core}, points_ref.at[local - HALO :], low_rim, 3 + core, 1)
        for core in range(2)
    ]
    high_copies = [
        copies.to({"pts": me - 1, "tp": core}, points_ref.at[0:HALO], high_rim, 3 + core, 2)
        for core in range(2)
    ]
    weight_copies = [
        copies.to(sibling(), encode_ref, encode_other, 5),
        copies.to(sibling(), output_ref, output_other, 6),
        copies.to(sibling(), expand_ref, expand_other, 7),
        copies.to(sibling(), reduce_ref, reduce_other, 8),
        copies.to(sibling(), bias_ref, bias_other, 9),
    ]

    up = (side == 1) & (me < patches - 1)
    down = (side == 0) & (me > 0)

    @pl.when(step == 0)
    def _():
        barrier = pltpu.get_barrier_semaphore()
        pl.semaphore_signal(barrier, inc=1, device_id=sibling(), device_id_type=MESH)

        @pl.when(me > 0)
        def _():
            pl.semaphore_signal(
                barrier, inc=1, device_id={"pts": me - 1, "tp": 1}, device_id_type=MESH
            )

        @pl.when(me < patches - 1)
        def _():
            pl.semaphore_signal(
                barrier, inc=1, device_id={"pts": me + 1, "tp": 0}, device_id_type=MESH
            )

        pl.semaphore_wait(barrier, jnp.where(up | down, 3, 1))
        points_copy.start()

        @pl.when(up)
        def _():
            for copy in low_copies:
                copy.start()

        @pl.when(down)
        def _():
            for copy in high_copies:
                copy.start()

        own_rows[...] = points_ref[...]
        total[...] = jnp.zeros_like(total)

        @pl.when(me == 0)
        def _():
            low_rim[...] = jnp.zeros_like(low_rim)

        @pl.when(me == patches - 1)
        def _():
            high_rim[...] = jnp.zeros_like(high_rim)

        points_copy.wait()
        for copy in weight_copies:
            copy.start()

    def wait_rims():
        @pl.when(me > 0)
        def _():
            low_copies[0].wait_recv()

        @pl.when(me < patches - 1)
        def _():
            high_copies[0].wait_recv()

        @pl.when(up)
        def _():
            for copy in low_copies:
                copy.wait_send()

        @pl.when(down)
        def _():
            for copy in high_copies:
                copy.wait_send()

        turned_ref[...] = to_low(
            product(nested_picks(channels, EXTRA_ORDERS[0]), window[...], 1, 1)
        )

    lane = lax.broadcasted_iota(jnp.int32, (BLOCK, near_ref.shape[1]), 1)
    slots = to_wide(lax.broadcasted_iota(jnp.int32, (BLOCK, 2 * BLOCK), 1))
    for block in (*range(1, blocks - 1), 0, blocks - 1):
        if block == 0:
            pl.when(step == 0)(wait_rims)
        part = window[block * BLOCK : (block + 2) * BLOCK, :]
        near = near_ref[block * BLOCK : (block + 1) * BLOCK, :]
        for offset in range(GROUP):
            chosen = jnp.where(lane == step * GROUP + offset, near, 0.0)
            column = jnp.sum(chosen, axis=1, keepdims=True) - float(block * BLOCK)
            select = to_low(jnp.where(column == slots, 1.0, 0.0))
            rows[
                block * BLOCK : (block + 1) * BLOCK,
                offset * channels : (offset + 1) * channels,
            ] = to_low(product(select, part, 1, 0))
    weight = weight_ref[...].reshape(GROUP * channels, weight_ref.shape[2])
    total[...] += product(rows[...], weight, 1, 0)

    @pl.when(step == pl.num_programs(0) - 1)
    def _():
        conved_ref[...] = to_low(total[...])
        mine = pl.ds(pl.multiple_of(side * local, local), local)
        theirs = pl.ds(pl.multiple_of((1 - side) * local, local), local)
        conved_copy = copies.to(sibling(), conved_ref.at[theirs], conved_other, 10)
        conved_copy.start()
        weight_copies[0].wait()
        linear = product(conved_ref[mine], encode_ref[...], 1, 0)
        conved_copy.wait()
        linear += product(conved_other[...], encode_other[...], 1, 0)
        linear_ref[...] = linear
        first = layer_norm(linear)[0] * encode_gain_ref[...] + encode_shift_ref[...]
        first += to_wide(points_ref[...])
        first_ref[...] = first
        attend_out = layer_norm(first)[0] * attend_gain_ref[...] + attend_shift_ref[...]
        attend_ref[0] = to_low(attend_out)
        attend_copy = copies.to(sibling(), attend_ref.at[0], attend_other, 11)
        attend_copy.start()
        turned = [heads_ref[index].T for index in range(3)]
        for index in range(3):
            projected_ref[index, :, :local] = to_low(product(turned[index], attend_ref[0], 1, 1))
        attend_copy.wait()
        attend_ref[1] = attend_other[...]
        for index in range(3):
            projected_ref[index, :, local:] = to_low(
                product(turned[index], attend_other[...], 1, 1)
            )
        for copy in weight_copies[1:]:
            copy.wait()


def forward_start(
    near, points, conv_weight, encode_weight, norms, heads_weight, output_weight, expand_weight,
    reduce_weight, expand_bias
):
    offsets, channels, width = conv_weight.shape
    local = points.shape[0]
    rows = 2 * local
    wide = rows + 2 * HALO
    low, full = jnp.bfloat16, jnp.float32
    shape = jax.ShapeDtypeStruct
    anywhere = pl.BlockSpec(memory_space=pl.ANY)
    outs = [
        shape((channels, wide), low),
        shape((rows, width), low),
        shape((local, channels), full),
        shape((local, channels), full),
        shape((2, local, channels), low),
        shape((3, width, rows), low),
    ]
    away = [
        shape(array.shape, array.dtype)
        for array in (output_weight, expand_weight, reduce_weight, expand_bias)
    ]
    return pl.pallas_call(
        forward_kernel,
        grid=(offsets // GROUP,),
        in_specs=[
            whole(near),
            whole(points),
            pl.BlockSpec((GROUP, channels, width), lambda i: (i, 0, 0)),
            whole(encode_weight),
            *[whole(norm) for norm in norms],
            whole(heads_weight),
            anywhere,
            anywhere,
            anywhere,
            anywhere,
        ],
        out_specs=[whole(out) for out in outs] + [anywhere] * 4,
        out_shape=outs + away,
        scratch_shapes=[
            pltpu.VMEM((wide, channels), low),
            pltpu.VMEM((rows, width), full),
            pltpu.VMEM((rows, GROUP * channels), low),
            pltpu.VMEM(encode_weight.shape, low),
            pltpu.VMEM((local, width), low),
            pltpu.VMEM((local, channels), low),
            *copy_sems(12),
        ],
        compiler_params=pltpu.CompilerParams(
            vmem_limit_bytes=VMEM_BYTES, collective_id=2, has_side_effects=True
        ),
        cost_estimate=pl.CostEstimate(
            flops=30 * 10**9, bytes_accessed=16 * 10**6, transcendentals=0
        ),
    )(
        near, points, conv_weight, encode_weight, *norms, heads_weight, output_weight,
        expand_weight, reduce_weight, expand_bias
    )


def staged(units, begin, finish):
    ready = begin(units[0])
    for index, unit in enumerate(units):
        later = begin(units[index + 1]) if index + 1 < len(units) else None
        finish(unit, ready)
        ready = later


def attend_kernel(chunk, query_ref, key_ref, value_ref, bias_ref, out_ref, log_ref):
    points = query_ref.shape[1]
    heads = query_ref.shape[0] // HEAD_DIM
    row = lax.broadcasted_iota(jnp.int32, (HEAD_DIM, points), 0)
    ones = to_low(jnp.where(row == 0, 1.0, 0.0))
    operands = []
    for head in range(heads):
        part = slice(head * HEAD_DIM, (head + 1) * HEAD_DIM)
        scaled = to_low(to_wide(query_ref[part]) * HEAD_DIM**-0.5)
        operands.append(
            (
                jnp.concatenate([scaled, ones], axis=0),
                jnp.concatenate([key_ref[part], bias_ref[...]], axis=0),
                jnp.concatenate([value_ref[part], ones], axis=0),
            )
        )

    def begin(unit):
        head, start = unit
        queries, keys, _ = operands[head]
        return product(keys, queries[:, start : start + chunk], 0, 0)

    def finish(unit, scores):
        head, start = unit
        top = jnp.max(scores, axis=0, keepdims=True)
        mixed = product(operands[head][2], to_low(jnp.exp(scores - top)), 1, 0)
        total = mixed[HEAD_DIM : HEAD_DIM + 1, :]
        out_ref[head * HEAD_DIM : (head + 1) * HEAD_DIM, start : start + chunk] = to_low(
            mixed[:HEAD_DIM] / total
        )
        log_ref[head, :, start : start + chunk] = top + jnp.log(total)

    staged([(h, c) for c in range(0, points, chunk) for h in range(heads)], begin, finish)


def attend(projected, bias):
    width, points = projected.shape[1:]
    heads = width // HEAD_DIM
    height = HEAD_DIM * HEADS_STEP
    return pl.pallas_call(
        functools.partial(attend_kernel, 512),
        grid=(heads // HEADS_STEP,),
        in_specs=[
            *[pl.BlockSpec((None, height, points), lambda i, j=j: (j, i, 0)) for j in range(3)],
            pl.BlockSpec(bias.shape, lambda i: (0, 0)),
        ],
        out_specs=[
            pl.BlockSpec((height, points), lambda i: (i, 0)),
            pl.BlockSpec((HEADS_STEP, 1, points), lambda i: (i, 0, 0)),
        ],
        out_shape=[
            jax.ShapeDtypeStruct((width, points), jnp.bfloat16),
            jax.ShapeDtypeStruct((heads, 1, points), jnp.float32),
        ],
        compiler_params=pltpu.CompilerParams(vmem_limit_bytes=VMEM_BYTES),
        cost_estimate=pl.CostEstimate(
            flops=36 * 10**9, bytes_accessed=3 * 10**6, transcendentals=0
        ),
    )(projected, projected, projected, bias)


def attend_back_kernel(
    chunk,
    query_ref,
    key_ref,
    value_ref,
    bias_ref,
    mixed_ref,
    log_ref,
    grad_ref,
    extra_ref,
    turned_ref,
    near_ref,
    out_ref,
    reduce_sum_ref,
    expand_sum_ref,
    output_sum_ref,
    turned_other,
    near_other,
    key_total,
    value_total,
    send_sem,
    arrive_sem,
    *scratch,
):
    points = query_ref.shape[1]
    heads = query_ref.shape[0] // HEAD_DIM
    scale = HEAD_DIM**-0.5
    sums = pair_sums(scratch)
    half = sums.keep.shape[2]
    step = pl.program_id(0)
    copies = Copies(send_sem, arrive_sem)
    partner = {"pts": partner_of(SHARE_BIT)}
    share_copies = [
        copies.to(partner, turned_ref.at[: turned_ref.shape[0] // 2], turned_other, 0),
        copies.to(partner, near_ref, near_other, 1),
    ]

    def finish_sum(index, total):
        hidden = expand_sum_ref.shape[1]
        part = output_sum_ref.shape[0] // 2
        if index == 0:
            reduce_sum_ref[...] = total[0, :, :hidden].T
        else:
            expand_sum_ref[...] = total[0, :, :hidden]
        output_sum_ref[index * part : (index + 1) * part, :] = total[0, :, hidden:].T

    @pl.when(step == 0)
    def _():
        pl.semaphore_wait(greet_partners(), KERNEL_BITS)
        for index in range(extra_ref.shape[0]):
            sums.sends[0][index] = to_low(extra_ref[index, :, :half])
            sums.start(0, index, ((True, ORDERS[index]),))
            sums.keep[index] = extra_ref[index, :, half:]
        for copy in share_copies:
            copy.start()

    for stage, due in enumerate(SUM_STEPS):

        @pl.when(step == due)
        def _(stage=stage):
            for index in range(extra_ref.shape[0]):
                sums.advance(
                    stage, index, ((True, ORDERS[index]),), functools.partial(finish_sum, index)
                )

    @pl.when(step == pl.num_programs(0) - 1)
    def _():
        for copy in share_copies:
            copy.wait()

    row = lax.broadcasted_iota(jnp.int32, (HEAD_DIM, points), 0)
    ones = to_low(jnp.where((row > 0) & (row < 4), 1.0, 0.0))

    def three_parts(values, lead):
        upper = to_wide(to_low(values))
        middle = to_wide(to_low(values - upper))
        lower = values - upper - middle
        tail = jnp.where(row == 1, -upper, jnp.where(row == 2, -middle, 0.0))
        tail = jnp.where(row == 3, -lower, tail)
        return to_low(jnp.where(row == 0, lead, tail))

    operands = []
    for head in range(heads):
        part = slice(head * HEAD_DIM, (head + 1) * HEAD_DIM)
        query, key, value, grad = query_ref[part], key_ref[part], value_ref[part], grad_ref[part]
        row_dot = column_sum(to_wide(grad) * to_wide(mixed_ref[part]))
        scaled = to_low(to_wide(query) * scale)
        operands.append(
            (
                jnp.concatenate([scaled, three_parts(log_ref[head], 1.0)], axis=0),
                jnp.concatenate([key, bias_ref[...] + ones], axis=0),
                jnp.concatenate([value, ones], axis=0),
                jnp.concatenate([grad, three_parts(row_dot, 0.0)], axis=0),
            )
        )

    def begin(unit):
        head, start = unit
        queries, keys, values, grads = operands[head]
        return (
            product(keys, queries[:, start : start + chunk], 0, 0),
            product(values, grads[:, start : start + chunk], 0, 0),
        )

    def finish(unit, ready):
        head, start = unit
        scores, prob_grad = ready
        part = slice(head * HEAD_DIM, (head + 1) * HEAD_DIM)
        now = slice(start, start + chunk)
        probs = jnp.exp(scores)
        score_grad = to_low(probs * prob_grad)
        out_ref[0, part, now] = to_low(product(key_ref[part], score_grad, 1, 0) * scale)
        value_part = product(grad_ref[part, now], to_low(probs), 1, 1)
        key_part = product(query_ref[part, now], score_grad, 1, 1)
        if start == 0:
            value_total[head] = value_part
            key_total[head] = key_part
        else:
            value_total[head] += value_part
            key_total[head] += key_part

    staged([(h, c) for c in range(0, points, chunk) for h in range(heads)], begin, finish)
    for head in range(heads):
        part = slice(head * HEAD_DIM, (head + 1) * HEAD_DIM)
        out_ref[1, part] = to_low(key_total[head] * scale)
        out_ref[2, part] = to_low(value_total[head])


def attend_back(projected, bias, mixed, logs, grads, extra, turned, near):
    width, points = projected.shape[1:]
    heads = width // HEAD_DIM
    height = HEAD_DIM * HEADS_BACK_STEP
    block = pl.BlockSpec((height, points), lambda i: (i, 0))
    channels = extra.shape[2]
    kept = channels >> KERNEL_BITS
    hidden = extra.shape[3] - width // 2
    full = jnp.float32
    outs = [
        jax.ShapeDtypeStruct((3, width, points), jnp.bfloat16),
        jax.ShapeDtypeStruct((hidden, kept), full),
        jax.ShapeDtypeStruct((kept, hidden), full),
        jax.ShapeDtypeStruct((width, kept), full),
        jax.ShapeDtypeStruct((channels // 2, turned.shape[1]), turned.dtype),
        jax.ShapeDtypeStruct(near.shape, near.dtype),
    ]
    anywhere = pl.BlockSpec(memory_space=pl.ANY)
    return pl.pallas_call(
        functools.partial(attend_back_kernel, 512),
        grid=(heads // HEADS_BACK_STEP,),
        in_specs=[
            *[pl.BlockSpec((None, height, points), lambda i, j=j: (j, i, 0)) for j in range(3)],
            pl.BlockSpec(bias.shape, lambda i: (0, 0)),
            block,
            pl.BlockSpec((HEADS_BACK_STEP, 1, points), lambda i: (i, 0, 0)),
            block,
            whole(extra),
            anywhere,
            anywhere,
        ],
        out_specs=[pl.BlockSpec((3, height, points), lambda i: (0, i, 0))]
        + [whole(out) for out in outs[1:4]]
        + [anywhere, anywhere],
        out_shape=outs,
        scratch_shapes=[pltpu.VMEM((HEADS_BACK_STEP, HEAD_DIM, points), jnp.float32)] * 2
        + copy_sems(2)
        + pair_scratch(*extra.shape, KERNEL_BITS),
        compiler_params=pltpu.CompilerParams(
            vmem_limit_bytes=VMEM_BYTES, collective_id=0, has_side_effects=True
        ),
        cost_estimate=pl.CostEstimate(
            flops=50 * 10**9, bytes_accessed=5 * 10**6, transcendentals=0
        ),
    )(projected, projected, projected, bias, mixed, logs, grads, extra, turned, near)


def feed_kernel(
    mixed_ref,
    first_ref,
    output_ref,
    output_other_ref,
    output_bias_ref,
    gain_ref,
    shift_ref,
    cotangent_ref,
    expand_ref,
    expand_other_ref,
    bias_ref,
    bias_other_ref,
    reduce_ref,
    reduce_other_ref,
    reduce_bias_ref,
    result_ref,
    second_grad_ref,
    mixed_grad_ref,
    sums_ref,
    vectors_ref,
    bias_grad_ref,
    mixed_other,
    second_own,
    second_other,
    away,
    arrived,
    send_sem,
    arrive_sem,
):
    local, channels = first_ref.shape
    width = output_ref.shape[0]
    hidden_width = bias_ref.shape[1]
    columns = hidden_width // 2
    copies = Copies(send_sem, arrive_sem)
    greet_sibling()
    mixed_copy = copies.to(sibling(), mixed_ref.at[:, local:], mixed_other, 0)
    mixed_copy.start()
    cotangent = cotangent_ref[...]
    cotangent_turned = to_low(product(nested_picks(channels, ORDERS[0]), cotangent, 1, 1))
    second = first_ref[...] + output_bias_ref[...]
    second += product(mixed_ref[:, :local], output_ref[...], 0, 0)
    mixed_copy.wait()
    second += product(mixed_other[...], output_other_ref[...], 0, 0)
    normal, inverse = layer_norm(second)
    feed_low = to_low(normal * gain_ref[...] + shift_ref[...])
    feed_turned = to_low(product(nested_picks(channels, ORDERS[1]), feed_low, 1, 1))
    result = second + reduce_bias_ref[...]
    feed_grad = jnp.zeros_like(second)
    weight_copies = []
    for index, (up_ref, up_bias_ref, down_ref) in enumerate(
        (
            (expand_other_ref, bias_other_ref, reduce_other_ref),
            (expand_ref, bias_ref, reduce_ref),
        )
    ):
        for start in range(0, hidden_width, columns):
            now = slice(start, start + columns)
            hidden = product(feed_low, up_ref[:, now], 1, 0) + up_bias_ref[:, now]
            below = 0.5 + 0.5 * lax.erf(hidden * 0.5**0.5)
            slope = below + hidden * (jnp.exp(-0.5 * hidden * hidden) * (0.5 / jnp.pi) ** 0.5)
            active = to_low(hidden * below)
            hidden_grad = to_low(product(cotangent, down_ref[now, :], 1, 1) * slope)
            result += product(active, down_ref[now, :], 1, 0)
            feed_grad += product(hidden_grad, up_ref[:, now], 1, 1)
            bias_grad_ref[index : index + 1, now] = column_sum(to_wide(hidden_grad))
            reduce_grad = product(cotangent_turned, active, 1, 0)
            expand_grad = product(feed_turned, hidden_grad, 1, 0)
            if index == 0:
                away[0, :, now] = reduce_grad
                away[1, :, now] = expand_grad
                for kind in range(2):
                    copy = copies.to(
                        sibling(),
                        away.at[kind, :, now],
                        arrived.at[kind, :, now],
                        2 + len(weight_copies),
                    )
                    copy.start()
                    weight_copies.append(copy)
            else:
                sums_ref[0, :, now] = reduce_grad
                sums_ref[1, :, now] = expand_grad
    result_ref[...] = to_low(result)
    upstream = to_wide(cotangent)
    second_grad = upstream + norm_back(feed_grad, normal, inverse, gain_ref[...])
    second_grad_ref[...] = second_grad
    second_own[...] = to_low(second_grad)
    second_copy = copies.to(sibling(), second_own, second_other, 1)
    second_copy.start()
    vectors_ref[0:1] = column_sum(second_grad)
    vectors_ref[1:2] = column_sum(feed_grad * normal)
    vectors_ref[2:3] = column_sum(feed_grad)
    vectors_ref[3:4] = column_sum(upstream)
    mixed_grad_ref[:, :local] = to_low(product(output_ref[...], second_own[...], 1, 1))
    picks = [nested_picks(channels, order) for order in ORDERS[:2]]
    part = width // 2
    for kind in range(2):
        turned = to_low(product(picks[kind], second_own[...], 1, 1))
        sums_ref[kind, :, hidden_width:] = product(
            turned, mixed_ref[kind * part : (kind + 1) * part, :local], 1, 1
        )
    second_copy.wait()
    mixed_grad_ref[:, local:] = to_low(product(output_ref[...], second_other[...], 1, 1))
    for kind in range(2):
        turned = to_low(product(picks[kind], second_other[...], 1, 1))
        sums_ref[kind, :, hidden_width:] += product(
            turned, mixed_ref[kind * part : (kind + 1) * part, local:], 1, 1
        )
    for copy in weight_copies:
        copy.wait()
    sums_ref[:, :, :hidden_width] += arrived[...]


def feed(operands):
    local, channels = operands[1].shape
    width, rows = operands[0].shape
    hidden = operands[10].shape[1]
    low, full = jnp.bfloat16, jnp.float32
    shape = jax.ShapeDtypeStruct
    return pl.pallas_call(
        feed_kernel,
        in_specs=[vmem()] * len(operands),
        out_specs=[vmem()] * 6,
        out_shape=[
            shape((local, channels), low),
            shape((local, channels), full),
            shape((width, rows), low),
            shape((2, channels, hidden + width // 2), full),
            shape((4, channels), full),
            shape((2, hidden), full),
        ],
        scratch_shapes=[
            pltpu.VMEM((width, local), low),
            pltpu.VMEM((local, channels), low),
            pltpu.VMEM((local, channels), low),
            pltpu.VMEM((2, channels, hidden), full),
            pltpu.VMEM((2, channels, hidden), full),
            *copy_sems(6),
        ],
        compiler_params=pltpu.CompilerParams(
            vmem_limit_bytes=VMEM_BYTES, collective_id=3, has_side_effects=True
        ),
        cost_estimate=pl.CostEstimate(
            flops=10 * 10**9, bytes_accessed=16 * 10**6, transcendentals=0
        ),
    )(*operands)


def return_kernel(
    grad_ref,
    heads_ref,
    attend_ref,
    second_grad_ref,
    first_ref,
    linear_ref,
    attend_gain_ref,
    encode_gain_ref,
    encode_ref,
    conved_ref,
    first_grad_ref,
    conved_grad_ref,
    extra_ref,
    vectors_ref,
    attend_away,
    attend_arrived,
    linear_own,
    linear_other,
    send_sem,
    arrive_sem,
):
    local, channels = first_ref.shape
    side = lax.axis_index("tp")
    mine = pl.ds(pl.multiple_of(side * local, local), local)
    theirs = pl.ds(pl.multiple_of((1 - side) * local, local), local)
    copies = Copies(send_sem, arrive_sem)

    def attend_grad(start):
        return sum(
            product(grad_ref[index, :, start : start + local].T, heads_ref[index], 1, 1)
            for index in range(3)
        )

    attend_away[...] = attend_grad(local)
    greet_sibling()
    attend_copy = copies.to(sibling(), attend_away, attend_arrived, 0)
    attend_copy.start()
    upstream = attend_grad(0)
    picks = [nested_picks(channels, order) for order in EXTRA_ORDERS]
    for kind in range(2):
        turned = [to_low(product(picks[kind], attend_ref[i], 1, 1)) for i in range(2)]
        for index in (0, 1) if kind == 0 else (2,):
            extra_ref[kind, index % 2] = product(
                turned[0], grad_ref[index, :, :local], 1, 1
            ) + product(turned[1], grad_ref[index, :, local:], 1, 1)
    normal, inverse = layer_norm(first_ref[...])
    attend_copy.wait()
    upstream += attend_arrived[...]
    first_grad = second_grad_ref[...] + norm_back(upstream, normal, inverse, attend_gain_ref[...])
    first_grad_ref[...] = first_grad
    vectors_ref[0:1] = column_sum(upstream * normal)
    vectors_ref[1:2] = column_sum(upstream)
    normal, inverse = layer_norm(linear_ref[...])
    linear_own[...] = to_low(norm_back(first_grad, normal, inverse, encode_gain_ref[...]))
    linear_copy = copies.to(sibling(), linear_own, linear_other, 1)
    linear_copy.start()
    vectors_ref[2:3] = column_sum(first_grad * normal)
    vectors_ref[3:4] = column_sum(first_grad)
    conved_grad_ref[mine] = to_low(product(linear_own[...], encode_ref[...], 1, 1))
    turned = to_low(product(picks[1], linear_own[...], 1, 1))
    extra_ref[1, 1] = product(turned, conved_ref[mine], 1, 0)
    linear_copy.wait()
    conved_grad_ref[theirs] = to_low(product(linear_other[...], encode_ref[...], 1, 1))
    turned = to_low(product(picks[1], linear_other[...], 1, 1))
    extra_ref[1, 1] += product(turned, conved_ref[theirs], 1, 0)


def return_to_conv(operands):
    local, channels = operands[4].shape
    rows, width = operands[9].shape
    low, full = jnp.bfloat16, jnp.float32
    shape = jax.ShapeDtypeStruct
    return pl.pallas_call(
        return_kernel,
        in_specs=[vmem()] * len(operands),
        out_specs=[vmem()] * 4,
        out_shape=[
            shape((local, channels), full),
            shape((rows, width), low),
            shape((2, 2, channels, width), full),
            shape((4, channels), full),
        ],
        scratch_shapes=[
            pltpu.VMEM((local, channels), full),
            pltpu.VMEM((local, channels), full),
            pltpu.VMEM((local, channels), low),
            pltpu.VMEM((local, channels), low),
            *copy_sems(2),
        ],
        compiler_params=pltpu.CompilerParams(
            vmem_limit_bytes=VMEM_BYTES, collective_id=4, has_side_effects=True
        ),
        cost_estimate=pl.CostEstimate(
            flops=6 * 10**9, bytes_accessed=12 * 10**6, transcendentals=0
        ),
    )(*operands)


def partner_of(bit):
    me = lax.axis_index("pts")
    return me + (1 - 2 * ((me // (1 << bit)) % 2)) * (1 << bit)


def greet_partners():
    barrier = pltpu.get_barrier_semaphore()
    for bit in range(KERNEL_BITS):
        pl.semaphore_signal(
            barrier, inc=1, device_id={"pts": partner_of(bit)}, device_id_type=MESH
        )
    return barrier


class PairSums:
    def __init__(self, keep, sends, arrivals, send_sem, arrive_sem):
        self.keep, self.sends, self.arrivals = keep, sends, arrivals
        self.send_sem, self.arrive_sem = send_sem, arrive_sem

    def copy(self, stage, chunk, bit):
        return pltpu.make_async_remote_copy(
            src_ref=self.sends[stage].at[chunk],
            dst_ref=self.arrivals[stage].at[chunk],
            send_sem=self.send_sem.at[stage, chunk],
            recv_sem=self.arrive_sem.at[stage, chunk],
            device_id={"pts": partner_of(bit)},
            device_id_type=MESH,
        )

    def start(self, stage, chunk, kinds):
        for holds, order in kinds:
            if holds is True:
                self.copy(stage, chunk, order[stage]).start()
            else:

                @pl.when(holds)
                def _(order=order):
                    self.copy(stage, chunk, order[stage]).start()

    def advance(self, stage, chunk, kinds, finish):
        self.copy(stage, chunk, 0).wait()
        rows = self.keep.shape[2]
        low = rows - (rows >> stage)
        half = (rows - low) // 2
        arrived = self.arrivals[stage]
        if stage == len(self.sends) - 1:
            finish(self.keep[chunk, :, low:] + to_wide(arrived[chunk]))
            return
        self.sends[stage + 1][chunk] = to_low(
            self.keep[chunk, :, low : low + half] + to_wide(arrived[chunk, :, :half])
        )
        self.start(stage + 1, chunk, kinds)
        self.keep[chunk, :, low + half :] += to_wide(arrived[chunk, :, half:])


def pair_scratch(chunks, lead, rows, width, stages):
    halves = [(chunks, lead, rows >> (stage + 1), width) for stage in range(stages)]
    return (
        [pltpu.VMEM(halves[0], jnp.float32)]
        + [pltpu.VMEM(shape, jnp.bfloat16) for shape in halves]
        + [pltpu.VMEM(shape, jnp.bfloat16) for shape in halves]
        + [pltpu.SemaphoreType.DMA((stages, chunks))] * 2
    )


def pair_sums(scratch):
    stages = (len(scratch) - 3) // 2
    keep, rest = scratch[0], scratch[1:]
    return PairSums(keep, rest[:stages], rest[stages : 2 * stages], *rest[-2:])


def conv_backward_kernel(
    near_ref,
    near_other_ref,
    turned_ref,
    turned_other_ref,
    grad_ref,
    weight_ref,
    extra_ref,
    vector_ref,
    first_grad_ref,
    conv_sum_ref,
    heads_sum_ref,
    encode_sum_ref,
    points_grad_ref,
    *refs,
):
    vector_refs, refs = refs[:9], refs[9:]
    (
        spread,
        windows,
        gathered,
        grad_other,
        input_grad,
        input_arrived,
        rim_away,
        rim_arrived,
        vector_away,
        vector_arrived,
        send_sem,
        arrive_sem,
    ) = refs[:12]
    sums, extra_sums = pair_sums(refs[12:21]), pair_sums(refs[21:])
    rows, width = grad_ref.shape
    local, channels = first_grad_ref.shape
    half = channels // 2
    quarter = half // 4
    blocks = rows // BLOCK
    extras = extra_ref.shape[0]
    chunks = conv_sum_ref.shape[0]
    patches = lax.axis_size("pts")
    me, side = lax.axis_index("pts"), lax.axis_index("tp")
    step = pl.program_id(0)
    copies = Copies(send_sem, arrive_sem)
    mine = pl.ds(pl.multiple_of(HALO + side * local, HALO), local)
    theirs = pl.ds(pl.multiple_of(HALO + (1 - side) * local, HALO), local)
    grad_copy = copies.to({"pts": partner_of(SHARE_BIT)}, grad_ref, grad_other, 0)
    input_copy = copies.to(sibling(), input_grad.at[theirs], input_arrived, 1)
    rims = (
        (me > 0, {"pts": me - 1, "tp": 1}, slice(0, HALO)),
        (me < patches - 1, {"pts": me + 1, "tp": 0}, slice(HALO + rows, rows + 2 * HALO)),
    )
    rim_copies = [
        [copies.to(rim[1], rim_away.at[i], rim_arrived.at[core], 2 + i, 4 + core) for core in (0, 1)]
        for i, rim in enumerate(rims)
    ]
    has_rim = ((side == 0) & (me > 0)) | ((side == 1) & (me < patches - 1))
    first_sum = chunks // GROUP
    first_input = first_sum + chunks
    input_steps = chunks // GROUP

    def vector_copy(stage):
        device = sibling() if stage == 0 else {"pts": partner_of(stage - 1)}
        return copies.to(device, vector_away.at[stage], vector_arrived.at[stage], 6 + stage)

    def kinds(chunk):
        return ((chunk % 2 == 0, CONV_ORDERS[0]), (chunk % 2 == 1, CONV_ORDERS[1]))

    @pl.when(step == 0)
    def _():
        barrier = greet_partners()
        pl.semaphore_signal(barrier, inc=1, device_id=sibling(), device_id_type=MESH)
        for core in range(2):

            @pl.when((side == 0) & (me > 0))
            def _(core=core):
                device = {"pts": me - 1, "tp": core}
                pl.semaphore_signal(barrier, inc=1, device_id=device, device_id_type=MESH)

            @pl.when((side == 1) & (me < patches - 1))
            def _(core=core):
                device = {"pts": me + 1, "tp": core}
                pl.semaphore_signal(barrier, inc=1, device_id=device, device_id_type=MESH)

        sent = jnp.where(me > 0, 1, 0) + jnp.where(me < patches - 1, 1, 0)
        pl.semaphore_wait(barrier, KERNEL_BITS + 1 + sent)
        grad_copy.start()
        for index in range(extras):
            extra_sums.sends[0][index] = to_low(extra_ref[index, :, :half])
            extra_sums.start(0, index, ((True, EXTRA_ORDERS[index]),))
            extra_sums.keep[index] = extra_ref[index, :, half:]
        vector_away[0] = vector_ref[...]
        vector_copy(0).start()
        for kind, places in enumerate(((0, 1, 2, 3), (0, 2, 1, 3))):
            for place, source in enumerate(places):
                now = slice(place * quarter, (place + 1) * quarter)
                low = source * quarter
                windows[kind, 0, now] = turned_ref[half + low : half + low + quarter, :]
                windows[kind, 1, now] = turned_other_ref[low : low + quarter, :]
        input_grad[...] = jnp.zeros_like(input_grad)

    @pl.when(step < first_sum)
    def _():
        slots = to_wide(lax.broadcasted_iota(jnp.int32, (BLOCK, 1), 0))

        def spread_group(group, _):
            for offset in range(GROUP):
                index = (step * GROUP + group) * GROUP + offset
                near = near_ref[pl.ds(index, 1), :]
                for part in range(blocks + 1):
                    low = max(part - 1, 0) * BLOCK
                    high = min(part + 1, blocks) * BLOCK
                    select = to_low(
                        jnp.where(near[:, low:high] - float(part * BLOCK) == slots, 1.0, 0.0)
                    )
                    spread[index, part * BLOCK : (part + 1) * BLOCK] = to_low(
                        product(select, grad_ref[low:high, :], 1, 0)
                    )
            return 0

        lax.fori_loop(0, GROUP, spread_group, 0)

    @pl.when((step >= first_sum) & (step < first_input))
    def _():
        chunk = step - first_sum
        pl.when(chunk == 0)(grad_copy.wait)
        slots = to_wide(lax.broadcasted_iota(jnp.int32, (2 * BLOCK, 1), 0))
        for offset in range(GROUP):
            near = near_other_ref[pl.ds(chunk * GROUP + offset, 1), :]
            for block in range(blocks):
                low = block * BLOCK
                select = to_low(
                    jnp.where(near[:, low : low + BLOCK] - float(low) == slots, 1.0, 0.0)
                )
                gathered[offset, :, low : low + BLOCK] = to_low(
                    product(windows[chunk % 2, 1, :, low : low + 2 * BLOCK], select, 1, 0)
                )
        for offset in range(GROUP):
            weight_grad = product(windows[chunk % 2, 0], spread[chunk * GROUP + offset], 1, 0)
            weight_grad += product(gathered[offset], grad_other[...], 1, 0)
            sums.sends[0][chunk, offset] = to_low(weight_grad[: half // 2])
            sums.keep[chunk, offset] = weight_grad[half // 2 :]
        sums.start(0, chunk, kinds(chunk))

    for phase, parts in enumerate(((theirs, rims[0][2], rims[1][2]), (mine,))):
        start = first_input + phase * input_steps

        @pl.when((step >= start) & (step < start + input_steps))
        def _(start=start, parts=parts):
            def input_group(group, _):
                for part in parts:
                    total = input_grad[part, :]
                    for offset in range(GROUP):
                        index = group * GROUP + offset
                        total += product(
                            spread[(step - start) * WIDE_GROUP + index, part, :],
                            weight_ref[index],
                            1,
                            1,
                        )
                    input_grad[part, :] = total
                return 0

            lax.fori_loop(0, GROUP, input_group, 0)

    @pl.when(step == first_input + input_steps - 1)
    def _():
        input_copy.start()
        for index, (has, _, part) in enumerate(rims):
            rim_away[index] = to_low(input_grad[part, :])

            @pl.when(has)
            def _(index=index):
                for core in range(2):

                    @pl.when(side == core)
                    def _(core=core):
                        rim_copies[index][core].start()

    @pl.when(step == pl.num_programs(0) - 1)
    def _():
        input_copy.wait()
        points_grad_ref[...] = first_grad_ref[...] + input_grad[mine, :] + input_arrived[...]

        @pl.when(has_rim)
        def _():
            edge = pl.ds(pl.multiple_of(side * (local - HALO), HALO), HALO)
            for core in range(2):
                rim_copies[0][core].wait_recv()
                points_grad_ref[edge, :] += to_wide(rim_arrived[core])

        for index, (has, _, part) in enumerate(rims):
            pl.when(has)(rim_copies[index][0].wait_send)

    for stage, due in enumerate(VECTOR_STEPS):

        @pl.when(step == due)
        def _(stage=stage):
            vector_copy(stage).wait()
            summed = vector_away[stage] + vector_arrived[stage]
            if stage < KERNEL_BITS:
                vector_away[stage + 1] = summed
                vector_copy(stage + 1).start()
                return
            for index in range(8):
                vector_refs[index][...] = summed[index : index + 1]
            for index in range(8, summed.shape[0]):
                low = (index - 8) * channels
                vector_refs[8][:, low : low + channels] = summed[index : index + 1]

    for stage in range(len(CONV_LAGS)):
        chunk = step - first_sum - CONV_LAGS[stage]

        @pl.when((chunk >= 0) & (chunk < chunks))
        def _(stage=stage, chunk=chunk):
            def finish(total):
                conv_sum_ref[chunk] = total

            sums.advance(stage, chunk, kinds(chunk), finish)

    def finish_extra(index, total):
        if index == 0:
            heads_sum_ref[0:2] = total
        else:
            heads_sum_ref[2] = total[0]
            encode_sum_ref[...] = total[1].T

    for stage, due in enumerate(EXTRA_STEPS):

        @pl.when(step == due)
        def _(stage=stage):
            for index in range(extras):
                extra_sums.advance(
                    stage,
                    index,
                    ((True, EXTRA_ORDERS[index]),),
                    functools.partial(finish_extra, index),
                )


def conv_backward(
    near, near_other, turned, turned_other, grad, weight, extra, vector, first_grad
):
    offsets, channels, width = weight.shape
    wide = turned.shape[1]
    rows = grad.shape[0]
    local = first_grad.shape[0]
    chunks = offsets // GROUP
    first_input = chunks // GROUP + chunks
    input_steps = chunks // GROUP
    low, full = jnp.bfloat16, jnp.float32
    kept = channels >> KERNEL_BITS
    shape = jax.ShapeDtypeStruct
    outs = [
        shape((chunks, GROUP, kept, width), full),
        shape((3, kept, width), full),
        shape((width, kept), full),
        shape(first_grad.shape, full),
        *[shape((1, channels), full)] * 8,
        shape((1, (vector.shape[0] - 8) * channels), full),
    ]

    def weight_block(i):
        return (jnp.maximum(i - first_input, 0) % input_steps, 0, 0)

    return pl.pallas_call(
        conv_backward_kernel,
        grid=(first_input + 2 * input_steps,),
        in_specs=[
            whole(near),
            whole(near_other),
            whole(turned),
            whole(turned_other),
            whole(grad),
            pl.BlockSpec((WIDE_GROUP, channels, width), weight_block),
            whole(extra),
            whole(vector),
            whole(first_grad),
        ],
        out_specs=[whole(out) for out in outs],
        out_shape=outs,
        scratch_shapes=[
            pltpu.VMEM((offsets, wide, width), low),
            pltpu.VMEM((2, 2, channels // 2, wide), low),
            pltpu.VMEM((GROUP, channels // 2, rows), low),
            pltpu.VMEM((rows, width), low),
            pltpu.VMEM((wide, channels), full),
            pltpu.VMEM((local, channels), full),
            pltpu.VMEM((2, HALO, channels), low),
            pltpu.VMEM((2, HALO, channels), low),
            pltpu.VMEM((KERNEL_BITS + 1, *vector.shape), full),
            pltpu.VMEM((KERNEL_BITS + 1, *vector.shape), full),
            *copy_sems(7 + KERNEL_BITS),
            *pair_scratch(chunks, GROUP, channels // 2, width, len(CONV_LAGS)),
            *pair_scratch(*extra.shape, KERNEL_BITS),
        ],
        compiler_params=pltpu.CompilerParams(
            vmem_limit_bytes=VMEM_BYTES, collective_id=1, has_side_effects=True
        ),
        cost_estimate=pl.CostEstimate(
            flops=80 * 10**9, bytes_accessed=16 * 10**6, transcendentals=0
        ),
    )(near, near_other, turned, turned_other, grad, weight, extra, vector, first_grad)


def exchange(values, bit):
    count = lax.axis_size("pts")
    return lax.ppermute(values, "pts", [(i, i ^ (1 << bit)) for i in range(count)])


def sum_rest(keep, axis):
    for bit in range(KERNEL_BITS, patch_bits()):
        half = keep.shape[axis] // 2
        away = lax.slice_in_dim(keep, 0, half, axis=axis)
        keep = lax.slice_in_dim(keep, half, 2 * half, axis=axis)
        keep = keep + to_wide(exchange(to_low(away), bit))
    return keep


def per_device(
    points,
    neighbours,
    valid_count,
    conv_weight,
    encode_weight,
    encode_gain,
    encode_shift,
    attend_gain,
    attend_shift,
    heads_weight,
    output_weight,
    output_bias,
    feed_gain,
    feed_shift,
    expand_weight,
    expand_bias,
    reduce_weight,
    reduce_bias,
    cotangent,
):
    local, channels = points.shape
    rows = 2 * local
    is_first = lax.axis_index("tp") == 0
    near = to_wide(neighbours)
    near_columns = near.T
    norms = [v[None, :] for v in (encode_gain, encode_shift, attend_gain, attend_shift)]
    (
        turned, conved, linear, first, attend_in, projected,
        output_other, expand_other, reduce_other, bias_other,
    ) = forward_start(
        near, points, conv_weight, encode_weight, norms, heads_weight, output_weight,
        expand_weight, reduce_weight, expand_bias[None, :]
    )

    place = jnp.arange(rows, dtype=jnp.int32)
    place = jnp.where(is_first, place, (place + local) % rows)
    bias = jnp.where(place < valid_count[0], 0.0, MASKED)
    bias = to_low(jnp.where(jnp.arange(HEAD_DIM)[:, None] == 0, bias[None, :], 0.0))
    mixed, logs = attend(projected, bias)
    result, second_grad, mixed_grad, feed_grads, feed_vectors, bias_grads = feed(
        [
            mixed, first, output_weight, output_other, output_bias[None, :], feed_gain[None, :],
            feed_shift[None, :], cotangent, expand_weight, expand_other, expand_bias[None, :],
            bias_other, reduce_weight, reduce_other, reduce_bias[None, :],
        ]
    )
    projected_grad, reduce_sum, expand_sum, output_sum, turned_other, near_other = attend_back(
        projected, bias, mixed, logs, mixed_grad, feed_grads[:, None], turned, near_columns
    )
    first_grad, conved_grad, extra, return_vectors = return_to_conv(
        [
            projected_grad, heads_weight, attend_in, second_grad, first, linear, norms[2],
            norms[0], encode_weight, conved,
        ]
    )
    own, other = bias_grads[1], bias_grads[0]
    vector = jnp.concatenate(
        [
            feed_vectors,
            return_vectors,
            jnp.where(is_first, own, other).reshape(-1, channels),
            jnp.where(is_first, other, own).reshape(-1, channels),
        ]
    )
    conv_sum, heads_sum, encode_sum, points_gradient, *vectors = conv_backward(
        near_columns, near_other, turned, turned_other, conved_grad, conv_weight, extra, vector,
        first_grad
    )
    for bit in range(KERNEL_BITS, patch_bits()):
        vectors = [each + exchange(each, bit) for each in vectors]
    vectors = [each.reshape(-1) for each in vectors]
    conv_sum = sum_rest(conv_sum, 2)
    return (
        result,
        points_gradient,
        conv_sum.reshape(-1, *conv_sum.shape[2:]),
        sum_rest(encode_sum, 1),
        vectors[6],
        vectors[7],
        vectors[4],
        vectors[5],
        sum_rest(heads_sum, 1),
        sum_rest(output_sum, 1),
        vectors[0],
        vectors[1],
        vectors[2],
        sum_rest(expand_sum, 0),
        vectors[8],
        sum_rest(reduce_sum, 1),
        vectors[3],
    )


def solution(mesh):
    placed = (
        P(("pts", "tp"), None),
        P("pts", None),
        P("pts"),
        P(None, None, "tp"),
        P("tp", None),
        P(),
        P(),
        P(),
        P(),
        P(None, None, "tp"),
        P("tp", None),
        P(),
        P(),
        P(),
        P(None, "tp"),
        P("tp"),
        P("tp", None),
        P(),
        P(("pts", "tp"), None),
    )
    return jax.shard_map(
        per_device,
        mesh=mesh,
        in_specs=placed,
        out_specs=(
            P(("pts", "tp"), None),
            P(("pts", "tp"), None),
            P(None, "pts", "tp"),
            P("tp", "pts"),
            P(),
            P(),
            P(),
            P(),
            P(None, "pts", "tp"),
            P("tp", "pts"),
            P(),
            P(),
            P(),
            P("pts", "tp"),
            P(),
            P("tp", "pts"),
            P(),
        ),
        check_vma=False,
    )
```

```python
import functools

import jax
import jax.numpy as jnp
from jax import lax
from jax.experimental import pallas as pl
from jax.experimental.pallas import tpu as pltpu
from jax.sharding import PartitionSpec as P

MESH = pl.DeviceIdType.MESH
HEAD_DIM = 16
HALO = 128
BLOCK = 256
GROUP = 3
EPSILON = 1e-05
MASKED = -1e30
KERNEL_BITS = 4
ORDERS = ((0, 1, 2, 3), (1, 0, 2, 3))
VMEM_BYTES = 60 << 20
HEADS_STEP = 4
HEADS_BACK_STEP = 2
SUM_STEPS = (3, 5, 6, 7)
SHARE_BIT = 2
CONV_ORDERS = ((0, 1, 3), (1, 0, 3))
WINDOW_ORDER = (2, 0, 1, 3)
CONV_LAGS = (2, 4, 6)
EXTRA_STEPS = (5, 8, 10, 12)
VECTOR_STEPS = (1, 2, 3, 4, 5)
WEIGHTS_AHEAD = 3
WIDE_GROUP = 9


def to_low(values):
    return values.astype(jnp.bfloat16)


def to_wide(values):
    return values.astype(jnp.float32)


def product(left, right, left_dim, right_dim):
    dims = (((left_dim,), (right_dim,)), ((), ()))
    return lax.dot_general(left, right, dims, preferred_element_type=jnp.float32)


def layer_norm(values):
    row_mean = jnp.mean(values, axis=-1, keepdims=True)
    centred = values - row_mean
    inverse = lax.rsqrt(jnp.mean(centred * centred, axis=-1, keepdims=True) + EPSILON)
    return centred * inverse, inverse


def norm_back(upstream, normal_part, inverse, norm_gain):
    scaled = upstream * norm_gain
    across = (
        scaled
        - jnp.mean(scaled, axis=-1, keepdims=True)
        - normal_part * jnp.mean(scaled * normal_part, axis=-1, keepdims=True)
    )
    return across * inverse


def column_sum(values):
    return jnp.sum(values, axis=0, keepdims=True)


def nested_picks(channels, order):
    me = lax.axis_index("pts")
    order = order + tuple(range(KERNEL_BITS, patch_bits()))
    depth = channels >> len(order)
    place = lax.broadcasted_iota(jnp.int32, (channels, channels), 0)
    picked = place & (depth - 1)
    for stage, bit in enumerate(order):
        kept = (place >> (channels.bit_length() - 2 - stage)) & 1
        picked = picked + (1 - ((kept + me // (1 << bit)) & 1)) * (depth << bit)
    column = lax.broadcasted_iota(jnp.int32, (channels, channels), 1)
    return to_low(jnp.where(picked == column, 1.0, 0.0))


class Copies:
    def __init__(self, send_sem, arrive_sem):
        self.send_sem, self.arrive_sem = send_sem, arrive_sem

    def to(self, device, source, target, send, arrive=None):
        return pltpu.make_async_remote_copy(
            src_ref=source,
            dst_ref=target,
            send_sem=self.send_sem.at[send],
            recv_sem=self.arrive_sem.at[send if arrive is None else arrive],
            device_id=device,
            device_id_type=MESH,
        )


def copy_sems(count):
    return [pltpu.SemaphoreType.DMA((count,))] * 2


def patch_bits():
    return lax.axis_size("pts").bit_length() - 1


def sibling():
    return {"tp": 1 - lax.axis_index("tp")}


def greet_sibling():
    barrier = pltpu.get_barrier_semaphore()
    pl.semaphore_signal(barrier, inc=1, device_id=sibling(), device_id_type=MESH)
    pl.semaphore_wait(barrier, 1)


def vmem():
    return pl.BlockSpec(memory_space=pltpu.VMEM)


def whole(array):
    zeros = (0,) * array.ndim
    return pl.BlockSpec(array.shape, lambda i: zeros, pipeline_mode=pl.Buffered(1))


def forward_kernel(
    near_ref,
    points_ref,
    weight_ref,
    weights_ref,
    encode_ref,
    encode_gain_ref,
    encode_shift_ref,
    attend_gain_ref,
    attend_shift_ref,
    heads_ref,
    output_ref,
    expand_ref,
    reduce_ref,
    bias_ref,
    turned_ref,
    near_columns_ref,
    conved_ref,
    linear_ref,
    first_ref,
    attend_ref,
    projected_ref,
    output_other,
    expand_other,
    reduce_other,
    bias_other,
    window,
    total,
    rows,
    weight_other,
    encode_other,
    conved_away,
    conved_other,
    attend_other,
    heads_turned,
    near_wide,
    weight_first,
    send_sem,
    arrive_sem,
):
    step = pl.program_id(0)
    steps = pl.num_programs(0)
    local, channels = points_ref.shape
    width = weight_ref.shape[2]
    patches = lax.axis_size("pts")
    me, side = lax.axis_index("pts"), lax.axis_index("tp")
    copies = Copies(send_sem, arrive_sem)
    own_place = pl.ds(pl.multiple_of(HALO + side * local, HALO), local)
    other_place = pl.ds(pl.multiple_of(HALO + (1 - side) * local, HALO), local)
    points_copy = copies.to(sibling(), points_ref, window.at[own_place], 0)
    low_rim, high_rim = slice(0, HALO), slice(HALO + 2 * local, 2 * HALO + 2 * local)
    low_copies = [
        copies.to(
            {"pts": me + 1, "tp": core},
            points_ref.at[local - HALO :],
            window.at[low_rim],
            3 + core,
            1,
        )
        for core in range(2)
    ]
    high_copies = [
        copies.to(
            {"pts": me - 1, "tp": core}, points_ref.at[0:HALO], window.at[high_rim], 3 + core, 2
        )
        for core in range(2)
    ]
    small_copies = [
        copies.to(sibling(), encode_ref, encode_other, 5),
        copies.to(sibling(), output_ref, output_other, 6),
        copies.to(sibling(), expand_ref, expand_other, 7),
        copies.to(sibling(), reduce_ref, reduce_other, 8),
        copies.to(sibling(), bias_ref, bias_other, 9),
    ]
    up = (side == 1) & (me < patches - 1)
    down = (side == 0) & (me > 0)

    def weight_copy(group):
        part = pl.ds(group * GROUP, GROUP)
        return copies.to(sibling(), weights_ref.at[part], weight_other.at[part], 12 + group)

    def turn(place):
        return to_low(product(nested_picks(channels, WINDOW_ORDER), window[place, :], 1, 1))

    @pl.when(step == 0)
    def _():
        barrier = pltpu.get_barrier_semaphore()
        pl.semaphore_signal(barrier, inc=1, device_id=sibling(), device_id_type=MESH)

        @pl.when(me > 0)
        def _():
            pl.semaphore_signal(
                barrier, inc=1, device_id={"pts": me - 1, "tp": 1}, device_id_type=MESH
            )

        @pl.when(me < patches - 1)
        def _():
            pl.semaphore_signal(
                barrier, inc=1, device_id={"pts": me + 1, "tp": 0}, device_id_type=MESH
            )

        pl.semaphore_wait(barrier, jnp.where(up | down, 3, 1))
        points_copy.start()

        @pl.when(up)
        def _():
            for copy in low_copies:
                copy.start()

        @pl.when(down)
        def _():
            for copy in high_copies:
                copy.start()

        for group in range(WEIGHTS_AHEAD):
            weight_copy(group).start()
        window[own_place, :] = points_ref[...]

        @pl.when(me == 0)
        def _():
            window[low_rim, :] = jnp.zeros((HALO, channels), jnp.bfloat16)

        @pl.when(me == patches - 1)
        def _():
            window[high_rim, :] = jnp.zeros((HALO, channels), jnp.bfloat16)

        turned_ref[:, own_place] = turn(own_place)
        for index in range(3):
            heads_turned[index] = heads_ref[index].T
        near_wide[...] = jnp.zeros_like(near_wide)
        near_wide[:, : near_ref.shape[1]] = to_wide(near_ref[...])
        near_columns_ref[...] = near_wide[...].T[: near_columns_ref.shape[0]]
        points_copy.wait()

    @pl.when(step == 2)
    def _():
        for place in (other_place, low_rim, high_rim):
            turned_ref[:, place] = turn(place)

        for copy in small_copies:
            copy.start()

    def wait_rims():
        @pl.when(me > 0)
        def _():
            low_copies[0].wait_recv()

        @pl.when(me < patches - 1)
        def _():
            high_copies[0].wait_recv()

        @pl.when(up)
        def _():
            for copy in low_copies:
                copy.wait_send()

        @pl.when(down)
        def _():
            for copy in high_copies:
                copy.wait_send()

    @pl.when((step > 0) & (step + WEIGHTS_AHEAD - 1 < steps))
    def _():
        weight_copy(step + WEIGHTS_AHEAD - 1).start()

    weight_copy(step).wait()
    lane = lax.broadcasted_iota(jnp.int32, (BLOCK, near_wide.shape[1]), 1)
    slots = to_wide(lax.broadcasted_iota(jnp.int32, (BLOCK, 2 * BLOCK), 1))
    places = [pl.ds(pl.multiple_of(block * BLOCK, BLOCK), BLOCK) for block in (1 - side, side)]

    def gather(index, group):
        low = pl.multiple_of(side * local + (1 - side, side)[index] * BLOCK, BLOCK)
        part = window[pl.ds(low, 2 * BLOCK), :]
        near = near_wide[pl.ds(low, BLOCK), :] - low.astype(jnp.float32)
        for offset in range(GROUP):
            chosen = jnp.where(lane == group * GROUP + offset, near, 0.0)
            column = jnp.sum(chosen, axis=1, keepdims=True)
            select = to_low(jnp.where(column == slots, 1.0, 0.0))
            rows[places[index], offset * channels : (offset + 1) * channels] = to_low(
                product(select, part, 1, 0)
            )

    def apply(place, own_ref, group):
        picked = rows[place, :]
        other = weight_other[pl.ds(group * GROUP, GROUP)]
        flat = (GROUP * channels, width)
        return (
            product(picked, own_ref[...].reshape(flat), 1, 0),
            product(picked, other.reshape(flat), 1, 0),
        )

    @pl.when(step == 0)
    def _():
        gather(0, 0)
        total[places[0], :width], total[places[0], width:] = apply(places[0], weight_ref, 0)
        weight_first[...] = weight_ref[...]

    @pl.when(step == 1)
    def _():
        wait_rims()
        gather(1, 0)
        total[places[1], :width], total[places[1], width:] = apply(places[1], weight_first, 0)

    @pl.when(step > 0)
    def _():
        gather(0, step)
        gather(1, step)
        own, other = apply(slice(None), weight_ref, step)
        total[:, :width] += own
        total[:, width:] += other

    @pl.when(step == steps - 1)
    def _():
        mine = pl.ds(pl.multiple_of(side * local, local), local)
        theirs = pl.ds(pl.multiple_of((1 - side) * local, local), local)
        conved_own = to_low(total[:, :width])
        conved_away[...] = to_low(total[:, width:])
        conved_ref[mine] = conved_own
        conved_copy = copies.to(sibling(), conved_away, conved_other, 10)
        conved_copy.start()
        small_copies[0].wait()
        linear = product(conved_own, encode_ref[...], 1, 0)
        linear += product(conved_away[...], encode_other[...], 1, 0)
        linear_ref[...] = linear
        first = layer_norm(linear)[0] * encode_gain_ref[...] + encode_shift_ref[...]
        first += to_wide(points_ref[...])
        first_ref[...] = first
        attend_out = layer_norm(first)[0] * attend_gain_ref[...] + attend_shift_ref[...]
        attend_ref[0] = to_low(attend_out)
        attend_copy = copies.to(sibling(), attend_ref.at[0], attend_other, 11)
        attend_copy.start()
        for index in range(3):
            projected_ref[index, :, :local] = to_low(
                product(heads_turned[index], attend_ref[0], 1, 1)
            )
        attend_copy.wait()
        attend_ref[1] = attend_other[...]
        for index in range(3):
            projected_ref[index, :, local:] = to_low(
                product(heads_turned[index], attend_other[...], 1, 1)
            )
        conved_copy.wait()
        conved_ref[theirs] = conved_other[...]
        for copy in small_copies[1:]:
            copy.wait()


def forward_start(
    near, points, conv_weight, encode_weight, norms, heads_weight, output_weight, expand_weight,
    reduce_weight, expand_bias
):
    offsets, channels, width = conv_weight.shape
    local = points.shape[0]
    rows = 2 * local
    wide = rows + 2 * HALO
    groups = offsets // GROUP
    low, full = jnp.bfloat16, jnp.float32
    shape = jax.ShapeDtypeStruct
    anywhere = pl.BlockSpec(memory_space=pl.ANY)
    outs = [
        shape((channels, wide), low),
        shape((32, rows), full),
        shape((rows, width), low),
        shape((local, channels), full),
        shape((local, channels), full),
        shape((2, local, channels), low),
        shape((3, width, rows), low),
    ]
    away = [
        shape(array.shape, array.dtype)
        for array in (output_weight, expand_weight, reduce_weight, expand_bias)
    ]
    return pl.pallas_call(
        forward_kernel,
        grid=(groups,),
        in_specs=[
            whole(near),
            whole(points),
            pl.BlockSpec((GROUP, channels, width), lambda i: (i, 0, 0)),
            anywhere,
            whole(encode_weight),
            *[whole(norm) for norm in norms],
            whole(heads_weight),
            anywhere,
            anywhere,
            anywhere,
            anywhere,
        ],
        out_specs=[whole(out) for out in outs] + [anywhere] * 4,
        out_shape=outs + away,
        scratch_shapes=[
            pltpu.VMEM((wide, channels), low),
            pltpu.VMEM((local, channels), full),
            pltpu.VMEM((local, GROUP * channels), low),
            pltpu.VMEM(conv_weight.shape, low),
            pltpu.VMEM(encode_weight.shape, low),
            pltpu.VMEM((local, width), low),
            pltpu.VMEM((local, width), low),
            pltpu.VMEM((local, channels), low),
            pltpu.VMEM((3, width, channels), low),
            pltpu.VMEM((rows, 128), full),
            pltpu.VMEM((GROUP, channels, width), low),
            *copy_sems(12 + groups),
        ],
        compiler_params=pltpu.CompilerParams(
            vmem_limit_bytes=VMEM_BYTES, collective_id=2, has_side_effects=True
        ),
        cost_estimate=pl.CostEstimate(
            flops=30 * 10**9, bytes_accessed=16 * 10**6, transcendentals=0
        ),
    )(
        near, points, conv_weight, conv_weight, encode_weight, *norms, heads_weight,
        output_weight, expand_weight, reduce_weight, expand_bias
    )


def staged(units, begin, finish):
    ready = begin(units[0])
    for index, unit in enumerate(units):
        later = begin(units[index + 1]) if index + 1 < len(units) else None
        finish(unit, ready)
        ready = later


def attend_kernel(chunk, query_ref, key_ref, value_ref, bias_ref, out_ref, log_ref):
    points = query_ref.shape[1]
    heads = query_ref.shape[0] // HEAD_DIM
    row = lax.broadcasted_iota(jnp.int32, (HEAD_DIM, points), 0)
    ones = to_low(jnp.where(row == 0, 1.0, 0.0))
    operands = []
    for head in range(heads):
        part = slice(head * HEAD_DIM, (head + 1) * HEAD_DIM)
        scaled = to_low(to_wide(query_ref[part]) * HEAD_DIM**-0.5)
        operands.append(
            (
                jnp.concatenate([scaled, ones], axis=0),
                jnp.concatenate([key_ref[part], bias_ref[...]], axis=0),
                jnp.concatenate([value_ref[part], ones], axis=0),
            )
        )

    def begin(unit):
        head, start = unit
        queries, keys, _ = operands[head]
        return product(keys, queries[:, start : start + chunk], 0, 0)

    def finish(unit, scores):
        head, start = unit
        top = jnp.max(scores, axis=0, keepdims=True)
        mixed = product(operands[head][2], to_low(jnp.exp(scores - top)), 1, 0)
        total = mixed[HEAD_DIM : HEAD_DIM + 1, :]
        out_ref[head * HEAD_DIM : (head + 1) * HEAD_DIM, start : start + chunk] = to_low(
            mixed[:HEAD_DIM] / total
        )
        log_ref[head, :, start : start + chunk] = top + jnp.log(total)

    staged([(h, c) for c in range(0, points, chunk) for h in range(heads)], begin, finish)


def attend(projected, bias):
    width, points = projected.shape[1:]
    heads = width // HEAD_DIM
    height = HEAD_DIM * HEADS_STEP
    return pl.pallas_call(
        functools.partial(attend_kernel, 512),
        grid=(heads // HEADS_STEP,),
        in_specs=[
            *[pl.BlockSpec((None, height, points), lambda i, j=j: (j, i, 0)) for j in range(3)],
            pl.BlockSpec(bias.shape, lambda i: (0, 0)),
        ],
        out_specs=[
            pl.BlockSpec((height, points), lambda i: (i, 0)),
            pl.BlockSpec((HEADS_STEP, 1, points), lambda i: (i, 0, 0)),
        ],
        out_shape=[
            jax.ShapeDtypeStruct((width, points), jnp.bfloat16),
            jax.ShapeDtypeStruct((heads, 1, points), jnp.float32),
        ],
        compiler_params=pltpu.CompilerParams(vmem_limit_bytes=VMEM_BYTES),
        cost_estimate=pl.CostEstimate(
            flops=36 * 10**9, bytes_accessed=3 * 10**6, transcendentals=0
        ),
    )(projected, projected, projected, bias)


def attend_back_kernel(
    chunk,
    query_ref,
    key_ref,
    value_ref,
    bias_ref,
    mixed_ref,
    log_ref,
    grad_ref,
    extra_ref,
    turned_ref,
    near_ref,
    out_ref,
    reduce_sum_ref,
    expand_sum_ref,
    output_sum_ref,
    turned_other,
    near_other,
    key_total,
    value_total,
    send_sem,
    arrive_sem,
    *scratch,
):
    points = query_ref.shape[1]
    heads = query_ref.shape[0] // HEAD_DIM
    scale = HEAD_DIM**-0.5
    sums = pair_sums(scratch)
    half = sums.keep.shape[2]
    step = pl.program_id(0)
    copies = Copies(send_sem, arrive_sem)
    partner = {"pts": partner_of(SHARE_BIT)}
    share_copies = [
        copies.to(partner, turned_ref.at[: turned_ref.shape[0] // 2], turned_other, 0),
        copies.to(partner, near_ref, near_other, 1),
    ]

    def finish_sum(index, total):
        hidden = expand_sum_ref.shape[1]
        part = output_sum_ref.shape[0] // 2
        if index == 0:
            reduce_sum_ref[...] = total[0, :, :hidden].T
        else:
            expand_sum_ref[...] = total[0, :, :hidden]
        output_sum_ref[index * part : (index + 1) * part, :] = total[0, :, hidden:].T

    @pl.when(step == 0)
    def _():
        pl.semaphore_wait(greet_partners(), KERNEL_BITS)
        for index in range(extra_ref.shape[0]):
            sums.sends[0][index] = to_low(extra_ref[index, :, :half])
            sums.start(0, index, ((True, ORDERS[index]),))
            sums.keep[index] = extra_ref[index, :, half:]
        for copy in share_copies:
            copy.start()

    for stage, due in enumerate(SUM_STEPS):

        @pl.when(step == due)
        def _(stage=stage):
            for index in range(extra_ref.shape[0]):
                sums.advance(
                    stage, index, ((True, ORDERS[index]),), functools.partial(finish_sum, index)
                )

    @pl.when(step == pl.num_programs(0) - 1)
    def _():
        for copy in share_copies:
            copy.wait()

    row = lax.broadcasted_iota(jnp.int32, (HEAD_DIM, points), 0)
    ones = to_low(jnp.where((row > 0) & (row < 4), 1.0, 0.0))

    def three_parts(values, lead):
        upper = to_wide(to_low(values))
        middle = to_wide(to_low(values - upper))
        lower = values - upper - middle
        tail = jnp.where(row == 1, -upper, jnp.where(row == 2, -middle, 0.0))
        tail = jnp.where(row == 3, -lower, tail)
        return to_low(jnp.where(row == 0, lead, tail))

    operands = []
    for head in range(heads):
        part = slice(head * HEAD_DIM, (head + 1) * HEAD_DIM)
        query, key, value, grad = query_ref[part], key_ref[part], value_ref[part], grad_ref[part]
        row_dot = column_sum(to_wide(grad) * to_wide(mixed_ref[part]))
        scaled = to_low(to_wide(query) * scale)
        operands.append(
            (
                jnp.concatenate([scaled, three_parts(log_ref[head], 1.0)], axis=0),
                jnp.concatenate([key, bias_ref[...] + ones], axis=0),
                jnp.concatenate([value, ones], axis=0),
                jnp.concatenate([grad, three_parts(row_dot, 0.0)], axis=0),
            )
        )

    def begin(unit):
        head, start = unit
        queries, keys, values, grads = operands[head]
        return (
            product(keys, queries[:, start : start + chunk], 0, 0),
            product(values, grads[:, start : start + chunk], 0, 0),
        )

    def finish(unit, ready):
        head, start = unit
        scores, prob_grad = ready
        part = slice(head * HEAD_DIM, (head + 1) * HEAD_DIM)
        now = slice(start, start + chunk)
        probs = jnp.exp(scores)
        score_grad = to_low(probs * prob_grad)
        out_ref[0, part, now] = to_low(product(key_ref[part], score_grad, 1, 0) * scale)
        value_part = product(grad_ref[part, now], to_low(probs), 1, 1)
        key_part = product(query_ref[part, now], score_grad, 1, 1)
        if start == 0:
            value_total[head] = value_part
            key_total[head] = key_part
        else:
            value_total[head] += value_part
            key_total[head] += key_part

    staged([(h, c) for c in range(0, points, chunk) for h in range(heads)], begin, finish)
    for head in range(heads):
        part = slice(head * HEAD_DIM, (head + 1) * HEAD_DIM)
        out_ref[1, part] = to_low(key_total[head] * scale)
        out_ref[2, part] = to_low(value_total[head])


def attend_back(projected, bias, mixed, logs, grads, extra, turned, near):
    width, points = projected.shape[1:]
    heads = width // HEAD_DIM
    height = HEAD_DIM * HEADS_BACK_STEP
    block = pl.BlockSpec((height, points), lambda i: (i, 0))
    channels = extra.shape[2]
    kept = channels >> KERNEL_BITS
    hidden = extra.shape[3] - width // 2
    full = jnp.float32
    outs = [
        jax.ShapeDtypeStruct((3, width, points), jnp.bfloat16),
        jax.ShapeDtypeStruct((hidden, kept), full),
        jax.ShapeDtypeStruct((kept, hidden), full),
        jax.ShapeDtypeStruct((width, kept), full),
        jax.ShapeDtypeStruct((channels // 2, turned.shape[1]), turned.dtype),
        jax.ShapeDtypeStruct(near.shape, near.dtype),
    ]
    anywhere = pl.BlockSpec(memory_space=pl.ANY)
    return pl.pallas_call(
        functools.partial(attend_back_kernel, 512),
        grid=(heads // HEADS_BACK_STEP,),
        in_specs=[
            *[pl.BlockSpec((None, height, points), lambda i, j=j: (j, i, 0)) for j in range(3)],
            pl.BlockSpec(bias.shape, lambda i: (0, 0)),
            block,
            pl.BlockSpec((HEADS_BACK_STEP, 1, points), lambda i: (i, 0, 0)),
            block,
            whole(extra),
            anywhere,
            anywhere,
        ],
        out_specs=[pl.BlockSpec((3, height, points), lambda i: (0, i, 0))]
        + [whole(out) for out in outs[1:4]]
        + [anywhere, anywhere],
        out_shape=outs,
        scratch_shapes=[pltpu.VMEM((HEADS_BACK_STEP, HEAD_DIM, points), jnp.float32)] * 2
        + copy_sems(2)
        + pair_scratch(*extra.shape, KERNEL_BITS),
        compiler_params=pltpu.CompilerParams(
            vmem_limit_bytes=VMEM_BYTES, collective_id=0, has_side_effects=True
        ),
        cost_estimate=pl.CostEstimate(
            flops=50 * 10**9, bytes_accessed=5 * 10**6, transcendentals=0
        ),
    )(projected, projected, projected, bias, mixed, logs, grads, extra, turned, near)


def feed_kernel(
    mixed_ref,
    first_ref,
    output_ref,
    output_other_ref,
    output_bias_ref,
    gain_ref,
    shift_ref,
    cotangent_ref,
    expand_ref,
    expand_other_ref,
    bias_ref,
    bias_other_ref,
    reduce_ref,
    reduce_other_ref,
    reduce_bias_ref,
    result_ref,
    second_grad_ref,
    mixed_grad_ref,
    sums_ref,
    vectors_ref,
    bias_grad_ref,
    mixed_other,
    second_own,
    second_other,
    away,
    arrived,
    send_sem,
    arrive_sem,
):
    local, channels = first_ref.shape
    width = output_ref.shape[0]
    hidden_width = bias_ref.shape[1]
    columns = hidden_width // 2
    copies = Copies(send_sem, arrive_sem)
    greet_sibling()
    mixed_copy = copies.to(sibling(), mixed_ref.at[:, local:], mixed_other, 0)
    mixed_copy.start()
    cotangent = cotangent_ref[...]
    cotangent_turned = to_low(product(nested_picks(channels, ORDERS[0]), cotangent, 1, 1))
    second = first_ref[...] + output_bias_ref[...]
    second += product(mixed_ref[:, :local], output_ref[...], 0, 0)
    mixed_copy.wait()
    second += product(mixed_other[...], output_other_ref[...], 0, 0)
    normal, inverse = layer_norm(second)
    feed_low = to_low(normal * gain_ref[...] + shift_ref[...])
    feed_turned = to_low(product(nested_picks(channels, ORDERS[1]), feed_low, 1, 1))
    result = second + reduce_bias_ref[...]
    feed_grad = jnp.zeros_like(second)
    weight_copies = []
    for index, (up_ref, up_bias_ref, down_ref) in enumerate(
        (
            (expand_other_ref, bias_other_ref, reduce_other_ref),
            (expand_ref, bias_ref, reduce_ref),
        )
    ):
        for start in range(0, hidden_width, columns):
            now = slice(start, start + columns)
            hidden = product(feed_low, up_ref[:, now], 1, 0) + up_bias_ref[:, now]
            below = 0.5 + 0.5 * lax.erf(hidden * 0.5**0.5)
            slope = below + hidden * (jnp.exp(-0.5 * hidden * hidden) * (0.5 / jnp.pi) ** 0.5)
            active = to_low(hidden * below)
            hidden_grad = to_low(product(cotangent, down_ref[now, :], 1, 1) * slope)
            result += product(active, down_ref[now, :], 1, 0)
            feed_grad += product(hidden_grad, up_ref[:, now], 1, 1)
            bias_grad_ref[index : index + 1, now] = column_sum(to_wide(hidden_grad))
            reduce_grad = product(cotangent_turned, active, 1, 0)
            expand_grad = product(feed_turned, hidden_grad, 1, 0)
            if index == 0:
                away[0, :, now] = reduce_grad
                away[1, :, now] = expand_grad
                for kind in range(2):
                    copy = copies.to(
                        sibling(),
                        away.at[kind, :, now],
                        arrived.at[kind, :, now],
                        2 + len(weight_copies),
                    )
                    copy.start()
                    weight_copies.append(copy)
            else:
                sums_ref[0, :, now] = reduce_grad
                sums_ref[1, :, now] = expand_grad
    result_ref[...] = to_low(result)
    upstream = to_wide(cotangent)
    second_grad = upstream + norm_back(feed_grad, normal, inverse, gain_ref[...])
    second_grad_ref[...] = second_grad
    second_own[...] = to_low(second_grad)
    second_copy = copies.to(sibling(), second_own, second_other, 1)
    second_copy.start()
    vectors_ref[0:1] = column_sum(second_grad)
    vectors_ref[1:2] = column_sum(feed_grad * normal)
    vectors_ref[2:3] = column_sum(feed_grad)
    vectors_ref[3:4] = column_sum(upstream)
    mixed_grad_ref[:, :local] = to_low(product(output_ref[...], second_own[...], 1, 1))
    picks = [nested_picks(channels, order) for order in ORDERS[:2]]
    part = width // 2
    for kind in range(2):
        turned = to_low(product(picks[kind], second_own[...], 1, 1))
        sums_ref[kind, :, hidden_width:] = product(
            turned, mixed_ref[kind * part : (kind + 1) * part, :local], 1, 1
        )
    second_copy.wait()
    mixed_grad_ref[:, local:] = to_low(product(output_ref[...], second_other[...], 1, 1))
    for kind in range(2):
        turned = to_low(product(picks[kind], second_other[...], 1, 1))
        sums_ref[kind, :, hidden_width:] += product(
            turned, mixed_ref[kind * part : (kind + 1) * part, local:], 1, 1
        )
    for copy in weight_copies:
        copy.wait()
    sums_ref[:, :, :hidden_width] += arrived[...]


def feed(operands):
    local, channels = operands[1].shape
    width, rows = operands[0].shape
    hidden = operands[10].shape[1]
    low, full = jnp.bfloat16, jnp.float32
    shape = jax.ShapeDtypeStruct
    return pl.pallas_call(
        feed_kernel,
        in_specs=[vmem()] * len(operands),
        out_specs=[vmem()] * 6,
        out_shape=[
            shape((local, channels), low),
            shape((local, channels), full),
            shape((width, rows), low),
            shape((2, channels, hidden + width // 2), full),
            shape((4, channels), full),
            shape((2, hidden), full),
        ],
        scratch_shapes=[
            pltpu.VMEM((width, local), low),
            pltpu.VMEM((local, channels), low),
            pltpu.VMEM((local, channels), low),
            pltpu.VMEM((2, channels, hidden), full),
            pltpu.VMEM((2, channels, hidden), full),
            *copy_sems(6),
        ],
        compiler_params=pltpu.CompilerParams(
            vmem_limit_bytes=VMEM_BYTES, collective_id=3, has_side_effects=True
        ),
        cost_estimate=pl.CostEstimate(
            flops=10 * 10**9, bytes_accessed=16 * 10**6, transcendentals=0
        ),
    )(*operands)


def return_kernel(
    grad_ref,
    heads_ref,
    attend_ref,
    second_grad_ref,
    first_ref,
    linear_ref,
    attend_gain_ref,
    encode_gain_ref,
    encode_ref,
    conved_ref,
    feed_vectors_ref,
    bias_grad_ref,
    first_grad_ref,
    conved_grad_ref,
    extra_ref,
    vectors_ref,
    attend_away,
    attend_arrived,
    linear_own,
    linear_other,
    send_sem,
    arrive_sem,
):
    local, channels = first_ref.shape
    side = lax.axis_index("tp")
    mine = pl.ds(pl.multiple_of(side * local, local), local)
    theirs = pl.ds(pl.multiple_of((1 - side) * local, local), local)
    copies = Copies(send_sem, arrive_sem)

    def attend_grad(start):
        return sum(
            product(grad_ref[index, :, start : start + local].T, heads_ref[index], 1, 1)
            for index in range(3)
        )

    attend_away[...] = attend_grad(local)
    greet_sibling()
    attend_copy = copies.to(sibling(), attend_away, attend_arrived, 0)
    attend_copy.start()
    upstream = attend_grad(0)
    picks = [nested_picks(channels, order) for order in ORDERS]
    for kind in range(2):
        turned = [to_low(product(picks[kind], attend_ref[i], 1, 1)) for i in range(2)]
        for index in (0, 1) if kind == 0 else (2,):
            extra_ref[kind, index % 2] = product(
                turned[0], grad_ref[index, :, :local], 1, 1
            ) + product(turned[1], grad_ref[index, :, local:], 1, 1)
    normal, inverse = layer_norm(first_ref[...])
    attend_copy.wait()
    upstream += attend_arrived[...]
    first_grad = second_grad_ref[...] + norm_back(upstream, normal, inverse, attend_gain_ref[...])
    first_grad_ref[...] = first_grad
    vectors_ref[0:4] = feed_vectors_ref[...]
    for index in range(2):
        chosen = jnp.where(side == index, bias_grad_ref[1:2], bias_grad_ref[0:1])
        for part in range(2):
            row = 8 + 2 * index + part
            vectors_ref[row : row + 1] = chosen[:, part * channels : (part + 1) * channels]
    vectors_ref[4:5] = column_sum(upstream * normal)
    vectors_ref[5:6] = column_sum(upstream)
    normal, inverse = layer_norm(linear_ref[...])
    linear_own[...] = to_low(norm_back(first_grad, normal, inverse, encode_gain_ref[...]))
    linear_copy = copies.to(sibling(), linear_own, linear_other, 1)
    linear_copy.start()
    vectors_ref[6:7] = column_sum(first_grad * normal)
    vectors_ref[7:8] = column_sum(first_grad)
    conved_grad_ref[mine] = to_low(product(linear_own[...], encode_ref[...], 1, 1))
    turned = to_low(product(picks[1], linear_own[...], 1, 1))
    extra_ref[1, 1] = product(turned, conved_ref[mine], 1, 0)
    linear_copy.wait()
    conved_grad_ref[theirs] = to_low(product(linear_other[...], encode_ref[...], 1, 1))
    turned = to_low(product(picks[1], linear_other[...], 1, 1))
    extra_ref[1, 1] += product(turned, conved_ref[theirs], 1, 0)


def return_to_conv(operands):
    local, channels = operands[4].shape
    rows, width = operands[9].shape
    low, full = jnp.bfloat16, jnp.float32
    shape = jax.ShapeDtypeStruct
    return pl.pallas_call(
        return_kernel,
        in_specs=[vmem()] * len(operands),
        out_specs=[vmem()] * 4,
        out_shape=[
            shape((local, channels), full),
            shape((rows, width), low),
            shape((2, 2, channels, width), full),
            shape((12, channels), full),
        ],
        scratch_shapes=[
            pltpu.VMEM((local, channels), full),
            pltpu.VMEM((local, channels), full),
            pltpu.VMEM((local, channels), low),
            pltpu.VMEM((local, channels), low),
            *copy_sems(2),
        ],
        compiler_params=pltpu.CompilerParams(
            vmem_limit_bytes=VMEM_BYTES, collective_id=4, has_side_effects=True
        ),
        cost_estimate=pl.CostEstimate(
            flops=6 * 10**9, bytes_accessed=12 * 10**6, transcendentals=0
        ),
    )(*operands)


def partner_of(bit):
    me = lax.axis_index("pts")
    return me + (1 - 2 * ((me // (1 << bit)) % 2)) * (1 << bit)


def greet_partners():
    barrier = pltpu.get_barrier_semaphore()
    for bit in range(KERNEL_BITS):
        pl.semaphore_signal(
            barrier, inc=1, device_id={"pts": partner_of(bit)}, device_id_type=MESH
        )
    return barrier


class PairSums:
    def __init__(self, keep, sends, arrivals, send_sem, arrive_sem):
        self.keep, self.sends, self.arrivals = keep, sends, arrivals
        self.send_sem, self.arrive_sem = send_sem, arrive_sem

    def copy(self, stage, chunk, bit):
        return pltpu.make_async_remote_copy(
            src_ref=self.sends[stage].at[chunk],
            dst_ref=self.arrivals[stage].at[chunk],
            send_sem=self.send_sem.at[stage, chunk],
            recv_sem=self.arrive_sem.at[stage, chunk],
            device_id={"pts": partner_of(bit)},
            device_id_type=MESH,
        )

    def start(self, stage, chunk, kinds):
        for holds, order in kinds:
            if holds is True:
                self.copy(stage, chunk, order[stage]).start()
            else:

                @pl.when(holds)
                def _(order=order):
                    self.copy(stage, chunk, order[stage]).start()

    def advance(self, stage, chunk, kinds, finish):
        self.copy(stage, chunk, 0).wait()
        rows = self.keep.shape[2]
        low = rows - (rows >> stage)
        half = (rows - low) // 2
        arrived = self.arrivals[stage]
        if stage == len(self.sends) - 1:
            finish(self.keep[chunk, :, low:] + to_wide(arrived[chunk]))
            return
        self.sends[stage + 1][chunk] = to_low(
            self.keep[chunk, :, low : low + half] + to_wide(arrived[chunk, :, :half])
        )
        self.start(stage + 1, chunk, kinds)
        self.keep[chunk, :, low + half :] += to_wide(arrived[chunk, :, half:])


def pair_scratch(chunks, lead, rows, width, stages):
    halves = [(chunks, lead, rows >> (stage + 1), width) for stage in range(stages)]
    return (
        [pltpu.VMEM(halves[0], jnp.float32)]
        + [pltpu.VMEM(shape, jnp.bfloat16) for shape in halves]
        + [pltpu.VMEM(shape, jnp.bfloat16) for shape in halves]
        + [pltpu.SemaphoreType.DMA((stages, chunks))] * 2
    )


def pair_sums(scratch):
    stages = (len(scratch) - 3) // 2
    keep, rest = scratch[0], scratch[1:]
    return PairSums(keep, rest[:stages], rest[stages : 2 * stages], *rest[-2:])


def conv_backward_kernel(
    near_ref,
    near_other_ref,
    turned_ref,
    turned_other_ref,
    grad_ref,
    weight_ref,
    extra_ref,
    vector_ref,
    first_grad_ref,
    conv_sum_ref,
    heads_sum_ref,
    encode_sum_ref,
    points_grad_ref,
    *refs,
):
    vector_refs, refs = refs[:9], refs[9:]
    (
        spread,
        windows,
        gathered,
        grad_other,
        input_grad,
        input_arrived,
        rim_away,
        rim_arrived,
        vector_away,
        vector_arrived,
        send_sem,
        arrive_sem,
    ) = refs[:12]
    sums, extra_sums = pair_sums(refs[12:21]), pair_sums(refs[21:])
    rows, width = grad_ref.shape
    local, channels = first_grad_ref.shape
    half = channels // 2
    quarter = half // 4
    blocks = rows // BLOCK
    extras = extra_ref.shape[0]
    chunks = conv_sum_ref.shape[0]
    patches = lax.axis_size("pts")
    me, side = lax.axis_index("pts"), lax.axis_index("tp")
    step = pl.program_id(0)
    copies = Copies(send_sem, arrive_sem)
    mine = pl.ds(pl.multiple_of(HALO + side * local, HALO), local)
    theirs = pl.ds(pl.multiple_of(HALO + (1 - side) * local, HALO), local)
    grad_copy = copies.to({"pts": partner_of(SHARE_BIT)}, grad_ref, grad_other, 0)
    input_copy = copies.to(sibling(), input_grad.at[theirs], input_arrived, 1)
    rims = (
        (me > 0, {"pts": me - 1, "tp": 1}, slice(0, HALO)),
        (me < patches - 1, {"pts": me + 1, "tp": 0}, slice(HALO + rows, rows + 2 * HALO)),
    )
    rim_copies = [
        [copies.to(rim[1], rim_away.at[i], rim_arrived.at[core], 2 + i, 4 + core) for core in (0, 1)]
        for i, rim in enumerate(rims)
    ]
    has_rim = ((side == 0) & (me > 0)) | ((side == 1) & (me < patches - 1))
    first_sum = chunks // GROUP
    first_input = first_sum + chunks
    input_steps = chunks // GROUP

    def vector_copy(stage):
        device = sibling() if stage == 0 else {"pts": partner_of(stage - 1)}
        return copies.to(device, vector_away.at[stage], vector_arrived.at[stage], 6 + stage)

    def kinds(chunk):
        return ((chunk % 2 == 0, CONV_ORDERS[0]), (chunk % 2 == 1, CONV_ORDERS[1]))

    @pl.when(step == 0)
    def _():
        barrier = greet_partners()
        pl.semaphore_signal(barrier, inc=1, device_id=sibling(), device_id_type=MESH)
        for core in range(2):

            @pl.when((side == 0) & (me > 0))
            def _(core=core):
                device = {"pts": me - 1, "tp": core}
                pl.semaphore_signal(barrier, inc=1, device_id=device, device_id_type=MESH)

            @pl.when((side == 1) & (me < patches - 1))
            def _(core=core):
                device = {"pts": me + 1, "tp": core}
                pl.semaphore_signal(barrier, inc=1, device_id=device, device_id_type=MESH)

        sent = jnp.where(me > 0, 1, 0) + jnp.where(me < patches - 1, 1, 0)
        pl.semaphore_wait(barrier, KERNEL_BITS + 1 + sent)
        grad_copy.start()
        for index in range(extras):
            extra_sums.sends[0][index] = to_low(extra_ref[index, :, :half])
            extra_sums.start(0, index, ((True, ORDERS[index]),))
            extra_sums.keep[index] = extra_ref[index, :, half:]
        vector_away[0] = vector_ref[...]
        vector_copy(0).start()
        for kind, places in enumerate(((0, 1, 2, 3), (0, 2, 1, 3))):
            for place, source in enumerate(places):
                now = slice(place * quarter, (place + 1) * quarter)
                low = source * quarter
                windows[kind, 0, now] = turned_ref[half + low : half + low + quarter, :]
                windows[kind, 1, now] = turned_other_ref[low : low + quarter, :]
        input_grad[...] = jnp.zeros_like(input_grad)

    @pl.when(step < first_sum)
    def _():
        slots = to_wide(lax.broadcasted_iota(jnp.int32, (BLOCK, 1), 0))

        def spread_group(group, _):
            for offset in range(GROUP):
                index = (step * GROUP + group) * GROUP + offset
                near = near_ref[pl.ds(index, 1), :]
                for part in range(blocks + 1):
                    low = max(part - 1, 0) * BLOCK
                    high = min(part + 1, blocks) * BLOCK
                    select = to_low(
                        jnp.where(near[:, low:high] - float(part * BLOCK) == slots, 1.0, 0.0)
                    )
                    spread[index, part * BLOCK : (part + 1) * BLOCK] = to_low(
                        product(select, grad_ref[low:high, :], 1, 0)
                    )
            return 0

        lax.fori_loop(0, GROUP, spread_group, 0)

    @pl.when((step >= first_sum) & (step < first_input))
    def _():
        chunk = step - first_sum
        pl.when(chunk == 0)(grad_copy.wait)
        slots = to_wide(lax.broadcasted_iota(jnp.int32, (2 * BLOCK, 1), 0))
        for offset in range(GROUP):
            near = near_other_ref[pl.ds(chunk * GROUP + offset, 1), :]
            for block in range(blocks):
                low = block * BLOCK
                select = to_low(
                    jnp.where(near[:, low : low + BLOCK] - float(low) == slots, 1.0, 0.0)
                )
                gathered[offset, :, low : low + BLOCK] = to_low(
                    product(windows[chunk % 2, 1, :, low : low + 2 * BLOCK], select, 1, 0)
                )
        for offset in range(GROUP):
            weight_grad = product(windows[chunk % 2, 0], spread[chunk * GROUP + offset], 1, 0)
            weight_grad += product(gathered[offset], grad_other[...], 1, 0)
            sums.sends[0][chunk, offset] = to_low(weight_grad[: half // 2])
            sums.keep[chunk, offset] = weight_grad[half // 2 :]
        sums.start(0, chunk, kinds(chunk))

    for phase, parts in enumerate(((theirs, rims[0][2], rims[1][2]), (mine,))):
        start = first_input + phase * input_steps

        @pl.when((step >= start) & (step < start + input_steps))
        def _(start=start, parts=parts):
            def input_group(group, _):
                for part in parts:
                    total = input_grad[part, :]
                    for offset in range(GROUP):
                        index = group * GROUP + offset
                        total += product(
                            spread[(step - start) * WIDE_GROUP + index, part, :],
                            weight_ref[index],
                            1,
                            1,
                        )
                    input_grad[part, :] = total
                return 0

            lax.fori_loop(0, GROUP, input_group, 0)

    @pl.when(step == first_input + input_steps - 1)
    def _():
        input_copy.start()
        for index, (has, _, part) in enumerate(rims):
            rim_away[index] = to_low(input_grad[part, :])

            @pl.when(has)
            def _(index=index):
                for core in range(2):

                    @pl.when(side == core)
                    def _(core=core):
                        rim_copies[index][core].start()

    @pl.when(step == pl.num_programs(0) - 1)
    def _():
        input_copy.wait()
        points_grad_ref[...] = first_grad_ref[...] + input_grad[mine, :] + input_arrived[...]

        @pl.when(has_rim)
        def _():
            edge = pl.ds(pl.multiple_of(side * (local - HALO), HALO), HALO)
            for core in range(2):
                rim_copies[0][core].wait_recv()
                points_grad_ref[edge, :] += to_wide(rim_arrived[core])

        for index, (has, _, part) in enumerate(rims):
            pl.when(has)(rim_copies[index][0].wait_send)

    for stage, due in enumerate(VECTOR_STEPS):

        @pl.when(step == due)
        def _(stage=stage):
            vector_copy(stage).wait()
            summed = vector_away[stage] + vector_arrived[stage]
            if stage < KERNEL_BITS:
                vector_away[stage + 1] = summed
                vector_copy(stage + 1).start()
                return
            for index in range(8):
                vector_refs[index][...] = summed[index : index + 1]
            for index in range(8, summed.shape[0]):
                low = (index - 8) * channels
                vector_refs[8][:, low : low + channels] = summed[index : index + 1]

    for stage in range(len(CONV_LAGS)):
        chunk = step - first_sum - CONV_LAGS[stage]

        @pl.when((chunk >= 0) & (chunk < chunks))
        def _(stage=stage, chunk=chunk):
            def finish(total):
                conv_sum_ref[chunk] = total

            sums.advance(stage, chunk, kinds(chunk), finish)

    def finish_extra(index, total):
        if index == 0:
            heads_sum_ref[0:2] = total
        else:
            heads_sum_ref[2] = total[0]
            encode_sum_ref[...] = total[1].T

    for stage, due in enumerate(EXTRA_STEPS):

        @pl.when(step == due)
        def _(stage=stage):
            for index in range(extras):
                extra_sums.advance(
                    stage,
                    index,
                    ((True, ORDERS[index]),),
                    functools.partial(finish_extra, index),
                )


def conv_backward(
    near, near_other, turned, turned_other, grad, weight, extra, vector, first_grad
):
    offsets, channels, width = weight.shape
    wide = turned.shape[1]
    rows = grad.shape[0]
    local = first_grad.shape[0]
    chunks = offsets // GROUP
    first_input = chunks // GROUP + chunks
    input_steps = chunks // GROUP
    low, full = jnp.bfloat16, jnp.float32
    kept = channels >> KERNEL_BITS
    shape = jax.ShapeDtypeStruct
    outs = [
        shape((chunks, GROUP, kept, width), full),
        shape((3, kept, width), full),
        shape((width, kept), full),
        shape(first_grad.shape, full),
        *[shape((1, channels), full)] * 8,
        shape((1, (vector.shape[0] - 8) * channels), full),
    ]

    def weight_block(i):
        return (jnp.maximum(i - first_input, 0) % input_steps, 0, 0)

    return pl.pallas_call(
        conv_backward_kernel,
        grid=(first_input + 2 * input_steps,),
        in_specs=[
            whole(near),
            whole(near_other),
            whole(turned),
            whole(turned_other),
            whole(grad),
            pl.BlockSpec((WIDE_GROUP, channels, width), weight_block),
            whole(extra),
            whole(vector),
            whole(first_grad),
        ],
        out_specs=[whole(out) for out in outs],
        out_shape=outs,
        scratch_shapes=[
            pltpu.VMEM((offsets, wide, width), low),
            pltpu.VMEM((2, 2, channels // 2, wide), low),
            pltpu.VMEM((GROUP, channels // 2, rows), low),
            pltpu.VMEM((rows, width), low),
            pltpu.VMEM((wide, channels), full),
            pltpu.VMEM((local, channels), full),
            pltpu.VMEM((2, HALO, channels), low),
            pltpu.VMEM((2, HALO, channels), low),
            pltpu.VMEM((KERNEL_BITS + 1, *vector.shape), full),
            pltpu.VMEM((KERNEL_BITS + 1, *vector.shape), full),
            *copy_sems(7 + KERNEL_BITS),
            *pair_scratch(chunks, GROUP, channels // 2, width, len(CONV_LAGS)),
            *pair_scratch(*extra.shape, KERNEL_BITS),
        ],
        compiler_params=pltpu.CompilerParams(
            vmem_limit_bytes=VMEM_BYTES, collective_id=1, has_side_effects=True
        ),
        cost_estimate=pl.CostEstimate(
            flops=80 * 10**9, bytes_accessed=16 * 10**6, transcendentals=0
        ),
    )(near, near_other, turned, turned_other, grad, weight, extra, vector, first_grad)


def hand_over_kernel(*refs):
    count = len(refs) // 2
    copies = [
        pltpu.make_async_copy(refs[i], refs[count + i], refs[-1].at[i]) for i in range(count)
    ]
    for copy in copies:
        copy.start()
    for copy in copies:
        copy.wait()


def hand_over(arrays):
    anywhere = pl.BlockSpec(memory_space=pl.ANY)
    return pl.pallas_call(
        hand_over_kernel,
        in_specs=[anywhere] * len(arrays),
        out_specs=[anywhere] * len(arrays),
        out_shape=[jax.ShapeDtypeStruct(each.shape, each.dtype) for each in arrays],
        scratch_shapes=[pltpu.SemaphoreType.DMA((len(arrays),))],
        compiler_params=pltpu.CompilerParams(vmem_limit_bytes=VMEM_BYTES),
    )(*arrays)


def exchange(values, bit):
    count = lax.axis_size("pts")
    return lax.ppermute(values, "pts", [(i, i ^ (1 << bit)) for i in range(count)])


def sum_rest(keep, axis):
    for bit in range(KERNEL_BITS, patch_bits()):
        half = keep.shape[axis] // 2
        away = lax.slice_in_dim(keep, 0, half, axis=axis)
        keep = lax.slice_in_dim(keep, half, 2 * half, axis=axis)
        keep = keep + to_wide(exchange(to_low(away), bit))
    return keep


def per_device(
    points,
    neighbours,
    valid_count,
    conv_weight,
    encode_weight,
    encode_gain,
    encode_shift,
    attend_gain,
    attend_shift,
    heads_weight,
    output_weight,
    output_bias,
    feed_gain,
    feed_shift,
    expand_weight,
    expand_bias,
    reduce_weight,
    reduce_bias,
    cotangent,
):
    local, channels = points.shape
    rows = 2 * local
    is_first = lax.axis_index("tp") == 0
    norms = [v[None, :] for v in (encode_gain, encode_shift, attend_gain, attend_shift)]
    (
        turned, near_columns, conved, linear, first, attend_in, projected,
        output_other, expand_other, reduce_other, bias_other,
    ) = forward_start(
        neighbours, points, conv_weight, encode_weight, norms, heads_weight, output_weight,
        expand_weight, reduce_weight, expand_bias[None, :]
    )

    place = jnp.arange(rows, dtype=jnp.int32)
    place = jnp.where(is_first, place, (place + local) % rows)
    bias = jnp.where(place < valid_count[0], 0.0, MASKED)
    bias = to_low(jnp.where(jnp.arange(HEAD_DIM)[:, None] == 0, bias[None, :], 0.0))
    mixed, logs = attend(projected, bias)
    result, second_grad, mixed_grad, feed_grads, feed_vectors, bias_grads = feed(
        [
            mixed, first, output_weight, output_other, output_bias[None, :], feed_gain[None, :],
            feed_shift[None, :], cotangent, expand_weight, expand_other, expand_bias[None, :],
            bias_other, reduce_weight, reduce_other, reduce_bias[None, :],
        ]
    )
    projected_grad, reduce_sum, expand_sum, output_sum, turned_other, near_other = attend_back(
        projected, bias, mixed, logs, mixed_grad, feed_grads[:, None], turned, near_columns
    )
    first_grad, conved_grad, extra, vector = return_to_conv(
        [
            projected_grad, heads_weight, attend_in, second_grad, first, linear, norms[2],
            norms[0], encode_weight, conved, feed_vectors, bias_grads,
        ]
    )
    conv_sum, heads_sum, encode_sum, points_gradient, *vectors = conv_backward(
        near_columns, near_other, turned, turned_other, conved_grad, conv_weight, extra, vector,
        first_grad
    )
    for bit in range(KERNEL_BITS, patch_bits()):
        vectors = [each + exchange(each, bit) for each in vectors]
    parts = hand_over(
        [
            result,
            points_gradient,
            sum_rest(conv_sum, 2),
            sum_rest(encode_sum, 1),
            sum_rest(heads_sum, 1),
            sum_rest(output_sum, 1),
            sum_rest(expand_sum, 0),
            sum_rest(reduce_sum, 1),
            *vectors,
        ]
    )
    vectors = [each.reshape(-1) for each in parts[8:]]
    return (
        parts[0],
        parts[1],
        parts[2].reshape(-1, *parts[2].shape[2:]),
        parts[3],
        vectors[6],
        vectors[7],
        vectors[4],
        vectors[5],
        parts[4],
        parts[5],
        vectors[0],
        vectors[1],
        vectors[2],
        parts[6],
        vectors[8],
        parts[7],
        vectors[3],
    )


def solution(mesh):
    placed = (
        P(("pts", "tp"), None),
        P("pts", None),
        P("pts"),
        P(None, None, "tp"),
        P("tp", None),
        P(),
        P(),
        P(),
        P(),
        P(None, None, "tp"),
        P("tp", None),
        P(),
        P(),
        P(),
        P(None, "tp"),
        P("tp"),
        P("tp", None),
        P(),
        P(("pts", "tp"), None),
    )
    return jax.shard_map(
        per_device,
        mesh=mesh,
        in_specs=placed,
        out_specs=(
            P(("pts", "tp"), None),
            P(("pts", "tp"), None),
            P(None, "pts", "tp"),
            P("tp", "pts"),
            P(),
            P(),
            P(),
            P(),
            P(None, "pts", "tp"),
            P("tp", "pts"),
            P(),
            P(),
            P(),
            P("pts", "tp"),
            P(),
            P("tp", "pts"),
            P(),
        ),
        check_vma=False,
    )
```

```python
import functools

import jax
import jax.numpy as jnp
from jax import lax
from jax.experimental import pallas as pl
from jax.experimental.pallas import tpu as pltpu
from jax.sharding import PartitionSpec as P

MESH = pl.DeviceIdType.MESH
HEAD_DIM = 16
HALO = 128
BLOCK = 256
GROUP = 3
EPSILON = 1e-05
MASKED = -1e30
KERNEL_BITS = 4
ORDERS = ((0, 1, 2, 3), (1, 0, 2, 3))
VMEM_BYTES = 60 << 20
HEADS_STEP = 4
HEADS_BACK_STEP = 2
SUM_STEPS = (3, 5, 6, 7)
SHARE_BIT = 2
CONV_ORDERS = ((0, 1, 3), (1, 0, 3))
WINDOW_ORDER = (2, 0, 1, 3)
CONV_LAGS = (2, 4, 6)
EXTRA_STEPS = (2, 3, 5, 7)
VECTOR_STEPS = (1, 2, 3, 4, 5)
WEIGHTS_AHEAD = 3
WIDE_GROUP = 9


def to_low(values):
    return values.astype(jnp.bfloat16)


def to_wide(values):
    return values.astype(jnp.float32)


def product(left, right, left_dim, right_dim):
    dims = (((left_dim,), (right_dim,)), ((), ()))
    return lax.dot_general(left, right, dims, preferred_element_type=jnp.float32)


def layer_norm(values):
    row_mean = jnp.mean(values, axis=-1, keepdims=True)
    centred = values - row_mean
    inverse = lax.rsqrt(jnp.mean(centred * centred, axis=-1, keepdims=True) + EPSILON)
    return centred * inverse, inverse


def norm_back(upstream, normal_part, inverse, norm_gain):
    scaled = upstream * norm_gain
    across = (
        scaled
        - jnp.mean(scaled, axis=-1, keepdims=True)
        - normal_part * jnp.mean(scaled * normal_part, axis=-1, keepdims=True)
    )
    return across * inverse


def column_sum(values):
    return jnp.sum(values, axis=0, keepdims=True)


def nested_picks(channels, order):
    me = lax.axis_index("pts")
    order = order + tuple(range(KERNEL_BITS, patch_bits()))
    depth = channels >> len(order)
    lanes = 128
    place = lax.broadcasted_iota(jnp.int32, (channels, lanes), 0)
    picked = place & (depth - 1)
    for stage, bit in enumerate(order):
        kept = (place >> (channels.bit_length() - 2 - stage)) & 1
        picked = picked + (1 - ((kept + me // (1 << bit)) & 1)) * (depth << bit)
    column = lax.broadcasted_iota(jnp.int32, (channels, lanes), 1)
    return to_low(
        jnp.concatenate(
            [
                jnp.where(picked == column + low, 1.0, 0.0)
                for low in range(0, channels, lanes)
            ],
            axis=1,
        )
    )


class Copies:
    def __init__(self, send_sem, arrive_sem):
        self.send_sem, self.arrive_sem = send_sem, arrive_sem

    def to(self, device, source, target, send, arrive=None):
        return pltpu.make_async_remote_copy(
            src_ref=source,
            dst_ref=target,
            send_sem=self.send_sem.at[send],
            recv_sem=self.arrive_sem.at[send if arrive is None else arrive],
            device_id=device,
            device_id_type=MESH,
        )


def copy_sems(count):
    return [pltpu.SemaphoreType.DMA((count,))] * 2


def patch_bits():
    return lax.axis_size("pts").bit_length() - 1


def sibling():
    return {"tp": 1 - lax.axis_index("tp")}


def greet_sibling():
    barrier = pltpu.get_barrier_semaphore()
    pl.semaphore_signal(barrier, inc=1, device_id=sibling(), device_id_type=MESH)
    pl.semaphore_wait(barrier, 1)


def vmem():
    return pl.BlockSpec(memory_space=pltpu.VMEM)


def whole(array):
    zeros = (0,) * array.ndim
    return pl.BlockSpec(array.shape, lambda i: zeros, pipeline_mode=pl.Buffered(1))


def forward_kernel(
    near_ref,
    points_ref,
    weight_ref,
    weights_ref,
    encode_ref,
    encode_gain_ref,
    encode_shift_ref,
    attend_gain_ref,
    attend_shift_ref,
    heads_ref,
    output_ref,
    expand_ref,
    reduce_ref,
    bias_ref,
    turned_ref,
    near_columns_ref,
    conved_ref,
    linear_ref,
    first_ref,
    attend_ref,
    projected_ref,
    output_other,
    expand_other,
    reduce_other,
    bias_other,
    window,
    total,
    rows,
    weight_other,
    encode_other,
    conved_away,
    conved_other,
    attend_other,
    heads_turned,
    near_wide,
    near_tall,
    picks,
    weight_first,
    send_sem,
    arrive_sem,
):
    step = pl.program_id(0)
    steps = pl.num_programs(0)
    local, channels = points_ref.shape
    width = weight_ref.shape[2]
    patches = lax.axis_size("pts")
    me, side = lax.axis_index("pts"), lax.axis_index("tp")
    copies = Copies(send_sem, arrive_sem)
    own_place = pl.ds(pl.multiple_of(HALO + side * local, HALO), local)
    other_place = pl.ds(pl.multiple_of(HALO + (1 - side) * local, HALO), local)
    points_copy = copies.to(sibling(), points_ref, window.at[own_place], 0)
    low_rim, high_rim = slice(0, HALO), slice(HALO + 2 * local, 2 * HALO + 2 * local)
    low_copies = [
        copies.to(
            {"pts": me + 1, "tp": core},
            points_ref.at[local - HALO :],
            window.at[low_rim],
            3 + core,
            1,
        )
        for core in range(2)
    ]
    high_copies = [
        copies.to(
            {"pts": me - 1, "tp": core}, points_ref.at[0:HALO], window.at[high_rim], 3 + core, 2
        )
        for core in range(2)
    ]
    small_copies = [
        copies.to(sibling(), encode_ref, encode_other, 5),
        copies.to(sibling(), output_ref, output_other, 6),
        copies.to(sibling(), expand_ref, expand_other, 7),
        copies.to(sibling(), reduce_ref, reduce_other, 8),
        copies.to(sibling(), bias_ref, bias_other, 9),
    ]
    up = (side == 1) & (me < patches - 1)
    down = (side == 0) & (me > 0)

    def weight_copy(group):
        part = pl.ds(group * GROUP, GROUP)
        return copies.to(sibling(), weights_ref.at[part], weight_other.at[part], 12 + group)

    def turn(place):
        return to_low(product(picks[...], window[place, :], 1, 1))

    @pl.when(step == 0)
    def _():
        barrier = pltpu.get_barrier_semaphore()
        pl.semaphore_signal(barrier, inc=1, device_id=sibling(), device_id_type=MESH)

        @pl.when(me > 0)
        def _():
            pl.semaphore_signal(
                barrier, inc=1, device_id={"pts": me - 1, "tp": 1}, device_id_type=MESH
            )

        @pl.when(me < patches - 1)
        def _():
            pl.semaphore_signal(
                barrier, inc=1, device_id={"pts": me + 1, "tp": 0}, device_id_type=MESH
            )

        pl.semaphore_wait(barrier, jnp.where(up | down, 3, 1))
        points_copy.start()

        @pl.when(up)
        def _():
            for copy in low_copies:
                copy.start()

        @pl.when(down)
        def _():
            for copy in high_copies:
                copy.start()

        for group in range(WEIGHTS_AHEAD):
            weight_copy(group).start()
        window[own_place, :] = points_ref[...]

        @pl.when(me == 0)
        def _():
            window[low_rim, :] = jnp.zeros((HALO, channels), jnp.bfloat16)

        @pl.when(me == patches - 1)
        def _():
            window[high_rim, :] = jnp.zeros((HALO, channels), jnp.bfloat16)

        picks[...] = nested_picks(channels, WINDOW_ORDER)
        turned_ref[:, own_place] = turn(own_place)
        for index in range(3):
            heads_turned[index] = heads_ref[index].T
        near_tall[...] = jnp.zeros_like(near_tall)
        near_tall[: near_ref.shape[0]] = to_wide(near_ref[...])
        near_columns_ref[...] = near_tall[: near_columns_ref.shape[0]]
        near_wide[...] = near_tall[...].T
        points_copy.wait()

    @pl.when(step == 2)
    def _():
        for place in (other_place, low_rim, high_rim):
            turned_ref[:, place] = turn(place)

        for copy in small_copies:
            copy.start()

    def wait_rims():
        @pl.when(me > 0)
        def _():
            low_copies[0].wait_recv()

        @pl.when(me < patches - 1)
        def _():
            high_copies[0].wait_recv()

        @pl.when(up)
        def _():
            for copy in low_copies:
                copy.wait_send()

        @pl.when(down)
        def _():
            for copy in high_copies:
                copy.wait_send()

    @pl.when((step > 0) & (step + WEIGHTS_AHEAD - 1 < steps))
    def _():
        weight_copy(step + WEIGHTS_AHEAD - 1).start()

    weight_copy(step).wait()
    lane = lax.broadcasted_iota(jnp.int32, (BLOCK, near_wide.shape[1]), 1)
    slots = to_wide(lax.broadcasted_iota(jnp.int32, (BLOCK, 2 * BLOCK), 1))
    places = [pl.ds(pl.multiple_of(block * BLOCK, BLOCK), BLOCK) for block in (1 - side, side)]

    def gather(index, group):
        low = pl.multiple_of(side * local + (1 - side, side)[index] * BLOCK, BLOCK)
        part = window[pl.ds(low, 2 * BLOCK), :]
        near = near_wide[pl.ds(low, BLOCK), :] - low.astype(jnp.float32)
        for offset in range(GROUP):
            chosen = jnp.where(lane == group * GROUP + offset, near, 0.0)
            column = jnp.sum(chosen, axis=1, keepdims=True)
            select = to_low(jnp.where(column == slots, 1.0, 0.0))
            rows[places[index], offset * channels : (offset + 1) * channels] = to_low(
                product(select, part, 1, 0)
            )

    def apply(place, own_ref, group):
        picked = rows[place, :]
        other = weight_other[pl.ds(group * GROUP, GROUP)]
        flat = (GROUP * channels, width)
        return (
            product(picked, own_ref[...].reshape(flat), 1, 0),
            product(picked, other.reshape(flat), 1, 0),
        )

    @pl.when(step == 0)
    def _():
        gather(0, 0)
        total[places[0], :width], total[places[0], width:] = apply(places[0], weight_ref, 0)
        weight_first[...] = weight_ref[...]

    @pl.when(step == 1)
    def _():
        wait_rims()
        gather(1, 0)
        total[places[1], :width], total[places[1], width:] = apply(places[1], weight_first, 0)

    @pl.when(step > 0)
    def _():
        gather(0, step)
        gather(1, step)
        own, other = apply(slice(None), weight_ref, step)
        total[:, :width] += own
        total[:, width:] += other

    @pl.when(step == steps - 1)
    def _():
        mine = pl.ds(pl.multiple_of(side * local, local), local)
        theirs = pl.ds(pl.multiple_of((1 - side) * local, local), local)
        conved_own = to_low(total[:, :width])
        conved_away[...] = to_low(total[:, width:])
        conved_ref[mine] = conved_own
        conved_copy = copies.to(sibling(), conved_away, conved_other, 10)
        conved_copy.start()
        small_copies[0].wait()
        linear = product(conved_own, encode_ref[...], 1, 0)
        linear += product(conved_away[...], encode_other[...], 1, 0)
        linear_ref[...] = linear
        first = layer_norm(linear)[0] * encode_gain_ref[...] + encode_shift_ref[...]
        first += to_wide(points_ref[...])
        first_ref[...] = first
        attend_out = layer_norm(first)[0] * attend_gain_ref[...] + attend_shift_ref[...]
        attend_ref[0] = to_low(attend_out)
        attend_copy = copies.to(sibling(), attend_ref.at[0], attend_other, 11)
        attend_copy.start()
        for index in range(3):
            projected_ref[index, :, :local] = to_low(
                product(heads_turned[index], attend_ref[0], 1, 1)
            )
        attend_copy.wait()
        attend_ref[1] = attend_other[...]
        for index in range(3):
            projected_ref[index, :, local:] = to_low(
                product(heads_turned[index], attend_other[...], 1, 1)
            )
        conved_copy.wait()
        conved_ref[theirs] = conved_other[...]
        for copy in small_copies[1:]:
            copy.wait()


def forward_start(
    near, points, conv_weight, encode_weight, norms, heads_weight, output_weight, expand_weight,
    reduce_weight, expand_bias
):
    offsets, channels, width = conv_weight.shape
    local = points.shape[0]
    rows = 2 * local
    wide = rows + 2 * HALO
    groups = offsets // GROUP
    low, full = jnp.bfloat16, jnp.float32
    shape = jax.ShapeDtypeStruct
    anywhere = pl.BlockSpec(memory_space=pl.ANY)
    outs = [
        shape((channels, wide), low),
        shape((32, rows), full),
        shape((rows, width), low),
        shape((local, channels), full),
        shape((local, channels), full),
        shape((2, local, channels), low),
        shape((3, width, rows), low),
    ]
    away = [
        shape(array.shape, array.dtype)
        for array in (output_weight, expand_weight, reduce_weight, expand_bias)
    ]
    return pl.pallas_call(
        forward_kernel,
        grid=(groups,),
        in_specs=[
            whole(near),
            whole(points),
            pl.BlockSpec((GROUP, channels, width), lambda i: (i, 0, 0)),
            anywhere,
            whole(encode_weight),
            *[whole(norm) for norm in norms],
            whole(heads_weight),
            anywhere,
            anywhere,
            anywhere,
            anywhere,
        ],
        out_specs=[whole(out) for out in outs] + [anywhere] * 4,
        out_shape=outs + away,
        scratch_shapes=[
            pltpu.VMEM((wide, channels), low),
            pltpu.VMEM((local, channels), full),
            pltpu.VMEM((local, GROUP * channels), low),
            pltpu.VMEM(conv_weight.shape, low),
            pltpu.VMEM(encode_weight.shape, low),
            pltpu.VMEM((local, width), low),
            pltpu.VMEM((local, width), low),
            pltpu.VMEM((local, channels), low),
            pltpu.VMEM((3, width, channels), low),
            pltpu.VMEM((rows, 128), full),
            pltpu.VMEM((128, rows), full),
            pltpu.VMEM((channels, channels), low),
            pltpu.VMEM((GROUP, channels, width), low),
            *copy_sems(12 + groups),
        ],
        compiler_params=pltpu.CompilerParams(
            vmem_limit_bytes=VMEM_BYTES, collective_id=2, has_side_effects=True
        ),
        cost_estimate=pl.CostEstimate(
            flops=30 * 10**9, bytes_accessed=16 * 10**6, transcendentals=0
        ),
    )(
        near, points, conv_weight, conv_weight, encode_weight, *norms, heads_weight,
        output_weight, expand_weight, reduce_weight, expand_bias
    )


def staged(units, begin, finish):
    ready = begin(units[0])
    for index, unit in enumerate(units):
        later = begin(units[index + 1]) if index + 1 < len(units) else None
        finish(unit, ready)
        ready = later


def attend_kernel(chunk, query_ref, key_ref, value_ref, bias_ref, out_ref, log_ref):
    points = query_ref.shape[1]
    heads = query_ref.shape[0] // HEAD_DIM
    row = lax.broadcasted_iota(jnp.int32, (HEAD_DIM, points), 0)
    ones = to_low(jnp.where(row == 0, 1.0, 0.0))
    operands = []
    for head in range(heads):
        part = slice(head * HEAD_DIM, (head + 1) * HEAD_DIM)
        scaled = to_low(to_wide(query_ref[part]) * HEAD_DIM**-0.5)
        operands.append(
            (
                jnp.concatenate([scaled, ones], axis=0),
                jnp.concatenate([key_ref[part], bias_ref[...]], axis=0),
                jnp.concatenate([value_ref[part], ones], axis=0),
            )
        )

    def begin(unit):
        head, start = unit
        queries, keys, _ = operands[head]
        return product(keys, queries[:, start : start + chunk], 0, 0)

    def finish(unit, scores):
        head, start = unit
        top = jnp.max(scores, axis=0, keepdims=True)
        mixed = product(operands[head][2], to_low(jnp.exp(scores - top)), 1, 0)
        total = mixed[HEAD_DIM : HEAD_DIM + 1, :]
        out_ref[head * HEAD_DIM : (head + 1) * HEAD_DIM, start : start + chunk] = to_low(
            mixed[:HEAD_DIM] / total
        )
        log_ref[head, :, start : start + chunk] = top + jnp.log(total)

    staged([(h, c) for c in range(0, points, chunk) for h in range(heads)], begin, finish)


def attend(projected, bias):
    width, points = projected.shape[1:]
    heads = width // HEAD_DIM
    height = HEAD_DIM * HEADS_STEP
    return pl.pallas_call(
        functools.partial(attend_kernel, 512),
        grid=(heads // HEADS_STEP,),
        in_specs=[
            *[pl.BlockSpec((None, height, points), lambda i, j=j: (j, i, 0)) for j in range(3)],
            pl.BlockSpec(bias.shape, lambda i: (0, 0)),
        ],
        out_specs=[
            pl.BlockSpec((height, points), lambda i: (i, 0)),
            pl.BlockSpec((HEADS_STEP, 1, points), lambda i: (i, 0, 0)),
        ],
        out_shape=[
            jax.ShapeDtypeStruct((width, points), jnp.bfloat16),
            jax.ShapeDtypeStruct((heads, 1, points), jnp.float32),
        ],
        compiler_params=pltpu.CompilerParams(vmem_limit_bytes=VMEM_BYTES),
        cost_estimate=pl.CostEstimate(
            flops=36 * 10**9, bytes_accessed=3 * 10**6, transcendentals=0
        ),
    )(projected, projected, projected, bias)


def attend_back_kernel(
    chunk,
    query_ref,
    key_ref,
    value_ref,
    bias_ref,
    mixed_ref,
    log_ref,
    grad_ref,
    extra_ref,
    turned_ref,
    near_ref,
    out_ref,
    reduce_sum_ref,
    expand_sum_ref,
    output_sum_ref,
    turned_other,
    near_other,
    key_total,
    value_total,
    send_sem,
    arrive_sem,
    *scratch,
):
    points = query_ref.shape[1]
    heads = query_ref.shape[0] // HEAD_DIM
    scale = HEAD_DIM**-0.5
    sums = pair_sums(scratch)
    half = sums.keep.shape[2]
    step = pl.program_id(0)
    copies = Copies(send_sem, arrive_sem)
    partner = {"pts": partner_of(SHARE_BIT)}
    share_copies = [
        copies.to(partner, turned_ref.at[: turned_ref.shape[0] // 2], turned_other, 0),
        copies.to(partner, near_ref, near_other, 1),
    ]

    def finish_sum(index, total):
        hidden = expand_sum_ref.shape[1]
        part = output_sum_ref.shape[1] // 2
        if index == 0:
            reduce_sum_ref[...] = total[0, :, :hidden]
        else:
            expand_sum_ref[...] = total[0, :, :hidden]
        output_sum_ref[:, index * part : (index + 1) * part] = total[0, :, hidden:]

    @pl.when(step == 0)
    def _():
        pl.semaphore_wait(greet_partners(), KERNEL_BITS)
        for index in range(extra_ref.shape[0]):
            sums.sends[0][index] = to_low(extra_ref[index, :, :half])
            sums.start(0, index, ((True, ORDERS[index]),))
            sums.keep[index] = extra_ref[index, :, half:]
        for copy in share_copies:
            copy.start()

    for stage, due in enumerate(SUM_STEPS):

        @pl.when(step == due)
        def _(stage=stage):
            for index in range(extra_ref.shape[0]):
                sums.advance(
                    stage, index, ((True, ORDERS[index]),), functools.partial(finish_sum, index)
                )

    @pl.when(step == pl.num_programs(0) - 1)
    def _():
        for copy in share_copies:
            copy.wait()

    row = lax.broadcasted_iota(jnp.int32, (HEAD_DIM, points), 0)
    ones = to_low(jnp.where((row > 0) & (row < 4), 1.0, 0.0))

    def three_parts(values, lead):
        upper = to_wide(to_low(values))
        middle = to_wide(to_low(values - upper))
        lower = values - upper - middle
        tail = jnp.where(row == 1, -upper, jnp.where(row == 2, -middle, 0.0))
        tail = jnp.where(row == 3, -lower, tail)
        return to_low(jnp.where(row == 0, lead, tail))

    operands = []
    for head in range(heads):
        part = slice(head * HEAD_DIM, (head + 1) * HEAD_DIM)
        query, key, value, grad = query_ref[part], key_ref[part], value_ref[part], grad_ref[part]
        row_dot = column_sum(to_wide(grad) * to_wide(mixed_ref[part]))
        scaled = to_low(to_wide(query) * scale)
        operands.append(
            (
                jnp.concatenate([scaled, three_parts(log_ref[head], 1.0)], axis=0),
                jnp.concatenate([key, bias_ref[...] + ones], axis=0),
                jnp.concatenate([value, ones], axis=0),
                jnp.concatenate([grad, three_parts(row_dot, 0.0)], axis=0),
            )
        )

    def begin(unit):
        head, start = unit
        queries, keys, values, grads = operands[head]
        return (
            product(keys, queries[:, start : start + chunk], 0, 0),
            product(values, grads[:, start : start + chunk], 0, 0),
        )

    def finish(unit, ready):
        head, start = unit
        scores, prob_grad = ready
        part = slice(head * HEAD_DIM, (head + 1) * HEAD_DIM)
        now = slice(start, start + chunk)
        probs = jnp.exp(scores)
        score_grad = to_low(probs * prob_grad)
        out_ref[0, part, now] = to_low(product(key_ref[part], score_grad, 1, 0) * scale)
        value_part = product(grad_ref[part, now], to_low(probs), 1, 1)
        key_part = product(query_ref[part, now], score_grad, 1, 1)
        if start == 0:
            value_total[head] = value_part
            key_total[head] = key_part
        else:
            value_total[head] += value_part
            key_total[head] += key_part

    staged([(h, c) for c in range(0, points, chunk) for h in range(heads)], begin, finish)
    for head in range(heads):
        part = slice(head * HEAD_DIM, (head + 1) * HEAD_DIM)
        out_ref[1, part] = to_low(key_total[head] * scale)
        out_ref[2, part] = to_low(value_total[head])


def attend_back(projected, bias, mixed, logs, grads, extra, turned, near):
    width, points = projected.shape[1:]
    heads = width // HEAD_DIM
    height = HEAD_DIM * HEADS_BACK_STEP
    block = pl.BlockSpec((height, points), lambda i: (i, 0))
    channels = extra.shape[2]
    kept = channels >> KERNEL_BITS
    hidden = extra.shape[3] - width // 2
    full = jnp.float32
    outs = [
        jax.ShapeDtypeStruct((3, width, points), jnp.bfloat16),
        jax.ShapeDtypeStruct((kept, hidden), full),
        jax.ShapeDtypeStruct((kept, hidden), full),
        jax.ShapeDtypeStruct((kept, width), full),
        jax.ShapeDtypeStruct((channels // 2, turned.shape[1]), turned.dtype),
        jax.ShapeDtypeStruct(near.shape, near.dtype),
    ]
    anywhere = pl.BlockSpec(memory_space=pl.ANY)
    return pl.pallas_call(
        functools.partial(attend_back_kernel, 512),
        grid=(heads // HEADS_BACK_STEP,),
        in_specs=[
            *[pl.BlockSpec((None, height, points), lambda i, j=j: (j, i, 0)) for j in range(3)],
            pl.BlockSpec(bias.shape, lambda i: (0, 0)),
            block,
            pl.BlockSpec((HEADS_BACK_STEP, 1, points), lambda i: (i, 0, 0)),
            block,
            whole(extra),
            anywhere,
            anywhere,
        ],
        out_specs=[pl.BlockSpec((3, height, points), lambda i: (0, i, 0))]
        + [whole(out) for out in outs[1:4]]
        + [anywhere, anywhere],
        out_shape=outs,
        scratch_shapes=[pltpu.VMEM((HEADS_BACK_STEP, HEAD_DIM, points), jnp.float32)] * 2
        + copy_sems(2)
        + pair_scratch(*extra.shape, KERNEL_BITS),
        compiler_params=pltpu.CompilerParams(
            vmem_limit_bytes=VMEM_BYTES, collective_id=0, has_side_effects=True
        ),
        cost_estimate=pl.CostEstimate(
            flops=50 * 10**9, bytes_accessed=5 * 10**6, transcendentals=0
        ),
    )(projected, projected, projected, bias, mixed, logs, grads, extra, turned, near)


def feed_kernel(
    mixed_ref,
    first_ref,
    output_ref,
    output_other_ref,
    output_bias_ref,
    gain_ref,
    shift_ref,
    cotangent_ref,
    expand_ref,
    expand_other_ref,
    bias_ref,
    bias_other_ref,
    reduce_ref,
    reduce_other_ref,
    reduce_bias_ref,
    result_ref,
    second_grad_ref,
    mixed_grad_ref,
    sums_ref,
    vectors_ref,
    bias_grad_ref,
    mixed_other,
    second_own,
    second_other,
    picks,
    away,
    arrived,
    send_sem,
    arrive_sem,
):
    local, channels = first_ref.shape
    width = output_ref.shape[0]
    hidden_width = bias_ref.shape[1]
    columns = hidden_width // 2
    copies = Copies(send_sem, arrive_sem)
    greet_sibling()
    mixed_copy = copies.to(sibling(), mixed_ref.at[:, local:], mixed_other, 0)
    mixed_copy.start()
    cotangent = cotangent_ref[...]
    for kind in range(2):
        picks[kind] = nested_picks(channels, ORDERS[kind])
    cotangent_turned = to_low(product(picks[0], cotangent, 1, 1))
    second = first_ref[...] + output_bias_ref[...]
    second += product(mixed_ref[:, :local], output_ref[...], 0, 0)
    mixed_copy.wait()
    second += product(mixed_other[...], output_other_ref[...], 0, 0)
    normal, inverse = layer_norm(second)
    feed_low = to_low(normal * gain_ref[...] + shift_ref[...])
    feed_turned = to_low(product(picks[1], feed_low, 1, 1))
    result = second + reduce_bias_ref[...]
    feed_grad = jnp.zeros_like(second)
    weight_copies = []
    for index, (up_ref, up_bias_ref, down_ref) in enumerate(
        (
            (expand_other_ref, bias_other_ref, reduce_other_ref),
            (expand_ref, bias_ref, reduce_ref),
        )
    ):
        for start in range(0, hidden_width, columns):
            now = slice(start, start + columns)
            hidden = product(feed_low, up_ref[:, now], 1, 0) + up_bias_ref[:, now]
            below = 0.5 + 0.5 * lax.erf(hidden * 0.5**0.5)
            slope = below + hidden * (jnp.exp(-0.5 * hidden * hidden) * (0.5 / jnp.pi) ** 0.5)
            active = to_low(hidden * below)
            hidden_grad = to_low(product(cotangent, down_ref[now, :], 1, 1) * slope)
            result += product(active, down_ref[now, :], 1, 0)
            feed_grad += product(hidden_grad, up_ref[:, now], 1, 1)
            bias_grad_ref[index : index + 1, now] = column_sum(to_wide(hidden_grad))
            reduce_grad = product(cotangent_turned, active, 1, 0)
            expand_grad = product(feed_turned, hidden_grad, 1, 0)
            if index == 0:
                away[0, :, now] = reduce_grad
                away[1, :, now] = expand_grad
                for kind in range(2):
                    copy = copies.to(
                        sibling(),
                        away.at[kind, :, now],
                        arrived.at[kind, :, now],
                        2 + len(weight_copies),
                    )
                    copy.start()
                    weight_copies.append(copy)
            else:
                sums_ref[0, :, now] = reduce_grad
                sums_ref[1, :, now] = expand_grad
    result_ref[...] = to_low(result)
    upstream = to_wide(cotangent)
    second_grad = upstream + norm_back(feed_grad, normal, inverse, gain_ref[...])
    second_grad_ref[...] = second_grad
    second_own[...] = to_low(second_grad)
    second_copy = copies.to(sibling(), second_own, second_other, 1)
    second_copy.start()
    vectors_ref[0:1] = column_sum(second_grad)
    vectors_ref[1:2] = column_sum(feed_grad * normal)
    vectors_ref[2:3] = column_sum(feed_grad)
    vectors_ref[3:4] = column_sum(upstream)
    mixed_grad_ref[:, :local] = to_low(product(output_ref[...], second_own[...], 1, 1))
    part = width // 2
    for kind in range(2):
        turned = to_low(product(picks[kind], second_own[...], 1, 1))
        sums_ref[kind, :, hidden_width:] = product(
            turned, mixed_ref[kind * part : (kind + 1) * part, :local], 1, 1
        )
    second_copy.wait()
    mixed_grad_ref[:, local:] = to_low(product(output_ref[...], second_other[...], 1, 1))
    for kind in range(2):
        turned = to_low(product(picks[kind], second_other[...], 1, 1))
        sums_ref[kind, :, hidden_width:] += product(
            turned, mixed_ref[kind * part : (kind + 1) * part, local:], 1, 1
        )
    for copy in weight_copies:
        copy.wait()
    sums_ref[:, :, :hidden_width] += arrived[...]


def feed(operands):
    local, channels = operands[1].shape
    width, rows = operands[0].shape
    hidden = operands[10].shape[1]
    low, full = jnp.bfloat16, jnp.float32
    shape = jax.ShapeDtypeStruct
    return pl.pallas_call(
        feed_kernel,
        in_specs=[vmem()] * len(operands),
        out_specs=[vmem()] * 6,
        out_shape=[
            shape((local, channels), low),
            shape((local, channels), full),
            shape((width, rows), low),
            shape((2, channels, hidden + width // 2), full),
            shape((4, channels), full),
            shape((2, hidden), full),
        ],
        scratch_shapes=[
            pltpu.VMEM((width, local), low),
            pltpu.VMEM((local, channels), low),
            pltpu.VMEM((local, channels), low),
            pltpu.VMEM((2, channels, channels), low),
            pltpu.VMEM((2, channels, hidden), full),
            pltpu.VMEM((2, channels, hidden), full),
            *copy_sems(6),
        ],
        compiler_params=pltpu.CompilerParams(
            vmem_limit_bytes=VMEM_BYTES, collective_id=3, has_side_effects=True
        ),
        cost_estimate=pl.CostEstimate(
            flops=10 * 10**9, bytes_accessed=16 * 10**6, transcendentals=0
        ),
    )(*operands)


def return_kernel(
    grad_ref,
    heads_ref,
    attend_ref,
    second_grad_ref,
    first_ref,
    linear_ref,
    attend_gain_ref,
    encode_gain_ref,
    encode_ref,
    conved_ref,
    feed_vectors_ref,
    bias_grad_ref,
    first_grad_ref,
    conved_grad_ref,
    extra_ref,
    vectors_ref,
    attend_away,
    attend_arrived,
    linear_own,
    linear_other,
    send_sem,
    arrive_sem,
):
    local, channels = first_ref.shape
    side = lax.axis_index("tp")
    mine = pl.ds(pl.multiple_of(side * local, local), local)
    theirs = pl.ds(pl.multiple_of((1 - side) * local, local), local)
    copies = Copies(send_sem, arrive_sem)

    def attend_grad(start):
        return sum(
            product(grad_ref[index, :, start : start + local].T, heads_ref[index], 1, 1)
            for index in range(3)
        )

    attend_away[...] = attend_grad(local)
    greet_sibling()
    attend_copy = copies.to(sibling(), attend_away, attend_arrived, 0)
    attend_copy.start()
    upstream = attend_grad(0)
    picks = [nested_picks(channels, order) for order in ORDERS]
    for kind in range(2):
        turned = [to_low(product(picks[kind], attend_ref[i], 1, 1)) for i in range(2)]
        for index in (0, 1) if kind == 0 else (2,):
            extra_ref[kind, index % 2] = product(
                turned[0], grad_ref[index, :, :local], 1, 1
            ) + product(turned[1], grad_ref[index, :, local:], 1, 1)
    normal, inverse = layer_norm(first_ref[...])
    attend_copy.wait()
    upstream += attend_arrived[...]
    first_grad = second_grad_ref[...] + norm_back(upstream, normal, inverse, attend_gain_ref[...])
    first_grad_ref[...] = first_grad
    vectors_ref[0:4] = feed_vectors_ref[...]
    for index in range(2):
        chosen = jnp.where(side == index, bias_grad_ref[1:2], bias_grad_ref[0:1])
        for part in range(2):
            row = 8 + 2 * index + part
            vectors_ref[row : row + 1] = chosen[:, part * channels : (part + 1) * channels]
    vectors_ref[4:5] = column_sum(upstream * normal)
    vectors_ref[5:6] = column_sum(upstream)
    normal, inverse = layer_norm(linear_ref[...])
    linear_own[...] = to_low(norm_back(first_grad, normal, inverse, encode_gain_ref[...]))
    linear_copy = copies.to(sibling(), linear_own, linear_other, 1)
    linear_copy.start()
    vectors_ref[6:7] = column_sum(first_grad * normal)
    vectors_ref[7:8] = column_sum(first_grad)
    conved_grad_ref[mine] = to_low(product(linear_own[...], encode_ref[...], 1, 1))
    turned = to_low(product(picks[1], linear_own[...], 1, 1))
    extra_ref[1, 1] = product(turned, conved_ref[mine], 1, 0)
    linear_copy.wait()
    conved_grad_ref[theirs] = to_low(product(linear_other[...], encode_ref[...], 1, 1))
    turned = to_low(product(picks[1], linear_other[...], 1, 1))
    extra_ref[1, 1] += product(turned, conved_ref[theirs], 1, 0)


def return_to_conv(operands):
    local, channels = operands[4].shape
    rows, width = operands[9].shape
    low, full = jnp.bfloat16, jnp.float32
    shape = jax.ShapeDtypeStruct
    return pl.pallas_call(
        return_kernel,
        in_specs=[vmem()] * len(operands),
        out_specs=[vmem()] * 4,
        out_shape=[
            shape((local, channels), full),
            shape((rows, width), low),
            shape((2, 2, channels, width), full),
            shape((12, channels), full),
        ],
        scratch_shapes=[
            pltpu.VMEM((local, channels), full),
            pltpu.VMEM((local, channels), full),
            pltpu.VMEM((local, channels), low),
            pltpu.VMEM((local, channels), low),
            *copy_sems(2),
        ],
        compiler_params=pltpu.CompilerParams(
            vmem_limit_bytes=VMEM_BYTES, collective_id=4, has_side_effects=True
        ),
        cost_estimate=pl.CostEstimate(
            flops=6 * 10**9, bytes_accessed=12 * 10**6, transcendentals=0
        ),
    )(*operands)


def partner_of(bit):
    me = lax.axis_index("pts")
    return me + (1 - 2 * ((me // (1 << bit)) % 2)) * (1 << bit)


def greet_partners():
    barrier = pltpu.get_barrier_semaphore()
    for bit in range(KERNEL_BITS):
        pl.semaphore_signal(
            barrier, inc=1, device_id={"pts": partner_of(bit)}, device_id_type=MESH
        )
    return barrier


class PairSums:
    def __init__(self, keep, sends, arrivals, send_sem, arrive_sem):
        self.keep, self.sends, self.arrivals = keep, sends, arrivals
        self.send_sem, self.arrive_sem = send_sem, arrive_sem

    def copy(self, stage, chunk, bit):
        return pltpu.make_async_remote_copy(
            src_ref=self.sends[stage].at[chunk],
            dst_ref=self.arrivals[stage].at[chunk],
            send_sem=self.send_sem.at[stage, chunk],
            recv_sem=self.arrive_sem.at[stage, chunk],
            device_id={"pts": partner_of(bit)},
            device_id_type=MESH,
        )

    def start(self, stage, chunk, kinds):
        for holds, order in kinds:
            if holds is True:
                self.copy(stage, chunk, order[stage]).start()
            else:

                @pl.when(holds)
                def _(order=order):
                    self.copy(stage, chunk, order[stage]).start()

    def advance(self, stage, chunk, kinds, finish):
        self.copy(stage, chunk, 0).wait()
        rows = self.keep.shape[2]
        low = rows - (rows >> stage)
        half = (rows - low) // 2
        arrived = self.arrivals[stage]
        if stage == len(self.sends) - 1:
            finish(self.keep[chunk, :, low:] + to_wide(arrived[chunk]))
            return
        self.sends[stage + 1][chunk] = to_low(
            self.keep[chunk, :, low : low + half] + to_wide(arrived[chunk, :, :half])
        )
        self.start(stage + 1, chunk, kinds)
        self.keep[chunk, :, low + half :] += to_wide(arrived[chunk, :, half:])


def pair_scratch(chunks, lead, rows, width, stages):
    halves = [(chunks, lead, rows >> (stage + 1), width) for stage in range(stages)]
    return (
        [pltpu.VMEM(halves[0], jnp.float32)]
        + [pltpu.VMEM(shape, jnp.bfloat16) for shape in halves]
        + [pltpu.VMEM(shape, jnp.bfloat16) for shape in halves]
        + [pltpu.SemaphoreType.DMA((stages, chunks))] * 2
    )


def pair_sums(scratch):
    stages = (len(scratch) - 3) // 2
    keep, rest = scratch[0], scratch[1:]
    return PairSums(keep, rest[:stages], rest[stages : 2 * stages], *rest[-2:])


def conv_backward_kernel(
    near_ref,
    near_other_ref,
    turned_ref,
    turned_other_ref,
    grad_ref,
    weight_ref,
    extra_ref,
    vector_ref,
    first_grad_ref,
    conv_sum_ref,
    heads_sum_ref,
    encode_sum_ref,
    points_grad_ref,
    *refs,
):
    vector_refs, refs = refs[:9], refs[9:]
    (
        spread,
        windows,
        gathered,
        grad_other,
        input_grad,
        input_arrived,
        rim_away,
        rim_arrived,
        vector_away,
        vector_arrived,
        send_sem,
        arrive_sem,
    ) = refs[:12]
    sums, extra_sums = pair_sums(refs[12:21]), pair_sums(refs[21:])
    rows, width = grad_ref.shape
    local, channels = first_grad_ref.shape
    half = channels // 2
    quarter = half // 4
    blocks = rows // BLOCK
    extras = extra_ref.shape[0]
    chunks = conv_sum_ref.shape[0]
    patches = lax.axis_size("pts")
    me, side = lax.axis_index("pts"), lax.axis_index("tp")
    step = pl.program_id(0)
    copies = Copies(send_sem, arrive_sem)
    mine = pl.ds(pl.multiple_of(HALO + side * local, HALO), local)
    theirs = pl.ds(pl.multiple_of(HALO + (1 - side) * local, HALO), local)
    grad_copy = copies.to({"pts": partner_of(SHARE_BIT)}, grad_ref, grad_other, 0)
    input_copy = copies.to(sibling(), input_grad.at[theirs], input_arrived, 1)
    rims = (
        (me > 0, {"pts": me - 1, "tp": 1}, slice(0, HALO)),
        (me < patches - 1, {"pts": me + 1, "tp": 0}, slice(HALO + rows, rows + 2 * HALO)),
    )
    rim_copies = [
        [copies.to(rim[1], rim_away.at[i], rim_arrived.at[core], 2 + i, 4 + core) for core in (0, 1)]
        for i, rim in enumerate(rims)
    ]
    has_rim = ((side == 0) & (me > 0)) | ((side == 1) & (me < patches - 1))
    first_sum = chunks // GROUP
    first_input = first_sum + chunks
    input_steps = chunks // GROUP

    def vector_copy(stage):
        device = sibling() if stage == 0 else {"pts": partner_of(stage - 1)}
        return copies.to(device, vector_away.at[stage], vector_arrived.at[stage], 6 + stage)

    def kinds(chunk):
        return ((chunk % 2 == 0, CONV_ORDERS[0]), (chunk % 2 == 1, CONV_ORDERS[1]))

    @pl.when(step == 0)
    def _():
        barrier = greet_partners()
        pl.semaphore_signal(barrier, inc=1, device_id=sibling(), device_id_type=MESH)
        for core in range(2):

            @pl.when((side == 0) & (me > 0))
            def _(core=core):
                device = {"pts": me - 1, "tp": core}
                pl.semaphore_signal(barrier, inc=1, device_id=device, device_id_type=MESH)

            @pl.when((side == 1) & (me < patches - 1))
            def _(core=core):
                device = {"pts": me + 1, "tp": core}
                pl.semaphore_signal(barrier, inc=1, device_id=device, device_id_type=MESH)

        sent = jnp.where(me > 0, 1, 0) + jnp.where(me < patches - 1, 1, 0)
        pl.semaphore_wait(barrier, KERNEL_BITS + 1 + sent)
        grad_copy.start()
        for index in range(extras):
            extra_sums.sends[0][index] = to_low(extra_ref[index, :, :half])
            extra_sums.start(0, index, ((True, ORDERS[index]),))
            extra_sums.keep[index] = extra_ref[index, :, half:]
        vector_away[0] = vector_ref[...]
        vector_copy(0).start()
        for kind, places in enumerate(((0, 1, 2, 3), (0, 2, 1, 3))):
            for place, source in enumerate(places):
                now = slice(place * quarter, (place + 1) * quarter)
                low = source * quarter
                windows[kind, 0, now] = turned_ref[half + low : half + low + quarter, :]
                windows[kind, 1, now] = turned_other_ref[low : low + quarter, :]
        input_grad[...] = jnp.zeros_like(input_grad)

    @pl.when(step < first_sum)
    def _():
        slots = to_wide(lax.broadcasted_iota(jnp.int32, (BLOCK, 1), 0))

        def spread_group(group, _):
            for offset in range(GROUP):
                index = (step * GROUP + group) * GROUP + offset
                near = near_ref[pl.ds(index, 1), :]
                for part in range(blocks + 1):
                    low = max(part - 1, 0) * BLOCK
                    high = min(part + 1, blocks) * BLOCK
                    select = to_low(
                        jnp.where(near[:, low:high] - float(part * BLOCK) == slots, 1.0, 0.0)
                    )
                    spread[index, part * BLOCK : (part + 1) * BLOCK] = to_low(
                        product(select, grad_ref[low:high, :], 1, 0)
                    )
            return 0

        lax.fori_loop(0, GROUP, spread_group, 0, unroll=True)

    @pl.when((step >= first_sum) & (step < first_input))
    def _():
        chunk = step - first_sum
        pl.when(chunk == 0)(grad_copy.wait)
        slots = to_wide(lax.broadcasted_iota(jnp.int32, (2 * BLOCK, 1), 0))
        for offset in range(GROUP):
            near = near_other_ref[pl.ds(chunk * GROUP + offset, 1), :]
            for block in range(blocks):
                low = block * BLOCK
                select = to_low(
                    jnp.where(near[:, low : low + BLOCK] - float(low) == slots, 1.0, 0.0)
                )
                gathered[offset, :, low : low + BLOCK] = to_low(
                    product(windows[chunk % 2, 1, :, low : low + 2 * BLOCK], select, 1, 0)
                )
        for offset in range(GROUP):
            weight_grad = product(windows[chunk % 2, 0], spread[chunk * GROUP + offset], 1, 0)
            weight_grad += product(gathered[offset], grad_other[...], 1, 0)
            sums.sends[0][chunk, offset] = to_low(weight_grad[: half // 2])
            sums.keep[chunk, offset] = weight_grad[half // 2 :]
        sums.start(0, chunk, kinds(chunk))

    beside = pl.ds(pl.multiple_of((1 - side) * (local + HALO), HALO), local + HALO)
    apart = pl.ds(pl.multiple_of(side * (2 * local + HALO), HALO), HALO)
    for phase, parts in enumerate(((beside, apart), (mine,))):
        start = first_input + phase * input_steps

        @pl.when((step >= start) & (step < start + input_steps))
        def _(start=start, parts=parts):
            def input_group(group, _):
                for part in parts:
                    total = input_grad[part, :]
                    for offset in range(GROUP):
                        index = group * GROUP + offset
                        total += product(
                            spread[(step - start) * WIDE_GROUP + index, part, :],
                            weight_ref[index],
                            1,
                            1,
                        )
                    input_grad[part, :] = total
                return 0

            lax.fori_loop(0, GROUP, input_group, 0, unroll=True)

    @pl.when(step == first_input + input_steps - 1)
    def _():
        input_copy.start()
        for index, (has, _, part) in enumerate(rims):
            rim_away[index] = to_low(input_grad[part, :])

            @pl.when(has)
            def _(index=index):
                for core in range(2):

                    @pl.when(side == core)
                    def _(core=core):
                        rim_copies[index][core].start()

    @pl.when(step == pl.num_programs(0) - 1)
    def _():
        input_copy.wait()
        points_grad_ref[...] = first_grad_ref[...] + input_grad[mine, :] + input_arrived[...]

        @pl.when(has_rim)
        def _():
            edge = pl.ds(pl.multiple_of(side * (local - HALO), HALO), HALO)
            for core in range(2):
                rim_copies[0][core].wait_recv()
                points_grad_ref[edge, :] += to_wide(rim_arrived[core])

        for index, (has, _, part) in enumerate(rims):
            pl.when(has)(rim_copies[index][0].wait_send)

    for stage, due in enumerate(VECTOR_STEPS):

        @pl.when(step == due)
        def _(stage=stage):
            vector_copy(stage).wait()
            summed = vector_away[stage] + vector_arrived[stage]
            if stage < KERNEL_BITS:
                vector_away[stage + 1] = summed
                vector_copy(stage + 1).start()
                return
            for index in range(8):
                vector_refs[index][...] = summed[index : index + 1]
            for index in range(8, summed.shape[0]):
                low = (index - 8) * channels
                vector_refs[8][:, low : low + channels] = summed[index : index + 1]

    for stage in range(len(CONV_LAGS)):
        chunk = step - first_sum - CONV_LAGS[stage]

        @pl.when((chunk >= 0) & (chunk < chunks))
        def _(stage=stage, chunk=chunk):
            def finish(total):
                conv_sum_ref[chunk] = total

            sums.advance(stage, chunk, kinds(chunk), finish)

    def finish_extra(index, total):
        if index == 0:
            heads_sum_ref[0:2] = total
        else:
            heads_sum_ref[2] = total[0]
            encode_sum_ref[...] = total[1]

    for stage, due in enumerate(EXTRA_STEPS):

        @pl.when(step == due)
        def _(stage=stage):
            for index in range(extras):
                extra_sums.advance(
                    stage,
                    index,
                    ((True, ORDERS[index]),),
                    functools.partial(finish_extra, index),
                )


def conv_backward(
    near, near_other, turned, turned_other, grad, weight, extra, vector, first_grad
):
    offsets, channels, width = weight.shape
    wide = turned.shape[1]
    rows = grad.shape[0]
    local = first_grad.shape[0]
    chunks = offsets // GROUP
    first_input = chunks // GROUP + chunks
    input_steps = chunks // GROUP
    low, full = jnp.bfloat16, jnp.float32
    kept = channels >> KERNEL_BITS
    shape = jax.ShapeDtypeStruct
    outs = [
        shape((chunks, GROUP, kept, width), full),
        shape((3, kept, width), full),
        shape((kept, width), full),
        shape(first_grad.shape, full),
        *[shape((1, channels), full)] * 8,
        shape((1, (vector.shape[0] - 8) * channels), full),
    ]

    def weight_block(i):
        return (jnp.maximum(i - first_input, 0) % input_steps, 0, 0)

    return pl.pallas_call(
        conv_backward_kernel,
        grid=(first_input + 2 * input_steps,),
        in_specs=[
            whole(near),
            whole(near_other),
            whole(turned),
            whole(turned_other),
            whole(grad),
            pl.BlockSpec((WIDE_GROUP, channels, width), weight_block),
            whole(extra),
            whole(vector),
            whole(first_grad),
        ],
        out_specs=[whole(out) for out in outs],
        out_shape=outs,
        scratch_shapes=[
            pltpu.VMEM((offsets, wide, width), low),
            pltpu.VMEM((2, 2, channels // 2, wide), low),
            pltpu.VMEM((GROUP, channels // 2, rows), low),
            pltpu.VMEM((rows, width), low),
            pltpu.VMEM((wide, channels), full),
            pltpu.VMEM((local, channels), full),
            pltpu.VMEM((2, HALO, channels), low),
            pltpu.VMEM((2, HALO, channels), low),
            pltpu.VMEM((KERNEL_BITS + 1, *vector.shape), full),
            pltpu.VMEM((KERNEL_BITS + 1, *vector.shape), full),
            *copy_sems(7 + KERNEL_BITS),
            *pair_scratch(chunks, GROUP, channels // 2, width, len(CONV_LAGS)),
            *pair_scratch(*extra.shape, KERNEL_BITS),
        ],
        compiler_params=pltpu.CompilerParams(
            vmem_limit_bytes=VMEM_BYTES, collective_id=1, has_side_effects=True
        ),
        cost_estimate=pl.CostEstimate(
            flops=80 * 10**9, bytes_accessed=16 * 10**6, transcendentals=0
        ),
    )(near, near_other, turned, turned_other, grad, weight, extra, vector, first_grad)


def hand_over_kernel(*refs):
    count = len(refs) // 2
    for source, target in zip(refs[:count], refs[count:]):
        target[...] = source[...]


def hand_over(arrays):
    return pl.pallas_call(
        hand_over_kernel,
        in_specs=[vmem()] * len(arrays),
        out_specs=[vmem()] * len(arrays),
        out_shape=[jax.ShapeDtypeStruct(each.shape, each.dtype) for each in arrays],
        compiler_params=pltpu.CompilerParams(vmem_limit_bytes=VMEM_BYTES),
    )(*arrays)


def exchange(values, bit):
    count = lax.axis_size("pts")
    return lax.ppermute(values, "pts", [(i, i ^ (1 << bit)) for i in range(count)])


def sum_rest(keep, axis):
    for bit in range(KERNEL_BITS, patch_bits()):
        half = keep.shape[axis] // 2
        away = lax.slice_in_dim(keep, 0, half, axis=axis)
        keep = lax.slice_in_dim(keep, half, 2 * half, axis=axis)
        keep = keep + to_wide(exchange(to_low(away), bit))
    return keep


def per_device(
    points,
    neighbours,
    valid_count,
    conv_weight,
    encode_weight,
    encode_gain,
    encode_shift,
    attend_gain,
    attend_shift,
    heads_weight,
    output_weight,
    output_bias,
    feed_gain,
    feed_shift,
    expand_weight,
    expand_bias,
    reduce_weight,
    reduce_bias,
    cotangent,
):
    local, channels = points.shape
    rows = 2 * local
    is_first = lax.axis_index("tp") == 0
    norms = [v[None, :] for v in (encode_gain, encode_shift, attend_gain, attend_shift)]
    (
        turned, near_columns, conved, linear, first, attend_in, projected,
        output_other, expand_other, reduce_other, bias_other,
    ) = forward_start(
        neighbours.T, points, conv_weight, encode_weight, norms, heads_weight, output_weight,
        expand_weight, reduce_weight, expand_bias[None, :]
    )

    place = jnp.arange(rows, dtype=jnp.int32)
    place = jnp.where(is_first, place, (place + local) % rows)
    bias = jnp.where(place < valid_count[0], 0.0, MASKED)
    bias = to_low(jnp.where(jnp.arange(HEAD_DIM)[:, None] == 0, bias[None, :], 0.0))
    mixed, logs = attend(projected, bias)
    result, second_grad, mixed_grad, feed_grads, feed_vectors, bias_grads = feed(
        [
            mixed, first, output_weight, output_other, output_bias[None, :], feed_gain[None, :],
            feed_shift[None, :], cotangent, expand_weight, expand_other, expand_bias[None, :],
            bias_other, reduce_weight, reduce_other, reduce_bias[None, :],
        ]
    )
    projected_grad, reduce_sum, expand_sum, output_sum, turned_other, near_other = attend_back(
        projected, bias, mixed, logs, mixed_grad, feed_grads[:, None], turned, near_columns
    )
    first_grad, conved_grad, extra, vector = return_to_conv(
        [
            projected_grad, heads_weight, attend_in, second_grad, first, linear, norms[2],
            norms[0], encode_weight, conved, feed_vectors, bias_grads,
        ]
    )
    conv_sum, heads_sum, encode_sum, points_gradient, *vectors = conv_backward(
        near_columns, near_other, turned, turned_other, conved_grad, conv_weight, extra, vector,
        first_grad
    )
    for bit in range(KERNEL_BITS, patch_bits()):
        vectors = [each + exchange(each, bit) for each in vectors]
    parts = hand_over(
        [
            result,
            points_gradient,
            sum_rest(conv_sum, 2),
            sum_rest(encode_sum, 0),
            sum_rest(heads_sum, 1),
            sum_rest(output_sum, 0),
            sum_rest(expand_sum, 0),
            sum_rest(reduce_sum, 0),
            *vectors,
        ]
    )
    vectors = [each.reshape(-1) for each in parts[8:]]
    return (
        parts[0],
        parts[1],
        parts[2].reshape(-1, *parts[2].shape[2:]),
        parts[3].T,
        vectors[6],
        vectors[7],
        vectors[4],
        vectors[5],
        parts[4],
        parts[5].T,
        vectors[0],
        vectors[1],
        vectors[2],
        parts[6],
        vectors[8],
        parts[7].T,
        vectors[3],
    )


def solution(mesh):
    placed = (
        P(("pts", "tp"), None),
        P("pts", None),
        P("pts"),
        P(None, None, "tp"),
        P("tp", None),
        P(),
        P(),
        P(),
        P(),
        P(None, None, "tp"),
        P("tp", None),
        P(),
        P(),
        P(),
        P(None, "tp"),
        P("tp"),
        P("tp", None),
        P(),
        P(("pts", "tp"), None),
    )
    return jax.shard_map(
        per_device,
        mesh=mesh,
        in_specs=placed,
        out_specs=(
            P(("pts", "tp"), None),
            P(("pts", "tp"), None),
            P(None, "pts", "tp"),
            P("tp", "pts"),
            P(),
            P(),
            P(),
            P(),
            P(None, "pts", "tp"),
            P("tp", "pts"),
            P(),
            P(),
            P(),
            P("pts", "tp"),
            P(),
            P("tp", "pts"),
            P(),
        ),
        check_vma=False,
    )
```

```python
import functools

import jax
import jax.numpy as jnp
from jax import lax
from jax.experimental import pallas as pl
from jax.experimental.pallas import tpu as pltpu
from jax.sharding import PartitionSpec as P

MESH = pl.DeviceIdType.MESH
HEAD_DIM = 16
HALO = 128
BLOCK = 256
GROUP = 3
EPSILON = 1e-05
MASKED = -1e30
KERNEL_BITS = 4
ORDERS = ((0, 1, 2, 3), (1, 0, 2, 3))
VMEM_BYTES = 60 << 20
CHUNK = 512
HEADS_STEP = 4
HEADS_BACK_STEP = 2
SUM_STEPS = (3, 5, 6, 7)
SHARE_BIT = 2
CONV_ORDERS = ((0, 1, 3), (1, 0, 3))
WINDOW_ORDER = (2, 0, 1, 3)
CONV_LAGS = (2, 4, 6)
EXTRA_STEPS = (2, 3, 5, 7)
VECTOR_STEPS = (1, 2, 3, 4, 5)
WEIGHTS_AHEAD = 3
WIDE_GROUP = 9


def to_low(values):
    return values.astype(jnp.bfloat16)


def to_wide(values):
    return values.astype(jnp.float32)


def product(left, right, left_dim, right_dim):
    dims = (((left_dim,), (right_dim,)), ((), ()))
    return lax.dot_general(left, right, dims, preferred_element_type=jnp.float32)


def layer_norm(values):
    row_mean = jnp.mean(values, axis=-1, keepdims=True)
    centred = values - row_mean
    inverse = lax.rsqrt(jnp.mean(centred * centred, axis=-1, keepdims=True) + EPSILON)
    return centred * inverse, inverse


def norm_back(upstream, normal_part, inverse, norm_gain):
    scaled = upstream * norm_gain
    across = (
        scaled
        - jnp.mean(scaled, axis=-1, keepdims=True)
        - normal_part * jnp.mean(scaled * normal_part, axis=-1, keepdims=True)
    )
    return across * inverse


def column_sum(values):
    return jnp.sum(values, axis=0, keepdims=True)


def nested_picks(channels, order):
    me = lax.axis_index("pts")
    order = order + tuple(range(KERNEL_BITS, patch_bits()))
    depth = channels >> len(order)
    lanes = 128
    place = lax.broadcasted_iota(jnp.int32, (channels, lanes), 0)
    picked = place & (depth - 1)
    for stage, bit in enumerate(order):
        kept = (place >> (channels.bit_length() - 2 - stage)) & 1
        picked = picked + (1 - ((kept + me // (1 << bit)) & 1)) * (depth << bit)
    column = lax.broadcasted_iota(jnp.int32, (channels, lanes), 1)
    return to_low(
        jnp.concatenate(
            [
                jnp.where(picked == column + low, 1.0, 0.0)
                for low in range(0, channels, lanes)
            ],
            axis=1,
        )
    )


class Copies:
    def __init__(self, send_sem, arrive_sem):
        self.send_sem, self.arrive_sem = send_sem, arrive_sem

    def to(self, device, source, target, send, arrive=None):
        return pltpu.make_async_remote_copy(
            src_ref=source,
            dst_ref=target,
            send_sem=self.send_sem.at[send],
            recv_sem=self.arrive_sem.at[send if arrive is None else arrive],
            device_id=device,
            device_id_type=MESH,
        )


def copy_sems(count):
    return [pltpu.SemaphoreType.DMA((count,))] * 2


def patch_bits():
    return lax.axis_size("pts").bit_length() - 1


def sibling():
    return {"tp": 1 - lax.axis_index("tp")}


def greet_sibling():
    barrier = pltpu.get_barrier_semaphore()
    pl.semaphore_signal(barrier, inc=1, device_id=sibling(), device_id_type=MESH)
    pl.semaphore_wait(barrier, 1)


def vmem():
    return pl.BlockSpec(memory_space=pltpu.VMEM)


def whole(array):
    zeros = (0,) * array.ndim
    return pl.BlockSpec(array.shape, lambda i: zeros, pipeline_mode=pl.Buffered(1))


def forward_kernel(
    near_ref,
    points_ref,
    weight_ref,
    weights_ref,
    encode_ref,
    encode_gain_ref,
    encode_shift_ref,
    attend_gain_ref,
    attend_shift_ref,
    heads_ref,
    output_ref,
    expand_ref,
    reduce_ref,
    bias_ref,
    turned_ref,
    near_columns_ref,
    conved_ref,
    linear_ref,
    first_ref,
    attend_ref,
    projected_ref,
    output_other,
    expand_other,
    reduce_other,
    bias_other,
    window,
    total,
    rows,
    weight_other,
    encode_other,
    conved_away,
    conved_other,
    attend_other,
    heads_turned,
    near_wide,
    near_tall,
    picks,
    weight_first,
    send_sem,
    arrive_sem,
):
    step = pl.program_id(0)
    steps = pl.num_programs(0)
    local, channels = points_ref.shape
    width = weight_ref.shape[2]
    patches = lax.axis_size("pts")
    me, side = lax.axis_index("pts"), lax.axis_index("tp")
    copies = Copies(send_sem, arrive_sem)
    own_place = pl.ds(pl.multiple_of(HALO + side * local, HALO), local)
    other_place = pl.ds(pl.multiple_of(HALO + (1 - side) * local, HALO), local)
    points_copy = copies.to(sibling(), points_ref, window.at[own_place], 0)
    low_rim, high_rim = slice(0, HALO), slice(HALO + 2 * local, 2 * HALO + 2 * local)
    low_copies = [
        copies.to(
            {"pts": me + 1, "tp": core},
            points_ref.at[local - HALO :],
            window.at[low_rim],
            3 + core,
            1,
        )
        for core in range(2)
    ]
    high_copies = [
        copies.to(
            {"pts": me - 1, "tp": core}, points_ref.at[0:HALO], window.at[high_rim], 3 + core, 2
        )
        for core in range(2)
    ]
    small_copies = [
        copies.to(sibling(), encode_ref, encode_other, 5),
        copies.to(sibling(), output_ref, output_other, 6),
        copies.to(sibling(), expand_ref, expand_other, 7),
        copies.to(sibling(), reduce_ref, reduce_other, 8),
        copies.to(sibling(), bias_ref, bias_other, 9),
    ]
    up = (side == 1) & (me < patches - 1)
    down = (side == 0) & (me > 0)

    def weight_copy(group):
        part = pl.ds(group * GROUP, GROUP)
        return copies.to(sibling(), weights_ref.at[part], weight_other.at[part], 12 + group)

    def turn(place):
        return to_low(product(picks[...], window[place, :], 1, 1))

    @pl.when(step == 0)
    def _():
        barrier = pltpu.get_barrier_semaphore()
        pl.semaphore_signal(barrier, inc=1, device_id=sibling(), device_id_type=MESH)

        @pl.when(me > 0)
        def _():
            pl.semaphore_signal(
                barrier, inc=1, device_id={"pts": me - 1, "tp": 1}, device_id_type=MESH
            )

        @pl.when(me < patches - 1)
        def _():
            pl.semaphore_signal(
                barrier, inc=1, device_id={"pts": me + 1, "tp": 0}, device_id_type=MESH
            )

        pl.semaphore_wait(barrier, jnp.where(up | down, 3, 1))
        points_copy.start()

        @pl.when(up)
        def _():
            for copy in low_copies:
                copy.start()

        @pl.when(down)
        def _():
            for copy in high_copies:
                copy.start()

        for group in range(WEIGHTS_AHEAD):
            weight_copy(group).start()
        window[own_place, :] = points_ref[...]

        @pl.when(me == 0)
        def _():
            window[low_rim, :] = jnp.zeros((HALO, channels), jnp.bfloat16)

        @pl.when(me == patches - 1)
        def _():
            window[high_rim, :] = jnp.zeros((HALO, channels), jnp.bfloat16)

        picks[...] = nested_picks(channels, WINDOW_ORDER)
        turned_ref[:, own_place] = turn(own_place)
        for index in range(3):
            heads_turned[index] = heads_ref[index].T
        near_tall[...] = jnp.zeros_like(near_tall)
        near_tall[: near_ref.shape[0]] = to_wide(near_ref[...])
        near_columns_ref[...] = near_tall[: near_columns_ref.shape[0]]
        near_wide[...] = near_tall[...].T
        points_copy.wait()

    @pl.when(step == 2)
    def _():
        for place in (other_place, low_rim, high_rim):
            turned_ref[:, place] = turn(place)

        for copy in small_copies:
            copy.start()

    def wait_rims():
        @pl.when(me > 0)
        def _():
            low_copies[0].wait_recv()

        @pl.when(me < patches - 1)
        def _():
            high_copies[0].wait_recv()

        @pl.when(up)
        def _():
            for copy in low_copies:
                copy.wait_send()

        @pl.when(down)
        def _():
            for copy in high_copies:
                copy.wait_send()

    @pl.when((step > 0) & (step + WEIGHTS_AHEAD - 1 < steps))
    def _():
        weight_copy(step + WEIGHTS_AHEAD - 1).start()

    weight_copy(step).wait()
    lane = lax.broadcasted_iota(jnp.int32, (BLOCK, near_wide.shape[1]), 1)
    slots = to_wide(lax.broadcasted_iota(jnp.int32, (BLOCK, 2 * BLOCK), 1))
    places = [pl.ds(pl.multiple_of(block * BLOCK, BLOCK), BLOCK) for block in (1 - side, side)]

    def gather(index, group):
        low = pl.multiple_of(side * local + (1 - side, side)[index] * BLOCK, BLOCK)
        part = window[pl.ds(low, 2 * BLOCK), :]
        near = near_wide[pl.ds(low, BLOCK), :] - low.astype(jnp.float32)
        for offset in range(GROUP):
            chosen = jnp.where(lane == group * GROUP + offset, near, 0.0)
            column = jnp.sum(chosen, axis=1, keepdims=True)
            select = to_low(jnp.where(column == slots, 1.0, 0.0))
            rows[places[index], offset * channels : (offset + 1) * channels] = to_low(
                product(select, part, 1, 0)
            )

    def apply(place, own_ref, group):
        picked = rows[place, :]
        other = weight_other[pl.ds(group * GROUP, GROUP)]
        flat = (GROUP * channels, width)
        return (
            product(picked, own_ref[...].reshape(flat), 1, 0),
            product(picked, other.reshape(flat), 1, 0),
        )

    @pl.when(step == 0)
    def _():
        gather(0, 0)
        total[places[0], :width], total[places[0], width:] = apply(places[0], weight_ref, 0)
        weight_first[...] = weight_ref[...]

    @pl.when(step == 1)
    def _():
        wait_rims()
        gather(1, 0)
        total[places[1], :width], total[places[1], width:] = apply(places[1], weight_first, 0)

    @pl.when(step > 0)
    def _():
        gather(0, step)
        gather(1, step)
        own, other = apply(slice(None), weight_ref, step)
        total[:, :width] += own
        total[:, width:] += other

    @pl.when(step == steps - 1)
    def _():
        mine = pl.ds(pl.multiple_of(side * local, local), local)
        theirs = pl.ds(pl.multiple_of((1 - side) * local, local), local)
        conved_own = to_low(total[:, :width])
        conved_away[...] = to_low(total[:, width:])
        conved_ref[mine] = conved_own
        conved_copy = copies.to(sibling(), conved_away, conved_other, 10)
        conved_copy.start()
        small_copies[0].wait()
        linear = product(conved_own, encode_ref[...], 1, 0)
        linear += product(conved_away[...], encode_other[...], 1, 0)
        linear_ref[...] = linear
        first = layer_norm(linear)[0] * encode_gain_ref[...] + encode_shift_ref[...]
        first += to_wide(points_ref[...])
        first_ref[...] = first
        attend_out = layer_norm(first)[0] * attend_gain_ref[...] + attend_shift_ref[...]
        attend_ref[0] = to_low(attend_out)
        attend_copy = copies.to(sibling(), attend_ref.at[0], attend_other, 11)
        attend_copy.start()
        for index in range(3):
            projected_ref[index, :, :local] = to_low(
                product(heads_turned[index], attend_ref[0], 1, 1)
            )
        attend_copy.wait()
        attend_ref[1] = attend_other[...]
        for index in range(3):
            projected_ref[index, :, local:] = to_low(
                product(heads_turned[index], attend_other[...], 1, 1)
            )
        conved_copy.wait()
        conved_ref[theirs] = conved_other[...]
        for copy in small_copies[1:]:
            copy.wait()


def forward_start(
    near, points, conv_weight, encode_weight, norms, heads_weight, output_weight, expand_weight,
    reduce_weight, expand_bias
):
    offsets, channels, width = conv_weight.shape
    local = points.shape[0]
    rows = 2 * local
    wide = rows + 2 * HALO
    groups = offsets // GROUP
    low, full = jnp.bfloat16, jnp.float32
    shape = jax.ShapeDtypeStruct
    anywhere = pl.BlockSpec(memory_space=pl.ANY)
    outs = [
        shape((channels, wide), low),
        shape((32, rows), full),
        shape((rows, width), low),
        shape((local, channels), full),
        shape((local, channels), full),
        shape((2, local, channels), low),
        shape((3, width, rows), low),
    ]
    away = [
        shape(array.shape, array.dtype)
        for array in (output_weight, expand_weight, reduce_weight, expand_bias)
    ]
    return pl.pallas_call(
        forward_kernel,
        grid=(groups,),
        in_specs=[
            whole(near),
            whole(points),
            pl.BlockSpec((GROUP, channels, width), lambda i: (i, 0, 0)),
            anywhere,
            whole(encode_weight),
            *[whole(norm) for norm in norms],
            whole(heads_weight),
            anywhere,
            anywhere,
            anywhere,
            anywhere,
        ],
        out_specs=[whole(out) for out in outs] + [anywhere] * 4,
        out_shape=outs + away,
        scratch_shapes=[
            pltpu.VMEM((wide, channels), low),
            pltpu.VMEM((local, channels), full),
            pltpu.VMEM((local, GROUP * channels), low),
            pltpu.VMEM(conv_weight.shape, low),
            pltpu.VMEM(encode_weight.shape, low),
            pltpu.VMEM((local, width), low),
            pltpu.VMEM((local, width), low),
            pltpu.VMEM((local, channels), low),
            pltpu.VMEM((3, width, channels), low),
            pltpu.VMEM((rows, 128), full),
            pltpu.VMEM((128, rows), full),
            pltpu.VMEM((channels, channels), low),
            pltpu.VMEM((GROUP, channels, width), low),
            *copy_sems(12 + groups),
        ],
        compiler_params=pltpu.CompilerParams(
            vmem_limit_bytes=VMEM_BYTES, collective_id=2, has_side_effects=True
        ),
        cost_estimate=pl.CostEstimate(
            flops=30 * 10**9, bytes_accessed=16 * 10**6, transcendentals=0
        ),
    )(
        near, points, conv_weight, conv_weight, encode_weight, *norms, heads_weight,
        output_weight, expand_weight, reduce_weight, expand_bias
    )


def staged(units, begin, finish):
    ready = begin(units[0])
    for index, unit in enumerate(units):
        later = begin(units[index + 1]) if index + 1 < len(units) else None
        finish(unit, ready)
        ready = later


def attend_kernel(chunk, query_ref, key_ref, value_ref, bias_ref, out_ref, log_ref):
    points = query_ref.shape[1]
    heads = query_ref.shape[0] // HEAD_DIM
    row = lax.broadcasted_iota(jnp.int32, (HEAD_DIM, points), 0)
    ones = to_low(jnp.where(row == 0, 1.0, 0.0))
    operands = []
    for head in range(heads):
        part = slice(head * HEAD_DIM, (head + 1) * HEAD_DIM)
        scaled = to_low(to_wide(query_ref[part]) * HEAD_DIM**-0.5)
        operands.append(
            (
                jnp.concatenate([scaled, ones], axis=0),
                jnp.concatenate([key_ref[part], bias_ref[...]], axis=0),
                jnp.concatenate([value_ref[part], ones], axis=0),
            )
        )

    def begin(unit):
        head, start = unit
        queries, keys, _ = operands[head]
        return product(keys, queries[:, start : start + chunk], 0, 0)

    def finish(unit, scores):
        head, start = unit
        top = jnp.max(scores, axis=0, keepdims=True)
        mixed = product(operands[head][2], to_low(jnp.exp(scores - top)), 1, 0)
        total = mixed[HEAD_DIM : HEAD_DIM + 1, :]
        out_ref[head * HEAD_DIM : (head + 1) * HEAD_DIM, start : start + chunk] = to_low(
            mixed[:HEAD_DIM] / total
        )
        log_ref[head, :, start : start + chunk] = top + jnp.log(total)

    staged([(h, c) for c in range(0, points, chunk) for h in range(heads)], begin, finish)


def attend(projected, bias):
    width, points = projected.shape[1:]
    heads = width // HEAD_DIM
    height = HEAD_DIM * HEADS_STEP
    return pl.pallas_call(
        functools.partial(attend_kernel, CHUNK),
        grid=(heads // HEADS_STEP,),
        in_specs=[
            *[pl.BlockSpec((None, height, points), lambda i, j=j: (j, i, 0)) for j in range(3)],
            pl.BlockSpec(bias.shape, lambda i: (0, 0)),
        ],
        out_specs=[
            pl.BlockSpec((height, points), lambda i: (i, 0)),
            pl.BlockSpec((HEADS_STEP, 1, points), lambda i: (i, 0, 0)),
        ],
        out_shape=[
            jax.ShapeDtypeStruct((width, points), jnp.bfloat16),
            jax.ShapeDtypeStruct((heads, 1, points), jnp.float32),
        ],
        compiler_params=pltpu.CompilerParams(vmem_limit_bytes=VMEM_BYTES),
        cost_estimate=pl.CostEstimate(
            flops=36 * 10**9, bytes_accessed=3 * 10**6, transcendentals=0
        ),
    )(projected, projected, projected, bias)


def partner_of(bit):
    me = lax.axis_index("pts")
    return me + (1 - 2 * ((me // (1 << bit)) % 2)) * (1 << bit)


def greet_partners():
    barrier = pltpu.get_barrier_semaphore()
    for bit in range(KERNEL_BITS):
        pl.semaphore_signal(
            barrier, inc=1, device_id={"pts": partner_of(bit)}, device_id_type=MESH
        )
    return barrier


class PairSums:
    def __init__(self, keep, sends, arrivals, send_sem, arrive_sem):
        self.keep, self.sends, self.arrivals = keep, sends, arrivals
        self.send_sem, self.arrive_sem = send_sem, arrive_sem

    def copy(self, stage, chunk, bit):
        return pltpu.make_async_remote_copy(
            src_ref=self.sends[stage].at[chunk],
            dst_ref=self.arrivals[stage].at[chunk],
            send_sem=self.send_sem.at[stage, chunk],
            recv_sem=self.arrive_sem.at[stage, chunk],
            device_id={"pts": partner_of(bit)},
            device_id_type=MESH,
        )

    def start(self, stage, chunk, kinds):
        for holds, order in kinds:
            if holds is True:
                self.copy(stage, chunk, order[stage]).start()
            else:

                @pl.when(holds)
                def _(order=order):
                    self.copy(stage, chunk, order[stage]).start()

    def advance(self, stage, chunk, kinds, finish):
        self.copy(stage, chunk, 0).wait()
        rows = self.keep.shape[2]
        low = rows - (rows >> stage)
        half = (rows - low) // 2
        arrived = self.arrivals[stage]
        if stage == len(self.sends) - 1:
            finish(self.keep[chunk, :, low:] + to_wide(arrived[chunk]))
            return
        self.sends[stage + 1][chunk] = to_low(
            self.keep[chunk, :, low : low + half] + to_wide(arrived[chunk, :, :half])
        )
        self.start(stage + 1, chunk, kinds)
        self.keep[chunk, :, low + half :] += to_wide(arrived[chunk, :, half:])


def pair_scratch(chunks, lead, rows, width, stages):
    halves = [(chunks, lead, rows >> (stage + 1), width) for stage in range(stages)]
    return (
        [pltpu.VMEM(halves[0], jnp.float32)]
        + [pltpu.VMEM(shape, jnp.bfloat16) for shape in halves]
        + [pltpu.VMEM(shape, jnp.bfloat16) for shape in halves]
        + [pltpu.SemaphoreType.DMA((stages, chunks))] * 2
    )


def pair_sums(scratch):
    stages = (len(scratch) - 3) // 2
    keep, rest = scratch[0], scratch[1:]
    return PairSums(keep, rest[:stages], rest[stages : 2 * stages], *rest[-2:])


def middle_kernel(
    mixed_ref,
    first_ref,
    output_ref,
    output_other_ref,
    output_bias_ref,
    gain_ref,
    shift_ref,
    cotangent_ref,
    bias_ref,
    bias_other_ref,
    reduce_bias_ref,
    mask_ref,
    log_ref,
    attend_gain_ref,
    encode_gain_ref,
    expand_hbm,
    expand_other_hbm,
    reduce_hbm,
    reduce_other_hbm,
    projected_hbm,
    heads_hbm,
    attend_hbm,
    linear_hbm,
    encode_hbm,
    conved_hbm,
    turned_hbm,
    near_hbm,
    first_grad_ref,
    conved_grad_ref,
    extra_ref,
    vectors_ref,
    reduce_sum_ref,
    expand_sum_ref,
    output_sum_ref,
    result_hbm,
    turned_other,
    near_other,
    expand_ref,
    expand_other_ref,
    reduce_ref,
    reduce_other_ref,
    projected_ref,
    heads_ref,
    attend_ref,
    linear_ref,
    encode_ref,
    conved_ref,
    result_ref,
    second_grad_ref,
    mixed_grad_ref,
    grad_ref,
    mixed_other,
    second_own,
    second_other,
    picks,
    top,
    away,
    arrived,
    attend_away,
    attend_arrived,
    linear_own,
    linear_other,
    load_sem,
    send_sem,
    arrive_sem,
    *scratch,
):
    local, channels = first_ref.shape
    width, points = mixed_ref.shape
    hidden_width = bias_ref.shape[1]
    columns = hidden_width // 2
    heads = width // HEAD_DIM
    half = channels // 2
    side = lax.axis_index("tp")
    mine = pl.ds(pl.multiple_of(side * local, local), local)
    theirs = pl.ds(pl.multiple_of((1 - side) * local, local), local)
    sums = pair_sums(scratch)
    copies = Copies(send_sem, arrive_sem)
    partner = {"pts": partner_of(SHARE_BIT)}
    share_copies = [
        copies.to(partner, turned_hbm.at[:half], turned_other, 0),
        copies.to(partner, near_hbm, near_other, 1),
    ]
    loads = [
        pltpu.make_async_copy(source, target, load_sem.at[index])
        for index, (source, target) in enumerate(
            (
                (expand_other_hbm, expand_other_ref),
                (reduce_other_hbm, reduce_other_ref),
                (expand_hbm, expand_ref),
                (reduce_hbm, reduce_ref),
                (projected_hbm, projected_ref),
                (heads_hbm, heads_ref),
                (attend_hbm, attend_ref),
                (linear_hbm, linear_ref),
                (encode_hbm, encode_ref),
                (conved_hbm, conved_ref),
            )
        )
    ]
    result_copy = pltpu.make_async_copy(result_ref, result_hbm, load_sem.at[len(loads)])

    for load in loads:
        load.start()
    barrier = greet_partners()
    pl.semaphore_signal(barrier, inc=1, device_id=sibling(), device_id_type=MESH)
    pl.semaphore_wait(barrier, KERNEL_BITS + 1)
    mixed_copy = copies.to(sibling(), mixed_ref.at[:, local:], mixed_other, 2)
    mixed_copy.start()
    for copy in share_copies:
        copy.start()

    cotangent = cotangent_ref[...]
    for kind in range(2):
        picks[kind] = nested_picks(channels, ORDERS[kind])
    cotangent_turned = to_low(product(picks[0], cotangent, 1, 1))
    second = first_ref[...] + output_bias_ref[...]
    second += product(mixed_ref[:, :local], output_ref[...], 0, 0)
    mixed_copy.wait()
    second += product(mixed_other[...], output_other_ref[...], 0, 0)
    normal, inverse = layer_norm(second)
    feed_low = to_low(normal * gain_ref[...] + shift_ref[...])
    feed_turned = to_low(product(picks[1], feed_low, 1, 1))
    result = second + reduce_bias_ref[...]
    feed_grad = jnp.zeros_like(second)
    for load in loads[:4]:
        load.wait()
    weight_copies = []
    for index, (up_ref, up_bias_ref, down_ref) in enumerate(
        (
            (expand_other_ref, bias_other_ref, reduce_other_ref),
            (expand_ref, bias_ref, reduce_ref),
        )
    ):
        bias_grads = []
        for start in range(0, hidden_width, columns):
            now = slice(start, start + columns)
            hidden = product(feed_low, up_ref[:, now], 1, 0) + up_bias_ref[:, now]
            below = 0.5 + 0.5 * lax.erf(hidden * 0.5**0.5)
            slope = below + hidden * (jnp.exp(-0.5 * hidden * hidden) * (0.5 / jnp.pi) ** 0.5)
            active = to_low(hidden * below)
            hidden_grad = to_low(product(cotangent, down_ref[now, :], 1, 1) * slope)
            result += product(active, down_ref[now, :], 1, 0)
            feed_grad += product(hidden_grad, up_ref[:, now], 1, 1)
            bias_grads.append(column_sum(to_wide(hidden_grad)))
            weight_grads = (
                product(cotangent_turned, active, 1, 0),
                product(feed_turned, hidden_grad, 1, 0),
            )
            for kind, weight_grad in enumerate(weight_grads):
                if index == 0:
                    away[kind, :, now] = weight_grad
                    copy = copies.to(
                        sibling(),
                        away.at[kind, :, now],
                        arrived.at[kind, :, now],
                        4 + len(weight_copies),
                    )
                    copy.start()
                    weight_copies.append(copy)
                else:
                    top[kind, :, now] = weight_grad[:half]
                    sums.keep[kind, 0, :, now] = weight_grad[half:]
        owner = (1 - side) if index == 0 else side
        for part, grads in enumerate(bias_grads):
            vectors_ref[pl.ds(8 + 2 * owner + part, 1), :] = grads
    result_ref[...] = to_low(result)
    result_copy.start()
    upstream = to_wide(cotangent)
    second_grad = upstream + norm_back(feed_grad, normal, inverse, gain_ref[...])
    second_grad_ref[...] = second_grad
    second_own[...] = to_low(second_grad)
    second_copy = copies.to(sibling(), second_own, second_other, 3)
    second_copy.start()
    vectors_ref[0:1] = column_sum(second_grad)
    vectors_ref[1:2] = column_sum(feed_grad * normal)
    vectors_ref[2:3] = column_sum(feed_grad)
    vectors_ref[3:4] = column_sum(upstream)
    mixed_grad_ref[:, :local] = to_low(product(output_ref[...], second_own[...], 1, 1))
    part = width // 2
    output_grads = [
        product(
            to_low(product(picks[kind], second_own[...], 1, 1)),
            mixed_ref[kind * part : (kind + 1) * part, :local],
            1,
            1,
        )
        for kind in range(2)
    ]
    second_copy.wait()
    mixed_grad_ref[:, local:] = to_low(product(output_ref[...], second_other[...], 1, 1))
    for kind in range(2):
        output_grad = output_grads[kind] + product(
            to_low(product(picks[kind], second_other[...], 1, 1)),
            mixed_ref[kind * part : (kind + 1) * part, local:],
            1,
            1,
        )
        sums.sends[0][kind, 0, :, hidden_width:] = to_low(output_grad[:half])
        sums.keep[kind, 0, :, hidden_width:] = output_grad[half:]
    for copy in weight_copies:
        copy.wait()
    for kind in range(2):
        sums.sends[0][kind, 0, :, :hidden_width] = to_low(top[kind] + arrived[kind, :half])
        sums.start(0, kind, ((True, ORDERS[kind]),))
        sums.keep[kind, 0, :, :hidden_width] += arrived[kind, half:]

    scale = HEAD_DIM**-0.5
    row = lax.broadcasted_iota(jnp.int32, (HEAD_DIM, points), 0)
    ones = to_low(jnp.where((row > 0) & (row < 4), 1.0, 0.0))
    for load in loads[4:]:
        load.wait()

    def three_parts(values, lead):
        upper = to_wide(to_low(values))
        middle = to_wide(to_low(values - upper))
        lower = values - upper - middle
        tail = jnp.where(row == 1, -upper, jnp.where(row == 2, -middle, 0.0))
        tail = jnp.where(row == 3, -lower, tail)
        return to_low(jnp.where(row == 0, lead, tail))

    def finish_sum(index, total):
        if index == 0:
            reduce_sum_ref[...] = total[0, :, :hidden_width]
        else:
            expand_sum_ref[...] = total[0, :, :hidden_width]
        output_sum_ref[:, index * part : (index + 1) * part] = total[0, :, hidden_width:]

    def heads_step(step, _):
        for stage, due in enumerate(SUM_STEPS):

            @pl.when(step == due)
            def _(stage=stage):
                for index in range(2):
                    sums.advance(
                        stage, index, ((True, ORDERS[index]),), functools.partial(finish_sum, index)
                    )

        operands, places = [], []
        for offset in range(HEADS_BACK_STEP):
            head = step * HEADS_BACK_STEP + offset
            place = pl.ds(pl.multiple_of(head * HEAD_DIM, HEAD_DIM), HEAD_DIM)
            places.append(place)
            query, key, value = (projected_ref[index, place] for index in range(3))
            grad = mixed_grad_ref[place]
            row_dot = column_sum(to_wide(grad) * to_wide(mixed_ref[place]))
            scaled = to_low(to_wide(query) * scale)
            operands.append(
                (
                    jnp.concatenate([scaled, three_parts(log_ref[head], 1.0)], axis=0),
                    jnp.concatenate([key, mask_ref[...] + ones], axis=0),
                    jnp.concatenate([value, ones], axis=0),
                    jnp.concatenate([grad, three_parts(row_dot, 0.0)], axis=0),
                    query,
                    key,
                    grad,
                )
            )
        totals = [None] * HEADS_BACK_STEP

        def begin(unit):
            offset, start = unit
            queries, keys, values, grads = operands[offset][:4]
            return (
                product(keys, queries[:, start : start + CHUNK], 0, 0),
                product(values, grads[:, start : start + CHUNK], 0, 0),
            )

        def finish(unit, ready):
            offset, start = unit
            scores, prob_grad = ready
            query, key, grad = operands[offset][4:]
            now = slice(start, start + CHUNK)
            probs = jnp.exp(scores)
            score_grad = to_low(probs * prob_grad)
            grad_ref[0, places[offset], now] = to_low(product(key, score_grad, 1, 0) * scale)
            value_part = product(grad[:, now], to_low(probs), 1, 1)
            key_part = product(query[:, now], score_grad, 1, 1)
            if totals[offset] is not None:
                key_part, value_part = key_part + totals[offset][0], value_part + totals[offset][1]
            totals[offset] = (key_part, value_part)

        units = [(h, c) for c in range(0, points, CHUNK) for h in range(HEADS_BACK_STEP)]
        staged(units, begin, finish)
        for offset in range(HEADS_BACK_STEP):
            grad_ref[1, places[offset]] = to_low(totals[offset][0] * scale)
            grad_ref[2, places[offset]] = to_low(totals[offset][1])
        return 0

    lax.fori_loop(0, heads // HEADS_BACK_STEP, heads_step, 0)

    def attend_grad(start):
        return sum(
            product(grad_ref[index, :, start : start + local].T, heads_ref[index], 1, 1)
            for index in range(3)
        )

    attend_away[...] = attend_grad(local)
    attend_copy = copies.to(sibling(), attend_away, attend_arrived, 8)
    attend_copy.start()
    upstream = attend_grad(0)
    for kind in range(2):
        turned = [to_low(product(picks[kind], attend_ref[i], 1, 1)) for i in range(2)]
        for index in (0, 1) if kind == 0 else (2,):
            extra_ref[kind, index % 2] = product(
                turned[0], grad_ref[index, :, :local], 1, 1
            ) + product(turned[1], grad_ref[index, :, local:], 1, 1)
    normal, inverse = layer_norm(first_ref[...])
    attend_copy.wait()
    upstream += attend_arrived[...]
    first_grad = second_grad_ref[...] + norm_back(upstream, normal, inverse, attend_gain_ref[...])
    first_grad_ref[...] = first_grad
    vectors_ref[4:5] = column_sum(upstream * normal)
    vectors_ref[5:6] = column_sum(upstream)
    normal, inverse = layer_norm(linear_ref[...])
    linear_own[...] = to_low(norm_back(first_grad, normal, inverse, encode_gain_ref[...]))
    linear_copy = copies.to(sibling(), linear_own, linear_other, 9)
    linear_copy.start()
    vectors_ref[6:7] = column_sum(first_grad * normal)
    vectors_ref[7:8] = column_sum(first_grad)
    conved_grad_ref[mine] = to_low(product(linear_own[...], encode_ref[...], 1, 1))
    encode_grad = product(
        to_low(product(picks[1], linear_own[...], 1, 1)), conved_ref[mine], 1, 0
    )
    linear_copy.wait()
    conved_grad_ref[theirs] = to_low(product(linear_other[...], encode_ref[...], 1, 1))
    extra_ref[1, 1] = encode_grad + product(
        to_low(product(picks[1], linear_other[...], 1, 1)), conved_ref[theirs], 1, 0
    )
    result_copy.wait()
    for copy in share_copies:
        copy.wait()


def middle(near_operands, far_operands):
    local, channels = near_operands[1].shape
    width, rows = near_operands[0].shape
    hidden = near_operands[8].shape[1]
    turned, near = far_operands[-2:]
    kept = channels >> KERNEL_BITS
    low, full = jnp.bfloat16, jnp.float32
    shape = jax.ShapeDtypeStruct
    anywhere = pl.BlockSpec(memory_space=pl.ANY)
    loaded = far_operands[:-2]
    square = (local, channels)
    return pl.pallas_call(
        middle_kernel,
        in_specs=[vmem()] * len(near_operands) + [anywhere] * len(far_operands),
        out_specs=[vmem()] * 7 + [anywhere] * 3,
        out_shape=[
            shape(square, full),
            shape((rows, width), low),
            shape((2, 2, channels, width), full),
            shape((8 + 2 * hidden // channels, channels), full),
            shape((kept, hidden), full),
            shape((kept, hidden), full),
            shape((kept, width), full),
            shape(square, low),
            shape((channels // 2, turned.shape[1]), low),
            shape(near.shape, full),
        ],
        scratch_shapes=[
            *[pltpu.VMEM(each.shape, each.dtype) for each in loaded],
            pltpu.VMEM(square, low),
            pltpu.VMEM(square, full),
            pltpu.VMEM((width, rows), low),
            pltpu.VMEM((3, width, rows), low),
            pltpu.VMEM((width, local), low),
            pltpu.VMEM(square, low),
            pltpu.VMEM(square, low),
            pltpu.VMEM((2, channels, channels), low),
            pltpu.VMEM((2, channels // 2, hidden), full),
            pltpu.VMEM((2, channels, hidden), full),
            pltpu.VMEM((2, channels, hidden), full),
            pltpu.VMEM(square, full),
            pltpu.VMEM(square, full),
            pltpu.VMEM(square, low),
            pltpu.VMEM(square, low),
            pltpu.SemaphoreType.DMA((len(loaded) + 1,)),
            *copy_sems(10),
            *pair_scratch(2, 1, channels, hidden + width // 2, KERNEL_BITS),
        ],
        compiler_params=pltpu.CompilerParams(
            vmem_limit_bytes=VMEM_BYTES, collective_id=3, has_side_effects=True
        ),
        cost_estimate=pl.CostEstimate(
            flops=70 * 10**9, bytes_accessed=20 * 10**6, transcendentals=0
        ),
    )(*near_operands, *far_operands)


def conv_backward_kernel(
    near_ref,
    near_other_ref,
    turned_ref,
    turned_other_ref,
    grad_ref,
    weight_hbm,
    extra_ref,
    vector_ref,
    first_grad_hbm,
    conv_sum_ref,
    heads_sum_ref,
    encode_sum_ref,
    points_grad_ref,
    *refs,
):
    vector_refs, refs = refs[:9], refs[9:]
    (
        spread,
        windows,
        gathered,
        grad_other,
        input_grad,
        input_arrived,
        rim_away,
        rim_arrived,
        vector_away,
        vector_arrived,
        send_sem,
        arrive_sem,
        weight_ref,
        first_grad_ref,
        load_sem,
    ) = refs[:15]
    sums, extra_sums = pair_sums(refs[15:24]), pair_sums(refs[24:])
    rows, width = grad_ref.shape
    local, channels = first_grad_ref.shape
    half = channels // 2
    quarter = half // 4
    blocks = rows // BLOCK
    extras = extra_ref.shape[0]
    chunks = conv_sum_ref.shape[0]
    patches = lax.axis_size("pts")
    me, side = lax.axis_index("pts"), lax.axis_index("tp")
    copies = Copies(send_sem, arrive_sem)
    loads = [
        pltpu.make_async_copy(weight_hbm, weight_ref, load_sem.at[0]),
        pltpu.make_async_copy(first_grad_hbm, first_grad_ref, load_sem.at[1]),
    ]
    mine = pl.ds(pl.multiple_of(HALO + side * local, HALO), local)
    theirs = pl.ds(pl.multiple_of(HALO + (1 - side) * local, HALO), local)
    grad_copy = copies.to({"pts": partner_of(SHARE_BIT)}, grad_ref, grad_other, 0)
    input_copy = copies.to(sibling(), input_grad.at[theirs], input_arrived, 1)
    rims = (
        (me > 0, {"pts": me - 1, "tp": 1}, slice(0, HALO)),
        (me < patches - 1, {"pts": me + 1, "tp": 0}, slice(HALO + rows, rows + 2 * HALO)),
    )
    rim_copies = [
        [copies.to(rim[1], rim_away.at[i], rim_arrived.at[core], 2 + i, 4 + core) for core in (0, 1)]
        for i, rim in enumerate(rims)
    ]
    has_rim = ((side == 0) & (me > 0)) | ((side == 1) & (me < patches - 1))
    first_sum = chunks // GROUP
    first_input = first_sum + chunks
    input_steps = chunks // GROUP

    def vector_copy(stage):
        device = sibling() if stage == 0 else {"pts": partner_of(stage - 1)}
        return copies.to(device, vector_away.at[stage], vector_arrived.at[stage], 6 + stage)

    def kinds(chunk):
        return ((chunk % 2 == 0, CONV_ORDERS[0]), (chunk % 2 == 1, CONV_ORDERS[1]))

    steps = first_input + 2 * input_steps

    def begin():
        barrier = greet_partners()
        pl.semaphore_signal(barrier, inc=1, device_id=sibling(), device_id_type=MESH)
        for core in range(2):

            @pl.when((side == 0) & (me > 0))
            def _(core=core):
                device = {"pts": me - 1, "tp": core}
                pl.semaphore_signal(barrier, inc=1, device_id=device, device_id_type=MESH)

            @pl.when((side == 1) & (me < patches - 1))
            def _(core=core):
                device = {"pts": me + 1, "tp": core}
                pl.semaphore_signal(barrier, inc=1, device_id=device, device_id_type=MESH)

        sent = jnp.where(me > 0, 1, 0) + jnp.where(me < patches - 1, 1, 0)
        pl.semaphore_wait(barrier, KERNEL_BITS + 1 + sent)
        grad_copy.start()
        for load in loads:
            load.start()
        for index in range(extras):
            extra_sums.sends[0][index] = to_low(extra_ref[index, :, :half])
            extra_sums.start(0, index, ((True, ORDERS[index]),))
            extra_sums.keep[index] = extra_ref[index, :, half:]
        vector_away[0] = vector_ref[...]
        vector_copy(0).start()
        for kind, places in enumerate(((0, 1, 2, 3), (0, 2, 1, 3))):
            for place, source in enumerate(places):
                now = slice(place * quarter, (place + 1) * quarter)
                low = source * quarter
                windows[kind, 0, now] = turned_ref[half + low : half + low + quarter, :]
                windows[kind, 1, now] = turned_other_ref[low : low + quarter, :]
        input_grad[...] = jnp.zeros_like(input_grad)

    def one_step(step, _):
        @pl.when(step < first_sum)
        def _():
            slots = to_wide(lax.broadcasted_iota(jnp.int32, (BLOCK, 1), 0))

            def spread_group(group, _):
                for offset in range(GROUP):
                    index = (step * GROUP + group) * GROUP + offset
                    near = near_ref[pl.ds(index, 1), :]
                    for part in range(blocks + 1):
                        low = max(part - 1, 0) * BLOCK
                        high = min(part + 1, blocks) * BLOCK
                        select = to_low(
                            jnp.where(near[:, low:high] - float(part * BLOCK) == slots, 1.0, 0.0)
                        )
                        spread[index, part * BLOCK : (part + 1) * BLOCK] = to_low(
                            product(select, grad_ref[low:high, :], 1, 0)
                        )
                return 0

            lax.fori_loop(0, GROUP, spread_group, 0, unroll=True)

        @pl.when((step >= first_sum) & (step < first_input))
        def _():
            chunk = step - first_sum
            pl.when(chunk == 0)(grad_copy.wait)
            slots = to_wide(lax.broadcasted_iota(jnp.int32, (2 * BLOCK, 1), 0))
            for offset in range(GROUP):
                near = near_other_ref[pl.ds(chunk * GROUP + offset, 1), :]
                for block in range(blocks):
                    low = block * BLOCK
                    select = to_low(
                        jnp.where(near[:, low : low + BLOCK] - float(low) == slots, 1.0, 0.0)
                    )
                    gathered[offset, :, low : low + BLOCK] = to_low(
                        product(windows[chunk % 2, 1, :, low : low + 2 * BLOCK], select, 1, 0)
                    )
            for offset in range(GROUP):
                weight_grad = product(windows[chunk % 2, 0], spread[chunk * GROUP + offset], 1, 0)
                weight_grad += product(gathered[offset], grad_other[...], 1, 0)
                sums.sends[0][chunk, offset] = to_low(weight_grad[: half // 2])
                sums.keep[chunk, offset] = weight_grad[half // 2 :]
            sums.start(0, chunk, kinds(chunk))

        @pl.when(step == first_input)
        def _():
            for load in loads:
                load.wait()

        beside = pl.ds(pl.multiple_of((1 - side) * (local + HALO), HALO), local + HALO)
        apart = pl.ds(pl.multiple_of(side * (2 * local + HALO), HALO), HALO)
        for phase, parts in enumerate(((beside, apart), (mine,))):
            start = first_input + phase * input_steps

            @pl.when((step >= start) & (step < start + input_steps))
            def _(start=start, parts=parts):
                def input_group(group, _):
                    for part in parts:
                        total = input_grad[part, :]
                        for offset in range(GROUP):
                            index = group * GROUP + offset
                            total += product(
                                spread[(step - start) * WIDE_GROUP + index, part, :],
                                weight_ref[(step - start) * WIDE_GROUP + index],
                                1,
                                1,
                            )
                        input_grad[part, :] = total
                    return 0

                lax.fori_loop(0, GROUP, input_group, 0, unroll=True)

        @pl.when(step == first_input + input_steps - 1)
        def _():
            input_copy.start()
            for index, (has, _, part) in enumerate(rims):
                rim_away[index] = to_low(input_grad[part, :])

                @pl.when(has)
                def _(index=index):
                    for core in range(2):

                        @pl.when(side == core)
                        def _(core=core):
                            rim_copies[index][core].start()

        @pl.when(step == steps - 1)
        def _():
            input_copy.wait()
            points_grad_ref[...] = first_grad_ref[...] + input_grad[mine, :] + input_arrived[...]

            @pl.when(has_rim)
            def _():
                edge = pl.ds(pl.multiple_of(side * (local - HALO), HALO), HALO)
                for core in range(2):
                    rim_copies[0][core].wait_recv()
                    points_grad_ref[edge, :] += to_wide(rim_arrived[core])

            for index, (has, _, part) in enumerate(rims):
                pl.when(has)(rim_copies[index][0].wait_send)

        for stage, due in enumerate(VECTOR_STEPS):

            @pl.when(step == due)
            def _(stage=stage):
                vector_copy(stage).wait()
                summed = vector_away[stage] + vector_arrived[stage]
                if stage < KERNEL_BITS:
                    vector_away[stage + 1] = summed
                    vector_copy(stage + 1).start()
                    return
                for index in range(8):
                    vector_refs[index][...] = summed[index : index + 1]
                for index in range(8, summed.shape[0]):
                    low = (index - 8) * channels
                    vector_refs[8][:, low : low + channels] = summed[index : index + 1]

        for stage in range(len(CONV_LAGS)):
            chunk = step - first_sum - CONV_LAGS[stage]

            @pl.when((chunk >= 0) & (chunk < chunks))
            def _(stage=stage, chunk=chunk):
                def finish(total):
                    conv_sum_ref[chunk] = total

                sums.advance(stage, chunk, kinds(chunk), finish)

        def finish_extra(index, total):
            if index == 0:
                heads_sum_ref[0:2] = total
            else:
                heads_sum_ref[2] = total[0]
                encode_sum_ref[...] = total[1]

        for stage, due in enumerate(EXTRA_STEPS):

            @pl.when(step == due)
            def _(stage=stage):
                for index in range(extras):
                    extra_sums.advance(
                        stage,
                        index,
                        ((True, ORDERS[index]),),
                        functools.partial(finish_extra, index),
                    )
        return 0

    begin()
    lax.fori_loop(0, steps, one_step, 0)


def conv_backward(
    near, near_other, turned, turned_other, grad, weight, extra, vector, first_grad
):
    offsets, channels, width = weight.shape
    wide = turned.shape[1]
    rows = grad.shape[0]
    local = first_grad.shape[0]
    chunks = offsets // GROUP
    low, full = jnp.bfloat16, jnp.float32
    kept = channels >> KERNEL_BITS
    shape = jax.ShapeDtypeStruct
    outs = [
        shape((chunks, GROUP, kept, width), full),
        shape((3, kept, width), full),
        shape((kept, width), full),
        shape(first_grad.shape, full),
        *[shape((1, channels), full)] * 8,
        shape((1, (vector.shape[0] - 8) * channels), full),
    ]

    anywhere = pl.BlockSpec(memory_space=pl.ANY)
    return pl.pallas_call(
        conv_backward_kernel,
        in_specs=[vmem()] * 5 + [anywhere, vmem(), vmem(), anywhere],
        out_specs=[vmem()] * len(outs),
        out_shape=outs,
        scratch_shapes=[
            pltpu.VMEM((offsets, wide, width), low),
            pltpu.VMEM((2, 2, channels // 2, wide), low),
            pltpu.VMEM((GROUP, channels // 2, rows), low),
            pltpu.VMEM((rows, width), low),
            pltpu.VMEM((wide, channels), full),
            pltpu.VMEM((local, channels), full),
            pltpu.VMEM((2, HALO, channels), low),
            pltpu.VMEM((2, HALO, channels), low),
            pltpu.VMEM((KERNEL_BITS + 1, *vector.shape), full),
            pltpu.VMEM((KERNEL_BITS + 1, *vector.shape), full),
            *copy_sems(7 + KERNEL_BITS),
            pltpu.VMEM(weight.shape, low),
            pltpu.VMEM(first_grad.shape, full),
            pltpu.SemaphoreType.DMA((2,)),
            *pair_scratch(chunks, GROUP, channels // 2, width, len(CONV_LAGS)),
            *pair_scratch(*extra.shape, KERNEL_BITS),
        ],
        compiler_params=pltpu.CompilerParams(
            vmem_limit_bytes=VMEM_BYTES, collective_id=1, has_side_effects=True
        ),
        cost_estimate=pl.CostEstimate(
            flops=80 * 10**9, bytes_accessed=16 * 10**6, transcendentals=0
        ),
    )(near, near_other, turned, turned_other, grad, weight, extra, vector, first_grad)


def hand_over_kernel(*refs):
    count = len(refs) // 2
    for source, target in zip(refs[:count], refs[count:]):
        target[...] = source[...]


def hand_over(arrays):
    return pl.pallas_call(
        hand_over_kernel,
        in_specs=[vmem()] * len(arrays),
        out_specs=[vmem()] * len(arrays),
        out_shape=[jax.ShapeDtypeStruct(each.shape, each.dtype) for each in arrays],
        compiler_params=pltpu.CompilerParams(vmem_limit_bytes=VMEM_BYTES),
    )(*arrays)


def exchange(values, bit):
    count = lax.axis_size("pts")
    return lax.ppermute(values, "pts", [(i, i ^ (1 << bit)) for i in range(count)])


def sum_rest(keep, axis):
    for bit in range(KERNEL_BITS, patch_bits()):
        half = keep.shape[axis] // 2
        away = lax.slice_in_dim(keep, 0, half, axis=axis)
        keep = lax.slice_in_dim(keep, half, 2 * half, axis=axis)
        keep = keep + to_wide(exchange(to_low(away), bit))
    return keep


def per_device(
    points,
    neighbours,
    valid_count,
    conv_weight,
    encode_weight,
    encode_gain,
    encode_shift,
    attend_gain,
    attend_shift,
    heads_weight,
    output_weight,
    output_bias,
    feed_gain,
    feed_shift,
    expand_weight,
    expand_bias,
    reduce_weight,
    reduce_bias,
    cotangent,
):
    local, channels = points.shape
    rows = 2 * local
    is_first = lax.axis_index("tp") == 0
    norms = [v[None, :] for v in (encode_gain, encode_shift, attend_gain, attend_shift)]
    (
        turned, near_columns, conved, linear, first, attend_in, projected,
        output_other, expand_other, reduce_other, bias_other,
    ) = forward_start(
        neighbours.T, points, conv_weight, encode_weight, norms, heads_weight, output_weight,
        expand_weight, reduce_weight, expand_bias[None, :]
    )

    place = jnp.arange(rows, dtype=jnp.int32)
    place = jnp.where(is_first, place, (place + local) % rows)
    bias = jnp.where(place < valid_count[0], 0.0, MASKED)
    bias = to_low(jnp.where(jnp.arange(HEAD_DIM)[:, None] == 0, bias[None, :], 0.0))
    mixed, logs = attend(projected, bias)
    (
        first_grad, conved_grad, extra, vector, reduce_sum, expand_sum, output_sum, result,
        turned_other, near_other,
    ) = middle(
        [
            mixed, first, output_weight, output_other, output_bias[None, :], feed_gain[None, :],
            feed_shift[None, :], cotangent, expand_bias[None, :], bias_other,
            reduce_bias[None, :], bias, logs, norms[2], norms[0],
        ],
        [
            expand_weight, expand_other, reduce_weight, reduce_other, projected, heads_weight,
            attend_in, linear, encode_weight, conved, turned, near_columns,
        ],
    )
    conv_sum, heads_sum, encode_sum, points_gradient, *vectors = conv_backward(
        near_columns, near_other, turned, turned_other, conved_grad, conv_weight, extra, vector,
        first_grad
    )
    for bit in range(KERNEL_BITS, patch_bits()):
        vectors = [each + exchange(each, bit) for each in vectors]
    parts = hand_over(
        [
            result,
            points_gradient,
            sum_rest(conv_sum, 2),
            sum_rest(encode_sum, 0),
            sum_rest(heads_sum, 1),
            sum_rest(output_sum, 0),
            sum_rest(expand_sum, 0),
            sum_rest(reduce_sum, 0),
            *vectors,
        ]
    )
    vectors = [each.reshape(-1) for each in parts[8:]]
    return (
        parts[0],
        parts[1],
        parts[2].reshape(-1, *parts[2].shape[2:]),
        parts[3].T,
        vectors[6],
        vectors[7],
        vectors[4],
        vectors[5],
        parts[4],
        parts[5].T,
        vectors[0],
        vectors[1],
        vectors[2],
        parts[6],
        vectors[8],
        parts[7].T,
        vectors[3],
    )


def solution(mesh):
    placed = (
        P(("pts", "tp"), None),
        P("pts", None),
        P("pts"),
        P(None, None, "tp"),
        P("tp", None),
        P(),
        P(),
        P(),
        P(),
        P(None, None, "tp"),
        P("tp", None),
        P(),
        P(),
        P(),
        P(None, "tp"),
        P("tp"),
        P("tp", None),
        P(),
        P(("pts", "tp"), None),
    )
    return jax.shard_map(
        per_device,
        mesh=mesh,
        in_specs=placed,
        out_specs=(
            P(("pts", "tp"), None),
            P(("pts", "tp"), None),
            P(None, "pts", "tp"),
            P("tp", "pts"),
            P(),
            P(),
            P(),
            P(),
            P(None, "pts", "tp"),
            P("tp", "pts"),
            P(),
            P(),
            P(),
            P("pts", "tp"),
            P(),
            P("tp", "pts"),
            P(),
        ),
        check_vma=False,
    )
```

```python
import functools

import jax
import jax.numpy as jnp
from jax import lax
from jax.experimental import pallas as pl
from jax.experimental.pallas import tpu as pltpu
from jax.sharding import PartitionSpec as P

MESH = pl.DeviceIdType.MESH
HEAD_DIM = 16
HALO = 128
BLOCK = 256
GROUP = 3
EPSILON = 1e-05
MASKED = -1e30
KERNEL_BITS = 4
ORDERS = ((0, 1, 2, 3), (1, 0, 2, 3))
VMEM_BYTES = 60 << 20
CHUNK = 512
HEADS_STEP = 4
HEADS_BACK_STEP = 2
SUM_STEPS = (3, 5, 6, 7)
SHARE_BIT = 2
CONV_ORDERS = ((0, 1, 3), (1, 0, 3))
WINDOW_ORDER = (2, 0, 1, 3)
CONV_LAGS = (2, 4, 6)
EXTRA_STEPS = (2, 3, 5, 7)
VECTOR_STEPS = (1, 2, 3, 4, 5)
WEIGHTS_AHEAD = 3
WIDE_GROUP = 9


def to_low(values):
    return values.astype(jnp.bfloat16)


def to_wide(values):
    return values.astype(jnp.float32)


def product(left, right, left_dim, right_dim):
    dims = (((left_dim,), (right_dim,)), ((), ()))
    return lax.dot_general(left, right, dims, preferred_element_type=jnp.float32)


def layer_norm(values):
    row_mean = jnp.mean(values, axis=-1, keepdims=True)
    centred = values - row_mean
    inverse = lax.rsqrt(jnp.mean(centred * centred, axis=-1, keepdims=True) + EPSILON)
    return centred * inverse, inverse


def norm_back(upstream, normal_part, inverse, norm_gain):
    scaled = upstream * norm_gain
    across = (
        scaled
        - jnp.mean(scaled, axis=-1, keepdims=True)
        - normal_part * jnp.mean(scaled * normal_part, axis=-1, keepdims=True)
    )
    return across * inverse


def column_sum(values):
    return jnp.sum(values, axis=0, keepdims=True)


def nested_picks(channels, order):
    me = lax.axis_index("pts")
    order = order + tuple(range(KERNEL_BITS, patch_bits()))
    depth = channels >> len(order)
    lanes = 128
    place = lax.broadcasted_iota(jnp.int32, (channels, lanes), 0)
    picked = place & (depth - 1)
    for stage, bit in enumerate(order):
        kept = (place >> (channels.bit_length() - 2 - stage)) & 1
        picked = picked + (1 - ((kept + me // (1 << bit)) & 1)) * (depth << bit)
    column = lax.broadcasted_iota(jnp.int32, (channels, lanes), 1)
    return to_low(
        jnp.concatenate(
            [
                jnp.where(picked == column + low, 1.0, 0.0)
                for low in range(0, channels, lanes)
            ],
            axis=1,
        )
    )


class Copies:
    def __init__(self, send_sem, arrive_sem):
        self.send_sem, self.arrive_sem = send_sem, arrive_sem

    def to(self, device, source, target, send, arrive=None):
        return pltpu.make_async_remote_copy(
            src_ref=source,
            dst_ref=target,
            send_sem=self.send_sem.at[send],
            recv_sem=self.arrive_sem.at[send if arrive is None else arrive],
            device_id=device,
            device_id_type=MESH,
        )


def copy_sems(count):
    return [pltpu.SemaphoreType.DMA((count,))] * 2


def patch_bits():
    return lax.axis_size("pts").bit_length() - 1


def sibling():
    return {"tp": 1 - lax.axis_index("tp")}


def greet_sibling():
    barrier = pltpu.get_barrier_semaphore()
    pl.semaphore_signal(barrier, inc=1, device_id=sibling(), device_id_type=MESH)
    pl.semaphore_wait(barrier, 1)


def vmem():
    return pl.BlockSpec(memory_space=pltpu.VMEM)


def whole(array):
    zeros = (0,) * array.ndim
    return pl.BlockSpec(array.shape, lambda i: zeros, pipeline_mode=pl.Buffered(1))


def staged(units, begin, finish):
    ready = begin(units[0])
    for index, unit in enumerate(units):
        later = begin(units[index + 1]) if index + 1 < len(units) else None
        finish(unit, ready)
        ready = later


def forward_kernel(
    near_ref,
    points_ref,
    encode_gain_ref,
    encode_shift_ref,
    attend_gain_ref,
    attend_shift_ref,
    mask_ref,
    weight_hbm,
    encode_hbm,
    heads_hbm,
    output_hbm,
    expand_hbm,
    reduce_hbm,
    bias_hbm,
    mixed_ref,
    log_ref,
    turned_hbm,
    near_hbm,
    conved_hbm,
    linear_hbm,
    first_hbm,
    attend_hbm,
    projected_hbm,
    output_other,
    expand_other,
    reduce_other,
    bias_other,
    turned_ref,
    near_columns_ref,
    conved_ref,
    linear_ref,
    first_ref,
    attend_ref,
    projected_ref,
    window,
    total,
    rows,
    weight_own,
    weight_other,
    encode_ref,
    encode_other,
    conved_away,
    conved_other,
    attend_other,
    heads_ref,
    heads_turned,
    near_wide,
    near_tall,
    picks,
    load_sem,
    store_sem,
    send_sem,
    arrive_sem,
):
    local, channels = points_ref.shape
    offsets, _, width = weight_own.shape
    groups = offsets // GROUP
    points = 2 * local
    patches = lax.axis_size("pts")
    me, side = lax.axis_index("pts"), lax.axis_index("tp")
    copies = Copies(send_sem, arrive_sem)
    own_place = pl.ds(pl.multiple_of(HALO + side * local, HALO), local)
    other_place = pl.ds(pl.multiple_of(HALO + (1 - side) * local, HALO), local)
    low_rim, high_rim = slice(0, HALO), slice(HALO + points, 2 * HALO + points)
    points_copy = copies.to(sibling(), points_ref, window.at[own_place], 0)
    low_copies = [
        copies.to(
            {"pts": me + 1, "tp": core},
            points_ref.at[local - HALO :],
            window.at[low_rim],
            3 + core,
            1,
        )
        for core in range(2)
    ]
    high_copies = [
        copies.to(
            {"pts": me - 1, "tp": core}, points_ref.at[0:HALO], window.at[high_rim], 3 + core, 2
        )
        for core in range(2)
    ]
    small_copies = [
        copies.to(sibling(), encode_hbm, encode_other, 5),
        copies.to(sibling(), output_hbm, output_other, 6),
        copies.to(sibling(), expand_hbm, expand_other, 7),
        copies.to(sibling(), reduce_hbm, reduce_other, 8),
        copies.to(sibling(), bias_hbm, bias_other, 9),
    ]
    small_loads = [
        pltpu.make_async_copy(encode_hbm, encode_ref, load_sem.at[groups]),
        pltpu.make_async_copy(heads_hbm, heads_ref, load_sem.at[groups + 1]),
    ]
    stores = [
        pltpu.make_async_copy(source, target, store_sem.at[index])
        for index, (source, target) in enumerate(
            (
                (turned_ref, turned_hbm),
                (near_columns_ref, near_hbm),
                (conved_ref, conved_hbm),
                (linear_ref, linear_hbm),
                (first_ref, first_hbm),
                (attend_ref, attend_hbm),
                (projected_ref, projected_hbm),
            )
        )
    ]
    up = (side == 1) & (me < patches - 1)
    down = (side == 0) & (me > 0)

    def weight_copy(group):
        part = pl.ds(group * GROUP, GROUP)
        return copies.to(sibling(), weight_hbm.at[part], weight_other.at[part], 12 + group)

    def weight_load(group):
        part = pl.ds(group * GROUP, GROUP)
        return pltpu.make_async_copy(
            weight_hbm.at[part], weight_own.at[part], load_sem.at[group]
        )

    def turn(place):
        return to_low(product(picks[...], window[place, :], 1, 1))

    for group in range(WEIGHTS_AHEAD):
        weight_load(group).start()
    for load in small_loads:
        load.start()
    barrier = pltpu.get_barrier_semaphore()
    pl.semaphore_signal(barrier, inc=1, device_id=sibling(), device_id_type=MESH)

    @pl.when(me > 0)
    def _():
        pl.semaphore_signal(
            barrier, inc=1, device_id={"pts": me - 1, "tp": 1}, device_id_type=MESH
        )

    @pl.when(me < patches - 1)
    def _():
        pl.semaphore_signal(
            barrier, inc=1, device_id={"pts": me + 1, "tp": 0}, device_id_type=MESH
        )

    pl.semaphore_wait(barrier, jnp.where(up | down, 3, 1))
    points_copy.start()

    @pl.when(up)
    def _():
        for copy in low_copies:
            copy.start()

    @pl.when(down)
    def _():
        for copy in high_copies:
            copy.start()

    for group in range(WEIGHTS_AHEAD):
        weight_copy(group).start()
    window[own_place, :] = points_ref[...]

    @pl.when(me == 0)
    def _():
        window[low_rim, :] = jnp.zeros((HALO, channels), jnp.bfloat16)

    @pl.when(me == patches - 1)
    def _():
        window[high_rim, :] = jnp.zeros((HALO, channels), jnp.bfloat16)

    near_tall[...] = jnp.zeros_like(near_tall)
    near_tall[: near_ref.shape[0]] = to_wide(near_ref[...])
    near_columns_ref[...] = near_tall[: near_columns_ref.shape[0]]
    near_wide[...] = near_tall[...].T
    picks[...] = nested_picks(channels, WINDOW_ORDER)
    turned_ref[:, own_place] = turn(own_place)
    stores[1].start()
    points_copy.wait()

    lane = lax.broadcasted_iota(jnp.int32, (BLOCK, near_wide.shape[1]), 1)
    slots = to_wide(lax.broadcasted_iota(jnp.int32, (BLOCK, 2 * BLOCK), 1))
    places = [pl.ds(pl.multiple_of(block * BLOCK, BLOCK), BLOCK) for block in (1 - side, side)]

    def gather(index, group):
        low = pl.multiple_of(side * local + (1 - side, side)[index] * BLOCK, BLOCK)
        part = window[pl.ds(low, 2 * BLOCK), :]
        near = near_wide[pl.ds(low, BLOCK), :] - low.astype(jnp.float32)
        for offset in range(GROUP):
            chosen = jnp.where(lane == group * GROUP + offset, near, 0.0)
            column = jnp.sum(chosen, axis=1, keepdims=True)
            select = to_low(jnp.where(column == slots, 1.0, 0.0))
            rows[places[index], offset * channels : (offset + 1) * channels] = to_low(
                product(select, part, 1, 0)
            )

    def apply(place, group):
        picked = rows[place, :]
        part = pl.ds(group * GROUP, GROUP)
        flat = (GROUP * channels, width)
        return (
            product(picked, weight_own[part].reshape(flat), 1, 0),
            product(picked, weight_other[part].reshape(flat), 1, 0),
        )

    def both_blocks(group):
        gather(0, group)
        gather(1, group)
        own, other = apply(slice(None), group)
        total[:, :width] += own
        total[:, width:] += other

    def next_weights(group):
        later = group + WEIGHTS_AHEAD

        @pl.when(later < groups)
        def _():
            weight_load(later).start()
            weight_copy(later).start()

        weight_load(group).wait()
        weight_copy(group).wait()

    next_weights(0)
    gather(0, 0)
    total[places[0], :width], total[places[0], width:] = apply(places[0], 0)
    next_weights(1)

    @pl.when(me > 0)
    def _():
        low_copies[0].wait_recv()

    @pl.when(me < patches - 1)
    def _():
        high_copies[0].wait_recv()

    gather(1, 0)
    total[places[1], :width], total[places[1], width:] = apply(places[1], 0)
    both_blocks(1)

    @pl.when(up)
    def _():
        for copy in low_copies:
            copy.wait_send()

    @pl.when(down)
    def _():
        for copy in high_copies:
            copy.wait_send()

    for copy in small_copies:
        copy.start()
    for load in small_loads:
        load.wait()
    for place in (other_place, low_rim, high_rim):
        turned_ref[:, place] = turn(place)
    stores[0].start()
    for index in range(3):
        heads_turned[index] = heads_ref[index].T

    def group_step(group, _):
        next_weights(group)
        both_blocks(group)
        return 0

    lax.fori_loop(2, groups, group_step, 0)

    mine = pl.ds(pl.multiple_of(side * local, local), local)
    theirs = pl.ds(pl.multiple_of((1 - side) * local, local), local)
    conved_own = to_low(total[:, :width])
    conved_away[...] = to_low(total[:, width:])
    conved_ref[mine] = conved_own
    conved_copy = copies.to(sibling(), conved_away, conved_other, 10)
    conved_copy.start()
    small_copies[0].wait()
    linear = product(conved_own, encode_ref[...], 1, 0)
    linear += product(conved_away[...], encode_other[...], 1, 0)
    linear_ref[...] = linear
    first = layer_norm(linear)[0] * encode_gain_ref[...] + encode_shift_ref[...]
    first += to_wide(points_ref[...])
    first_ref[...] = first
    attend_out = layer_norm(first)[0] * attend_gain_ref[...] + attend_shift_ref[...]
    attend_ref[0] = to_low(attend_out)
    attend_copy = copies.to(sibling(), attend_ref.at[0], attend_other, 11)
    attend_copy.start()
    for index in range(3):
        projected_ref[index, :, :local] = to_low(
            product(heads_turned[index], attend_ref[0], 1, 1)
        )
    attend_copy.wait()
    attend_ref[1] = attend_other[...]
    for index in range(3):
        projected_ref[index, :, local:] = to_low(
            product(heads_turned[index], attend_other[...], 1, 1)
        )
    conved_copy.wait()
    conved_ref[theirs] = conved_other[...]
    for store in stores[2:]:
        store.start()

    row = lax.broadcasted_iota(jnp.int32, (HEAD_DIM, points), 0)
    ones = to_low(jnp.where(row == 0, 1.0, 0.0))

    def heads_step(step, _):
        operands, heads = [], []
        for offset in range(HEADS_STEP):
            head = step * HEADS_STEP + offset
            place = pl.ds(pl.multiple_of(head * HEAD_DIM, HEAD_DIM), HEAD_DIM)
            query, key, value = (projected_ref[index, place] for index in range(3))
            scaled = to_low(to_wide(query) * HEAD_DIM**-0.5)
            heads.append((head, place))
            operands.append(
                (
                    jnp.concatenate([scaled, ones], axis=0),
                    jnp.concatenate([key, mask_ref[...]], axis=0),
                    jnp.concatenate([value, ones], axis=0),
                )
            )

        def begin(unit):
            offset, start = unit
            queries, keys, _ = operands[offset]
            return product(keys, queries[:, start : start + CHUNK], 0, 0)

        def finish(unit, scores):
            offset, start = unit
            head, place = heads[offset]
            top = jnp.max(scores, axis=0, keepdims=True)
            mixed = product(operands[offset][2], to_low(jnp.exp(scores - top)), 1, 0)
            total = mixed[HEAD_DIM : HEAD_DIM + 1, :]
            now = slice(start, start + CHUNK)
            mixed_ref[place, now] = to_low(mixed[:HEAD_DIM] / total)
            log_ref[head, :, now] = top + jnp.log(total)

        units = [(h, c) for c in range(0, points, CHUNK) for h in range(HEADS_STEP)]
        staged(units, begin, finish)
        return 0

    lax.fori_loop(0, width // HEAD_DIM // HEADS_STEP, heads_step, 0)
    for copy in small_copies[1:]:
        copy.wait()
    for store in stores:
        store.wait()


def forward_start(
    near, points, conv_weight, encode_weight, norms, heads_weight, output_weight, expand_weight,
    reduce_weight, expand_bias, mask
):
    offsets, channels, width = conv_weight.shape
    local = points.shape[0]
    rows = 2 * local
    wide = rows + 2 * HALO
    groups = offsets // GROUP
    low, full = jnp.bfloat16, jnp.float32
    shape = jax.ShapeDtypeStruct
    anywhere = pl.BlockSpec(memory_space=pl.ANY)
    stored = [
        shape((channels, wide), low),
        shape((32, rows), full),
        shape((rows, width), low),
        shape((local, channels), full),
        shape((local, channels), full),
        shape((2, local, channels), low),
        shape((3, width, rows), low),
    ]
    away = [
        shape(array.shape, array.dtype)
        for array in (output_weight, expand_weight, reduce_weight, expand_bias)
    ]
    return pl.pallas_call(
        forward_kernel,
        in_specs=[vmem()] * 7 + [anywhere] * 7,
        out_specs=[vmem()] * 2 + [anywhere] * 11,
        out_shape=[shape((width, rows), low), shape((width // HEAD_DIM, 1, rows), full)]
        + stored
        + away,
        scratch_shapes=[
            *[pltpu.VMEM(each.shape, each.dtype) for each in stored],
            pltpu.VMEM((wide, channels), low),
            pltpu.VMEM((local, channels), full),
            pltpu.VMEM((local, GROUP * channels), low),
            pltpu.VMEM(conv_weight.shape, low),
            pltpu.VMEM(conv_weight.shape, low),
            pltpu.VMEM(encode_weight.shape, low),
            pltpu.VMEM(encode_weight.shape, low),
            pltpu.VMEM((local, width), low),
            pltpu.VMEM((local, width), low),
            pltpu.VMEM((local, channels), low),
            pltpu.VMEM(heads_weight.shape, low),
            pltpu.VMEM((3, width, channels), low),
            pltpu.VMEM((rows, 128), full),
            pltpu.VMEM((128, rows), full),
            pltpu.VMEM((channels, channels), low),
            pltpu.SemaphoreType.DMA((groups + 2,)),
            pltpu.SemaphoreType.DMA((len(stored),)),
            *copy_sems(12 + groups),
        ],
        compiler_params=pltpu.CompilerParams(
            vmem_limit_bytes=VMEM_BYTES, collective_id=2, has_side_effects=True
        ),
        cost_estimate=pl.CostEstimate(
            flops=60 * 10**9, bytes_accessed=20 * 10**6, transcendentals=0
        ),
    )(
        near, points, *norms, mask, conv_weight, encode_weight, heads_weight, output_weight,
        expand_weight, reduce_weight, expand_bias
    )


def partner_of(bit):
    me = lax.axis_index("pts")
    return me + (1 - 2 * ((me // (1 << bit)) % 2)) * (1 << bit)


def greet_partners():
    barrier = pltpu.get_barrier_semaphore()
    for bit in range(KERNEL_BITS):
        pl.semaphore_signal(
            barrier, inc=1, device_id={"pts": partner_of(bit)}, device_id_type=MESH
        )
    return barrier


class PairSums:
    def __init__(self, keep, sends, arrivals, send_sem, arrive_sem):
        self.keep, self.sends, self.arrivals = keep, sends, arrivals
        self.send_sem, self.arrive_sem = send_sem, arrive_sem

    def copy(self, stage, chunk, bit):
        return pltpu.make_async_remote_copy(
            src_ref=self.sends[stage].at[chunk],
            dst_ref=self.arrivals[stage].at[chunk],
            send_sem=self.send_sem.at[stage, chunk],
            recv_sem=self.arrive_sem.at[stage, chunk],
            device_id={"pts": partner_of(bit)},
            device_id_type=MESH,
        )

    def start(self, stage, chunk, kinds):
        for holds, order in kinds:
            if holds is True:
                self.copy(stage, chunk, order[stage]).start()
            else:

                @pl.when(holds)
                def _(order=order):
                    self.copy(stage, chunk, order[stage]).start()

    def advance(self, stage, chunk, kinds, finish):
        self.copy(stage, chunk, 0).wait()
        rows = self.keep.shape[2]
        low = rows - (rows >> stage)
        half = (rows - low) // 2
        arrived = self.arrivals[stage]
        if stage == len(self.sends) - 1:
            finish(self.keep[chunk, :, low:] + to_wide(arrived[chunk]))
            return
        self.sends[stage + 1][chunk] = to_low(
            self.keep[chunk, :, low : low + half] + to_wide(arrived[chunk, :, :half])
        )
        self.start(stage + 1, chunk, kinds)
        self.keep[chunk, :, low + half :] += to_wide(arrived[chunk, :, half:])


def pair_scratch(chunks, lead, rows, width, stages):
    halves = [(chunks, lead, rows >> (stage + 1), width) for stage in range(stages)]
    return (
        [pltpu.VMEM(halves[0], jnp.float32)]
        + [pltpu.VMEM(shape, jnp.bfloat16) for shape in halves]
        + [pltpu.VMEM(shape, jnp.bfloat16) for shape in halves]
        + [pltpu.SemaphoreType.DMA((stages, chunks))] * 2
    )


def pair_sums(scratch):
    stages = (len(scratch) - 3) // 2
    keep, rest = scratch[0], scratch[1:]
    return PairSums(keep, rest[:stages], rest[stages : 2 * stages], *rest[-2:])


def middle_kernel(
    mixed_ref,
    first_ref,
    output_ref,
    output_other_ref,
    output_bias_ref,
    gain_ref,
    shift_ref,
    cotangent_ref,
    bias_ref,
    bias_other_ref,
    reduce_bias_ref,
    mask_ref,
    log_ref,
    attend_gain_ref,
    encode_gain_ref,
    expand_hbm,
    expand_other_hbm,
    reduce_hbm,
    reduce_other_hbm,
    projected_hbm,
    heads_hbm,
    attend_hbm,
    linear_hbm,
    encode_hbm,
    conved_hbm,
    turned_hbm,
    near_hbm,
    first_grad_ref,
    conved_grad_ref,
    extra_ref,
    vectors_ref,
    reduce_sum_ref,
    expand_sum_ref,
    output_sum_ref,
    result_hbm,
    turned_other,
    near_other,
    expand_ref,
    expand_other_ref,
    reduce_ref,
    reduce_other_ref,
    projected_ref,
    heads_ref,
    attend_ref,
    linear_ref,
    encode_ref,
    conved_ref,
    result_ref,
    second_grad_ref,
    mixed_grad_ref,
    grad_ref,
    mixed_other,
    second_own,
    second_other,
    picks,
    top,
    away,
    arrived,
    attend_away,
    attend_arrived,
    linear_own,
    linear_other,
    load_sem,
    send_sem,
    arrive_sem,
    *scratch,
):
    local, channels = first_ref.shape
    width, points = mixed_ref.shape
    hidden_width = bias_ref.shape[1]
    columns = hidden_width // 2
    heads = width // HEAD_DIM
    half = channels // 2
    side = lax.axis_index("tp")
    mine = pl.ds(pl.multiple_of(side * local, local), local)
    theirs = pl.ds(pl.multiple_of((1 - side) * local, local), local)
    sums = pair_sums(scratch)
    copies = Copies(send_sem, arrive_sem)
    partner = {"pts": partner_of(SHARE_BIT)}
    share_copies = [
        copies.to(partner, turned_hbm.at[:half], turned_other, 0),
        copies.to(partner, near_hbm, near_other, 1),
    ]
    loads = [
        pltpu.make_async_copy(source, target, load_sem.at[index])
        for index, (source, target) in enumerate(
            (
                (expand_other_hbm, expand_other_ref),
                (reduce_other_hbm, reduce_other_ref),
                (expand_hbm, expand_ref),
                (reduce_hbm, reduce_ref),
                (projected_hbm, projected_ref),
                (heads_hbm, heads_ref),
                (attend_hbm, attend_ref),
                (linear_hbm, linear_ref),
                (encode_hbm, encode_ref),
                (conved_hbm, conved_ref),
            )
        )
    ]
    result_copy = pltpu.make_async_copy(result_ref, result_hbm, load_sem.at[len(loads)])

    for load in loads:
        load.start()
    barrier = greet_partners()
    pl.semaphore_signal(barrier, inc=1, device_id=sibling(), device_id_type=MESH)
    pl.semaphore_wait(barrier, KERNEL_BITS + 1)
    mixed_copy = copies.to(sibling(), mixed_ref.at[:, local:], mixed_other, 2)
    mixed_copy.start()
    for copy in share_copies:
        copy.start()

    cotangent = cotangent_ref[...]
    for kind in range(2):
        picks[kind] = nested_picks(channels, ORDERS[kind])
    cotangent_turned = to_low(product(picks[0], cotangent, 1, 1))
    second = first_ref[...] + output_bias_ref[...]
    second += product(mixed_ref[:, :local], output_ref[...], 0, 0)
    mixed_copy.wait()
    second += product(mixed_other[...], output_other_ref[...], 0, 0)
    normal, inverse = layer_norm(second)
    feed_low = to_low(normal * gain_ref[...] + shift_ref[...])
    feed_turned = to_low(product(picks[1], feed_low, 1, 1))
    result = second + reduce_bias_ref[...]
    feed_grad = jnp.zeros_like(second)
    for load in loads[:4]:
        load.wait()
    weight_copies = []
    for index, (up_ref, up_bias_ref, down_ref) in enumerate(
        (
            (expand_other_ref, bias_other_ref, reduce_other_ref),
            (expand_ref, bias_ref, reduce_ref),
        )
    ):
        bias_grads = []
        for start in range(0, hidden_width, columns):
            now = slice(start, start + columns)
            hidden = product(feed_low, up_ref[:, now], 1, 0) + up_bias_ref[:, now]
            below = 0.5 + 0.5 * lax.erf(hidden * 0.5**0.5)
            slope = below + hidden * (jnp.exp(-0.5 * hidden * hidden) * (0.5 / jnp.pi) ** 0.5)
            active = to_low(hidden * below)
            hidden_grad = to_low(product(cotangent, down_ref[now, :], 1, 1) * slope)
            result += product(active, down_ref[now, :], 1, 0)
            feed_grad += product(hidden_grad, up_ref[:, now], 1, 1)
            bias_grads.append(column_sum(to_wide(hidden_grad)))
            weight_grads = (
                product(cotangent_turned, active, 1, 0),
                product(feed_turned, hidden_grad, 1, 0),
            )
            for kind, weight_grad in enumerate(weight_grads):
                if index == 0:
                    away[kind, :, now] = weight_grad
                    copy = copies.to(
                        sibling(),
                        away.at[kind, :, now],
                        arrived.at[kind, :, now],
                        4 + len(weight_copies),
                    )
                    copy.start()
                    weight_copies.append(copy)
                else:
                    top[kind, :, now] = weight_grad[:half]
                    sums.keep[kind, 0, :, now] = weight_grad[half:]
        owner = (1 - side) if index == 0 else side
        for part, grads in enumerate(bias_grads):
            vectors_ref[pl.ds(8 + 2 * owner + part, 1), :] = grads
    result_ref[...] = to_low(result)
    result_copy.start()
    upstream = to_wide(cotangent)
    second_grad = upstream + norm_back(feed_grad, normal, inverse, gain_ref[...])
    second_grad_ref[...] = second_grad
    second_own[...] = to_low(second_grad)
    second_copy = copies.to(sibling(), second_own, second_other, 3)
    second_copy.start()
    vectors_ref[0:1] = column_sum(second_grad)
    vectors_ref[1:2] = column_sum(feed_grad * normal)
    vectors_ref[2:3] = column_sum(feed_grad)
    vectors_ref[3:4] = column_sum(upstream)
    mixed_grad_ref[:, :local] = to_low(product(output_ref[...], second_own[...], 1, 1))
    part = width // 2
    output_grads = [
        product(
            to_low(product(picks[kind], second_own[...], 1, 1)),
            mixed_ref[kind * part : (kind + 1) * part, :local],
            1,
            1,
        )
        for kind in range(2)
    ]
    second_copy.wait()
    mixed_grad_ref[:, local:] = to_low(product(output_ref[...], second_other[...], 1, 1))
    for kind in range(2):
        output_grad = output_grads[kind] + product(
            to_low(product(picks[kind], second_other[...], 1, 1)),
            mixed_ref[kind * part : (kind + 1) * part, local:],
            1,
            1,
        )
        sums.sends[0][kind, 0, :, hidden_width:] = to_low(output_grad[:half])
        sums.keep[kind, 0, :, hidden_width:] = output_grad[half:]
    for copy in weight_copies:
        copy.wait()
    for kind in range(2):
        sums.sends[0][kind, 0, :, :hidden_width] = to_low(top[kind] + arrived[kind, :half])
        sums.start(0, kind, ((True, ORDERS[kind]),))
        sums.keep[kind, 0, :, :hidden_width] += arrived[kind, half:]

    scale = HEAD_DIM**-0.5
    row = lax.broadcasted_iota(jnp.int32, (HEAD_DIM, points), 0)
    ones = to_low(jnp.where((row > 0) & (row < 4), 1.0, 0.0))
    for load in loads[4:]:
        load.wait()

    def three_parts(values, lead):
        upper = to_wide(to_low(values))
        middle = to_wide(to_low(values - upper))
        lower = values - upper - middle
        tail = jnp.where(row == 1, -upper, jnp.where(row == 2, -middle, 0.0))
        tail = jnp.where(row == 3, -lower, tail)
        return to_low(jnp.where(row == 0, lead, tail))

    def finish_sum(index, total):
        if index == 0:
            reduce_sum_ref[...] = total[0, :, :hidden_width]
        else:
            expand_sum_ref[...] = total[0, :, :hidden_width]
        output_sum_ref[:, index * part : (index + 1) * part] = total[0, :, hidden_width:]

    def heads_step(step, _):
        for stage, due in enumerate(SUM_STEPS):

            @pl.when(step == due)
            def _(stage=stage):
                for index in range(2):
                    sums.advance(
                        stage, index, ((True, ORDERS[index]),), functools.partial(finish_sum, index)
                    )

        operands, places = [], []
        for offset in range(HEADS_BACK_STEP):
            head = step * HEADS_BACK_STEP + offset
            place = pl.ds(pl.multiple_of(head * HEAD_DIM, HEAD_DIM), HEAD_DIM)
            places.append(place)
            query, key, value = (projected_ref[index, place] for index in range(3))
            grad = mixed_grad_ref[place]
            row_dot = column_sum(to_wide(grad) * to_wide(mixed_ref[place]))
            scaled = to_low(to_wide(query) * scale)
            operands.append(
                (
                    jnp.concatenate([scaled, three_parts(log_ref[head], 1.0)], axis=0),
                    jnp.concatenate([key, mask_ref[...] + ones], axis=0),
                    jnp.concatenate([value, ones], axis=0),
                    jnp.concatenate([grad, three_parts(row_dot, 0.0)], axis=0),
                    query,
                    key,
                    grad,
                )
            )
        totals = [None] * HEADS_BACK_STEP

        def begin(unit):
            offset, start = unit
            queries, keys, values, grads = operands[offset][:4]
            return (
                product(keys, queries[:, start : start + CHUNK], 0, 0),
                product(values, grads[:, start : start + CHUNK], 0, 0),
            )

        def finish(unit, ready):
            offset, start = unit
            scores, prob_grad = ready
            query, key, grad = operands[offset][4:]
            now = slice(start, start + CHUNK)
            probs = jnp.exp(scores)
            score_grad = to_low(probs * prob_grad)
            grad_ref[0, places[offset], now] = to_low(product(key, score_grad, 1, 0) * scale)
            value_part = product(grad[:, now], to_low(probs), 1, 1)
            key_part = product(query[:, now], score_grad, 1, 1)
            if totals[offset] is not None:
                key_part, value_part = key_part + totals[offset][0], value_part + totals[offset][1]
            totals[offset] = (key_part, value_part)

        units = [(h, c) for c in range(0, points, CHUNK) for h in range(HEADS_BACK_STEP)]
        staged(units, begin, finish)
        for offset in range(HEADS_BACK_STEP):
            grad_ref[1, places[offset]] = to_low(totals[offset][0] * scale)
            grad_ref[2, places[offset]] = to_low(totals[offset][1])
        return 0

    lax.fori_loop(0, heads // HEADS_BACK_STEP, heads_step, 0)

    def attend_grad(start):
        return sum(
            product(grad_ref[index, :, start : start + local].T, heads_ref[index], 1, 1)
            for index in range(3)
        )

    attend_away[...] = attend_grad(local)
    attend_copy = copies.to(sibling(), attend_away, attend_arrived, 8)
    attend_copy.start()
    upstream = attend_grad(0)
    for kind in range(2):
        turned = [to_low(product(picks[kind], attend_ref[i], 1, 1)) for i in range(2)]
        for index in (0, 1) if kind == 0 else (2,):
            extra_ref[kind, index % 2] = product(
                turned[0], grad_ref[index, :, :local], 1, 1
            ) + product(turned[1], grad_ref[index, :, local:], 1, 1)
    normal, inverse = layer_norm(first_ref[...])
    attend_copy.wait()
    upstream += attend_arrived[...]
    first_grad = second_grad_ref[...] + norm_back(upstream, normal, inverse, attend_gain_ref[...])
    first_grad_ref[...] = first_grad
    vectors_ref[4:5] = column_sum(upstream * normal)
    vectors_ref[5:6] = column_sum(upstream)
    normal, inverse = layer_norm(linear_ref[...])
    linear_own[...] = to_low(norm_back(first_grad, normal, inverse, encode_gain_ref[...]))
    linear_copy = copies.to(sibling(), linear_own, linear_other, 9)
    linear_copy.start()
    vectors_ref[6:7] = column_sum(first_grad * normal)
    vectors_ref[7:8] = column_sum(first_grad)
    conved_grad_ref[mine] = to_low(product(linear_own[...], encode_ref[...], 1, 1))
    encode_grad = product(
        to_low(product(picks[1], linear_own[...], 1, 1)), conved_ref[mine], 1, 0
    )
    linear_copy.wait()
    conved_grad_ref[theirs] = to_low(product(linear_other[...], encode_ref[...], 1, 1))
    extra_ref[1, 1] = encode_grad + product(
        to_low(product(picks[1], linear_other[...], 1, 1)), conved_ref[theirs], 1, 0
    )
    result_copy.wait()
    for copy in share_copies:
        copy.wait()


def middle(near_operands, far_operands):
    local, channels = near_operands[1].shape
    width, rows = near_operands[0].shape
    hidden = near_operands[8].shape[1]
    turned, near = far_operands[-2:]
    kept = channels >> KERNEL_BITS
    low, full = jnp.bfloat16, jnp.float32
    shape = jax.ShapeDtypeStruct
    anywhere = pl.BlockSpec(memory_space=pl.ANY)
    loaded = far_operands[:-2]
    square = (local, channels)
    return pl.pallas_call(
        middle_kernel,
        in_specs=[vmem()] * len(near_operands) + [anywhere] * len(far_operands),
        out_specs=[vmem()] * 7 + [anywhere] * 3,
        out_shape=[
            shape(square, full),
            shape((rows, width), low),
            shape((2, 2, channels, width), full),
            shape((8 + 2 * hidden // channels, channels), full),
            shape((kept, hidden), full),
            shape((kept, hidden), full),
            shape((kept, width), full),
            shape(square, low),
            shape((channels // 2, turned.shape[1]), low),
            shape(near.shape, full),
        ],
        scratch_shapes=[
            *[pltpu.VMEM(each.shape, each.dtype) for each in loaded],
            pltpu.VMEM(square, low),
            pltpu.VMEM(square, full),
            pltpu.VMEM((width, rows), low),
            pltpu.VMEM((3, width, rows), low),
            pltpu.VMEM((width, local), low),
            pltpu.VMEM(square, low),
            pltpu.VMEM(square, low),
            pltpu.VMEM((2, channels, channels), low),
            pltpu.VMEM((2, channels // 2, hidden), full),
            pltpu.VMEM((2, channels, hidden), full),
            pltpu.VMEM((2, channels, hidden), full),
            pltpu.VMEM(square, full),
            pltpu.VMEM(square, full),
            pltpu.VMEM(square, low),
            pltpu.VMEM(square, low),
            pltpu.SemaphoreType.DMA((len(loaded) + 1,)),
            *copy_sems(10),
            *pair_scratch(2, 1, channels, hidden + width // 2, KERNEL_BITS),
        ],
        compiler_params=pltpu.CompilerParams(
            vmem_limit_bytes=VMEM_BYTES, collective_id=3, has_side_effects=True
        ),
        cost_estimate=pl.CostEstimate(
            flops=70 * 10**9, bytes_accessed=20 * 10**6, transcendentals=0
        ),
    )(*near_operands, *far_operands)


def conv_backward_kernel(
    near_ref,
    near_other_ref,
    turned_ref,
    turned_other_ref,
    grad_ref,
    weight_hbm,
    extra_ref,
    vector_ref,
    first_grad_hbm,
    conv_sum_ref,
    heads_sum_ref,
    encode_sum_ref,
    points_grad_ref,
    *refs,
):
    vector_refs, refs = refs[:9], refs[9:]
    (
        spread,
        windows,
        gathered,
        grad_other,
        input_grad,
        input_arrived,
        rim_away,
        rim_arrived,
        vector_away,
        vector_arrived,
        send_sem,
        arrive_sem,
        weight_ref,
        first_grad_ref,
        load_sem,
    ) = refs[:15]
    sums, extra_sums = pair_sums(refs[15:24]), pair_sums(refs[24:])
    rows, width = grad_ref.shape
    local, channels = first_grad_ref.shape
    half = channels // 2
    quarter = half // 4
    blocks = rows // BLOCK
    extras = extra_ref.shape[0]
    chunks = conv_sum_ref.shape[0]
    patches = lax.axis_size("pts")
    me, side = lax.axis_index("pts"), lax.axis_index("tp")
    copies = Copies(send_sem, arrive_sem)
    loads = [
        pltpu.make_async_copy(weight_hbm, weight_ref, load_sem.at[0]),
        pltpu.make_async_copy(first_grad_hbm, first_grad_ref, load_sem.at[1]),
    ]
    mine = pl.ds(pl.multiple_of(HALO + side * local, HALO), local)
    theirs = pl.ds(pl.multiple_of(HALO + (1 - side) * local, HALO), local)
    grad_copy = copies.to({"pts": partner_of(SHARE_BIT)}, grad_ref, grad_other, 0)
    input_copy = copies.to(sibling(), input_grad.at[theirs], input_arrived, 1)
    rims = (
        (me > 0, {"pts": me - 1, "tp": 1}, slice(0, HALO)),
        (me < patches - 1, {"pts": me + 1, "tp": 0}, slice(HALO + rows, rows + 2 * HALO)),
    )
    rim_copies = [
        [copies.to(rim[1], rim_away.at[i], rim_arrived.at[core], 2 + i, 4 + core) for core in (0, 1)]
        for i, rim in enumerate(rims)
    ]
    has_rim = ((side == 0) & (me > 0)) | ((side == 1) & (me < patches - 1))
    first_sum = chunks // GROUP
    first_input = first_sum + chunks
    input_steps = chunks // GROUP

    def vector_copy(stage):
        device = sibling() if stage == 0 else {"pts": partner_of(stage - 1)}
        return copies.to(device, vector_away.at[stage], vector_arrived.at[stage], 6 + stage)

    def kinds(chunk):
        return ((chunk % 2 == 0, CONV_ORDERS[0]), (chunk % 2 == 1, CONV_ORDERS[1]))

    steps = first_input + 2 * input_steps

    def begin():
        barrier = greet_partners()
        pl.semaphore_signal(barrier, inc=1, device_id=sibling(), device_id_type=MESH)
        for core in range(2):

            @pl.when((side == 0) & (me > 0))
            def _(core=core):
                device = {"pts": me - 1, "tp": core}
                pl.semaphore_signal(barrier, inc=1, device_id=device, device_id_type=MESH)

            @pl.when((side == 1) & (me < patches - 1))
            def _(core=core):
                device = {"pts": me + 1, "tp": core}
                pl.semaphore_signal(barrier, inc=1, device_id=device, device_id_type=MESH)

        sent = jnp.where(me > 0, 1, 0) + jnp.where(me < patches - 1, 1, 0)
        pl.semaphore_wait(barrier, KERNEL_BITS + 1 + sent)
        grad_copy.start()
        for load in loads:
            load.start()
        for index in range(extras):
            extra_sums.sends[0][index] = to_low(extra_ref[index, :, :half])
            extra_sums.start(0, index, ((True, ORDERS[index]),))
            extra_sums.keep[index] = extra_ref[index, :, half:]
        vector_away[0] = vector_ref[...]
        vector_copy(0).start()
        for kind, places in enumerate(((0, 1, 2, 3), (0, 2, 1, 3))):
            for place, source in enumerate(places):
                now = slice(place * quarter, (place + 1) * quarter)
                low = source * quarter
                windows[kind, 0, now] = turned_ref[half + low : half + low + quarter, :]
                windows[kind, 1, now] = turned_other_ref[low : low + quarter, :]
        input_grad[...] = jnp.zeros_like(input_grad)

    def one_step(step, _):
        @pl.when(step < first_sum)
        def _():
            slots = to_wide(lax.broadcasted_iota(jnp.int32, (BLOCK, 1), 0))

            def spread_group(group, _):
                for offset in range(GROUP):
                    index = (step * GROUP + group) * GROUP + offset
                    near = near_ref[pl.ds(index, 1), :]
                    for part in range(blocks + 1):
                        low = max(part - 1, 0) * BLOCK
                        high = min(part + 1, blocks) * BLOCK
                        select = to_low(
                            jnp.where(near[:, low:high] - float(part * BLOCK) == slots, 1.0, 0.0)
                        )
                        spread[index, part * BLOCK : (part + 1) * BLOCK] = to_low(
                            product(select, grad_ref[low:high, :], 1, 0)
                        )
                return 0

            lax.fori_loop(0, GROUP, spread_group, 0, unroll=True)

        @pl.when((step >= first_sum) & (step < first_input))
        def _():
            chunk = step - first_sum
            pl.when(chunk == 0)(grad_copy.wait)
            slots = to_wide(lax.broadcasted_iota(jnp.int32, (2 * BLOCK, 1), 0))
            for offset in range(GROUP):
                near = near_other_ref[pl.ds(chunk * GROUP + offset, 1), :]
                for block in range(blocks):
                    low = block * BLOCK
                    select = to_low(
                        jnp.where(near[:, low : low + BLOCK] - float(low) == slots, 1.0, 0.0)
                    )
                    gathered[offset, :, low : low + BLOCK] = to_low(
                        product(windows[chunk % 2, 1, :, low : low + 2 * BLOCK], select, 1, 0)
                    )
            for offset in range(GROUP):
                weight_grad = product(windows[chunk % 2, 0], spread[chunk * GROUP + offset], 1, 0)
                weight_grad += product(gathered[offset], grad_other[...], 1, 0)
                sums.sends[0][chunk, offset] = to_low(weight_grad[: half // 2])
                sums.keep[chunk, offset] = weight_grad[half // 2 :]
            sums.start(0, chunk, kinds(chunk))

        @pl.when(step == first_input)
        def _():
            for load in loads:
                load.wait()

        beside = pl.ds(pl.multiple_of((1 - side) * (local + HALO), HALO), local + HALO)
        apart = pl.ds(pl.multiple_of(side * (2 * local + HALO), HALO), HALO)
        for phase, parts in enumerate(((beside, apart), (mine,))):
            start = first_input + phase * input_steps

            @pl.when((step >= start) & (step < start + input_steps))
            def _(start=start, parts=parts):
                def input_group(group, _):
                    for part in parts:
                        total = input_grad[part, :]
                        for offset in range(GROUP):
                            index = group * GROUP + offset
                            total += product(
                                spread[(step - start) * WIDE_GROUP + index, part, :],
                                weight_ref[(step - start) * WIDE_GROUP + index],
                                1,
                                1,
                            )
                        input_grad[part, :] = total
                    return 0

                lax.fori_loop(0, GROUP, input_group, 0, unroll=True)

        @pl.when(step == first_input + input_steps - 1)
        def _():
            input_copy.start()
            for index, (has, _, part) in enumerate(rims):
                rim_away[index] = to_low(input_grad[part, :])

                @pl.when(has)
                def _(index=index):
                    for core in range(2):

                        @pl.when(side == core)
                        def _(core=core):
                            rim_copies[index][core].start()

        @pl.when(step == steps - 1)
        def _():
            input_copy.wait()
            points_grad_ref[...] = first_grad_ref[...] + input_grad[mine, :] + input_arrived[...]

            @pl.when(has_rim)
            def _():
                edge = pl.ds(pl.multiple_of(side * (local - HALO), HALO), HALO)
                for core in range(2):
                    rim_copies[0][core].wait_recv()
                    points_grad_ref[edge, :] += to_wide(rim_arrived[core])

            for index, (has, _, part) in enumerate(rims):
                pl.when(has)(rim_copies[index][0].wait_send)

        for stage, due in enumerate(VECTOR_STEPS):

            @pl.when(step == due)
            def _(stage=stage):
                vector_copy(stage).wait()
                summed = vector_away[stage] + vector_arrived[stage]
                if stage < KERNEL_BITS:
                    vector_away[stage + 1] = summed
                    vector_copy(stage + 1).start()
                    return
                for index in range(8):
                    vector_refs[index][...] = summed[index : index + 1]
                for index in range(8, summed.shape[0]):
                    low = (index - 8) * channels
                    vector_refs[8][:, low : low + channels] = summed[index : index + 1]

        for stage in range(len(CONV_LAGS)):
            chunk = step - first_sum - CONV_LAGS[stage]

            @pl.when((chunk >= 0) & (chunk < chunks))
            def _(stage=stage, chunk=chunk):
                def finish(total):
                    conv_sum_ref[chunk] = total

                sums.advance(stage, chunk, kinds(chunk), finish)

        def finish_extra(index, total):
            if index == 0:
                heads_sum_ref[0:2] = total
            else:
                heads_sum_ref[2] = total[0]
                encode_sum_ref[...] = total[1]

        for stage, due in enumerate(EXTRA_STEPS):

            @pl.when(step == due)
            def _(stage=stage):
                for index in range(extras):
                    extra_sums.advance(
                        stage,
                        index,
                        ((True, ORDERS[index]),),
                        functools.partial(finish_extra, index),
                    )
        return 0

    begin()
    lax.fori_loop(0, steps, one_step, 0)


def conv_backward(
    near, near_other, turned, turned_other, grad, weight, extra, vector, first_grad
):
    offsets, channels, width = weight.shape
    wide = turned.shape[1]
    rows = grad.shape[0]
    local = first_grad.shape[0]
    chunks = offsets // GROUP
    low, full = jnp.bfloat16, jnp.float32
    kept = channels >> KERNEL_BITS
    shape = jax.ShapeDtypeStruct
    outs = [
        shape((chunks, GROUP, kept, width), full),
        shape((3, kept, width), full),
        shape((kept, width), full),
        shape(first_grad.shape, full),
        *[shape((1, channels), full)] * 8,
        shape((1, (vector.shape[0] - 8) * channels), full),
    ]

    anywhere = pl.BlockSpec(memory_space=pl.ANY)
    return pl.pallas_call(
        conv_backward_kernel,
        in_specs=[vmem()] * 5 + [anywhere, vmem(), vmem(), anywhere],
        out_specs=[vmem()] * len(outs),
        out_shape=outs,
        scratch_shapes=[
            pltpu.VMEM((offsets, wide, width), low),
            pltpu.VMEM((2, 2, channels // 2, wide), low),
            pltpu.VMEM((GROUP, channels // 2, rows), low),
            pltpu.VMEM((rows, width), low),
            pltpu.VMEM((wide, channels), full),
            pltpu.VMEM((local, channels), full),
            pltpu.VMEM((2, HALO, channels), low),
            pltpu.VMEM((2, HALO, channels), low),
            pltpu.VMEM((KERNEL_BITS + 1, *vector.shape), full),
            pltpu.VMEM((KERNEL_BITS + 1, *vector.shape), full),
            *copy_sems(7 + KERNEL_BITS),
            pltpu.VMEM(weight.shape, low),
            pltpu.VMEM(first_grad.shape, full),
            pltpu.SemaphoreType.DMA((2,)),
            *pair_scratch(chunks, GROUP, channels // 2, width, len(CONV_LAGS)),
            *pair_scratch(*extra.shape, KERNEL_BITS),
        ],
        compiler_params=pltpu.CompilerParams(
            vmem_limit_bytes=VMEM_BYTES, collective_id=1, has_side_effects=True
        ),
        cost_estimate=pl.CostEstimate(
            flops=80 * 10**9, bytes_accessed=16 * 10**6, transcendentals=0
        ),
    )(near, near_other, turned, turned_other, grad, weight, extra, vector, first_grad)


def hand_over_kernel(*refs):
    count = (len(refs) - 1) // 3
    sem = refs[-1]
    inward = [
        pltpu.make_async_copy(refs[i], refs[2 * count + i], sem.at[i]) for i in range(count)
    ]
    outward = [
        pltpu.make_async_copy(refs[2 * count + i], refs[count + i], sem.at[count + i])
        for i in range(count)
    ]
    for copy in inward:
        copy.start()
    for arrive, leave in zip(inward, outward):
        arrive.wait()
        leave.start()
    for copy in outward:
        copy.wait()


def hand_over(arrays):
    anywhere = pl.BlockSpec(memory_space=pl.ANY)
    return pl.pallas_call(
        hand_over_kernel,
        in_specs=[anywhere] * len(arrays),
        out_specs=[anywhere] * len(arrays),
        out_shape=[jax.ShapeDtypeStruct(each.shape, each.dtype) for each in arrays],
        scratch_shapes=[pltpu.VMEM(each.shape, each.dtype) for each in arrays]
        + [pltpu.SemaphoreType.DMA((2 * len(arrays),))],
        compiler_params=pltpu.CompilerParams(vmem_limit_bytes=VMEM_BYTES),
    )(*arrays)


def exchange(values, bit):
    count = lax.axis_size("pts")
    return lax.ppermute(values, "pts", [(i, i ^ (1 << bit)) for i in range(count)])


def sum_rest(keep, axis):
    for bit in range(KERNEL_BITS, patch_bits()):
        half = keep.shape[axis] // 2
        away = lax.slice_in_dim(keep, 0, half, axis=axis)
        keep = lax.slice_in_dim(keep, half, 2 * half, axis=axis)
        keep = keep + to_wide(exchange(to_low(away), bit))
    return keep


def per_device(
    points,
    neighbours,
    valid_count,
    conv_weight,
    encode_weight,
    encode_gain,
    encode_shift,
    attend_gain,
    attend_shift,
    heads_weight,
    output_weight,
    output_bias,
    feed_gain,
    feed_shift,
    expand_weight,
    expand_bias,
    reduce_weight,
    reduce_bias,
    cotangent,
):
    local, channels = points.shape
    rows = 2 * local
    is_first = lax.axis_index("tp") == 0
    norms = [v[None, :] for v in (encode_gain, encode_shift, attend_gain, attend_shift)]
    place = jnp.arange(rows, dtype=jnp.int32)
    place = jnp.where(is_first, place, (place + local) % rows)
    mask = jnp.where(place < valid_count[0], 0.0, MASKED)
    mask = to_low(jnp.where(jnp.arange(HEAD_DIM)[:, None] == 0, mask[None, :], 0.0))
    (
        mixed, logs, turned, near_columns, conved, linear, first, attend_in, projected,
        output_other, expand_other, reduce_other, bias_other,
    ) = forward_start(
        neighbours.T, points, conv_weight, encode_weight, norms, heads_weight, output_weight,
        expand_weight, reduce_weight, expand_bias[None, :], mask
    )
    (
        first_grad, conved_grad, extra, vector, reduce_sum, expand_sum, output_sum, result,
        turned_other, near_other,
    ) = middle(
        [
            mixed, first, output_weight, output_other, output_bias[None, :], feed_gain[None, :],
            feed_shift[None, :], cotangent, expand_bias[None, :], bias_other,
            reduce_bias[None, :], mask, logs, norms[2], norms[0],
        ],
        [
            expand_weight, expand_other, reduce_weight, reduce_other, projected, heads_weight,
            attend_in, linear, encode_weight, conved, turned, near_columns,
        ],
    )
    conv_sum, heads_sum, encode_sum, points_gradient, *vectors = conv_backward(
        near_columns, near_other, turned, turned_other, conved_grad, conv_weight, extra, vector,
        first_grad
    )
    for bit in range(KERNEL_BITS, patch_bits()):
        vectors = [each + exchange(each, bit) for each in vectors]
    parts = hand_over(
        [
            result,
            points_gradient,
            sum_rest(conv_sum, 2),
            sum_rest(encode_sum, 0),
            sum_rest(heads_sum, 1),
            sum_rest(output_sum, 0),
            sum_rest(expand_sum, 0),
            sum_rest(reduce_sum, 0),
            *vectors,
        ]
    )
    vectors = [each.reshape(-1) for each in parts[8:]]
    return (
        parts[0],
        parts[1],
        parts[2].reshape(-1, *parts[2].shape[2:]),
        parts[3].T,
        vectors[6],
        vectors[7],
        vectors[4],
        vectors[5],
        parts[4],
        parts[5].T,
        vectors[0],
        vectors[1],
        vectors[2],
        parts[6],
        vectors[8],
        parts[7].T,
        vectors[3],
    )


def solution(mesh):
    placed = (
        P(("pts", "tp"), None),
        P("pts", None),
        P("pts"),
        P(None, None, "tp"),
        P("tp", None),
        P(),
        P(),
        P(),
        P(),
        P(None, None, "tp"),
        P("tp", None),
        P(),
        P(),
        P(),
        P(None, "tp"),
        P("tp"),
        P("tp", None),
        P(),
        P(("pts", "tp"), None),
    )
    return jax.shard_map(
        per_device,
        mesh=mesh,
        in_specs=placed,
        out_specs=(
            P(("pts", "tp"), None),
            P(("pts", "tp"), None),
            P(None, "pts", "tp"),
            P("tp", "pts"),
            P(),
            P(),
            P(),
            P(),
            P(None, "pts", "tp"),
            P("tp", "pts"),
            P(),
            P(),
            P(),
            P("pts", "tp"),
            P(),
            P("tp", "pts"),
            P(),
        ),
        check_vma=False,
    )
```

```python
import functools

import jax
import jax.numpy as jnp
from jax import lax
from jax.experimental import pallas as pl
from jax.experimental.pallas import tpu as pltpu
from jax.sharding import PartitionSpec as P

MESH = pl.DeviceIdType.MESH
HEAD_DIM = 16
HALO = 128
BLOCK = 256
GROUP = 3
EPSILON = 1e-05
MASKED = -1e30
KERNEL_BITS = 4
ORDERS = ((0, 1, 2, 3), (1, 0, 2, 3))
VMEM_BYTES = 60 << 20
CHUNK = 512
BACK_CHUNK = 256
HEADS_STEP = 8
HEADS_BACK_STEP = 2
SUM_STEPS = (3, 5, 7)
SHARE_BIT = 2
CONV_ORDERS = ((0, 1, 3), (1, 0, 3))
WINDOW_ORDER = (2, 0, 1, 3)
CONV_LAGS = (2, 4, 6)
EXTRA_STEPS = (2, 3, 5, 7)
VECTOR_STEPS = (1, 2, 3, 4, 5)
WEIGHTS_AHEAD = 3
WIDE_GROUP = 9


def to_low(values):
    return values.astype(jnp.bfloat16)


def to_wide(values):
    return values.astype(jnp.float32)


def product(left, right, left_dim, right_dim):
    dims = (((left_dim,), (right_dim,)), ((), ()))
    return lax.dot_general(left, right, dims, preferred_element_type=jnp.float32)


def layer_norm(values):
    row_mean = jnp.mean(values, axis=-1, keepdims=True)
    centred = values - row_mean
    inverse = lax.rsqrt(jnp.mean(centred * centred, axis=-1, keepdims=True) + EPSILON)
    return centred * inverse, inverse


def norm_back(upstream, normal_part, inverse, norm_gain):
    scaled = upstream * norm_gain
    across = (
        scaled
        - jnp.mean(scaled, axis=-1, keepdims=True)
        - normal_part * jnp.mean(scaled * normal_part, axis=-1, keepdims=True)
    )
    return across * inverse


def column_sum(values):
    return jnp.sum(values, axis=0, keepdims=True)


def nested_picks(channels, order):
    me = lax.axis_index("pts")
    order = order + tuple(range(KERNEL_BITS, patch_bits()))
    depth = channels >> len(order)
    lanes = 128
    place = lax.broadcasted_iota(jnp.int32, (channels, lanes), 0)
    picked = place & (depth - 1)
    for stage, bit in enumerate(order):
        kept = (place >> (channels.bit_length() - 2 - stage)) & 1
        picked = picked + (1 - ((kept + me // (1 << bit)) & 1)) * (depth << bit)
    column = lax.broadcasted_iota(jnp.int32, (channels, lanes), 1)
    return to_low(
        jnp.concatenate(
            [
                jnp.where(picked == column + low, 1.0, 0.0)
                for low in range(0, channels, lanes)
            ],
            axis=1,
        )
    )


class Copies:
    def __init__(self, send_sem, arrive_sem):
        self.send_sem, self.arrive_sem = send_sem, arrive_sem

    def to(self, device, source, target, send, arrive=None):
        return pltpu.make_async_remote_copy(
            src_ref=source,
            dst_ref=target,
            send_sem=self.send_sem.at[send],
            recv_sem=self.arrive_sem.at[send if arrive is None else arrive],
            device_id=device,
            device_id_type=MESH,
        )


def copy_sems(count):
    return [pltpu.SemaphoreType.DMA((count,))] * 2


def patch_bits():
    return lax.axis_size("pts").bit_length() - 1


def sibling():
    return {"tp": 1 - lax.axis_index("tp")}


def greet_sibling():
    barrier = pltpu.get_barrier_semaphore()
    pl.semaphore_signal(barrier, inc=1, device_id=sibling(), device_id_type=MESH)
    pl.semaphore_wait(barrier, 1)


def vmem():
    return pl.BlockSpec(memory_space=pltpu.VMEM)


def whole(array):
    zeros = (0,) * array.ndim
    return pl.BlockSpec(array.shape, lambda i: zeros, pipeline_mode=pl.Buffered(1))


def staged(units, begin, finish):
    ready = begin(units[0])
    for index, unit in enumerate(units):
        later = begin(units[index + 1]) if index + 1 < len(units) else None
        finish(unit, ready)
        ready = later


def forward_kernel(
    near_ref,
    points_ref,
    encode_gain_ref,
    encode_shift_ref,
    attend_gain_ref,
    attend_shift_ref,
    valid_ref,
    weight_hbm,
    encode_hbm,
    heads_hbm,
    output_hbm,
    expand_hbm,
    reduce_hbm,
    bias_hbm,
    mixed_ref,
    log_ref,
    mask_ref,
    turned_hbm,
    near_hbm,
    conved_hbm,
    linear_hbm,
    first_hbm,
    attend_hbm,
    projected_hbm,
    output_other,
    expand_other,
    reduce_other,
    bias_other,
    turned_ref,
    near_columns_ref,
    conved_ref,
    linear_ref,
    first_ref,
    attend_ref,
    projected_ref,
    window,
    total,
    rows,
    weight_own,
    weight_other,
    encode_ref,
    encode_other,
    conved_away,
    conved_other,
    attend_other,
    heads_ref,
    heads_turned,
    near_wide,
    near_tall,
    picks,
    load_sem,
    store_sem,
    send_sem,
    arrive_sem,
):
    local, channels = points_ref.shape
    offsets, _, width = weight_own.shape
    groups = offsets // GROUP
    points = 2 * local
    patches = lax.axis_size("pts")
    me, side = lax.axis_index("pts"), lax.axis_index("tp")
    copies = Copies(send_sem, arrive_sem)
    own_place = pl.ds(pl.multiple_of(HALO + side * local, HALO), local)
    other_place = pl.ds(pl.multiple_of(HALO + (1 - side) * local, HALO), local)
    low_rim, high_rim = slice(0, HALO), slice(HALO + points, 2 * HALO + points)
    points_copy = copies.to(sibling(), points_ref, window.at[own_place], 0)
    low_copies = [
        copies.to(
            {"pts": me + 1, "tp": core},
            points_ref.at[local - HALO :],
            window.at[low_rim],
            3 + core,
            1,
        )
        for core in range(2)
    ]
    high_copies = [
        copies.to(
            {"pts": me - 1, "tp": core}, points_ref.at[0:HALO], window.at[high_rim], 3 + core, 2
        )
        for core in range(2)
    ]
    small_copies = [
        copies.to(sibling(), encode_hbm, encode_other, 5),
        copies.to(sibling(), output_hbm, output_other, 6),
        copies.to(sibling(), expand_hbm, expand_other, 7),
        copies.to(sibling(), reduce_hbm, reduce_other, 8),
        copies.to(sibling(), bias_hbm, bias_other, 9),
    ]
    small_loads = [
        pltpu.make_async_copy(encode_hbm, encode_ref, load_sem.at[groups]),
        pltpu.make_async_copy(heads_hbm, heads_ref, load_sem.at[groups + 1]),
    ]
    stores = [
        pltpu.make_async_copy(source, target, store_sem.at[index])
        for index, (source, target) in enumerate(
            (
                (turned_ref, turned_hbm),
                (near_columns_ref, near_hbm),
                (conved_ref, conved_hbm),
                (linear_ref, linear_hbm),
                (first_ref, first_hbm),
                (attend_ref, attend_hbm),
                (projected_ref, projected_hbm),
            )
        )
    ]
    up = (side == 1) & (me < patches - 1)
    down = (side == 0) & (me > 0)

    def weight_copy(group):
        part = pl.ds(group * GROUP, GROUP)
        return copies.to(sibling(), weight_hbm.at[part], weight_other.at[part], 12 + group)

    def weight_load(group):
        part = pl.ds(group * GROUP, GROUP)
        return pltpu.make_async_copy(
            weight_hbm.at[part], weight_own.at[part], load_sem.at[group]
        )

    def turn(place):
        return to_low(product(picks[...], window[place, :], 1, 1))

    for group in range(WEIGHTS_AHEAD):
        weight_load(group).start()
    for load in small_loads:
        load.start()
    barrier = pltpu.get_barrier_semaphore()
    pl.semaphore_signal(barrier, inc=1, device_id=sibling(), device_id_type=MESH)

    @pl.when(me > 0)
    def _():
        pl.semaphore_signal(
            barrier, inc=1, device_id={"pts": me - 1, "tp": 1}, device_id_type=MESH
        )

    @pl.when(me < patches - 1)
    def _():
        pl.semaphore_signal(
            barrier, inc=1, device_id={"pts": me + 1, "tp": 0}, device_id_type=MESH
        )

    pl.semaphore_wait(barrier, jnp.where(up | down, 3, 1))
    points_copy.start()

    @pl.when(up)
    def _():
        for copy in low_copies:
            copy.start()

    @pl.when(down)
    def _():
        for copy in high_copies:
            copy.start()

    for group in range(WEIGHTS_AHEAD):
        weight_copy(group).start()
    window[own_place, :] = points_ref[...]

    @pl.when(me == 0)
    def _():
        window[low_rim, :] = jnp.zeros((HALO, channels), jnp.bfloat16)

    @pl.when(me == patches - 1)
    def _():
        window[high_rim, :] = jnp.zeros((HALO, channels), jnp.bfloat16)

    near_tall[...] = jnp.zeros_like(near_tall)
    near_tall[: near_ref.shape[0]] = to_wide(near_ref[...])
    near_columns_ref[...] = near_tall[: near_columns_ref.shape[0]]
    near_wide[...] = near_tall[...].T
    picks[...] = nested_picks(channels, WINDOW_ORDER)
    turned_ref[:, own_place] = turn(own_place)
    stores[1].start()
    points_copy.wait()

    lane = lax.broadcasted_iota(jnp.int32, (BLOCK, near_wide.shape[1]), 1)
    slots = to_wide(lax.broadcasted_iota(jnp.int32, (BLOCK, 2 * BLOCK), 1))
    places = [pl.ds(pl.multiple_of(block * BLOCK, BLOCK), BLOCK) for block in (1 - side, side)]

    def gather(index, group):
        low = pl.multiple_of(side * local + (1 - side, side)[index] * BLOCK, BLOCK)
        part = window[pl.ds(low, 2 * BLOCK), :]
        near = near_wide[pl.ds(low, BLOCK), :] - low.astype(jnp.float32)
        for offset in range(GROUP):
            chosen = jnp.where(lane == group * GROUP + offset, near, 0.0)
            column = jnp.sum(chosen, axis=1, keepdims=True)
            select = to_low(jnp.where(column == slots, 1.0, 0.0))
            rows[places[index], offset * channels : (offset + 1) * channels] = to_low(
                product(select, part, 1, 0)
            )

    def apply(place, group):
        picked = rows[place, :]
        part = pl.ds(group * GROUP, GROUP)
        flat = (GROUP * channels, width)
        return (
            product(picked, weight_own[part].reshape(flat), 1, 0),
            product(picked, weight_other[part].reshape(flat), 1, 0),
        )

    def both_blocks(group):
        gather(0, group)
        gather(1, group)
        own, other = apply(slice(None), group)
        total[:, :width] += own
        total[:, width:] += other

    def next_weights(group):
        later = group + WEIGHTS_AHEAD

        @pl.when(later < groups)
        def _():
            weight_load(later).start()
            weight_copy(later).start()

        weight_load(group).wait()
        weight_copy(group).wait()

    next_weights(0)
    gather(0, 0)
    total[places[0], :width], total[places[0], width:] = apply(places[0], 0)
    next_weights(1)
    gather(0, 1)
    own, other = apply(places[0], 1)
    total[places[0], :width] += own
    total[places[0], width:] += other

    @pl.when(me > 0)
    def _():
        low_copies[0].wait_recv()

    @pl.when(me < patches - 1)
    def _():
        high_copies[0].wait_recv()

    gather(1, 0)
    total[places[1], :width], total[places[1], width:] = apply(places[1], 0)
    gather(1, 1)
    own, other = apply(places[1], 1)
    total[places[1], :width] += own
    total[places[1], width:] += other

    @pl.when(up)
    def _():
        for copy in low_copies:
            copy.wait_send()

    @pl.when(down)
    def _():
        for copy in high_copies:
            copy.wait_send()

    for copy in small_copies:
        copy.start()
    for load in small_loads:
        load.wait()
    for place in (other_place, low_rim, high_rim):
        turned_ref[:, place] = turn(place)
    stores[0].start()
    for index in range(3):
        heads_turned[index] = heads_ref[index].T

    def group_step(group, _):
        next_weights(group)
        both_blocks(group)
        return 0

    lax.fori_loop(2, groups, group_step, 0)

    mine = pl.ds(pl.multiple_of(side * local, local), local)
    theirs = pl.ds(pl.multiple_of((1 - side) * local, local), local)
    conved_own = to_low(total[:, :width])
    conved_away[...] = to_low(total[:, width:])
    conved_ref[mine] = conved_own
    conved_copy = copies.to(sibling(), conved_away, conved_other, 10)
    conved_copy.start()
    small_copies[0].wait()
    linear = product(conved_own, encode_ref[...], 1, 0)
    linear += product(conved_away[...], encode_other[...], 1, 0)
    linear_ref[...] = linear
    first = layer_norm(linear)[0] * encode_gain_ref[...] + encode_shift_ref[...]
    first += to_wide(points_ref[...])
    first_ref[...] = first
    attend_out = layer_norm(first)[0] * attend_gain_ref[...] + attend_shift_ref[...]
    attend_ref[0] = to_low(attend_out)
    attend_copy = copies.to(sibling(), attend_ref.at[0], attend_other, 11)
    attend_copy.start()
    for index in range(3):
        projected_ref[index, :, :local] = to_low(
            product(heads_turned[index], attend_ref[0], 1, 1)
        )
    attend_copy.wait()
    attend_ref[1] = attend_other[...]
    for index in range(3):
        projected_ref[index, :, local:] = to_low(
            product(heads_turned[index], attend_other[...], 1, 1)
        )
    conved_copy.wait()
    conved_ref[theirs] = conved_other[...]
    for store in stores[2:]:
        store.start()

    row = lax.broadcasted_iota(jnp.int32, (HEAD_DIM, points), 0)
    ones = to_low(jnp.where(row == 0, 1.0, 0.0))
    place = (lax.broadcasted_iota(jnp.int32, (HEAD_DIM, points), 1) + side * local) & (points - 1)
    excluded = jnp.where(place < valid_ref[0], 0.0, MASKED)
    mask_ref[...] = to_low(jnp.where(row == 0, excluded, 0.0))

    def heads_step(step, _):
        operands, heads = [], []
        for offset in range(HEADS_STEP):
            head = step * HEADS_STEP + offset
            place = pl.ds(pl.multiple_of(head * HEAD_DIM, HEAD_DIM), HEAD_DIM)
            query, key, value = (projected_ref[index, place] for index in range(3))
            scaled = to_low(to_wide(query) * HEAD_DIM**-0.5)
            heads.append((head, place))
            operands.append(
                (
                    jnp.concatenate([scaled, ones], axis=0),
                    jnp.concatenate([key, mask_ref[...]], axis=0),
                    jnp.concatenate([value, ones], axis=0),
                )
            )

        def begin(unit):
            offset, start = unit
            queries, keys, _ = operands[offset]
            return product(keys, queries[:, start : start + CHUNK], 0, 0)

        def finish(unit, scores):
            offset, start = unit
            head, place = heads[offset]
            top = jnp.max(scores, axis=0, keepdims=True)
            mixed = product(operands[offset][2], to_low(jnp.exp(scores - top)), 1, 0)
            total = mixed[HEAD_DIM : HEAD_DIM + 1, :]
            now = slice(start, start + CHUNK)
            mixed_ref[place, now] = to_low(mixed[:HEAD_DIM] / total)
            log_ref[head, :, now] = top + jnp.log(total)

        units = [(h, c) for c in range(0, points, CHUNK) for h in range(HEADS_STEP)]
        staged(units, begin, finish)
        return 0

    lax.fori_loop(0, width // HEAD_DIM // HEADS_STEP, heads_step, 0)
    for copy in small_copies[1:]:
        copy.wait()
    for store in stores:
        store.wait()


def forward_start(
    near, points, conv_weight, encode_weight, norms, heads_weight, output_weight, expand_weight,
    reduce_weight, expand_bias, valid_count
):
    offsets, channels, width = conv_weight.shape
    local = points.shape[0]
    rows = 2 * local
    wide = rows + 2 * HALO
    groups = offsets // GROUP
    low, full = jnp.bfloat16, jnp.float32
    shape = jax.ShapeDtypeStruct
    anywhere = pl.BlockSpec(memory_space=pl.ANY)
    stored = [
        shape((channels, wide), low),
        shape((32, rows), full),
        shape((rows, width), low),
        shape((local, channels), full),
        shape((local, channels), full),
        shape((2, local, channels), low),
        shape((3, width, rows), low),
    ]
    away = [
        shape(array.shape, array.dtype)
        for array in (output_weight, expand_weight, reduce_weight, expand_bias)
    ]
    return pl.pallas_call(
        forward_kernel,
        in_specs=[vmem()] * 6 + [pl.BlockSpec(memory_space=pltpu.SMEM)] + [anywhere] * 7,
        out_specs=[vmem()] * 3 + [anywhere] * 11,
        out_shape=[
            shape((width, rows), low),
            shape((width // HEAD_DIM, 1, rows), full),
            shape((HEAD_DIM, rows), low),
        ]
        + stored
        + away,
        scratch_shapes=[
            *[pltpu.VMEM(each.shape, each.dtype) for each in stored],
            pltpu.VMEM((wide, channels), low),
            pltpu.VMEM((local, channels), full),
            pltpu.VMEM((local, GROUP * channels), low),
            pltpu.VMEM(conv_weight.shape, low),
            pltpu.VMEM(conv_weight.shape, low),
            pltpu.VMEM(encode_weight.shape, low),
            pltpu.VMEM(encode_weight.shape, low),
            pltpu.VMEM((local, width), low),
            pltpu.VMEM((local, width), low),
            pltpu.VMEM((local, channels), low),
            pltpu.VMEM(heads_weight.shape, low),
            pltpu.VMEM((3, width, channels), low),
            pltpu.VMEM((rows, 128), full),
            pltpu.VMEM((128, rows), full),
            pltpu.VMEM((channels, channels), low),
            pltpu.SemaphoreType.DMA((groups + 2,)),
            pltpu.SemaphoreType.DMA((len(stored),)),
            *copy_sems(12 + groups),
        ],
        compiler_params=pltpu.CompilerParams(
            vmem_limit_bytes=VMEM_BYTES, collective_id=2, has_side_effects=True
        ),
        cost_estimate=pl.CostEstimate(
            flops=60 * 10**9, bytes_accessed=20 * 10**6, transcendentals=0
        ),
    )(
        near, points, *norms, valid_count, conv_weight, encode_weight, heads_weight, output_weight,
        expand_weight, reduce_weight, expand_bias
    )


def partner_of(bit):
    me = lax.axis_index("pts")
    return me + (1 - 2 * ((me // (1 << bit)) % 2)) * (1 << bit)


def greet_partners():
    barrier = pltpu.get_barrier_semaphore()
    for bit in range(KERNEL_BITS):
        pl.semaphore_signal(
            barrier, inc=1, device_id={"pts": partner_of(bit)}, device_id_type=MESH
        )
    return barrier


class PairSums:
    def __init__(self, keep, sends, arrivals, send_sem, arrive_sem):
        self.keep, self.sends, self.arrivals = keep, sends, arrivals
        self.send_sem, self.arrive_sem = send_sem, arrive_sem

    def copy(self, stage, chunk, bit):
        return pltpu.make_async_remote_copy(
            src_ref=self.sends[stage].at[chunk],
            dst_ref=self.arrivals[stage].at[chunk],
            send_sem=self.send_sem.at[stage, chunk],
            recv_sem=self.arrive_sem.at[stage, chunk],
            device_id={"pts": partner_of(bit)},
            device_id_type=MESH,
        )

    def start(self, stage, chunk, kinds):
        for holds, order in kinds:
            if holds is True:
                self.copy(stage, chunk, order[stage]).start()
            else:

                @pl.when(holds)
                def _(order=order):
                    self.copy(stage, chunk, order[stage]).start()

    def advance(self, stage, chunk, kinds, finish):
        self.copy(stage, chunk, 0).wait()
        rows = self.keep.shape[2]
        low = rows - (rows >> stage)
        half = (rows - low) // 2
        arrived = self.arrivals[stage]
        if stage == len(self.sends) - 1:
            finish(self.keep[chunk, :, low:] + to_wide(arrived[chunk]))
            return
        self.sends[stage + 1][chunk] = to_low(
            self.keep[chunk, :, low : low + half] + to_wide(arrived[chunk, :, :half])
        )
        self.start(stage + 1, chunk, kinds)
        self.keep[chunk, :, low + half :] += to_wide(arrived[chunk, :, half:])


def pair_scratch(chunks, lead, rows, width, stages):
    halves = [(chunks, lead, rows >> (stage + 1), width) for stage in range(stages)]
    return (
        [pltpu.VMEM(halves[0], jnp.float32)]
        + [pltpu.VMEM(shape, jnp.bfloat16) for shape in halves]
        + [pltpu.VMEM(shape, jnp.bfloat16) for shape in halves]
        + [pltpu.SemaphoreType.DMA((stages, chunks))] * 2
    )


def pair_sums(scratch):
    stages = (len(scratch) - 3) // 2
    keep, rest = scratch[0], scratch[1:]
    return PairSums(keep, rest[:stages], rest[stages : 2 * stages], *rest[-2:])


def middle_kernel(
    mixed_ref,
    first_ref,
    output_ref,
    output_other_ref,
    output_bias_ref,
    gain_ref,
    shift_ref,
    cotangent_ref,
    bias_ref,
    bias_other_ref,
    reduce_bias_ref,
    mask_ref,
    log_ref,
    attend_gain_ref,
    encode_gain_ref,
    expand_hbm,
    expand_other_hbm,
    reduce_hbm,
    reduce_other_hbm,
    projected_hbm,
    heads_hbm,
    attend_hbm,
    linear_hbm,
    encode_hbm,
    conved_hbm,
    turned_hbm,
    near_hbm,
    first_grad_ref,
    conved_grad_ref,
    extra_ref,
    vectors_ref,
    reduce_sum_ref,
    expand_sum_ref,
    output_sum_ref,
    result_hbm,
    turned_other,
    near_other,
    expand_ref,
    expand_other_ref,
    reduce_ref,
    reduce_other_ref,
    projected_ref,
    heads_ref,
    attend_ref,
    linear_ref,
    encode_ref,
    conved_ref,
    result_ref,
    second_grad_ref,
    mixed_grad_ref,
    grad_ref,
    mixed_other,
    second_own,
    second_other,
    picks,
    top,
    away,
    arrived,
    attend_away,
    attend_arrived,
    linear_own,
    linear_other,
    load_sem,
    send_sem,
    arrive_sem,
    *scratch,
):
    local, channels = first_ref.shape
    width, points = mixed_ref.shape
    hidden_width = bias_ref.shape[1]
    columns = hidden_width // 2
    heads = width // HEAD_DIM
    half = channels // 2
    side = lax.axis_index("tp")
    mine = pl.ds(pl.multiple_of(side * local, local), local)
    theirs = pl.ds(pl.multiple_of((1 - side) * local, local), local)
    sums = pair_sums(scratch)
    copies = Copies(send_sem, arrive_sem)
    partner = {"pts": partner_of(SHARE_BIT)}
    share_copies = [
        copies.to(partner, turned_hbm.at[:half], turned_other, 0),
        copies.to(partner, near_hbm, near_other, 1),
    ]
    loads = [
        pltpu.make_async_copy(source, target, load_sem.at[index])
        for index, (source, target) in enumerate(
            (
                (expand_other_hbm, expand_other_ref),
                (reduce_other_hbm, reduce_other_ref),
                (expand_hbm, expand_ref),
                (reduce_hbm, reduce_ref),
                (projected_hbm, projected_ref),
                (heads_hbm, heads_ref),
                (attend_hbm, attend_ref),
                (linear_hbm, linear_ref),
                (encode_hbm, encode_ref),
                (conved_hbm, conved_ref),
            )
        )
    ]
    result_copy = pltpu.make_async_copy(result_ref, result_hbm, load_sem.at[len(loads)])

    for load in loads:
        load.start()
    barrier = greet_partners()
    pl.semaphore_signal(barrier, inc=1, device_id=sibling(), device_id_type=MESH)
    pl.semaphore_wait(barrier, KERNEL_BITS + 1)
    mixed_copy = copies.to(sibling(), mixed_ref.at[:, local:], mixed_other, 2)
    mixed_copy.start()
    for copy in share_copies:
        copy.start()

    cotangent = cotangent_ref[...]
    for kind in range(2):
        picks[kind] = nested_picks(channels, ORDERS[kind])
    cotangent_turned = to_low(product(picks[0], cotangent, 1, 1))
    second = first_ref[...] + output_bias_ref[...]
    second += product(mixed_ref[:, :local], output_ref[...], 0, 0)
    mixed_copy.wait()
    second += product(mixed_other[...], output_other_ref[...], 0, 0)
    normal, inverse = layer_norm(second)
    feed_low = to_low(normal * gain_ref[...] + shift_ref[...])
    feed_turned = to_low(product(picks[1], feed_low, 1, 1))
    result = second + reduce_bias_ref[...]
    feed_grad = jnp.zeros_like(second)
    for load in loads[:4]:
        load.wait()
    weight_copies = []
    for index, (up_ref, up_bias_ref, down_ref) in enumerate(
        (
            (expand_other_ref, bias_other_ref, reduce_other_ref),
            (expand_ref, bias_ref, reduce_ref),
        )
    ):
        bias_grads = []
        for start in range(0, hidden_width, columns):
            now = slice(start, start + columns)
            hidden = product(feed_low, up_ref[:, now], 1, 0) + up_bias_ref[:, now]
            below = 0.5 + 0.5 * lax.erf(hidden * 0.5**0.5)
            slope = below + hidden * (jnp.exp(-0.5 * hidden * hidden) * (0.5 / jnp.pi) ** 0.5)
            active = to_low(hidden * below)
            hidden_grad = to_low(product(cotangent, down_ref[now, :], 1, 1) * slope)
            result += product(active, down_ref[now, :], 1, 0)
            feed_grad += product(hidden_grad, up_ref[:, now], 1, 1)
            bias_grads.append(column_sum(to_wide(hidden_grad)))
            weight_grads = (
                product(cotangent_turned, active, 1, 0),
                product(feed_turned, hidden_grad, 1, 0),
            )
            for kind, weight_grad in enumerate(weight_grads):
                if index == 0:
                    away[kind, :, now] = weight_grad
                    copy = copies.to(
                        sibling(),
                        away.at[kind, :, now],
                        arrived.at[kind, :, now],
                        4 + len(weight_copies),
                    )
                    copy.start()
                    weight_copies.append(copy)
                else:
                    top[kind, :, now] = weight_grad[:half]
                    sums.keep[kind, 0, :, now] = weight_grad[half:]
        owner = (1 - side) if index == 0 else side
        for part, grads in enumerate(bias_grads):
            vectors_ref[pl.ds(8 + 2 * owner + part, 1), :] = grads
    result_ref[...] = to_low(result)
    result_copy.start()
    upstream = to_wide(cotangent)
    second_grad = upstream + norm_back(feed_grad, normal, inverse, gain_ref[...])
    second_grad_ref[...] = second_grad
    second_own[...] = to_low(second_grad)
    second_copy = copies.to(sibling(), second_own, second_other, 3)
    second_copy.start()
    vectors_ref[0:1] = column_sum(second_grad)
    vectors_ref[1:2] = column_sum(feed_grad * normal)
    vectors_ref[2:3] = column_sum(feed_grad)
    vectors_ref[3:4] = column_sum(upstream)
    mixed_grad_ref[:, :local] = to_low(product(output_ref[...], second_own[...], 1, 1))
    part = width // 2
    output_grads = [
        product(
            to_low(product(picks[kind], second_own[...], 1, 1)),
            mixed_ref[kind * part : (kind + 1) * part, :local],
            1,
            1,
        )
        for kind in range(2)
    ]
    second_copy.wait()
    mixed_grad_ref[:, local:] = to_low(product(output_ref[...], second_other[...], 1, 1))
    for kind in range(2):
        output_grad = output_grads[kind] + product(
            to_low(product(picks[kind], second_other[...], 1, 1)),
            mixed_ref[kind * part : (kind + 1) * part, local:],
            1,
            1,
        )
        sums.sends[0][kind, 0, :, hidden_width:] = to_low(output_grad[:half])
        sums.keep[kind, 0, :, hidden_width:] = output_grad[half:]
    for copy in weight_copies:
        copy.wait()
    for kind in range(2):
        sums.sends[0][kind, 0, :, :hidden_width] = to_low(top[kind] + arrived[kind, :half])
        sums.start(0, kind, ((True, ORDERS[kind]),))
        sums.keep[kind, 0, :, :hidden_width] += arrived[kind, half:]

    scale = HEAD_DIM**-0.5
    row = lax.broadcasted_iota(jnp.int32, (HEAD_DIM, points), 0)
    ones = to_low(jnp.where((row > 0) & (row < 4), 1.0, 0.0))
    for load in loads[4:]:
        load.wait()

    def three_parts(values, lead):
        upper = to_wide(to_low(values))
        middle = to_wide(to_low(values - upper))
        lower = values - upper - middle
        tail = jnp.where(row == 1, -upper, jnp.where(row == 2, -middle, 0.0))
        tail = jnp.where(row == 3, -lower, tail)
        return to_low(jnp.where(row == 0, lead, tail))

    def finish_sum(index, total):
        if index == 0:
            reduce_sum_ref[...] = total[0, :, :hidden_width]
        else:
            expand_sum_ref[...] = total[0, :, :hidden_width]
        output_sum_ref[:, index * part : (index + 1) * part] = total[0, :, hidden_width:]

    def heads_step(step, _):
        for stage, due in enumerate(SUM_STEPS):

            @pl.when(step == due)
            def _(stage=stage):
                for index in range(2):
                    sums.advance(
                        stage, index, ((True, ORDERS[index]),), functools.partial(finish_sum, index)
                    )

        operands, places = [], []
        for offset in range(HEADS_BACK_STEP):
            head = step * HEADS_BACK_STEP + offset
            place = pl.ds(pl.multiple_of(head * HEAD_DIM, HEAD_DIM), HEAD_DIM)
            places.append(place)
            query, key, value = (projected_ref[index, place] for index in range(3))
            grad = mixed_grad_ref[place]
            row_dot = column_sum(to_wide(grad) * to_wide(mixed_ref[place]))
            scaled = to_low(to_wide(query) * scale)
            operands.append(
                (
                    jnp.concatenate([scaled, three_parts(log_ref[head], 1.0)], axis=0),
                    jnp.concatenate([key, mask_ref[...] + ones], axis=0),
                    jnp.concatenate([value, ones], axis=0),
                    jnp.concatenate([grad, three_parts(row_dot, 0.0)], axis=0),
                    query,
                    key,
                    grad,
                )
            )
        totals = [None] * HEADS_BACK_STEP

        def begin(unit):
            offset, start = unit
            queries, keys, values, grads = operands[offset][:4]
            return (
                product(keys, queries[:, start : start + BACK_CHUNK], 0, 0),
                product(values, grads[:, start : start + BACK_CHUNK], 0, 0),
            )

        def finish(unit, ready):
            offset, start = unit
            scores, prob_grad = ready
            query, key, grad = operands[offset][4:]
            now = slice(start, start + BACK_CHUNK)
            probs = jnp.exp(scores)
            score_grad = to_low(probs * prob_grad)
            grad_ref[0, places[offset], now] = to_low(product(key, score_grad, 1, 0) * scale)
            value_part = product(grad[:, now], to_low(probs), 1, 1)
            key_part = product(query[:, now], score_grad, 1, 1)
            if totals[offset] is not None:
                key_part, value_part = key_part + totals[offset][0], value_part + totals[offset][1]
            totals[offset] = (key_part, value_part)

        units = [(h, c) for c in range(0, points, BACK_CHUNK) for h in range(HEADS_BACK_STEP)]
        staged(units, begin, finish)
        for offset in range(HEADS_BACK_STEP):
            grad_ref[1, places[offset]] = to_low(totals[offset][0] * scale)
            grad_ref[2, places[offset]] = to_low(totals[offset][1])
        return 0

    lax.fori_loop(0, heads // HEADS_BACK_STEP, heads_step, 0)

    def attend_grad(start):
        return sum(
            product(grad_ref[index, :, start : start + local].T, heads_ref[index], 1, 1)
            for index in range(3)
        )

    attend_away[...] = attend_grad(local)
    attend_copy = copies.to(sibling(), attend_away, attend_arrived, 8)
    attend_copy.start()
    for stage in range(len(SUM_STEPS), KERNEL_BITS):
        for index in range(2):
            sums.advance(
                stage, index, ((True, ORDERS[index]),), functools.partial(finish_sum, index)
            )
    upstream = attend_grad(0)
    for kind in range(2):
        turned = [to_low(product(picks[kind], attend_ref[i], 1, 1)) for i in range(2)]
        for index in (0, 1) if kind == 0 else (2,):
            extra_ref[kind, index % 2] = product(
                turned[0], grad_ref[index, :, :local], 1, 1
            ) + product(turned[1], grad_ref[index, :, local:], 1, 1)
    normal, inverse = layer_norm(first_ref[...])
    attend_copy.wait()
    upstream += attend_arrived[...]
    first_grad = second_grad_ref[...] + norm_back(upstream, normal, inverse, attend_gain_ref[...])
    first_grad_ref[...] = first_grad
    vectors_ref[4:5] = column_sum(upstream * normal)
    vectors_ref[5:6] = column_sum(upstream)
    normal, inverse = layer_norm(linear_ref[...])
    linear_own[...] = to_low(norm_back(first_grad, normal, inverse, encode_gain_ref[...]))
    linear_copy = copies.to(sibling(), linear_own, linear_other, 9)
    linear_copy.start()
    vectors_ref[6:7] = column_sum(first_grad * normal)
    vectors_ref[7:8] = column_sum(first_grad)
    conved_grad_ref[mine] = to_low(product(linear_own[...], encode_ref[...], 1, 1))
    encode_grad = product(
        to_low(product(picks[1], linear_own[...], 1, 1)), conved_ref[mine], 1, 0
    )
    linear_copy.wait()
    conved_grad_ref[theirs] = to_low(product(linear_other[...], encode_ref[...], 1, 1))
    extra_ref[1, 1] = encode_grad + product(
        to_low(product(picks[1], linear_other[...], 1, 1)), conved_ref[theirs], 1, 0
    )
    result_copy.wait()
    for copy in share_copies:
        copy.wait()


def middle(near_operands, far_operands):
    local, channels = near_operands[1].shape
    width, rows = near_operands[0].shape
    hidden = near_operands[8].shape[1]
    turned, near = far_operands[-2:]
    kept = channels >> KERNEL_BITS
    low, full = jnp.bfloat16, jnp.float32
    shape = jax.ShapeDtypeStruct
    anywhere = pl.BlockSpec(memory_space=pl.ANY)
    loaded = far_operands[:-2]
    square = (local, channels)
    return pl.pallas_call(
        middle_kernel,
        in_specs=[vmem()] * len(near_operands) + [anywhere] * len(far_operands),
        out_specs=[vmem()] * 7 + [anywhere] * 3,
        out_shape=[
            shape(square, full),
            shape((rows, width), low),
            shape((2, 2, channels, width), full),
            shape((8 + 2 * hidden // channels, channels), full),
            shape((kept, hidden), full),
            shape((kept, hidden), full),
            shape((kept, width), full),
            shape(square, low),
            shape((channels // 2, turned.shape[1]), low),
            shape(near.shape, full),
        ],
        scratch_shapes=[
            *[pltpu.VMEM(each.shape, each.dtype) for each in loaded],
            pltpu.VMEM(square, low),
            pltpu.VMEM(square, full),
            pltpu.VMEM((width, rows), low),
            pltpu.VMEM((3, width, rows), low),
            pltpu.VMEM((width, local), low),
            pltpu.VMEM(square, low),
            pltpu.VMEM(square, low),
            pltpu.VMEM((2, channels, channels), low),
            pltpu.VMEM((2, channels // 2, hidden), full),
            pltpu.VMEM((2, channels, hidden), full),
            pltpu.VMEM((2, channels, hidden), full),
            pltpu.VMEM(square, full),
            pltpu.VMEM(square, full),
            pltpu.VMEM(square, low),
            pltpu.VMEM(square, low),
            pltpu.SemaphoreType.DMA((len(loaded) + 1,)),
            *copy_sems(10),
            *pair_scratch(2, 1, channels, hidden + width // 2, KERNEL_BITS),
        ],
        compiler_params=pltpu.CompilerParams(
            vmem_limit_bytes=VMEM_BYTES, collective_id=3, has_side_effects=True
        ),
        cost_estimate=pl.CostEstimate(
            flops=70 * 10**9, bytes_accessed=20 * 10**6, transcendentals=0
        ),
    )(*near_operands, *far_operands)


def conv_backward_kernel(
    near_ref,
    near_other_ref,
    turned_ref,
    turned_other_ref,
    grad_ref,
    weight_hbm,
    extra_ref,
    vector_ref,
    first_grad_hbm,
    conv_sum_ref,
    heads_sum_ref,
    encode_sum_ref,
    points_grad_ref,
    *refs,
):
    vector_refs, refs = refs[:9], refs[9:]
    (
        spread,
        windows,
        gathered,
        grad_other,
        input_grad,
        input_arrived,
        rim_away,
        rim_arrived,
        vector_away,
        vector_arrived,
        send_sem,
        arrive_sem,
        weight_ref,
        first_grad_ref,
        load_sem,
    ) = refs[:15]
    sums, extra_sums = pair_sums(refs[15:24]), pair_sums(refs[24:])
    rows, width = grad_ref.shape
    local, channels = first_grad_ref.shape
    half = channels // 2
    quarter = half // 4
    blocks = rows // BLOCK
    extras = extra_ref.shape[0]
    chunks = conv_sum_ref.shape[0]
    patches = lax.axis_size("pts")
    me, side = lax.axis_index("pts"), lax.axis_index("tp")
    copies = Copies(send_sem, arrive_sem)
    loads = [
        pltpu.make_async_copy(weight_hbm, weight_ref, load_sem.at[0]),
        pltpu.make_async_copy(first_grad_hbm, first_grad_ref, load_sem.at[1]),
    ]
    mine = pl.ds(pl.multiple_of(HALO + side * local, HALO), local)
    theirs = pl.ds(pl.multiple_of(HALO + (1 - side) * local, HALO), local)
    grad_copy = copies.to({"pts": partner_of(SHARE_BIT)}, grad_ref, grad_other, 0)
    input_copy = copies.to(sibling(), input_grad.at[theirs], input_arrived, 1)
    rims = (
        (me > 0, {"pts": me - 1, "tp": 1}, slice(0, HALO)),
        (me < patches - 1, {"pts": me + 1, "tp": 0}, slice(HALO + rows, rows + 2 * HALO)),
    )
    rim_copies = [
        [copies.to(rim[1], rim_away.at[i], rim_arrived.at[core], 2 + i, 4 + core) for core in (0, 1)]
        for i, rim in enumerate(rims)
    ]
    has_rim = ((side == 0) & (me > 0)) | ((side == 1) & (me < patches - 1))
    first_sum = chunks // GROUP
    first_input = first_sum + chunks
    input_steps = chunks // GROUP

    def vector_copy(stage):
        device = sibling() if stage == 0 else {"pts": partner_of(stage - 1)}
        return copies.to(device, vector_away.at[stage], vector_arrived.at[stage], 6 + stage)

    def kinds(chunk):
        return ((chunk % 2 == 0, CONV_ORDERS[0]), (chunk % 2 == 1, CONV_ORDERS[1]))

    steps = first_input + 2 * input_steps

    def begin():
        barrier = greet_partners()
        pl.semaphore_signal(barrier, inc=1, device_id=sibling(), device_id_type=MESH)
        for core in range(2):

            @pl.when((side == 0) & (me > 0))
            def _(core=core):
                device = {"pts": me - 1, "tp": core}
                pl.semaphore_signal(barrier, inc=1, device_id=device, device_id_type=MESH)

            @pl.when((side == 1) & (me < patches - 1))
            def _(core=core):
                device = {"pts": me + 1, "tp": core}
                pl.semaphore_signal(barrier, inc=1, device_id=device, device_id_type=MESH)

        sent = jnp.where(me > 0, 1, 0) + jnp.where(me < patches - 1, 1, 0)
        pl.semaphore_wait(barrier, KERNEL_BITS + 1 + sent)
        grad_copy.start()
        for load in loads:
            load.start()
        for index in range(extras):
            extra_sums.sends[0][index] = to_low(extra_ref[index, :, :half])
            extra_sums.start(0, index, ((True, ORDERS[index]),))
            extra_sums.keep[index] = extra_ref[index, :, half:]
        vector_away[0] = vector_ref[...]
        vector_copy(0).start()
        for kind, places in enumerate(((0, 1, 2, 3), (0, 2, 1, 3))):
            for place, source in enumerate(places):
                now = slice(place * quarter, (place + 1) * quarter)
                low = source * quarter
                windows[kind, 0, now] = turned_ref[half + low : half + low + quarter, :]
                windows[kind, 1, now] = turned_other_ref[low : low + quarter, :]
        input_grad[...] = jnp.zeros_like(input_grad)

    def one_step(step, _):
        @pl.when(step < first_sum)
        def _():
            slots = to_wide(lax.broadcasted_iota(jnp.int32, (BLOCK, 1), 0))

            def spread_group(group, _):
                for offset in range(GROUP):
                    index = (step * GROUP + group) * GROUP + offset
                    near = near_ref[pl.ds(index, 1), :]
                    for part in range(blocks + 1):
                        low = max(part - 1, 0) * BLOCK
                        high = min(part + 1, blocks) * BLOCK
                        select = to_low(
                            jnp.where(near[:, low:high] - float(part * BLOCK) == slots, 1.0, 0.0)
                        )
                        spread[index, part * BLOCK : (part + 1) * BLOCK] = to_low(
                            product(select, grad_ref[low:high, :], 1, 0)
                        )
                return 0

            lax.fori_loop(0, GROUP, spread_group, 0, unroll=True)

        @pl.when((step >= first_sum) & (step < first_input))
        def _():
            chunk = step - first_sum
            pl.when(chunk == 0)(grad_copy.wait)
            slots = to_wide(lax.broadcasted_iota(jnp.int32, (2 * BLOCK, 1), 0))
            for offset in range(GROUP):
                near = near_other_ref[pl.ds(chunk * GROUP + offset, 1), :]
                for block in range(blocks):
                    low = block * BLOCK
                    select = to_low(
                        jnp.where(near[:, low : low + BLOCK] - float(low) == slots, 1.0, 0.0)
                    )
                    gathered[offset, :, low : low + BLOCK] = to_low(
                        product(windows[chunk % 2, 1, :, low : low + 2 * BLOCK], select, 1, 0)
                    )
            for offset in range(GROUP):
                weight_grad = product(windows[chunk % 2, 0], spread[chunk * GROUP + offset], 1, 0)
                weight_grad += product(gathered[offset], grad_other[...], 1, 0)
                sums.sends[0][chunk, offset] = to_low(weight_grad[: half // 2])
                sums.keep[chunk, offset] = weight_grad[half // 2 :]
            sums.start(0, chunk, kinds(chunk))

        @pl.when(step == first_input)
        def _():
            for load in loads:
                load.wait()

        beside = pl.ds(pl.multiple_of((1 - side) * (local + HALO), HALO), local + HALO)
        apart = pl.ds(pl.multiple_of(side * (2 * local + HALO), HALO), HALO)
        for phase, parts in enumerate(((beside, apart), (mine,))):
            start = first_input + phase * input_steps

            @pl.when((step >= start) & (step < start + input_steps))
            def _(start=start, parts=parts):
                def input_group(group, _):
                    for part in parts:
                        total = input_grad[part, :]
                        for offset in range(GROUP):
                            index = group * GROUP + offset
                            total += product(
                                spread[(step - start) * WIDE_GROUP + index, part, :],
                                weight_ref[(step - start) * WIDE_GROUP + index],
                                1,
                                1,
                            )
                        input_grad[part, :] = total
                    return 0

                lax.fori_loop(0, GROUP, input_group, 0, unroll=True)

        @pl.when(step == first_input + input_steps - 1)
        def _():
            input_copy.start()
            for index, (has, _, part) in enumerate(rims):
                rim_away[index] = to_low(input_grad[part, :])

                @pl.when(has)
                def _(index=index):
                    for core in range(2):

                        @pl.when(side == core)
                        def _(core=core):
                            rim_copies[index][core].start()

        @pl.when(step == steps - 1)
        def _():
            input_copy.wait()
            points_grad_ref[...] = first_grad_ref[...] + input_grad[mine, :] + input_arrived[...]

            @pl.when(has_rim)
            def _():
                edge = pl.ds(pl.multiple_of(side * (local - HALO), HALO), HALO)
                for core in range(2):
                    rim_copies[0][core].wait_recv()
                    points_grad_ref[edge, :] += to_wide(rim_arrived[core])

            for index, (has, _, part) in enumerate(rims):
                pl.when(has)(rim_copies[index][0].wait_send)

        for stage, due in enumerate(VECTOR_STEPS):

            @pl.when(step == due)
            def _(stage=stage):
                vector_copy(stage).wait()
                summed = vector_away[stage] + vector_arrived[stage]
                if stage < KERNEL_BITS:
                    vector_away[stage + 1] = summed
                    vector_copy(stage + 1).start()
                    return
                for index in range(8):
                    vector_refs[index][...] = summed[index : index + 1]
                for index in range(8, summed.shape[0]):
                    low = (index - 8) * channels
                    vector_refs[8][:, low : low + channels] = summed[index : index + 1]

        for stage in range(len(CONV_LAGS)):
            chunk = step - first_sum - CONV_LAGS[stage]

            @pl.when((chunk >= 0) & (chunk < chunks))
            def _(stage=stage, chunk=chunk):
                def finish(total):
                    conv_sum_ref[chunk] = total

                sums.advance(stage, chunk, kinds(chunk), finish)

        def finish_extra(index, total):
            if index == 0:
                heads_sum_ref[0:2] = total
            else:
                heads_sum_ref[2] = total[0]
                encode_sum_ref[...] = total[1]

        for stage, due in enumerate(EXTRA_STEPS):

            @pl.when(step == due)
            def _(stage=stage):
                for index in range(extras):
                    extra_sums.advance(
                        stage,
                        index,
                        ((True, ORDERS[index]),),
                        functools.partial(finish_extra, index),
                    )
        return 0

    begin()
    lax.fori_loop(0, steps, one_step, 0)


def conv_backward(
    near, near_other, turned, turned_other, grad, weight, extra, vector, first_grad
):
    offsets, channels, width = weight.shape
    wide = turned.shape[1]
    rows = grad.shape[0]
    local = first_grad.shape[0]
    chunks = offsets // GROUP
    low, full = jnp.bfloat16, jnp.float32
    kept = channels >> KERNEL_BITS
    shape = jax.ShapeDtypeStruct
    outs = [
        shape((chunks, GROUP, kept, width), full),
        shape((3, kept, width), full),
        shape((kept, width), full),
        shape(first_grad.shape, full),
        *[shape((1, channels), full)] * 8,
        shape((1, (vector.shape[0] - 8) * channels), full),
    ]

    anywhere = pl.BlockSpec(memory_space=pl.ANY)
    return pl.pallas_call(
        conv_backward_kernel,
        in_specs=[vmem()] * 5 + [anywhere, vmem(), vmem(), anywhere],
        out_specs=[vmem()] * len(outs),
        out_shape=outs,
        scratch_shapes=[
            pltpu.VMEM((offsets, wide, width), low),
            pltpu.VMEM((2, 2, channels // 2, wide), low),
            pltpu.VMEM((GROUP, channels // 2, rows), low),
            pltpu.VMEM((rows, width), low),
            pltpu.VMEM((wide, channels), full),
            pltpu.VMEM((local, channels), full),
            pltpu.VMEM((2, HALO, channels), low),
            pltpu.VMEM((2, HALO, channels), low),
            pltpu.VMEM((KERNEL_BITS + 1, *vector.shape), full),
            pltpu.VMEM((KERNEL_BITS + 1, *vector.shape), full),
            *copy_sems(7 + KERNEL_BITS),
            pltpu.VMEM(weight.shape, low),
            pltpu.VMEM(first_grad.shape, full),
            pltpu.SemaphoreType.DMA((2,)),
            *pair_scratch(chunks, GROUP, channels // 2, width, len(CONV_LAGS)),
            *pair_scratch(*extra.shape, KERNEL_BITS),
        ],
        compiler_params=pltpu.CompilerParams(
            vmem_limit_bytes=VMEM_BYTES, collective_id=1, has_side_effects=True
        ),
        cost_estimate=pl.CostEstimate(
            flops=80 * 10**9, bytes_accessed=16 * 10**6, transcendentals=0
        ),
    )(near, near_other, turned, turned_other, grad, weight, extra, vector, first_grad)


def hand_over_kernel(*refs):
    count = (len(refs) - 1) // 3
    sem = refs[-1]
    inward = [
        pltpu.make_async_copy(refs[i], refs[2 * count + i], sem.at[i]) for i in range(count)
    ]
    outward = [
        pltpu.make_async_copy(refs[2 * count + i], refs[count + i], sem.at[count + i])
        for i in range(count)
    ]
    for copy in inward:
        copy.start()
    for arrive, leave in zip(inward, outward):
        arrive.wait()
        leave.start()
    for copy in outward:
        copy.wait()


def hand_over(arrays):
    anywhere = pl.BlockSpec(memory_space=pl.ANY)
    return pl.pallas_call(
        hand_over_kernel,
        in_specs=[anywhere] * len(arrays),
        out_specs=[anywhere] * len(arrays),
        out_shape=[jax.ShapeDtypeStruct(each.shape, each.dtype) for each in arrays],
        scratch_shapes=[pltpu.VMEM(each.shape, each.dtype) for each in arrays]
        + [pltpu.SemaphoreType.DMA((2 * len(arrays),))],
        compiler_params=pltpu.CompilerParams(vmem_limit_bytes=VMEM_BYTES),
    )(*arrays)


def exchange(values, bit):
    count = lax.axis_size("pts")
    return lax.ppermute(values, "pts", [(i, i ^ (1 << bit)) for i in range(count)])


def sum_rest(keep, axis):
    for bit in range(KERNEL_BITS, patch_bits()):
        half = keep.shape[axis] // 2
        away = lax.slice_in_dim(keep, 0, half, axis=axis)
        keep = lax.slice_in_dim(keep, half, 2 * half, axis=axis)
        keep = keep + to_wide(exchange(to_low(away), bit))
    return keep


def per_device(
    points,
    neighbours,
    valid_count,
    conv_weight,
    encode_weight,
    encode_gain,
    encode_shift,
    attend_gain,
    attend_shift,
    heads_weight,
    output_weight,
    output_bias,
    feed_gain,
    feed_shift,
    expand_weight,
    expand_bias,
    reduce_weight,
    reduce_bias,
    cotangent,
):
    local, channels = points.shape
    norms = [v[None, :] for v in (encode_gain, encode_shift, attend_gain, attend_shift)]
    (
        mixed, logs, mask, turned, near_columns, conved, linear, first, attend_in, projected,
        output_other, expand_other, reduce_other, bias_other,
    ) = forward_start(
        neighbours.T, points, conv_weight, encode_weight, norms, heads_weight, output_weight,
        expand_weight, reduce_weight, expand_bias[None, :], valid_count
    )
    (
        first_grad, conved_grad, extra, vector, reduce_sum, expand_sum, output_sum, result,
        turned_other, near_other,
    ) = middle(
        [
            mixed, first, output_weight, output_other, output_bias[None, :], feed_gain[None, :],
            feed_shift[None, :], cotangent, expand_bias[None, :], bias_other,
            reduce_bias[None, :], mask, logs, norms[2], norms[0],
        ],
        [
            expand_weight, expand_other, reduce_weight, reduce_other, projected, heads_weight,
            attend_in, linear, encode_weight, conved, turned, near_columns,
        ],
    )
    conv_sum, heads_sum, encode_sum, points_gradient, *vectors = conv_backward(
        near_columns, near_other, turned, turned_other, conved_grad, conv_weight, extra, vector,
        first_grad
    )
    for bit in range(KERNEL_BITS, patch_bits()):
        vectors = [each + exchange(each, bit) for each in vectors]
    parts = hand_over(
        [
            result,
            points_gradient,
            sum_rest(conv_sum, 2),
            sum_rest(encode_sum, 0),
            sum_rest(heads_sum, 1),
            sum_rest(output_sum, 0),
            sum_rest(expand_sum, 0),
            sum_rest(reduce_sum, 0),
            *vectors,
        ]
    )
    vectors = [each.reshape(-1) for each in parts[8:]]
    return (
        parts[0],
        parts[1],
        parts[2].reshape(-1, *parts[2].shape[2:]),
        parts[3].T,
        vectors[6],
        vectors[7],
        vectors[4],
        vectors[5],
        parts[4],
        parts[5].T,
        vectors[0],
        vectors[1],
        vectors[2],
        parts[6],
        vectors[8],
        parts[7].T,
        vectors[3],
    )


def solution(mesh):
    placed = (
        P(("pts", "tp"), None),
        P("pts", None),
        P("pts"),
        P(None, None, "tp"),
        P("tp", None),
        P(),
        P(),
        P(),
        P(),
        P(None, None, "tp"),
        P("tp", None),
        P(),
        P(),
        P(),
        P(None, "tp"),
        P("tp"),
        P("tp", None),
        P(),
        P(("pts", "tp"), None),
    )
    return jax.shard_map(
        per_device,
        mesh=mesh,
        in_specs=placed,
        out_specs=(
            P(("pts", "tp"), None),
            P(("pts", "tp"), None),
            P(None, "pts", "tp"),
            P("tp", "pts"),
            P(),
            P(),
            P(),
            P(),
            P(None, "pts", "tp"),
            P("tp", "pts"),
            P(),
            P(),
            P(),
            P("pts", "tp"),
            P(),
            P("tp", "pts"),
            P(),
        ),
        check_vma=False,
    )
```

```python
import functools

import jax
import jax.numpy as jnp
from jax import lax
from jax.experimental import pallas as pl
from jax.experimental.pallas import tpu as pltpu
from jax.sharding import PartitionSpec as P

MESH = pl.DeviceIdType.MESH
HEAD_DIM = 16
HALO = 128
BLOCK = 256
GROUP = 3
EPSILON = 1e-05
MASKED = -1e30
KERNEL_BITS = 4
ORDERS = ((0, 1, 2, 3), (1, 0, 2, 3))
VMEM_BYTES = 60 << 20
CHUNK = 512
BACK_CHUNK = 256
HEADS_STEP = 8
HEADS_BACK_STEP = 2
SUM_STEPS = (3, 5, 7)
SHARE_BIT = 2
CONV_ORDERS = ((0, 1, 3), (1, 0, 3))
WINDOW_ORDER = (2, 0, 1, 3)
CONV_LAGS = (2, 4, 6)
EXTRA_STEPS = (2, 3, 5, 7)
VECTOR_STEPS = (1, 2, 3, 4, 5)
WEIGHTS_AHEAD = 3
WIDE_GROUP = 9


def to_low(values):
    return values.astype(jnp.bfloat16)


def to_wide(values):
    return values.astype(jnp.float32)


def product(left, right, left_dim, right_dim):
    dims = (((left_dim,), (right_dim,)), ((), ()))
    return lax.dot_general(left, right, dims, preferred_element_type=jnp.float32)


def layer_norm(values):
    row_mean = jnp.mean(values, axis=-1, keepdims=True)
    centred = values - row_mean
    inverse = lax.rsqrt(jnp.mean(centred * centred, axis=-1, keepdims=True) + EPSILON)
    return centred * inverse, inverse


def norm_back(upstream, normal_part, inverse, norm_gain):
    scaled = upstream * norm_gain
    across = (
        scaled
        - jnp.mean(scaled, axis=-1, keepdims=True)
        - normal_part * jnp.mean(scaled * normal_part, axis=-1, keepdims=True)
    )
    return across * inverse


def column_sum(values):
    return jnp.sum(values, axis=0, keepdims=True)


def nested_picks(channels, order):
    me = lax.axis_index("pts")
    order = order + tuple(range(KERNEL_BITS, patch_bits()))
    depth = channels >> len(order)
    lanes = 128
    place = lax.broadcasted_iota(jnp.int32, (channels, lanes), 0)
    picked = place & (depth - 1)
    for stage, bit in enumerate(order):
        kept = (place >> (channels.bit_length() - 2 - stage)) & 1
        picked = picked + (1 - ((kept + me // (1 << bit)) & 1)) * (depth << bit)
    column = lax.broadcasted_iota(jnp.int32, (channels, lanes), 1)
    return to_low(
        jnp.concatenate(
            [
                jnp.where(picked == column + low, 1.0, 0.0)
                for low in range(0, channels, lanes)
            ],
            axis=1,
        )
    )


class Copies:
    def __init__(self, send_sem, arrive_sem):
        self.send_sem, self.arrive_sem = send_sem, arrive_sem

    def to(self, device, source, target, send, arrive=None):
        return pltpu.make_async_remote_copy(
            src_ref=source,
            dst_ref=target,
            send_sem=self.send_sem.at[send],
            recv_sem=self.arrive_sem.at[send if arrive is None else arrive],
            device_id=device,
            device_id_type=MESH,
        )


def copy_sems(count):
    return [pltpu.SemaphoreType.DMA((count,))] * 2


def patch_bits():
    return lax.axis_size("pts").bit_length() - 1


def sibling():
    return {"tp": 1 - lax.axis_index("tp")}


def greet_sibling():
    barrier = pltpu.get_barrier_semaphore()
    pl.semaphore_signal(barrier, inc=1, device_id=sibling(), device_id_type=MESH)
    pl.semaphore_wait(barrier, 1)


def vmem():
    return pl.BlockSpec(memory_space=pltpu.VMEM)


def whole(array):
    zeros = (0,) * array.ndim
    return pl.BlockSpec(array.shape, lambda i: zeros, pipeline_mode=pl.Buffered(1))


def staged(units, begin, finish):
    ready = begin(units[0])
    for index, unit in enumerate(units):
        later = begin(units[index + 1]) if index + 1 < len(units) else None
        finish(unit, ready)
        ready = later


def forward_kernel(
    near_ref,
    points_ref,
    encode_gain_ref,
    encode_shift_ref,
    attend_gain_ref,
    attend_shift_ref,
    valid_ref,
    weight_hbm,
    encode_hbm,
    heads_hbm,
    output_hbm,
    expand_hbm,
    reduce_hbm,
    bias_hbm,
    mixed_ref,
    log_ref,
    mask_ref,
    turned_hbm,
    near_hbm,
    conved_hbm,
    linear_hbm,
    first_hbm,
    attend_hbm,
    projected_hbm,
    output_other,
    expand_other,
    reduce_other,
    bias_other,
    turned_ref,
    near_columns_ref,
    conved_ref,
    linear_ref,
    first_ref,
    attend_ref,
    projected_ref,
    window,
    total,
    rows,
    weight_own,
    weight_other,
    encode_ref,
    encode_other,
    conved_away,
    conved_other,
    attend_other,
    heads_ref,
    heads_turned,
    near_wide,
    near_tall,
    picks,
    load_sem,
    store_sem,
    send_sem,
    arrive_sem,
):
    local, channels = points_ref.shape
    offsets, _, width = weight_own.shape
    groups = offsets // GROUP
    points = 2 * local
    patches = lax.axis_size("pts")
    me, side = lax.axis_index("pts"), lax.axis_index("tp")
    copies = Copies(send_sem, arrive_sem)
    own_place = pl.ds(pl.multiple_of(HALO + side * local, HALO), local)
    other_place = pl.ds(pl.multiple_of(HALO + (1 - side) * local, HALO), local)
    low_rim, high_rim = slice(0, HALO), slice(HALO + points, 2 * HALO + points)
    points_copy = copies.to(sibling(), points_ref, window.at[own_place], 0)
    low_copies = [
        copies.to(
            {"pts": me + 1, "tp": core},
            points_ref.at[local - HALO :],
            window.at[low_rim],
            3 + core,
            1,
        )
        for core in range(2)
    ]
    high_copies = [
        copies.to(
            {"pts": me - 1, "tp": core}, points_ref.at[0:HALO], window.at[high_rim], 3 + core, 2
        )
        for core in range(2)
    ]
    small_copies = [
        copies.to(sibling(), encode_hbm, encode_other, 5),
        copies.to(sibling(), output_hbm, output_other, 6),
        copies.to(sibling(), expand_hbm, expand_other, 7),
        copies.to(sibling(), reduce_hbm, reduce_other, 8),
        copies.to(sibling(), bias_hbm, bias_other, 9),
    ]
    small_loads = [
        pltpu.make_async_copy(encode_hbm, encode_ref, load_sem.at[groups]),
        pltpu.make_async_copy(heads_hbm, heads_ref, load_sem.at[groups + 1]),
    ]
    stores = [
        pltpu.make_async_copy(source, target, store_sem.at[index])
        for index, (source, target) in enumerate(
            (
                (turned_ref, turned_hbm),
                (near_columns_ref, near_hbm),
                (conved_ref, conved_hbm),
                (linear_ref, linear_hbm),
                (first_ref, first_hbm),
                (attend_ref, attend_hbm),
                (projected_ref, projected_hbm),
            )
        )
    ]
    up = (side == 1) & (me < patches - 1)
    down = (side == 0) & (me > 0)

    def weight_copy(group):
        part = pl.ds(group * GROUP, GROUP)
        return copies.to(sibling(), weight_hbm.at[part], weight_other.at[part], 12 + group)

    def weight_load(group):
        part = pl.ds(group * GROUP, GROUP)
        return pltpu.make_async_copy(
            weight_hbm.at[part], weight_own.at[part], load_sem.at[group]
        )

    def turn(place):
        return to_low(product(picks[...], window[place, :], 1, 1))

    for group in range(WEIGHTS_AHEAD):
        weight_load(group).start()
    for load in small_loads:
        load.start()
    barrier = pltpu.get_barrier_semaphore()
    pl.semaphore_signal(barrier, inc=1, device_id=sibling(), device_id_type=MESH)

    @pl.when(me > 0)
    def _():
        pl.semaphore_signal(
            barrier, inc=1, device_id={"pts": me - 1, "tp": 1}, device_id_type=MESH
        )

    @pl.when(me < patches - 1)
    def _():
        pl.semaphore_signal(
            barrier, inc=1, device_id={"pts": me + 1, "tp": 0}, device_id_type=MESH
        )

    pl.semaphore_wait(barrier, jnp.where(up | down, 3, 1))
    points_copy.start()

    @pl.when(up)
    def _():
        for copy in low_copies:
            copy.start()

    @pl.when(down)
    def _():
        for copy in high_copies:
            copy.start()

    for group in range(WEIGHTS_AHEAD):
        weight_copy(group).start()
    window[own_place, :] = points_ref[...]

    @pl.when(me == 0)
    def _():
        window[low_rim, :] = jnp.zeros((HALO, channels), jnp.bfloat16)

    @pl.when(me == patches - 1)
    def _():
        window[high_rim, :] = jnp.zeros((HALO, channels), jnp.bfloat16)

    near_tall[...] = jnp.zeros_like(near_tall)
    near_tall[: near_ref.shape[0]] = to_wide(near_ref[...])
    near_columns_ref[...] = near_tall[: near_columns_ref.shape[0]]
    near_wide[...] = near_tall[...].T
    picks[...] = nested_picks(channels, WINDOW_ORDER)
    turned_ref[:, own_place] = turn(own_place)
    stores[1].start()
    points_copy.wait()

    lane = lax.broadcasted_iota(jnp.int32, (BLOCK, near_wide.shape[1]), 1)
    slots = to_wide(lax.broadcasted_iota(jnp.int32, (BLOCK, 2 * BLOCK), 1))
    places = [pl.ds(pl.multiple_of(block * BLOCK, BLOCK), BLOCK) for block in (1 - side, side)]

    def gather(index, group):
        low = pl.multiple_of(side * local + (1 - side, side)[index] * BLOCK, BLOCK)
        part = window[pl.ds(low, 2 * BLOCK), :]
        near = near_wide[pl.ds(low, BLOCK), :] - low.astype(jnp.float32)
        for offset in range(GROUP):
            chosen = jnp.where(lane == group * GROUP + offset, near, 0.0)
            column = jnp.sum(chosen, axis=1, keepdims=True)
            select = to_low(jnp.where(column == slots, 1.0, 0.0))
            rows[places[index], offset * channels : (offset + 1) * channels] = to_low(
                product(select, part, 1, 0)
            )

    def apply(place, group):
        picked = rows[place, :]
        part = pl.ds(group * GROUP, GROUP)
        flat = (GROUP * channels, width)
        return (
            product(picked, weight_own[part].reshape(flat), 1, 0),
            product(picked, weight_other[part].reshape(flat), 1, 0),
        )

    def both_blocks(group):
        gather(0, group)
        gather(1, group)
        own, other = apply(slice(None), group)
        total[:, :width] += own
        total[:, width:] += other

    def next_weights(group):
        later = group + WEIGHTS_AHEAD

        @pl.when(later < groups)
        def _():
            weight_load(later).start()
            weight_copy(later).start()

        weight_load(group).wait()
        weight_copy(group).wait()

    next_weights(0)
    gather(0, 0)
    total[places[0], :width], total[places[0], width:] = apply(places[0], 0)
    next_weights(1)
    gather(0, 1)
    own, other = apply(places[0], 1)
    total[places[0], :width] += own
    total[places[0], width:] += other

    @pl.when(me > 0)
    def _():
        low_copies[0].wait_recv()

    @pl.when(me < patches - 1)
    def _():
        high_copies[0].wait_recv()

    gather(1, 0)
    total[places[1], :width], total[places[1], width:] = apply(places[1], 0)
    gather(1, 1)
    own, other = apply(places[1], 1)
    total[places[1], :width] += own
    total[places[1], width:] += other

    @pl.when(up)
    def _():
        for copy in low_copies:
            copy.wait_send()

    @pl.when(down)
    def _():
        for copy in high_copies:
            copy.wait_send()

    for copy in small_copies:
        copy.start()
    for load in small_loads:
        load.wait()
    for place in (other_place, low_rim, high_rim):
        turned_ref[:, place] = turn(place)
    stores[0].start()
    for index in range(3):
        heads_turned[index] = heads_ref[index].T

    def group_step(group, _):
        next_weights(group)
        both_blocks(group)
        return 0

    lax.fori_loop(2, groups, group_step, 0)

    mine = pl.ds(pl.multiple_of(side * local, local), local)
    theirs = pl.ds(pl.multiple_of((1 - side) * local, local), local)
    conved_own = to_low(total[:, :width])
    conved_away[...] = to_low(total[:, width:])
    conved_ref[mine] = conved_own
    conved_copy = copies.to(sibling(), conved_away, conved_other, 10)
    conved_copy.start()
    small_copies[0].wait()
    linear = product(conved_own, encode_ref[...], 1, 0)
    linear += product(conved_away[...], encode_other[...], 1, 0)
    linear_ref[...] = linear
    first = layer_norm(linear)[0] * encode_gain_ref[...] + encode_shift_ref[...]
    first += to_wide(points_ref[...])
    first_ref[...] = first
    attend_out = layer_norm(first)[0] * attend_gain_ref[...] + attend_shift_ref[...]
    attend_ref[0] = to_low(attend_out)
    attend_copy = copies.to(sibling(), attend_ref.at[0], attend_other, 11)
    attend_copy.start()
    for index in range(3):
        projected_ref[index, :, :local] = to_low(
            product(heads_turned[index], attend_ref[0], 1, 1)
        )
    attend_copy.wait()
    attend_ref[1] = attend_other[...]
    for index in range(3):
        projected_ref[index, :, local:] = to_low(
            product(heads_turned[index], attend_other[...], 1, 1)
        )
    conved_copy.wait()
    conved_ref[theirs] = conved_other[...]
    for store in stores[2:]:
        store.start()

    row = lax.broadcasted_iota(jnp.int32, (HEAD_DIM, points), 0)
    ones = to_low(jnp.where(row == 0, 1.0, 0.0))
    place = (lax.broadcasted_iota(jnp.int32, (HEAD_DIM, points), 1) + side * local) & (points - 1)
    excluded = jnp.where(place < valid_ref[0], 0.0, MASKED)
    mask_ref[...] = to_low(jnp.where(row == 0, excluded, 0.0))

    def heads_step(step, _):
        operands, heads = [], []
        for offset in range(HEADS_STEP):
            head = step * HEADS_STEP + offset
            place = pl.ds(pl.multiple_of(head * HEAD_DIM, HEAD_DIM), HEAD_DIM)
            query, key, value = (projected_ref[index, place] for index in range(3))
            scaled = to_low(to_wide(query) * HEAD_DIM**-0.5)
            heads.append((head, place))
            operands.append(
                (
                    jnp.concatenate([scaled, ones], axis=0),
                    jnp.concatenate([key, mask_ref[...]], axis=0),
                    jnp.concatenate([value, ones], axis=0),
                )
            )

        def begin(unit):
            offset, start = unit
            queries, keys, _ = operands[offset]
            return product(keys, queries[:, start : start + CHUNK], 0, 0)

        def finish(unit, scores):
            offset, start = unit
            head, place = heads[offset]
            top = jnp.max(scores, axis=0, keepdims=True)
            mixed = product(operands[offset][2], to_low(jnp.exp(scores - top)), 1, 0)
            total = mixed[HEAD_DIM : HEAD_DIM + 1, :]
            now = slice(start, start + CHUNK)
            mixed_ref[place, now] = to_low(mixed[:HEAD_DIM] / total)
            log_ref[head, :, now] = top + jnp.log(total)

        units = [(h, c) for c in range(0, points, CHUNK) for h in range(HEADS_STEP)]
        staged(units, begin, finish)
        return 0

    lax.fori_loop(0, width // HEAD_DIM // HEADS_STEP, heads_step, 0)
    for copy in small_copies[1:]:
        copy.wait()
    for store in stores:
        store.wait()


def forward_start(
    near, points, conv_weight, encode_weight, norms, heads_weight, output_weight, expand_weight,
    reduce_weight, expand_bias, valid_count
):
    offsets, channels, width = conv_weight.shape
    local = points.shape[0]
    rows = 2 * local
    wide = rows + 2 * HALO
    groups = offsets // GROUP
    low, full = jnp.bfloat16, jnp.float32
    shape = jax.ShapeDtypeStruct
    anywhere = pl.BlockSpec(memory_space=pl.ANY)
    stored = [
        shape((channels, wide), low),
        shape((32, rows), full),
        shape((rows, width), low),
        shape((local, channels), full),
        shape((local, channels), full),
        shape((2, local, channels), low),
        shape((3, width, rows), low),
    ]
    away = [
        shape(array.shape, array.dtype)
        for array in (output_weight, expand_weight, reduce_weight, expand_bias)
    ]
    return pl.pallas_call(
        forward_kernel,
        in_specs=[vmem()] * 6 + [pl.BlockSpec(memory_space=pltpu.SMEM)] + [anywhere] * 7,
        out_specs=[vmem()] * 3 + [anywhere] * 11,
        out_shape=[
            shape((width, rows), low),
            shape((width // HEAD_DIM, 1, rows), full),
            shape((HEAD_DIM, rows), low),
        ]
        + stored
        + away,
        scratch_shapes=[
            *[pltpu.VMEM(each.shape, each.dtype) for each in stored],
            pltpu.VMEM((wide, channels), low),
            pltpu.VMEM((local, channels), full),
            pltpu.VMEM((local, GROUP * channels), low),
            pltpu.VMEM(conv_weight.shape, low),
            pltpu.VMEM(conv_weight.shape, low),
            pltpu.VMEM(encode_weight.shape, low),
            pltpu.VMEM(encode_weight.shape, low),
            pltpu.VMEM((local, width), low),
            pltpu.VMEM((local, width), low),
            pltpu.VMEM((local, channels), low),
            pltpu.VMEM(heads_weight.shape, low),
            pltpu.VMEM((3, width, channels), low),
            pltpu.VMEM((rows, 128), full),
            pltpu.VMEM((128, rows), full),
            pltpu.VMEM((channels, channels), low),
            pltpu.SemaphoreType.DMA((groups + 2,)),
            pltpu.SemaphoreType.DMA((len(stored),)),
            *copy_sems(12 + groups),
        ],
        compiler_params=pltpu.CompilerParams(
            vmem_limit_bytes=VMEM_BYTES, collective_id=2, has_side_effects=True
        ),
        cost_estimate=pl.CostEstimate(
            flops=60 * 10**9, bytes_accessed=20 * 10**6, transcendentals=0
        ),
    )(
        near, points, *norms, valid_count, conv_weight, encode_weight, heads_weight, output_weight,
        expand_weight, reduce_weight, expand_bias
    )


def partner_of(bit):
    me = lax.axis_index("pts")
    return me + (1 - 2 * ((me // (1 << bit)) % 2)) * (1 << bit)


def greet_partners():
    barrier = pltpu.get_barrier_semaphore()
    for bit in range(KERNEL_BITS):
        pl.semaphore_signal(
            barrier, inc=1, device_id={"pts": partner_of(bit)}, device_id_type=MESH
        )
    return barrier


class PairSums:
    def __init__(self, keep, sends, arrivals, send_sem, arrive_sem):
        self.keep, self.sends, self.arrivals = keep, sends, arrivals
        self.send_sem, self.arrive_sem = send_sem, arrive_sem

    def copy(self, stage, chunk, bit):
        return pltpu.make_async_remote_copy(
            src_ref=self.sends[stage].at[chunk],
            dst_ref=self.arrivals[stage].at[chunk],
            send_sem=self.send_sem.at[stage, chunk],
            recv_sem=self.arrive_sem.at[stage, chunk],
            device_id={"pts": partner_of(bit)},
            device_id_type=MESH,
        )

    def start(self, stage, chunk, kinds):
        for holds, order in kinds:
            if holds is True:
                self.copy(stage, chunk, order[stage]).start()
            else:

                @pl.when(holds)
                def _(order=order):
                    self.copy(stage, chunk, order[stage]).start()

    def advance(self, stage, chunk, kinds, finish):
        self.copy(stage, chunk, 0).wait()
        rows = self.keep.shape[2]
        low = rows - (rows >> stage)
        half = (rows - low) // 2
        arrived = self.arrivals[stage]
        if stage == len(self.sends) - 1:
            finish(self.keep[chunk, :, low:] + to_wide(arrived[chunk]))
            return
        self.sends[stage + 1][chunk] = to_low(
            self.keep[chunk, :, low : low + half] + to_wide(arrived[chunk, :, :half])
        )
        self.start(stage + 1, chunk, kinds)
        self.keep[chunk, :, low + half :] += to_wide(arrived[chunk, :, half:])


def pair_scratch(chunks, lead, rows, width, stages):
    halves = [(chunks, lead, rows >> (stage + 1), width) for stage in range(stages)]
    return (
        [pltpu.VMEM(halves[0], jnp.float32)]
        + [pltpu.VMEM(shape, jnp.bfloat16) for shape in halves]
        + [pltpu.VMEM(shape, jnp.bfloat16) for shape in halves]
        + [pltpu.SemaphoreType.DMA((stages, chunks))] * 2
    )


def pair_sums(scratch):
    stages = (len(scratch) - 3) // 2
    keep, rest = scratch[0], scratch[1:]
    return PairSums(keep, rest[:stages], rest[stages : 2 * stages], *rest[-2:])


def middle_kernel(
    mixed_ref,
    first_ref,
    output_ref,
    output_other_ref,
    output_bias_ref,
    gain_ref,
    shift_ref,
    cotangent_ref,
    bias_ref,
    bias_other_ref,
    reduce_bias_ref,
    mask_ref,
    log_ref,
    attend_gain_ref,
    encode_gain_ref,
    expand_hbm,
    expand_other_hbm,
    reduce_hbm,
    reduce_other_hbm,
    projected_hbm,
    heads_hbm,
    attend_hbm,
    linear_hbm,
    encode_hbm,
    conved_hbm,
    turned_hbm,
    near_hbm,
    conved_grad_ref,
    vectors_ref,
    reduce_sum_ref,
    expand_sum_ref,
    output_sum_ref,
    result_hbm,
    first_grad_hbm,
    extra_hbm,
    turned_other,
    near_other,
    first_grad_ref,
    extra_ref,
    expand_ref,
    expand_other_ref,
    reduce_ref,
    reduce_other_ref,
    projected_ref,
    heads_ref,
    attend_ref,
    linear_ref,
    encode_ref,
    conved_ref,
    result_ref,
    second_grad_ref,
    mixed_grad_ref,
    grad_ref,
    mixed_other,
    second_own,
    second_other,
    picks,
    top,
    away,
    arrived,
    attend_away,
    attend_arrived,
    linear_own,
    linear_other,
    load_sem,
    send_sem,
    arrive_sem,
    *scratch,
):
    local, channels = first_ref.shape
    width, points = mixed_ref.shape
    hidden_width = bias_ref.shape[1]
    columns = hidden_width // 2
    heads = width // HEAD_DIM
    half = channels // 2
    side = lax.axis_index("tp")
    mine = pl.ds(pl.multiple_of(side * local, local), local)
    theirs = pl.ds(pl.multiple_of((1 - side) * local, local), local)
    sums = pair_sums(scratch)
    copies = Copies(send_sem, arrive_sem)
    partner = {"pts": partner_of(SHARE_BIT)}
    share_copies = [
        copies.to(partner, turned_hbm.at[:half], turned_other, 0),
        copies.to(partner, near_hbm, near_other, 1),
    ]
    loads = [
        pltpu.make_async_copy(source, target, load_sem.at[index])
        for index, (source, target) in enumerate(
            (
                (expand_other_hbm, expand_other_ref),
                (reduce_other_hbm, reduce_other_ref),
                (expand_hbm, expand_ref),
                (reduce_hbm, reduce_ref),
                (projected_hbm, projected_ref),
                (heads_hbm, heads_ref),
                (attend_hbm, attend_ref),
                (linear_hbm, linear_ref),
                (encode_hbm, encode_ref),
                (conved_hbm, conved_ref),
            )
        )
    ]
    result_copy = pltpu.make_async_copy(result_ref, result_hbm, load_sem.at[len(loads)])
    first_store = pltpu.make_async_copy(first_grad_ref, first_grad_hbm, load_sem.at[len(loads) + 1])
    extra_stores = [
        pltpu.make_async_copy(
            extra_ref.at[kind], extra_hbm.at[kind], load_sem.at[len(loads) + 2 + kind]
        )
        for kind in range(2)
    ]

    for load in loads:
        load.start()
    barrier = greet_partners()
    pl.semaphore_signal(barrier, inc=1, device_id=sibling(), device_id_type=MESH)
    pl.semaphore_wait(barrier, KERNEL_BITS + 1)
    mixed_copy = copies.to(sibling(), mixed_ref.at[:, local:], mixed_other, 2)
    mixed_copy.start()
    for copy in share_copies:
        copy.start()

    cotangent = cotangent_ref[...]
    for kind in range(2):
        picks[kind] = nested_picks(channels, ORDERS[kind])
    cotangent_turned = to_low(product(picks[0], cotangent, 1, 1))
    second = first_ref[...] + output_bias_ref[...]
    second += product(mixed_ref[:, :local], output_ref[...], 0, 0)
    mixed_copy.wait()
    second += product(mixed_other[...], output_other_ref[...], 0, 0)
    normal, inverse = layer_norm(second)
    feed_low = to_low(normal * gain_ref[...] + shift_ref[...])
    feed_turned = to_low(product(picks[1], feed_low, 1, 1))
    result = second + reduce_bias_ref[...]
    feed_grad = jnp.zeros_like(second)
    for load in loads[:4]:
        load.wait()
    weight_copies = []
    for index, (up_ref, up_bias_ref, down_ref) in enumerate(
        (
            (expand_other_ref, bias_other_ref, reduce_other_ref),
            (expand_ref, bias_ref, reduce_ref),
        )
    ):
        bias_grads = []
        for start in range(0, hidden_width, columns):
            now = slice(start, start + columns)
            hidden = product(feed_low, up_ref[:, now], 1, 0) + up_bias_ref[:, now]
            below = 0.5 + 0.5 * lax.erf(hidden * 0.5**0.5)
            slope = below + hidden * (jnp.exp(-0.5 * hidden * hidden) * (0.5 / jnp.pi) ** 0.5)
            active = to_low(hidden * below)
            hidden_grad = to_low(product(cotangent, down_ref[now, :], 1, 1) * slope)
            result += product(active, down_ref[now, :], 1, 0)
            feed_grad += product(hidden_grad, up_ref[:, now], 1, 1)
            bias_grads.append(column_sum(to_wide(hidden_grad)))
            weight_grads = (
                product(cotangent_turned, active, 1, 0),
                product(feed_turned, hidden_grad, 1, 0),
            )
            for kind, weight_grad in enumerate(weight_grads):
                if index == 0:
                    away[kind, :, now] = weight_grad
                    copy = copies.to(
                        sibling(),
                        away.at[kind, :, now],
                        arrived.at[kind, :, now],
                        4 + len(weight_copies),
                    )
                    copy.start()
                    weight_copies.append(copy)
                else:
                    top[kind, :, now] = weight_grad[:half]
                    sums.keep[kind, 0, :, now] = weight_grad[half:]
        owner = (1 - side) if index == 0 else side
        for part, grads in enumerate(bias_grads):
            vectors_ref[pl.ds(8 + 2 * owner + part, 1), :] = grads
    result_ref[...] = to_low(result)
    result_copy.start()
    upstream = to_wide(cotangent)
    second_grad = upstream + norm_back(feed_grad, normal, inverse, gain_ref[...])
    second_grad_ref[...] = second_grad
    second_own[...] = to_low(second_grad)
    second_copy = copies.to(sibling(), second_own, second_other, 3)
    second_copy.start()
    vectors_ref[0:1] = column_sum(second_grad)
    vectors_ref[1:2] = column_sum(feed_grad * normal)
    vectors_ref[2:3] = column_sum(feed_grad)
    vectors_ref[3:4] = column_sum(upstream)
    mixed_grad_ref[:, :local] = to_low(product(output_ref[...], second_own[...], 1, 1))
    part = width // 2
    output_grads = [
        product(
            to_low(product(picks[kind], second_own[...], 1, 1)),
            mixed_ref[kind * part : (kind + 1) * part, :local],
            1,
            1,
        )
        for kind in range(2)
    ]
    second_copy.wait()
    mixed_grad_ref[:, local:] = to_low(product(output_ref[...], second_other[...], 1, 1))
    for kind in range(2):
        output_grad = output_grads[kind] + product(
            to_low(product(picks[kind], second_other[...], 1, 1)),
            mixed_ref[kind * part : (kind + 1) * part, local:],
            1,
            1,
        )
        sums.sends[0][kind, 0, :, hidden_width:] = to_low(output_grad[:half])
        sums.keep[kind, 0, :, hidden_width:] = output_grad[half:]
    for copy in weight_copies:
        copy.wait()
    for kind in range(2):
        sums.sends[0][kind, 0, :, :hidden_width] = to_low(top[kind] + arrived[kind, :half])
        sums.start(0, kind, ((True, ORDERS[kind]),))
        sums.keep[kind, 0, :, :hidden_width] += arrived[kind, half:]

    scale = HEAD_DIM**-0.5
    row = lax.broadcasted_iota(jnp.int32, (HEAD_DIM, points), 0)
    ones = to_low(jnp.where((row > 0) & (row < 4), 1.0, 0.0))
    for load in loads[4:]:
        load.wait()

    def three_parts(values, lead):
        upper = to_wide(to_low(values))
        middle = to_wide(to_low(values - upper))
        lower = values - upper - middle
        tail = jnp.where(row == 1, -upper, jnp.where(row == 2, -middle, 0.0))
        tail = jnp.where(row == 3, -lower, tail)
        return to_low(jnp.where(row == 0, lead, tail))

    def finish_sum(index, total):
        if index == 0:
            reduce_sum_ref[...] = total[0, :, :hidden_width]
        else:
            expand_sum_ref[...] = total[0, :, :hidden_width]
        output_sum_ref[:, index * part : (index + 1) * part] = total[0, :, hidden_width:]

    def heads_step(step, _):
        for stage, due in enumerate(SUM_STEPS):

            @pl.when(step == due)
            def _(stage=stage):
                for index in range(2):
                    sums.advance(
                        stage, index, ((True, ORDERS[index]),), functools.partial(finish_sum, index)
                    )

        operands, places = [], []
        for offset in range(HEADS_BACK_STEP):
            head = step * HEADS_BACK_STEP + offset
            place = pl.ds(pl.multiple_of(head * HEAD_DIM, HEAD_DIM), HEAD_DIM)
            places.append(place)
            query, key, value = (projected_ref[index, place] for index in range(3))
            grad = mixed_grad_ref[place]
            row_dot = column_sum(to_wide(grad) * to_wide(mixed_ref[place]))
            scaled = to_low(to_wide(query) * scale)
            operands.append(
                (
                    jnp.concatenate([scaled, three_parts(log_ref[head], 1.0)], axis=0),
                    jnp.concatenate([key, mask_ref[...] + ones], axis=0),
                    jnp.concatenate([value, ones], axis=0),
                    jnp.concatenate([grad, three_parts(row_dot, 0.0)], axis=0),
                    query,
                    key,
                    grad,
                )
            )
        totals = [None] * HEADS_BACK_STEP

        def begin(unit):
            offset, start = unit
            queries, keys, values, grads = operands[offset][:4]
            return (
                product(keys, queries[:, start : start + BACK_CHUNK], 0, 0),
                product(values, grads[:, start : start + BACK_CHUNK], 0, 0),
            )

        def finish(unit, ready):
            offset, start = unit
            scores, prob_grad = ready
            query, key, grad = operands[offset][4:]
            now = slice(start, start + BACK_CHUNK)
            probs = jnp.exp(scores)
            score_grad = to_low(probs * prob_grad)
            grad_ref[0, places[offset], now] = to_low(product(key, score_grad, 1, 0) * scale)
            value_part = product(grad[:, now], to_low(probs), 1, 1)
            key_part = product(query[:, now], score_grad, 1, 1)
            if totals[offset] is not None:
                key_part, value_part = key_part + totals[offset][0], value_part + totals[offset][1]
            totals[offset] = (key_part, value_part)

        units = [(h, c) for c in range(0, points, BACK_CHUNK) for h in range(HEADS_BACK_STEP)]
        staged(units, begin, finish)
        for offset in range(HEADS_BACK_STEP):
            grad_ref[1, places[offset]] = to_low(totals[offset][0] * scale)
            grad_ref[2, places[offset]] = to_low(totals[offset][1])
        return 0

    lax.fori_loop(0, heads // HEADS_BACK_STEP, heads_step, 0)

    def attend_grad(start):
        return sum(
            product(grad_ref[index, :, start : start + local].T, heads_ref[index], 1, 1)
            for index in range(3)
        )

    attend_away[...] = attend_grad(local)
    attend_copy = copies.to(sibling(), attend_away, attend_arrived, 8)
    attend_copy.start()
    for stage in range(len(SUM_STEPS), KERNEL_BITS):
        for index in range(2):
            sums.advance(
                stage, index, ((True, ORDERS[index]),), functools.partial(finish_sum, index)
            )
    upstream = attend_grad(0)
    for kind in range(2):
        turned = [to_low(product(picks[kind], attend_ref[i], 1, 1)) for i in range(2)]
        for index in (0, 1) if kind == 0 else (2,):
            extra_ref[kind, index % 2] = product(
                turned[0], grad_ref[index, :, :local], 1, 1
            ) + product(turned[1], grad_ref[index, :, local:], 1, 1)
    extra_stores[0].start()
    normal, inverse = layer_norm(first_ref[...])
    attend_copy.wait()
    upstream += attend_arrived[...]
    first_grad = second_grad_ref[...] + norm_back(upstream, normal, inverse, attend_gain_ref[...])
    first_grad_ref[...] = first_grad
    first_store.start()
    vectors_ref[4:5] = column_sum(upstream * normal)
    vectors_ref[5:6] = column_sum(upstream)
    normal, inverse = layer_norm(linear_ref[...])
    linear_own[...] = to_low(norm_back(first_grad, normal, inverse, encode_gain_ref[...]))
    linear_copy = copies.to(sibling(), linear_own, linear_other, 9)
    linear_copy.start()
    vectors_ref[6:7] = column_sum(first_grad * normal)
    vectors_ref[7:8] = column_sum(first_grad)
    conved_grad_ref[mine] = to_low(product(linear_own[...], encode_ref[...], 1, 1))
    encode_grad = product(
        to_low(product(picks[1], linear_own[...], 1, 1)), conved_ref[mine], 1, 0
    )
    linear_copy.wait()
    conved_grad_ref[theirs] = to_low(product(linear_other[...], encode_ref[...], 1, 1))
    extra_ref[1, 1] = encode_grad + product(
        to_low(product(picks[1], linear_other[...], 1, 1)), conved_ref[theirs], 1, 0
    )
    extra_stores[1].start()
    for store in (result_copy, first_store, *extra_stores):
        store.wait()
    for copy in share_copies:
        copy.wait()


def middle(near_operands, far_operands):
    local, channels = near_operands[1].shape
    width, rows = near_operands[0].shape
    hidden = near_operands[8].shape[1]
    turned, near = far_operands[-2:]
    kept = channels >> KERNEL_BITS
    low, full = jnp.bfloat16, jnp.float32
    shape = jax.ShapeDtypeStruct
    anywhere = pl.BlockSpec(memory_space=pl.ANY)
    loaded = far_operands[:-2]
    square = (local, channels)
    return pl.pallas_call(
        middle_kernel,
        in_specs=[vmem()] * len(near_operands) + [anywhere] * len(far_operands),
        out_specs=[vmem()] * 5 + [anywhere] * 5,
        out_shape=[
            shape((rows, width), low),
            shape((8 + 2 * hidden // channels, channels), full),
            shape((kept, hidden), full),
            shape((kept, hidden), full),
            shape((kept, width), full),
            shape(square, low),
            shape(square, full),
            shape((2, 2, channels, width), full),
            shape((channels // 2, turned.shape[1]), low),
            shape(near.shape, full),
        ],
        scratch_shapes=[
            pltpu.VMEM(square, full),
            pltpu.VMEM((2, 2, channels, width), full),
            *[pltpu.VMEM(each.shape, each.dtype) for each in loaded],
            pltpu.VMEM(square, low),
            pltpu.VMEM(square, full),
            pltpu.VMEM((width, rows), low),
            pltpu.VMEM((3, width, rows), low),
            pltpu.VMEM((width, local), low),
            pltpu.VMEM(square, low),
            pltpu.VMEM(square, low),
            pltpu.VMEM((2, channels, channels), low),
            pltpu.VMEM((2, channels // 2, hidden), full),
            pltpu.VMEM((2, channels, hidden), full),
            pltpu.VMEM((2, channels, hidden), full),
            pltpu.VMEM(square, full),
            pltpu.VMEM(square, full),
            pltpu.VMEM(square, low),
            pltpu.VMEM(square, low),
            pltpu.SemaphoreType.DMA((len(loaded) + 4,)),
            *copy_sems(10),
            *pair_scratch(2, 1, channels, hidden + width // 2, KERNEL_BITS),
        ],
        compiler_params=pltpu.CompilerParams(
            vmem_limit_bytes=VMEM_BYTES, collective_id=3, has_side_effects=True
        ),
        cost_estimate=pl.CostEstimate(
            flops=70 * 10**9, bytes_accessed=20 * 10**6, transcendentals=0
        ),
    )(*near_operands, *far_operands)


def conv_backward_kernel(
    near_ref,
    near_other_ref,
    turned_hbm,
    turned_other_hbm,
    grad_ref,
    weight_hbm,
    extra_hbm,
    vector_ref,
    first_grad_hbm,
    conv_sum_ref,
    heads_sum_ref,
    encode_sum_ref,
    points_grad_ref,
    *refs,
):
    vector_refs, refs = refs[:9], refs[9:]
    (
        spread,
        windows,
        gathered,
        grad_other,
        input_grad,
        input_arrived,
        rim_away,
        rim_arrived,
        vector_away,
        vector_arrived,
        send_sem,
        arrive_sem,
        weight_ref,
        first_grad_ref,
        turned_ref,
        turned_other_ref,
        extra_ref,
        load_sem,
    ) = refs[:18]
    sums, extra_sums = pair_sums(refs[18:27]), pair_sums(refs[27:])
    rows, width = grad_ref.shape
    local, channels = first_grad_ref.shape
    half = channels // 2
    quarter = half // 4
    blocks = rows // BLOCK
    extras = extra_hbm.shape[0]
    chunks = conv_sum_ref.shape[0]
    patches = lax.axis_size("pts")
    me, side = lax.axis_index("pts"), lax.axis_index("tp")
    copies = Copies(send_sem, arrive_sem)
    loads = [
        pltpu.make_async_copy(weight_hbm, weight_ref, load_sem.at[0]),
        pltpu.make_async_copy(first_grad_hbm, first_grad_ref, load_sem.at[1]),
    ]
    early_loads = [
        pltpu.make_async_copy(extra_hbm, extra_ref, load_sem.at[2]),
        pltpu.make_async_copy(turned_hbm.at[half:], turned_ref, load_sem.at[3]),
        pltpu.make_async_copy(turned_other_hbm, turned_other_ref, load_sem.at[4]),
    ]
    mine = pl.ds(pl.multiple_of(HALO + side * local, HALO), local)
    theirs = pl.ds(pl.multiple_of(HALO + (1 - side) * local, HALO), local)
    grad_copy = copies.to({"pts": partner_of(SHARE_BIT)}, grad_ref, grad_other, 0)
    input_copy = copies.to(sibling(), input_grad.at[theirs], input_arrived, 1)
    rims = (
        (me > 0, {"pts": me - 1, "tp": 1}, slice(0, HALO)),
        (me < patches - 1, {"pts": me + 1, "tp": 0}, slice(HALO + rows, rows + 2 * HALO)),
    )
    rim_copies = [
        [copies.to(rim[1], rim_away.at[i], rim_arrived.at[core], 2 + i, 4 + core) for core in (0, 1)]
        for i, rim in enumerate(rims)
    ]
    has_rim = ((side == 0) & (me > 0)) | ((side == 1) & (me < patches - 1))
    first_sum = chunks // GROUP
    first_input = first_sum + chunks
    input_steps = chunks // GROUP

    def vector_copy(stage):
        device = sibling() if stage == 0 else {"pts": partner_of(stage - 1)}
        return copies.to(device, vector_away.at[stage], vector_arrived.at[stage], 6 + stage)

    def kinds(chunk):
        return ((chunk % 2 == 0, CONV_ORDERS[0]), (chunk % 2 == 1, CONV_ORDERS[1]))

    steps = first_input + 2 * input_steps

    def begin():
        for load in early_loads:
            load.start()
        barrier = greet_partners()
        pl.semaphore_signal(barrier, inc=1, device_id=sibling(), device_id_type=MESH)
        for core in range(2):

            @pl.when((side == 0) & (me > 0))
            def _(core=core):
                device = {"pts": me - 1, "tp": core}
                pl.semaphore_signal(barrier, inc=1, device_id=device, device_id_type=MESH)

            @pl.when((side == 1) & (me < patches - 1))
            def _(core=core):
                device = {"pts": me + 1, "tp": core}
                pl.semaphore_signal(barrier, inc=1, device_id=device, device_id_type=MESH)

        sent = jnp.where(me > 0, 1, 0) + jnp.where(me < patches - 1, 1, 0)
        pl.semaphore_wait(barrier, KERNEL_BITS + 1 + sent)
        grad_copy.start()
        for load in loads:
            load.start()
        early_loads[0].wait()
        for index in range(extras):
            extra_sums.sends[0][index] = to_low(extra_ref[index, :, :half])
            extra_sums.start(0, index, ((True, ORDERS[index]),))
            extra_sums.keep[index] = extra_ref[index, :, half:]
        vector_away[0] = vector_ref[...]
        vector_copy(0).start()
        for load in early_loads[1:]:
            load.wait()
        for kind, places in enumerate(((0, 1, 2, 3), (0, 2, 1, 3))):
            for place, source in enumerate(places):
                now = slice(place * quarter, (place + 1) * quarter)
                low = source * quarter
                windows[kind, 0, now] = turned_ref[low : low + quarter, :]
                windows[kind, 1, now] = turned_other_ref[low : low + quarter, :]
        input_grad[...] = jnp.zeros_like(input_grad)

    def one_step(step, _):
        @pl.when(step < first_sum)
        def _():
            slots = to_wide(lax.broadcasted_iota(jnp.int32, (BLOCK, 1), 0))

            def spread_group(group, _):
                for offset in range(GROUP):
                    index = (step * GROUP + group) * GROUP + offset
                    near = near_ref[pl.ds(index, 1), :]
                    for part in range(blocks + 1):
                        low = max(part - 1, 0) * BLOCK
                        high = min(part + 1, blocks) * BLOCK
                        select = to_low(
                            jnp.where(near[:, low:high] - float(part * BLOCK) == slots, 1.0, 0.0)
                        )
                        spread[index, part * BLOCK : (part + 1) * BLOCK] = to_low(
                            product(select, grad_ref[low:high, :], 1, 0)
                        )
                return 0

            lax.fori_loop(0, GROUP, spread_group, 0, unroll=True)

        @pl.when((step >= first_sum) & (step < first_input))
        def _():
            chunk = step - first_sum
            pl.when(chunk == 0)(grad_copy.wait)
            slots = to_wide(lax.broadcasted_iota(jnp.int32, (2 * BLOCK, 1), 0))
            for offset in range(GROUP):
                near = near_other_ref[pl.ds(chunk * GROUP + offset, 1), :]
                for block in range(blocks):
                    low = block * BLOCK
                    select = to_low(
                        jnp.where(near[:, low : low + BLOCK] - float(low) == slots, 1.0, 0.0)
                    )
                    gathered[offset, :, low : low + BLOCK] = to_low(
                        product(windows[chunk % 2, 1, :, low : low + 2 * BLOCK], select, 1, 0)
                    )
            for offset in range(GROUP):
                weight_grad = product(windows[chunk % 2, 0], spread[chunk * GROUP + offset], 1, 0)
                weight_grad += product(gathered[offset], grad_other[...], 1, 0)
                sums.sends[0][chunk, offset] = to_low(weight_grad[: half // 2])
                sums.keep[chunk, offset] = weight_grad[half // 2 :]
            sums.start(0, chunk, kinds(chunk))

        @pl.when(step == first_input)
        def _():
            for load in loads:
                load.wait()

        beside = pl.ds(pl.multiple_of((1 - side) * (local + HALO), HALO), local + HALO)
        apart = pl.ds(pl.multiple_of(side * (2 * local + HALO), HALO), HALO)
        for phase, parts in enumerate(((beside, apart), (mine,))):
            start = first_input + phase * input_steps

            @pl.when((step >= start) & (step < start + input_steps))
            def _(start=start, parts=parts):
                def input_group(group, _):
                    for part in parts:
                        total = input_grad[part, :]
                        for offset in range(GROUP):
                            index = group * GROUP + offset
                            total += product(
                                spread[(step - start) * WIDE_GROUP + index, part, :],
                                weight_ref[(step - start) * WIDE_GROUP + index],
                                1,
                                1,
                            )
                        input_grad[part, :] = total
                    return 0

                lax.fori_loop(0, GROUP, input_group, 0, unroll=True)

        @pl.when(step == first_input + input_steps - 1)
        def _():
            input_copy.start()
            for index, (has, _, part) in enumerate(rims):
                rim_away[index] = to_low(input_grad[part, :])

                @pl.when(has)
                def _(index=index):
                    for core in range(2):

                        @pl.when(side == core)
                        def _(core=core):
                            rim_copies[index][core].start()

        @pl.when(step == steps - 1)
        def _():
            input_copy.wait()
            points_grad_ref[...] = first_grad_ref[...] + input_grad[mine, :] + input_arrived[...]

            @pl.when(has_rim)
            def _():
                edge = pl.ds(pl.multiple_of(side * (local - HALO), HALO), HALO)
                for core in range(2):
                    rim_copies[0][core].wait_recv()
                    points_grad_ref[edge, :] += to_wide(rim_arrived[core])

            for index, (has, _, part) in enumerate(rims):
                pl.when(has)(rim_copies[index][0].wait_send)

        for stage, due in enumerate(VECTOR_STEPS):

            @pl.when(step == due)
            def _(stage=stage):
                vector_copy(stage).wait()
                summed = vector_away[stage] + vector_arrived[stage]
                if stage < KERNEL_BITS:
                    vector_away[stage + 1] = summed
                    vector_copy(stage + 1).start()
                    return
                for index in range(8):
                    vector_refs[index][...] = summed[index : index + 1]
                for index in range(8, summed.shape[0]):
                    low = (index - 8) * channels
                    vector_refs[8][:, low : low + channels] = summed[index : index + 1]

        for stage in range(len(CONV_LAGS)):
            chunk = step - first_sum - CONV_LAGS[stage]

            @pl.when((chunk >= 0) & (chunk < chunks))
            def _(stage=stage, chunk=chunk):
                def finish(total):
                    conv_sum_ref[chunk] = total

                sums.advance(stage, chunk, kinds(chunk), finish)

        def finish_extra(index, total):
            if index == 0:
                heads_sum_ref[0:2] = total
            else:
                heads_sum_ref[2] = total[0]
                encode_sum_ref[...] = total[1]

        for stage, due in enumerate(EXTRA_STEPS):

            @pl.when(step == due)
            def _(stage=stage):
                for index in range(extras):
                    extra_sums.advance(
                        stage,
                        index,
                        ((True, ORDERS[index]),),
                        functools.partial(finish_extra, index),
                    )
        return 0

    begin()
    lax.fori_loop(0, steps, one_step, 0)


def conv_backward(
    near, near_other, turned, turned_other, grad, weight, extra, vector, first_grad
):
    offsets, channels, width = weight.shape
    wide = turned.shape[1]
    rows = grad.shape[0]
    local = first_grad.shape[0]
    chunks = offsets // GROUP
    low, full = jnp.bfloat16, jnp.float32
    kept = channels >> KERNEL_BITS
    shape = jax.ShapeDtypeStruct
    outs = [
        shape((chunks, GROUP, kept, width), full),
        shape((3, kept, width), full),
        shape((kept, width), full),
        shape(first_grad.shape, full),
        *[shape((1, channels), full)] * 8,
        shape((1, (vector.shape[0] - 8) * channels), full),
    ]

    anywhere = pl.BlockSpec(memory_space=pl.ANY)
    return pl.pallas_call(
        conv_backward_kernel,
        in_specs=[vmem()] * 2 + [anywhere] * 2 + [vmem()] + [anywhere] * 2 + [vmem(), anywhere],
        out_specs=[vmem()] * len(outs),
        out_shape=outs,
        scratch_shapes=[
            pltpu.VMEM((offsets, wide, width), low),
            pltpu.VMEM((2, 2, channels // 2, wide), low),
            pltpu.VMEM((GROUP, channels // 2, rows), low),
            pltpu.VMEM((rows, width), low),
            pltpu.VMEM((wide, channels), full),
            pltpu.VMEM((local, channels), full),
            pltpu.VMEM((2, HALO, channels), low),
            pltpu.VMEM((2, HALO, channels), low),
            pltpu.VMEM((KERNEL_BITS + 1, *vector.shape), full),
            pltpu.VMEM((KERNEL_BITS + 1, *vector.shape), full),
            *copy_sems(7 + KERNEL_BITS),
            pltpu.VMEM(weight.shape, low),
            pltpu.VMEM(first_grad.shape, full),
            pltpu.VMEM(turned_other.shape, low),
            pltpu.VMEM(turned_other.shape, low),
            pltpu.VMEM(extra.shape, full),
            pltpu.SemaphoreType.DMA((5,)),
            *pair_scratch(chunks, GROUP, channels // 2, width, len(CONV_LAGS)),
            *pair_scratch(*extra.shape, KERNEL_BITS),
        ],
        compiler_params=pltpu.CompilerParams(
            vmem_limit_bytes=VMEM_BYTES, collective_id=1, has_side_effects=True
        ),
        cost_estimate=pl.CostEstimate(
            flops=80 * 10**9, bytes_accessed=16 * 10**6, transcendentals=0
        ),
    )(near, near_other, turned, turned_other, grad, weight, extra, vector, first_grad)


def hand_over_kernel(*refs):
    count = (len(refs) - 1) // 3
    sem = refs[-1]
    inward = [
        pltpu.make_async_copy(refs[i], refs[2 * count + i], sem.at[i]) for i in range(count)
    ]
    outward = [
        pltpu.make_async_copy(refs[2 * count + i], refs[count + i], sem.at[count + i])
        for i in range(count)
    ]
    for copy in inward:
        copy.start()
    for arrive, leave in zip(inward, outward):
        arrive.wait()
        leave.start()
    for copy in outward:
        copy.wait()


def hand_over(arrays):
    anywhere = pl.BlockSpec(memory_space=pl.ANY)
    return pl.pallas_call(
        hand_over_kernel,
        in_specs=[anywhere] * len(arrays),
        out_specs=[anywhere] * len(arrays),
        out_shape=[jax.ShapeDtypeStruct(each.shape, each.dtype) for each in arrays],
        scratch_shapes=[pltpu.VMEM(each.shape, each.dtype) for each in arrays]
        + [pltpu.SemaphoreType.DMA((2 * len(arrays),))],
        compiler_params=pltpu.CompilerParams(vmem_limit_bytes=VMEM_BYTES),
    )(*arrays)


def exchange(values, bit):
    count = lax.axis_size("pts")
    return lax.ppermute(values, "pts", [(i, i ^ (1 << bit)) for i in range(count)])


def sum_rest(keep, axis):
    for bit in range(KERNEL_BITS, patch_bits()):
        half = keep.shape[axis] // 2
        away = lax.slice_in_dim(keep, 0, half, axis=axis)
        keep = lax.slice_in_dim(keep, half, 2 * half, axis=axis)
        keep = keep + to_wide(exchange(to_low(away), bit))
    return keep


def per_device(
    points,
    neighbours,
    valid_count,
    conv_weight,
    encode_weight,
    encode_gain,
    encode_shift,
    attend_gain,
    attend_shift,
    heads_weight,
    output_weight,
    output_bias,
    feed_gain,
    feed_shift,
    expand_weight,
    expand_bias,
    reduce_weight,
    reduce_bias,
    cotangent,
):
    local, channels = points.shape
    norms = [v[None, :] for v in (encode_gain, encode_shift, attend_gain, attend_shift)]
    (
        mixed, logs, mask, turned, near_columns, conved, linear, first, attend_in, projected,
        output_other, expand_other, reduce_other, bias_other,
    ) = forward_start(
        neighbours.T, points, conv_weight, encode_weight, norms, heads_weight, output_weight,
        expand_weight, reduce_weight, expand_bias[None, :], valid_count
    )
    (
        conved_grad, vector, reduce_sum, expand_sum, output_sum, result, first_grad, extra,
        turned_other, near_other,
    ) = middle(
        [
            mixed, first, output_weight, output_other, output_bias[None, :], feed_gain[None, :],
            feed_shift[None, :], cotangent, expand_bias[None, :], bias_other,
            reduce_bias[None, :], mask, logs, norms[2], norms[0],
        ],
        [
            expand_weight, expand_other, reduce_weight, reduce_other, projected, heads_weight,
            attend_in, linear, encode_weight, conved, turned, near_columns,
        ],
    )
    conv_sum, heads_sum, encode_sum, points_gradient, *vectors = conv_backward(
        near_columns, near_other, turned, turned_other, conved_grad, conv_weight, extra, vector,
        first_grad
    )
    for bit in range(KERNEL_BITS, patch_bits()):
        vectors = [each + exchange(each, bit) for each in vectors]
    parts = hand_over(
        [
            result,
            points_gradient,
            sum_rest(conv_sum, 2),
            sum_rest(encode_sum, 0),
            sum_rest(heads_sum, 1),
            sum_rest(output_sum, 0),
            sum_rest(expand_sum, 0),
            sum_rest(reduce_sum, 0),
            *vectors,
        ]
    )
    vectors = [each.reshape(-1) for each in parts[8:]]
    return (
        parts[0],
        parts[1],
        parts[2].reshape(-1, *parts[2].shape[2:]),
        parts[3].T,
        vectors[6],
        vectors[7],
        vectors[4],
        vectors[5],
        parts[4],
        parts[5].T,
        vectors[0],
        vectors[1],
        vectors[2],
        parts[6],
        vectors[8],
        parts[7].T,
        vectors[3],
    )


def solution(mesh):
    placed = (
        P(("pts", "tp"), None),
        P("pts", None),
        P("pts"),
        P(None, None, "tp"),
        P("tp", None),
        P(),
        P(),
        P(),
        P(),
        P(None, None, "tp"),
        P("tp", None),
        P(),
        P(),
        P(),
        P(None, "tp"),
        P("tp"),
        P("tp", None),
        P(),
        P(("pts", "tp"), None),
    )
    return jax.shard_map(
        per_device,
        mesh=mesh,
        in_specs=placed,
        out_specs=(
            P(("pts", "tp"), None),
            P(("pts", "tp"), None),
            P(None, "pts", "tp"),
            P("tp", "pts"),
            P(),
            P(),
            P(),
            P(),
            P(None, "pts", "tp"),
            P("tp", "pts"),
            P(),
            P(),
            P(),
            P("pts", "tp"),
            P(),
            P("tp", "pts"),
            P(),
        ),
        check_vma=False,
    )
```

```python
import functools

import jax
import jax.numpy as jnp
from jax import lax
from jax.experimental import pallas as pl
from jax.experimental.pallas import tpu as pltpu
from jax.sharding import PartitionSpec as P

MESH = pl.DeviceIdType.MESH
HEAD_DIM = 16
HALO = 128
BLOCK = 256
GROUP = 3
EPSILON = 1e-05
MASKED = -1e30
KERNEL_BITS = 4
ORDERS = ((0, 1, 2, 3), (1, 0, 2, 3))
VMEM_BYTES = 60 << 20
CHUNK = 512
BACK_CHUNK = 256
HEADS_STEP = 8
HEADS_BACK_STEP = 2
SUM_STEPS = (3, 5, 7)
SHARE_BIT = 2
CONV_ORDERS = ((0, 1, 3), (1, 0, 3))
WINDOW_ORDER = (2, 0, 1, 3)
CONV_LAGS = (2, 4, 6)
EXTRA_STEPS = (2, 3, 5, 7)
VECTOR_STEPS = (1, 2, 3, 4, 5)
WEIGHTS_AHEAD = 3
WIDE_GROUP = 9


def to_low(values):
    return values.astype(jnp.bfloat16)


def to_wide(values):
    return values.astype(jnp.float32)


def product(left, right, left_dim, right_dim):
    dims = (((left_dim,), (right_dim,)), ((), ()))
    return lax.dot_general(left, right, dims, preferred_element_type=jnp.float32)


def layer_norm(values):
    row_mean = jnp.mean(values, axis=-1, keepdims=True)
    centred = values - row_mean
    inverse = lax.rsqrt(jnp.mean(centred * centred, axis=-1, keepdims=True) + EPSILON)
    return centred * inverse, inverse


def norm_back(upstream, normal_part, inverse, norm_gain):
    scaled = upstream * norm_gain
    across = (
        scaled
        - jnp.mean(scaled, axis=-1, keepdims=True)
        - normal_part * jnp.mean(scaled * normal_part, axis=-1, keepdims=True)
    )
    return across * inverse


def column_sum(values):
    return jnp.sum(values, axis=0, keepdims=True)


def nested_picks(channels, order):
    me = lax.axis_index("pts")
    order = order + tuple(range(KERNEL_BITS, patch_bits()))
    depth = channels >> len(order)
    lanes = 128
    place = lax.broadcasted_iota(jnp.int32, (channels, lanes), 0)
    picked = place & (depth - 1)
    for stage, bit in enumerate(order):
        kept = (place >> (channels.bit_length() - 2 - stage)) & 1
        picked = picked + (1 - ((kept + me // (1 << bit)) & 1)) * (depth << bit)
    column = lax.broadcasted_iota(jnp.int32, (channels, lanes), 1)
    return to_low(
        jnp.concatenate(
            [
                jnp.where(picked == column + low, 1.0, 0.0)
                for low in range(0, channels, lanes)
            ],
            axis=1,
        )
    )


class Copies:
    def __init__(self, send_sem, arrive_sem):
        self.send_sem, self.arrive_sem = send_sem, arrive_sem

    def to(self, device, source, target, send, arrive=None):
        return pltpu.make_async_remote_copy(
            src_ref=source,
            dst_ref=target,
            send_sem=self.send_sem.at[send],
            recv_sem=self.arrive_sem.at[send if arrive is None else arrive],
            device_id=device,
            device_id_type=MESH,
        )


def copy_sems(count):
    return [pltpu.SemaphoreType.DMA((count,))] * 2


def patch_bits():
    return lax.axis_size("pts").bit_length() - 1


def sibling():
    return {"tp": 1 - lax.axis_index("tp")}


def greet_sibling():
    barrier = pltpu.get_barrier_semaphore()
    pl.semaphore_signal(barrier, inc=1, device_id=sibling(), device_id_type=MESH)
    pl.semaphore_wait(barrier, 1)


def vmem():
    return pl.BlockSpec(memory_space=pltpu.VMEM)


def whole(array):
    zeros = (0,) * array.ndim
    return pl.BlockSpec(array.shape, lambda i: zeros, pipeline_mode=pl.Buffered(1))


def staged(units, begin, finish):
    ready = begin(units[0])
    for index, unit in enumerate(units):
        later = begin(units[index + 1]) if index + 1 < len(units) else None
        finish(unit, ready)
        ready = later


def forward_kernel(
    near_ref,
    points_ref,
    encode_gain_ref,
    encode_shift_ref,
    attend_gain_ref,
    attend_shift_ref,
    valid_ref,
    weight_hbm,
    encode_hbm,
    heads_hbm,
    output_hbm,
    expand_hbm,
    reduce_hbm,
    bias_hbm,
    mixed_ref,
    log_ref,
    mask_ref,
    turned_hbm,
    near_hbm,
    conved_hbm,
    linear_hbm,
    first_hbm,
    attend_hbm,
    projected_hbm,
    output_other,
    expand_other,
    reduce_other,
    bias_other,
    turned_ref,
    near_columns_ref,
    conved_ref,
    linear_ref,
    first_ref,
    attend_ref,
    projected_ref,
    window,
    total,
    rows,
    weight_own,
    weight_other,
    encode_ref,
    encode_other,
    conved_away,
    conved_other,
    attend_other,
    heads_ref,
    heads_turned,
    near_wide,
    near_tall,
    picks,
    load_sem,
    store_sem,
    send_sem,
    arrive_sem,
):
    local, channels = points_ref.shape
    offsets, _, width = weight_own.shape
    groups = offsets // GROUP
    points = 2 * local
    patches = lax.axis_size("pts")
    me, side = lax.axis_index("pts"), lax.axis_index("tp")
    copies = Copies(send_sem, arrive_sem)
    own_place = pl.ds(pl.multiple_of(HALO + side * local, HALO), local)
    other_place = pl.ds(pl.multiple_of(HALO + (1 - side) * local, HALO), local)
    low_rim, high_rim = slice(0, HALO), slice(HALO + points, 2 * HALO + points)
    points_copy = copies.to(sibling(), points_ref, window.at[own_place], 0)
    low_copies = [
        copies.to(
            {"pts": (me + 1) % patches, "tp": core},
            points_ref.at[local - HALO :],
            window.at[low_rim],
            3 + core,
            1,
        )
        for core in range(2)
    ]
    high_copies = [
        copies.to(
            {"pts": (me + patches - 1) % patches, "tp": core}, points_ref.at[0:HALO], window.at[high_rim], 3 + core, 2
        )
        for core in range(2)
    ]
    small_copies = [
        copies.to(sibling(), encode_hbm, encode_other, 5),
        copies.to(sibling(), output_hbm, output_other, 6),
        copies.to(sibling(), expand_hbm, expand_other, 7),
        copies.to(sibling(), reduce_hbm, reduce_other, 8),
        copies.to(sibling(), bias_hbm, bias_other, 9),
    ]
    small_loads = [
        pltpu.make_async_copy(encode_hbm, encode_ref, load_sem.at[groups]),
        pltpu.make_async_copy(heads_hbm, heads_ref, load_sem.at[groups + 1]),
    ]
    stores = [
        pltpu.make_async_copy(source, target, store_sem.at[index])
        for index, (source, target) in enumerate(
            (
                (turned_ref, turned_hbm),
                (near_columns_ref, near_hbm),
                (conved_ref, conved_hbm),
                (linear_ref, linear_hbm),
                (first_ref, first_hbm),
                (attend_ref, attend_hbm),
                (projected_ref, projected_hbm),
            )
        )
    ]
    up = (side == 1) & (me < patches - 1)
    down = (side == 0) & (me > 0)

    def weight_copy(group):
        part = pl.ds(group * GROUP, GROUP)
        return copies.to(sibling(), weight_hbm.at[part], weight_other.at[part], 12 + group)

    def weight_load(group):
        part = pl.ds(group * GROUP, GROUP)
        return pltpu.make_async_copy(
            weight_hbm.at[part], weight_own.at[part], load_sem.at[group]
        )

    def turn(place):
        return to_low(product(picks[...], window[place, :], 1, 1))

    for group in range(WEIGHTS_AHEAD):
        weight_load(group).start()
    for load in small_loads:
        load.start()
    barrier = pltpu.get_barrier_semaphore()
    pl.semaphore_signal(barrier, inc=1, device_id=sibling(), device_id_type=MESH)

    @pl.when(me > 0)
    def _():
        pl.semaphore_signal(
            barrier, inc=1, device_id={"pts": (me + patches - 1) % patches, "tp": 1}, device_id_type=MESH
        )

    @pl.when(me < patches - 1)
    def _():
        pl.semaphore_signal(
            barrier, inc=1, device_id={"pts": (me + 1) % patches, "tp": 0}, device_id_type=MESH
        )

    pl.semaphore_wait(barrier, jnp.where(up | down, 3, 1))
    points_copy.start()

    @pl.when(up)
    def _():
        for copy in low_copies:
            copy.start()

    @pl.when(down)
    def _():
        for copy in high_copies:
            copy.start()

    for group in range(WEIGHTS_AHEAD):
        weight_copy(group).start()
    window[own_place, :] = points_ref[...]

    @pl.when(me == 0)
    def _():
        window[low_rim, :] = jnp.zeros((HALO, channels), jnp.bfloat16)

    @pl.when(me == patches - 1)
    def _():
        window[high_rim, :] = jnp.zeros((HALO, channels), jnp.bfloat16)

    near_tall[...] = jnp.zeros_like(near_tall)
    near_tall[: near_ref.shape[0]] = to_wide(near_ref[...])
    near_columns_ref[...] = near_tall[: near_columns_ref.shape[0]]
    near_wide[...] = near_tall[...].T
    picks[...] = nested_picks(channels, WINDOW_ORDER)
    turned_ref[:, own_place] = turn(own_place)
    stores[1].start()
    points_copy.wait()

    lane = lax.broadcasted_iota(jnp.int32, (BLOCK, near_wide.shape[1]), 1)
    slots = to_wide(lax.broadcasted_iota(jnp.int32, (BLOCK, 2 * BLOCK), 1))
    places = [pl.ds(pl.multiple_of(block * BLOCK, BLOCK), BLOCK) for block in (1 - side, side)]

    def gather(index, group):
        low = pl.multiple_of(side * local + (1 - side, side)[index] * BLOCK, BLOCK)
        part = window[pl.ds(low, 2 * BLOCK), :]
        near = near_wide[pl.ds(low, BLOCK), :] - low.astype(jnp.float32)
        for offset in range(GROUP):
            chosen = jnp.where(lane == group * GROUP + offset, near, 0.0)
            column = jnp.sum(chosen, axis=1, keepdims=True)
            select = to_low(jnp.where(column == slots, 1.0, 0.0))
            rows[places[index], offset * channels : (offset + 1) * channels] = to_low(
                product(select, part, 1, 0)
            )

    def apply(place, group):
        picked = rows[place, :]
        part = pl.ds(group * GROUP, GROUP)
        flat = (GROUP * channels, width)
        return (
            product(picked, weight_own[part].reshape(flat), 1, 0),
            product(picked, weight_other[part].reshape(flat), 1, 0),
        )

    def both_blocks(group):
        gather(0, group)
        gather(1, group)
        own, other = apply(slice(None), group)
        total[:, :width] += own
        total[:, width:] += other

    def next_weights(group):
        later = group + WEIGHTS_AHEAD

        @pl.when(later < groups)
        def _():
            weight_load(later).start()
            weight_copy(later).start()

        weight_load(group).wait()
        weight_copy(group).wait()

    next_weights(0)
    gather(0, 0)
    total[places[0], :width], total[places[0], width:] = apply(places[0], 0)
    next_weights(1)
    gather(0, 1)
    own, other = apply(places[0], 1)
    total[places[0], :width] += own
    total[places[0], width:] += other

    @pl.when(me > 0)
    def _():
        low_copies[0].wait_recv()

    @pl.when(me < patches - 1)
    def _():
        high_copies[0].wait_recv()

    gather(1, 0)
    total[places[1], :width], total[places[1], width:] = apply(places[1], 0)
    gather(1, 1)
    own, other = apply(places[1], 1)
    total[places[1], :width] += own
    total[places[1], width:] += other

    @pl.when(up)
    def _():
        for copy in low_copies:
            copy.wait_send()

    @pl.when(down)
    def _():
        for copy in high_copies:
            copy.wait_send()

    for copy in small_copies:
        copy.start()
    for load in small_loads:
        load.wait()
    for place in (other_place, low_rim, high_rim):
        turned_ref[:, place] = turn(place)
    stores[0].start()
    for index in range(3):
        heads_turned[index] = heads_ref[index].T

    def group_step(group, _):
        next_weights(group)
        both_blocks(group)
        return 0

    lax.fori_loop(2, groups, group_step, 0)

    mine = pl.ds(pl.multiple_of(side * local, local), local)
    theirs = pl.ds(pl.multiple_of((1 - side) * local, local), local)
    conved_own = to_low(total[:, :width])
    conved_away[...] = to_low(total[:, width:])
    conved_ref[mine] = conved_own
    conved_copy = copies.to(sibling(), conved_away, conved_other, 10)
    conved_copy.start()
    small_copies[0].wait()
    linear = product(conved_own, encode_ref[...], 1, 0)
    linear += product(conved_away[...], encode_other[...], 1, 0)
    linear_ref[...] = linear
    first = layer_norm(linear)[0] * encode_gain_ref[...] + encode_shift_ref[...]
    first += to_wide(points_ref[...])
    first_ref[...] = first
    attend_out = layer_norm(first)[0] * attend_gain_ref[...] + attend_shift_ref[...]
    attend_ref[0] = to_low(attend_out)
    attend_copy = copies.to(sibling(), attend_ref.at[0], attend_other, 11)
    attend_copy.start()
    for index in range(3):
        projected_ref[index, :, :local] = to_low(
            product(heads_turned[index], attend_ref[0], 1, 1)
        )
    attend_copy.wait()
    attend_ref[1] = attend_other[...]
    for index in range(3):
        projected_ref[index, :, local:] = to_low(
            product(heads_turned[index], attend_other[...], 1, 1)
        )
    conved_copy.wait()
    conved_ref[theirs] = conved_other[...]
    for store in stores[2:]:
        store.start()

    row = lax.broadcasted_iota(jnp.int32, (HEAD_DIM, points), 0)
    ones = to_low(jnp.where(row == 0, 1.0, 0.0))
    place = (lax.broadcasted_iota(jnp.int32, (HEAD_DIM, points), 1) + side * local) & (points - 1)
    excluded = jnp.where(place < valid_ref[0], 0.0, MASKED)
    mask_ref[...] = to_low(jnp.where(row == 0, excluded, 0.0))

    def heads_step(step, _):
        operands, heads = [], []
        for offset in range(HEADS_STEP):
            head = step * HEADS_STEP + offset
            place = pl.ds(pl.multiple_of(head * HEAD_DIM, HEAD_DIM), HEAD_DIM)
            query, key, value = (projected_ref[index, place] for index in range(3))
            scaled = to_low(to_wide(query) * HEAD_DIM**-0.5)
            heads.append((head, place))
            operands.append(
                (
                    jnp.concatenate([scaled, ones], axis=0),
                    jnp.concatenate([key, mask_ref[...]], axis=0),
                    jnp.concatenate([value, ones], axis=0),
                )
            )

        def begin(unit):
            offset, start = unit
            queries, keys, _ = operands[offset]
            return product(keys, queries[:, start : start + CHUNK], 0, 0)

        def finish(unit, scores):
            offset, start = unit
            head, place = heads[offset]
            top = jnp.max(scores, axis=0, keepdims=True)
            mixed = product(operands[offset][2], to_low(jnp.exp(scores - top)), 1, 0)
            total = mixed[HEAD_DIM : HEAD_DIM + 1, :]
            now = slice(start, start + CHUNK)
            mixed_ref[place, now] = to_low(mixed[:HEAD_DIM] / total)
            log_ref[head, :, now] = top + jnp.log(total)

        units = [(h, c) for c in range(0, points, CHUNK) for h in range(HEADS_STEP)]
        staged(units, begin, finish)
        return 0

    lax.fori_loop(0, width // HEAD_DIM // HEADS_STEP, heads_step, 0)
    for copy in small_copies[1:]:
        copy.wait()
    for store in stores:
        store.wait()


def forward_start(
    near, points, conv_weight, encode_weight, norms, heads_weight, output_weight, expand_weight,
    reduce_weight, expand_bias, valid_count
):
    offsets, channels, width = conv_weight.shape
    local = points.shape[0]
    rows = 2 * local
    wide = rows + 2 * HALO
    groups = offsets // GROUP
    low, full = jnp.bfloat16, jnp.float32
    shape = jax.ShapeDtypeStruct
    anywhere = pl.BlockSpec(memory_space=pl.ANY)
    stored = [
        shape((channels, wide), low),
        shape((32, rows), full),
        shape((rows, width), low),
        shape((local, channels), full),
        shape((local, channels), full),
        shape((2, local, channels), low),
        shape((3, width, rows), low),
    ]
    away = [
        shape(array.shape, array.dtype)
        for array in (output_weight, expand_weight, reduce_weight, expand_bias)
    ]
    return pl.pallas_call(
        forward_kernel,
        in_specs=[vmem()] * 6 + [pl.BlockSpec(memory_space=pltpu.SMEM)] + [anywhere] * 7,
        out_specs=[vmem()] * 3 + [anywhere] * 11,
        out_shape=[
            shape((width, rows), low),
            shape((width // HEAD_DIM, 1, rows), full),
            shape((HEAD_DIM, rows), low),
        ]
        + stored
        + away,
        scratch_shapes=[
            *[pltpu.VMEM(each.shape, each.dtype) for each in stored],
            pltpu.VMEM((wide, channels), low),
            pltpu.VMEM((local, channels), full),
            pltpu.VMEM((local, GROUP * channels), low),
            pltpu.VMEM(conv_weight.shape, low),
            pltpu.VMEM(conv_weight.shape, low),
            pltpu.VMEM(encode_weight.shape, low),
            pltpu.VMEM(encode_weight.shape, low),
            pltpu.VMEM((local, width), low),
            pltpu.VMEM((local, width), low),
            pltpu.VMEM((local, channels), low),
            pltpu.VMEM(heads_weight.shape, low),
            pltpu.VMEM((3, width, channels), low),
            pltpu.VMEM((rows, 128), full),
            pltpu.VMEM((128, rows), full),
            pltpu.VMEM((channels, channels), low),
            pltpu.SemaphoreType.DMA((groups + 2,)),
            pltpu.SemaphoreType.DMA((len(stored),)),
            *copy_sems(12 + groups),
        ],
        compiler_params=pltpu.CompilerParams(
            vmem_limit_bytes=VMEM_BYTES, collective_id=2, has_side_effects=True
        ),
        cost_estimate=pl.CostEstimate(
            flops=60 * 10**9, bytes_accessed=20 * 10**6, transcendentals=0
        ),
    )(
        near, points, *norms, valid_count, conv_weight, encode_weight, heads_weight, output_weight,
        expand_weight, reduce_weight, expand_bias
    )


def partner_of(bit):
    me = lax.axis_index("pts")
    return me + (1 - 2 * ((me // (1 << bit)) % 2)) * (1 << bit)


def greet_partners():
    barrier = pltpu.get_barrier_semaphore()
    for bit in range(KERNEL_BITS):
        pl.semaphore_signal(
            barrier, inc=1, device_id={"pts": partner_of(bit)}, device_id_type=MESH
        )
    return barrier


class PairSums:
    def __init__(self, keep, sends, arrivals, send_sem, arrive_sem):
        self.keep, self.sends, self.arrivals = keep, sends, arrivals
        self.send_sem, self.arrive_sem = send_sem, arrive_sem

    def copy(self, stage, chunk, bit):
        return pltpu.make_async_remote_copy(
            src_ref=self.sends[stage].at[chunk],
            dst_ref=self.arrivals[stage].at[chunk],
            send_sem=self.send_sem.at[stage, chunk],
            recv_sem=self.arrive_sem.at[stage, chunk],
            device_id={"pts": partner_of(bit)},
            device_id_type=MESH,
        )

    def start(self, stage, chunk, kinds):
        for holds, order in kinds:
            if holds is True:
                self.copy(stage, chunk, order[stage]).start()
            else:

                @pl.when(holds)
                def _(order=order):
                    self.copy(stage, chunk, order[stage]).start()

    def advance(self, stage, chunk, kinds, finish):
        self.copy(stage, chunk, 0).wait()
        rows = self.keep.shape[2]
        low = rows - (rows >> stage)
        half = (rows - low) // 2
        arrived = self.arrivals[stage]
        if stage == len(self.sends) - 1:
            finish(self.keep[chunk, :, low:] + to_wide(arrived[chunk]))
            return
        self.sends[stage + 1][chunk] = to_low(
            self.keep[chunk, :, low : low + half] + to_wide(arrived[chunk, :, :half])
        )
        self.start(stage + 1, chunk, kinds)
        self.keep[chunk, :, low + half :] += to_wide(arrived[chunk, :, half:])


def pair_scratch(chunks, lead, rows, width, stages):
    halves = [(chunks, lead, rows >> (stage + 1), width) for stage in range(stages)]
    return (
        [pltpu.VMEM(halves[0], jnp.float32)]
        + [pltpu.VMEM(shape, jnp.bfloat16) for shape in halves]
        + [pltpu.VMEM(shape, jnp.bfloat16) for shape in halves]
        + [pltpu.SemaphoreType.DMA((stages, chunks))] * 2
    )


def pair_sums(scratch):
    stages = (len(scratch) - 3) // 2
    keep, rest = scratch[0], scratch[1:]
    return PairSums(keep, rest[:stages], rest[stages : 2 * stages], *rest[-2:])


def middle_kernel(
    mixed_ref,
    first_ref,
    output_ref,
    output_other_ref,
    output_bias_ref,
    gain_ref,
    shift_ref,
    cotangent_ref,
    bias_ref,
    bias_other_ref,
    reduce_bias_ref,
    mask_ref,
    log_ref,
    attend_gain_ref,
    encode_gain_ref,
    expand_hbm,
    expand_other_hbm,
    reduce_hbm,
    reduce_other_hbm,
    projected_hbm,
    heads_hbm,
    attend_hbm,
    linear_hbm,
    encode_hbm,
    conved_hbm,
    turned_hbm,
    near_hbm,
    conved_grad_ref,
    vectors_ref,
    reduce_sum_ref,
    expand_sum_ref,
    output_sum_ref,
    result_hbm,
    first_grad_hbm,
    extra_hbm,
    turned_other,
    near_other,
    first_grad_ref,
    extra_ref,
    expand_ref,
    expand_other_ref,
    reduce_ref,
    reduce_other_ref,
    projected_ref,
    heads_ref,
    attend_ref,
    linear_ref,
    encode_ref,
    conved_ref,
    result_ref,
    second_grad_ref,
    mixed_grad_ref,
    grad_ref,
    mixed_other,
    second_own,
    second_other,
    picks,
    top,
    away,
    arrived,
    attend_away,
    attend_arrived,
    linear_own,
    linear_other,
    load_sem,
    send_sem,
    arrive_sem,
    *scratch,
):
    local, channels = first_ref.shape
    width, points = mixed_ref.shape
    hidden_width = bias_ref.shape[1]
    columns = hidden_width // 2
    heads = width // HEAD_DIM
    half = channels // 2
    side = lax.axis_index("tp")
    mine = pl.ds(pl.multiple_of(side * local, local), local)
    theirs = pl.ds(pl.multiple_of((1 - side) * local, local), local)
    sums = pair_sums(scratch)
    copies = Copies(send_sem, arrive_sem)
    partner = {"pts": partner_of(SHARE_BIT)}
    share_copies = [
        copies.to(partner, turned_hbm.at[:half], turned_other, 0),
        copies.to(partner, near_hbm, near_other, 1),
    ]
    loads = [
        pltpu.make_async_copy(source, target, load_sem.at[index])
        for index, (source, target) in enumerate(
            (
                (expand_other_hbm, expand_other_ref),
                (reduce_other_hbm, reduce_other_ref),
                (expand_hbm, expand_ref),
                (reduce_hbm, reduce_ref),
                (projected_hbm, projected_ref),
                (heads_hbm, heads_ref),
                (attend_hbm, attend_ref),
                (linear_hbm, linear_ref),
                (encode_hbm, encode_ref),
                (conved_hbm, conved_ref),
            )
        )
    ]
    result_copy = pltpu.make_async_copy(result_ref, result_hbm, load_sem.at[len(loads)])
    first_store = pltpu.make_async_copy(first_grad_ref, first_grad_hbm, load_sem.at[len(loads) + 1])
    extra_stores = [
        pltpu.make_async_copy(
            extra_ref.at[kind], extra_hbm.at[kind], load_sem.at[len(loads) + 2 + kind]
        )
        for kind in range(2)
    ]

    for load in loads:
        load.start()
    barrier = greet_partners()
    pl.semaphore_signal(barrier, inc=1, device_id=sibling(), device_id_type=MESH)
    pl.semaphore_wait(barrier, KERNEL_BITS + 1)
    mixed_copy = copies.to(sibling(), mixed_ref.at[:, local:], mixed_other, 2)
    mixed_copy.start()
    for copy in share_copies:
        copy.start()

    cotangent = cotangent_ref[...]
    for kind in range(2):
        picks[kind] = nested_picks(channels, ORDERS[kind])
    cotangent_turned = to_low(product(picks[0], cotangent, 1, 1))
    second = first_ref[...] + output_bias_ref[...]
    second += product(mixed_ref[:, :local], output_ref[...], 0, 0)
    mixed_copy.wait()
    second += product(mixed_other[...], output_other_ref[...], 0, 0)
    normal, inverse = layer_norm(second)
    feed_low = to_low(normal * gain_ref[...] + shift_ref[...])
    feed_turned = to_low(product(picks[1], feed_low, 1, 1))
    result = second + reduce_bias_ref[...]
    feed_grad = jnp.zeros_like(second)
    for load in loads[:4]:
        load.wait()
    weight_copies = []
    for index, (up_ref, up_bias_ref, down_ref) in enumerate(
        (
            (expand_other_ref, bias_other_ref, reduce_other_ref),
            (expand_ref, bias_ref, reduce_ref),
        )
    ):
        bias_grads = []
        for start in range(0, hidden_width, columns):
            now = slice(start, start + columns)
            hidden = product(feed_low, up_ref[:, now], 1, 0) + up_bias_ref[:, now]
            below = 0.5 + 0.5 * lax.erf(hidden * 0.5**0.5)
            slope = below + hidden * (jnp.exp(-0.5 * hidden * hidden) * (0.5 / jnp.pi) ** 0.5)
            active = to_low(hidden * below)
            hidden_grad = to_low(product(cotangent, down_ref[now, :], 1, 1) * slope)
            result += product(active, down_ref[now, :], 1, 0)
            feed_grad += product(hidden_grad, up_ref[:, now], 1, 1)
            bias_grads.append(column_sum(to_wide(hidden_grad)))
            weight_grads = (
                product(cotangent_turned, active, 1, 0),
                product(feed_turned, hidden_grad, 1, 0),
            )
            for kind, weight_grad in enumerate(weight_grads):
                if index == 0:
                    away[kind, :, now] = weight_grad
                    copy = copies.to(
                        sibling(),
                        away.at[kind, :, now],
                        arrived.at[kind, :, now],
                        4 + len(weight_copies),
                    )
                    copy.start()
                    weight_copies.append(copy)
                else:
                    top[kind, :, now] = weight_grad[:half]
                    sums.keep[kind, 0, :, now] = weight_grad[half:]
        owner = (1 - side) if index == 0 else side
        for part, grads in enumerate(bias_grads):
            vectors_ref[pl.ds(8 + 2 * owner + part, 1), :] = grads
    result_ref[...] = to_low(result)
    result_copy.start()
    upstream = to_wide(cotangent)
    second_grad = upstream + norm_back(feed_grad, normal, inverse, gain_ref[...])
    second_grad_ref[...] = second_grad
    second_own[...] = to_low(second_grad)
    second_copy = copies.to(sibling(), second_own, second_other, 3)
    second_copy.start()
    vectors_ref[0:1] = column_sum(second_grad)
    vectors_ref[1:2] = column_sum(feed_grad * normal)
    vectors_ref[2:3] = column_sum(feed_grad)
    vectors_ref[3:4] = column_sum(upstream)
    mixed_grad_ref[:, :local] = to_low(product(output_ref[...], second_own[...], 1, 1))
    part = width // 2
    output_grads = [
        product(
            to_low(product(picks[kind], second_own[...], 1, 1)),
            mixed_ref[kind * part : (kind + 1) * part, :local],
            1,
            1,
        )
        for kind in range(2)
    ]
    second_copy.wait()
    mixed_grad_ref[:, local:] = to_low(product(output_ref[...], second_other[...], 1, 1))
    for kind in range(2):
        output_grad = output_grads[kind] + product(
            to_low(product(picks[kind], second_other[...], 1, 1)),
            mixed_ref[kind * part : (kind + 1) * part, local:],
            1,
            1,
        )
        sums.sends[0][kind, 0, :, hidden_width:] = to_low(output_grad[:half])
        sums.keep[kind, 0, :, hidden_width:] = output_grad[half:]
    for copy in weight_copies:
        copy.wait()
    for kind in range(2):
        sums.sends[0][kind, 0, :, :hidden_width] = to_low(top[kind] + arrived[kind, :half])
        sums.start(0, kind, ((True, ORDERS[kind]),))
        sums.keep[kind, 0, :, :hidden_width] += arrived[kind, half:]

    scale = HEAD_DIM**-0.5
    row = lax.broadcasted_iota(jnp.int32, (HEAD_DIM, points), 0)
    ones = to_low(jnp.where((row > 0) & (row < 4), 1.0, 0.0))
    for load in loads[4:]:
        load.wait()

    def three_parts(values, lead):
        upper = to_wide(to_low(values))
        middle = to_wide(to_low(values - upper))
        lower = values - upper - middle
        tail = jnp.where(row == 1, -upper, jnp.where(row == 2, -middle, 0.0))
        tail = jnp.where(row == 3, -lower, tail)
        return to_low(jnp.where(row == 0, lead, tail))

    def finish_sum(index, total):
        if index == 0:
            reduce_sum_ref[...] = total[0, :, :hidden_width]
        else:
            expand_sum_ref[...] = total[0, :, :hidden_width]
        output_sum_ref[:, index * part : (index + 1) * part] = total[0, :, hidden_width:]

    def heads_step(step, _):
        for stage, due in enumerate(SUM_STEPS):

            @pl.when(step == due)
            def _(stage=stage):
                for index in range(2):
                    sums.advance(
                        stage, index, ((True, ORDERS[index]),), functools.partial(finish_sum, index)
                    )

        operands, places = [], []
        for offset in range(HEADS_BACK_STEP):
            head = step * HEADS_BACK_STEP + offset
            place = pl.ds(pl.multiple_of(head * HEAD_DIM, HEAD_DIM), HEAD_DIM)
            places.append(place)
            query, key, value = (projected_ref[index, place] for index in range(3))
            grad = mixed_grad_ref[place]
            row_dot = column_sum(to_wide(grad) * to_wide(mixed_ref[place]))
            scaled = to_low(to_wide(query) * scale)
            operands.append(
                (
                    jnp.concatenate([scaled, three_parts(log_ref[head], 1.0)], axis=0),
                    jnp.concatenate([key, mask_ref[...] + ones], axis=0),
                    jnp.concatenate([value, ones], axis=0),
                    jnp.concatenate([grad, three_parts(row_dot, 0.0)], axis=0),
                    query,
                    key,
                    grad,
                )
            )
        totals = [None] * HEADS_BACK_STEP

        def begin(unit):
            offset, start = unit
            queries, keys, values, grads = operands[offset][:4]
            return (
                product(keys, queries[:, start : start + BACK_CHUNK], 0, 0),
                product(values, grads[:, start : start + BACK_CHUNK], 0, 0),
            )

        def finish(unit, ready):
            offset, start = unit
            scores, prob_grad = ready
            query, key, grad = operands[offset][4:]
            now = slice(start, start + BACK_CHUNK)
            probs = jnp.exp(scores)
            score_grad = to_low(probs * prob_grad)
            grad_ref[0, places[offset], now] = to_low(product(key, score_grad, 1, 0) * scale)
            value_part = product(grad[:, now], to_low(probs), 1, 1)
            key_part = product(query[:, now], score_grad, 1, 1)
            if totals[offset] is not None:
                key_part, value_part = key_part + totals[offset][0], value_part + totals[offset][1]
            totals[offset] = (key_part, value_part)

        units = [(h, c) for c in range(0, points, BACK_CHUNK) for h in range(HEADS_BACK_STEP)]
        staged(units, begin, finish)
        for offset in range(HEADS_BACK_STEP):
            grad_ref[1, places[offset]] = to_low(totals[offset][0] * scale)
            grad_ref[2, places[offset]] = to_low(totals[offset][1])
        return 0

    lax.fori_loop(0, heads // HEADS_BACK_STEP, heads_step, 0)

    def attend_grad(start):
        return sum(
            product(grad_ref[index, :, start : start + local].T, heads_ref[index], 1, 1)
            for index in range(3)
        )

    attend_away[...] = attend_grad(local)
    attend_copy = copies.to(sibling(), attend_away, attend_arrived, 8)
    attend_copy.start()
    for stage in range(len(SUM_STEPS), KERNEL_BITS):
        for index in range(2):
            sums.advance(
                stage, index, ((True, ORDERS[index]),), functools.partial(finish_sum, index)
            )
    upstream = attend_grad(0)
    for kind in range(2):
        turned = [to_low(product(picks[kind], attend_ref[i], 1, 1)) for i in range(2)]
        for index in (0, 1) if kind == 0 else (2,):
            extra_ref[kind, index % 2] = product(
                turned[0], grad_ref[index, :, :local], 1, 1
            ) + product(turned[1], grad_ref[index, :, local:], 1, 1)
    extra_stores[0].start()
    normal, inverse = layer_norm(first_ref[...])
    attend_copy.wait()
    upstream += attend_arrived[...]
    first_grad = second_grad_ref[...] + norm_back(upstream, normal, inverse, attend_gain_ref[...])
    first_grad_ref[...] = first_grad
    first_store.start()
    vectors_ref[4:5] = column_sum(upstream * normal)
    vectors_ref[5:6] = column_sum(upstream)
    normal, inverse = layer_norm(linear_ref[...])
    linear_own[...] = to_low(norm_back(first_grad, normal, inverse, encode_gain_ref[...]))
    linear_copy = copies.to(sibling(), linear_own, linear_other, 9)
    linear_copy.start()
    vectors_ref[6:7] = column_sum(first_grad * normal)
    vectors_ref[7:8] = column_sum(first_grad)
    conved_grad_ref[mine] = to_low(product(linear_own[...], encode_ref[...], 1, 1))
    encode_grad = product(
        to_low(product(picks[1], linear_own[...], 1, 1)), conved_ref[mine], 1, 0
    )
    linear_copy.wait()
    conved_grad_ref[theirs] = to_low(product(linear_other[...], encode_ref[...], 1, 1))
    extra_ref[1, 1] = encode_grad + product(
        to_low(product(picks[1], linear_other[...], 1, 1)), conved_ref[theirs], 1, 0
    )
    extra_stores[1].start()
    for store in (result_copy, first_store, *extra_stores):
        store.wait()
    for copy in share_copies:
        copy.wait()


def middle(near_operands, far_operands):
    local, channels = near_operands[1].shape
    width, rows = near_operands[0].shape
    hidden = near_operands[8].shape[1]
    turned, near = far_operands[-2:]
    kept = channels >> KERNEL_BITS
    low, full = jnp.bfloat16, jnp.float32
    shape = jax.ShapeDtypeStruct
    anywhere = pl.BlockSpec(memory_space=pl.ANY)
    loaded = far_operands[:-2]
    square = (local, channels)
    return pl.pallas_call(
        middle_kernel,
        in_specs=[vmem()] * len(near_operands) + [anywhere] * len(far_operands),
        out_specs=[vmem()] * 5 + [anywhere] * 5,
        out_shape=[
            shape((rows, width), low),
            shape((8 + 2 * hidden // channels, channels), full),
            shape((kept, hidden), full),
            shape((kept, hidden), full),
            shape((kept, width), full),
            shape(square, low),
            shape(square, full),
            shape((2, 2, channels, width), full),
            shape((channels // 2, turned.shape[1]), low),
            shape(near.shape, full),
        ],
        scratch_shapes=[
            pltpu.VMEM(square, full),
            pltpu.VMEM((2, 2, channels, width), full),
            *[pltpu.VMEM(each.shape, each.dtype) for each in loaded],
            pltpu.VMEM(square, low),
            pltpu.VMEM(square, full),
            pltpu.VMEM((width, rows), low),
            pltpu.VMEM((3, width, rows), low),
            pltpu.VMEM((width, local), low),
            pltpu.VMEM(square, low),
            pltpu.VMEM(square, low),
            pltpu.VMEM((2, channels, channels), low),
            pltpu.VMEM((2, channels // 2, hidden), full),
            pltpu.VMEM((2, channels, hidden), full),
            pltpu.VMEM((2, channels, hidden), full),
            pltpu.VMEM(square, full),
            pltpu.VMEM(square, full),
            pltpu.VMEM(square, low),
            pltpu.VMEM(square, low),
            pltpu.SemaphoreType.DMA((len(loaded) + 4,)),
            *copy_sems(10),
            *pair_scratch(2, 1, channels, hidden + width // 2, KERNEL_BITS),
        ],
        compiler_params=pltpu.CompilerParams(
            vmem_limit_bytes=VMEM_BYTES, collective_id=3, has_side_effects=True
        ),
        cost_estimate=pl.CostEstimate(
            flops=70 * 10**9, bytes_accessed=20 * 10**6, transcendentals=0
        ),
    )(*near_operands, *far_operands)


def conv_backward_kernel(
    near_ref,
    near_other_ref,
    turned_hbm,
    turned_other_hbm,
    grad_ref,
    weight_hbm,
    extra_hbm,
    vector_ref,
    first_grad_hbm,
    conv_sum_ref,
    heads_sum_ref,
    encode_sum_ref,
    points_grad_ref,
    *refs,
):
    vector_refs, refs = refs[:9], refs[9:]
    (
        spread,
        windows,
        gathered,
        grad_other,
        input_grad,
        input_arrived,
        rim_away,
        rim_arrived,
        vector_away,
        vector_arrived,
        send_sem,
        arrive_sem,
        weight_ref,
        first_grad_ref,
        turned_ref,
        turned_other_ref,
        extra_ref,
        load_sem,
    ) = refs[:18]
    sums, extra_sums = pair_sums(refs[18:27]), pair_sums(refs[27:])
    rows, width = grad_ref.shape
    local, channels = first_grad_ref.shape
    half = channels // 2
    quarter = half // 4
    blocks = rows // BLOCK
    extras = extra_hbm.shape[0]
    chunks = conv_sum_ref.shape[0]
    patches = lax.axis_size("pts")
    me, side = lax.axis_index("pts"), lax.axis_index("tp")
    copies = Copies(send_sem, arrive_sem)
    loads = [
        pltpu.make_async_copy(weight_hbm, weight_ref, load_sem.at[0]),
        pltpu.make_async_copy(first_grad_hbm, first_grad_ref, load_sem.at[1]),
    ]
    early_loads = [
        pltpu.make_async_copy(extra_hbm, extra_ref, load_sem.at[2]),
        pltpu.make_async_copy(turned_hbm.at[half:], turned_ref, load_sem.at[3]),
        pltpu.make_async_copy(turned_other_hbm, turned_other_ref, load_sem.at[4]),
    ]
    mine = pl.ds(pl.multiple_of(HALO + side * local, HALO), local)
    theirs = pl.ds(pl.multiple_of(HALO + (1 - side) * local, HALO), local)
    grad_copy = copies.to({"pts": partner_of(SHARE_BIT)}, grad_ref, grad_other, 0)
    input_copy = copies.to(sibling(), input_grad.at[theirs], input_arrived, 1)
    rims = (
        (me > 0, {"pts": (me + patches - 1) % patches, "tp": 1}, slice(0, HALO)),
        (me < patches - 1, {"pts": (me + 1) % patches, "tp": 0}, slice(HALO + rows, rows + 2 * HALO)),
    )
    rim_copies = [
        [copies.to(rim[1], rim_away.at[i], rim_arrived.at[core], 2 + i, 4 + core) for core in (0, 1)]
        for i, rim in enumerate(rims)
    ]
    has_rim = ((side == 0) & (me > 0)) | ((side == 1) & (me < patches - 1))
    first_sum = chunks // GROUP
    first_input = first_sum + chunks
    input_steps = chunks // GROUP

    def vector_copy(stage):
        device = sibling() if stage == 0 else {"pts": partner_of(stage - 1)}
        return copies.to(device, vector_away.at[stage], vector_arrived.at[stage], 6 + stage)

    def kinds(chunk):
        return ((chunk % 2 == 0, CONV_ORDERS[0]), (chunk % 2 == 1, CONV_ORDERS[1]))

    steps = first_input + 2 * input_steps

    def begin():
        for load in early_loads:
            load.start()
        barrier = greet_partners()
        pl.semaphore_signal(barrier, inc=1, device_id=sibling(), device_id_type=MESH)
        for core in range(2):

            @pl.when((side == 0) & (me > 0))
            def _(core=core):
                device = {"pts": (me + patches - 1) % patches, "tp": core}
                pl.semaphore_signal(barrier, inc=1, device_id=device, device_id_type=MESH)

            @pl.when((side == 1) & (me < patches - 1))
            def _(core=core):
                device = {"pts": (me + 1) % patches, "tp": core}
                pl.semaphore_signal(barrier, inc=1, device_id=device, device_id_type=MESH)

        sent = jnp.where(me > 0, 1, 0) + jnp.where(me < patches - 1, 1, 0)
        pl.semaphore_wait(barrier, KERNEL_BITS + 1 + sent)
        grad_copy.start()
        for load in loads:
            load.start()
        early_loads[0].wait()
        for index in range(extras):
            extra_sums.sends[0][index] = to_low(extra_ref[index, :, :half])
            extra_sums.start(0, index, ((True, ORDERS[index]),))
            extra_sums.keep[index] = extra_ref[index, :, half:]
        vector_away[0] = vector_ref[...]
        vector_copy(0).start()
        for load in early_loads[1:]:
            load.wait()
        for kind, places in enumerate(((0, 1, 2, 3), (0, 2, 1, 3))):
            for place, source in enumerate(places):
                now = slice(place * quarter, (place + 1) * quarter)
                low = source * quarter
                windows[kind, 0, now] = turned_ref[low : low + quarter, :]
                windows[kind, 1, now] = turned_other_ref[low : low + quarter, :]
        input_grad[...] = jnp.zeros_like(input_grad)

    def one_step(step, _):
        @pl.when(step < first_sum)
        def _():
            slots = to_wide(lax.broadcasted_iota(jnp.int32, (BLOCK, 1), 0))

            def spread_group(group, _):
                for offset in range(GROUP):
                    index = (step * GROUP + group) * GROUP + offset
                    near = near_ref[pl.ds(index, 1), :]
                    for part in range(blocks + 1):
                        low = max(part - 1, 0) * BLOCK
                        high = min(part + 1, blocks) * BLOCK
                        select = to_low(
                            jnp.where(near[:, low:high] - float(part * BLOCK) == slots, 1.0, 0.0)
                        )
                        spread[index, part * BLOCK : (part + 1) * BLOCK] = to_low(
                            product(select, grad_ref[low:high, :], 1, 0)
                        )
                return 0

            lax.fori_loop(0, GROUP, spread_group, 0, unroll=True)

        @pl.when((step >= first_sum) & (step < first_input))
        def _():
            chunk = step - first_sum
            pl.when(chunk == 0)(grad_copy.wait)
            slots = to_wide(lax.broadcasted_iota(jnp.int32, (2 * BLOCK, 1), 0))
            for offset in range(GROUP):
                near = near_other_ref[pl.ds(chunk * GROUP + offset, 1), :]
                for block in range(blocks):
                    low = block * BLOCK
                    select = to_low(
                        jnp.where(near[:, low : low + BLOCK] - float(low) == slots, 1.0, 0.0)
                    )
                    gathered[offset, :, low : low + BLOCK] = to_low(
                        product(windows[chunk % 2, 1, :, low : low + 2 * BLOCK], select, 1, 0)
                    )
            for offset in range(GROUP):
                weight_grad = product(windows[chunk % 2, 0], spread[chunk * GROUP + offset], 1, 0)
                weight_grad += product(gathered[offset], grad_other[...], 1, 0)
                sums.sends[0][chunk, offset] = to_low(weight_grad[: half // 2])
                sums.keep[chunk, offset] = weight_grad[half // 2 :]
            sums.start(0, chunk, kinds(chunk))

        @pl.when(step == first_input)
        def _():
            for load in loads:
                load.wait()

        beside = pl.ds(pl.multiple_of((1 - side) * (local + HALO), HALO), local + HALO)
        apart = pl.ds(pl.multiple_of(side * (2 * local + HALO), HALO), HALO)
        for phase, parts in enumerate(((beside, apart), (mine,))):
            start = first_input + phase * input_steps

            @pl.when((step >= start) & (step < start + input_steps))
            def _(start=start, parts=parts):
                def input_group(group, _):
                    for part in parts:
                        total = input_grad[part, :]
                        for offset in range(GROUP):
                            index = group * GROUP + offset
                            total += product(
                                spread[(step - start) * WIDE_GROUP + index, part, :],
                                weight_ref[(step - start) * WIDE_GROUP + index],
                                1,
                                1,
                            )
                        input_grad[part, :] = total
                    return 0

                lax.fori_loop(0, GROUP, input_group, 0, unroll=True)

        @pl.when(step == first_input + input_steps - 1)
        def _():
            input_copy.start()
            for index, (has, _, part) in enumerate(rims):
                rim_away[index] = to_low(input_grad[part, :])

                @pl.when(has)
                def _(index=index):
                    for core in range(2):

                        @pl.when(side == core)
                        def _(core=core):
                            rim_copies[index][core].start()

        @pl.when(step == steps - 1)
        def _():
            input_copy.wait()
            points_grad_ref[...] = first_grad_ref[...] + input_grad[mine, :] + input_arrived[...]

            @pl.when(has_rim)
            def _():
                edge = pl.ds(pl.multiple_of(side * (local - HALO), HALO), HALO)
                for core in range(2):
                    rim_copies[0][core].wait_recv()
                    points_grad_ref[edge, :] += to_wide(rim_arrived[core])

            for index, (has, _, part) in enumerate(rims):
                pl.when(has)(rim_copies[index][0].wait_send)

        for stage, due in enumerate(VECTOR_STEPS):

            @pl.when(step == due)
            def _(stage=stage):
                vector_copy(stage).wait()
                summed = vector_away[stage] + vector_arrived[stage]
                if stage < KERNEL_BITS:
                    vector_away[stage + 1] = summed
                    vector_copy(stage + 1).start()
                    return
                for index in range(8):
                    vector_refs[index][...] = summed[index : index + 1]
                for index in range(8, summed.shape[0]):
                    low = (index - 8) * channels
                    vector_refs[8][:, low : low + channels] = summed[index : index + 1]

        for stage in range(len(CONV_LAGS)):
            chunk = step - first_sum - CONV_LAGS[stage]

            @pl.when((chunk >= 0) & (chunk < chunks))
            def _(stage=stage, chunk=chunk):
                def finish(total):
                    conv_sum_ref[chunk] = total

                sums.advance(stage, chunk, kinds(chunk), finish)

        def finish_extra(index, total):
            if index == 0:
                heads_sum_ref[0:2] = total
            else:
                heads_sum_ref[2] = total[0]
                encode_sum_ref[...] = total[1]

        for stage, due in enumerate(EXTRA_STEPS):

            @pl.when(step == due)
            def _(stage=stage):
                for index in range(extras):
                    extra_sums.advance(
                        stage,
                        index,
                        ((True, ORDERS[index]),),
                        functools.partial(finish_extra, index),
                    )
        return 0

    begin()
    lax.fori_loop(0, steps, one_step, 0)


def conv_backward(
    near, near_other, turned, turned_other, grad, weight, extra, vector, first_grad
):
    offsets, channels, width = weight.shape
    wide = turned.shape[1]
    rows = grad.shape[0]
    local = first_grad.shape[0]
    chunks = offsets // GROUP
    low, full = jnp.bfloat16, jnp.float32
    kept = channels >> KERNEL_BITS
    shape = jax.ShapeDtypeStruct
    outs = [
        shape((chunks, GROUP, kept, width), full),
        shape((3, kept, width), full),
        shape((kept, width), full),
        shape(first_grad.shape, full),
        *[shape((1, channels), full)] * 8,
        shape((1, (vector.shape[0] - 8) * channels), full),
    ]

    anywhere = pl.BlockSpec(memory_space=pl.ANY)
    return pl.pallas_call(
        conv_backward_kernel,
        in_specs=[vmem()] * 2 + [anywhere] * 2 + [vmem()] + [anywhere] * 2 + [vmem(), anywhere],
        out_specs=[vmem()] * len(outs),
        out_shape=outs,
        scratch_shapes=[
            pltpu.VMEM((offsets, wide, width), low),
            pltpu.VMEM((2, 2, channels // 2, wide), low),
            pltpu.VMEM((GROUP, channels // 2, rows), low),
            pltpu.VMEM((rows, width), low),
            pltpu.VMEM((wide, channels), full),
            pltpu.VMEM((local, channels), full),
            pltpu.VMEM((2, HALO, channels), low),
            pltpu.VMEM((2, HALO, channels), low),
            pltpu.VMEM((KERNEL_BITS + 1, *vector.shape), full),
            pltpu.VMEM((KERNEL_BITS + 1, *vector.shape), full),
            *copy_sems(7 + KERNEL_BITS),
            pltpu.VMEM(weight.shape, low),
            pltpu.VMEM(first_grad.shape, full),
            pltpu.VMEM(turned_other.shape, low),
            pltpu.VMEM(turned_other.shape, low),
            pltpu.VMEM(extra.shape, full),
            pltpu.SemaphoreType.DMA((5,)),
            *pair_scratch(chunks, GROUP, channels // 2, width, len(CONV_LAGS)),
            *pair_scratch(*extra.shape, KERNEL_BITS),
        ],
        compiler_params=pltpu.CompilerParams(
            vmem_limit_bytes=VMEM_BYTES, collective_id=1, has_side_effects=True
        ),
        cost_estimate=pl.CostEstimate(
            flops=80 * 10**9, bytes_accessed=16 * 10**6, transcendentals=0
        ),
    )(near, near_other, turned, turned_other, grad, weight, extra, vector, first_grad)


def hand_over_kernel(*refs):
    count = (len(refs) - 1) // 3
    sem = refs[-1]
    inward = [
        pltpu.make_async_copy(refs[i], refs[2 * count + i], sem.at[i]) for i in range(count)
    ]
    outward = [
        pltpu.make_async_copy(refs[2 * count + i], refs[count + i], sem.at[count + i])
        for i in range(count)
    ]
    for copy in inward:
        copy.start()
    for arrive, leave in zip(inward, outward):
        arrive.wait()
        leave.start()
    for copy in outward:
        copy.wait()


def hand_over(arrays):
    anywhere = pl.BlockSpec(memory_space=pl.ANY)
    return pl.pallas_call(
        hand_over_kernel,
        in_specs=[anywhere] * len(arrays),
        out_specs=[anywhere] * len(arrays),
        out_shape=[jax.ShapeDtypeStruct(each.shape, each.dtype) for each in arrays],
        scratch_shapes=[pltpu.VMEM(each.shape, each.dtype) for each in arrays]
        + [pltpu.SemaphoreType.DMA((2 * len(arrays),))],
        compiler_params=pltpu.CompilerParams(vmem_limit_bytes=VMEM_BYTES),
    )(*arrays)


def exchange(values, bit):
    count = lax.axis_size("pts")
    return lax.ppermute(values, "pts", [(i, i ^ (1 << bit)) for i in range(count)])


def sum_rest(keep, axis):
    for bit in range(KERNEL_BITS, patch_bits()):
        half = keep.shape[axis] // 2
        away = lax.slice_in_dim(keep, 0, half, axis=axis)
        keep = lax.slice_in_dim(keep, half, 2 * half, axis=axis)
        keep = keep + to_wide(exchange(to_low(away), bit))
    return keep


def per_device(
    points,
    neighbours,
    valid_count,
    conv_weight,
    encode_weight,
    encode_gain,
    encode_shift,
    attend_gain,
    attend_shift,
    heads_weight,
    output_weight,
    output_bias,
    feed_gain,
    feed_shift,
    expand_weight,
    expand_bias,
    reduce_weight,
    reduce_bias,
    cotangent,
):
    local, channels = points.shape
    norms = [v[None, :] for v in (encode_gain, encode_shift, attend_gain, attend_shift)]
    (
        mixed, logs, mask, turned, near_columns, conved, linear, first, attend_in, projected,
        output_other, expand_other, reduce_other, bias_other,
    ) = forward_start(
        neighbours.T, points, conv_weight, encode_weight, norms, heads_weight, output_weight,
        expand_weight, reduce_weight, expand_bias[None, :], valid_count
    )
    (
        conved_grad, vector, reduce_sum, expand_sum, output_sum, result, first_grad, extra,
        turned_other, near_other,
    ) = middle(
        [
            mixed, first, output_weight, output_other, output_bias[None, :], feed_gain[None, :],
            feed_shift[None, :], cotangent, expand_bias[None, :], bias_other,
            reduce_bias[None, :], mask, logs, norms[2], norms[0],
        ],
        [
            expand_weight, expand_other, reduce_weight, reduce_other, projected, heads_weight,
            attend_in, linear, encode_weight, conved, turned, near_columns,
        ],
    )
    conv_sum, heads_sum, encode_sum, points_gradient, *vectors = conv_backward(
        near_columns, near_other, turned, turned_other, conved_grad, conv_weight, extra, vector,
        first_grad
    )
    for bit in range(KERNEL_BITS, patch_bits()):
        vectors = [each + exchange(each, bit) for each in vectors]
    parts = hand_over(
        [
            result,
            points_gradient,
            sum_rest(conv_sum, 2),
            sum_rest(encode_sum, 0),
            sum_rest(heads_sum, 1),
            sum_rest(output_sum, 0),
            sum_rest(expand_sum, 0),
            sum_rest(reduce_sum, 0),
            *vectors,
        ]
    )
    vectors = [each.reshape(-1) for each in parts[8:]]
    return (
        parts[0],
        parts[1],
        parts[2].reshape(-1, *parts[2].shape[2:]),
        parts[3].T,
        vectors[6],
        vectors[7],
        vectors[4],
        vectors[5],
        parts[4],
        parts[5].T,
        vectors[0],
        vectors[1],
        vectors[2],
        parts[6],
        vectors[8],
        parts[7].T,
        vectors[3],
    )


def solution(mesh):
    placed = (
        P(("pts", "tp"), None),
        P("pts", None),
        P("pts"),
        P(None, None, "tp"),
        P("tp", None),
        P(),
        P(),
        P(),
        P(),
        P(None, None, "tp"),
        P("tp", None),
        P(),
        P(),
        P(),
        P(None, "tp"),
        P("tp"),
        P("tp", None),
        P(),
        P(("pts", "tp"), None),
    )
    return jax.shard_map(
        per_device,
        mesh=mesh,
        in_specs=placed,
        out_specs=(
            P(("pts", "tp"), None),
            P(("pts", "tp"), None),
            P(None, "pts", "tp"),
            P("tp", "pts"),
            P(),
            P(),
            P(),
            P(),
            P(None, "pts", "tp"),
            P("tp", "pts"),
            P(),
            P(),
            P(),
            P("pts", "tp"),
            P(),
            P("tp", "pts"),
            P(),
        ),
        check_vma=False,
    )
```

```python
import functools

import jax
import jax.numpy as jnp
from jax import lax
from jax.experimental import pallas as pl
from jax.experimental.pallas import tpu as pltpu
from jax.sharding import PartitionSpec as P

MESH = pl.DeviceIdType.MESH
HEAD_DIM = 16
HALO = 128
BLOCK = 256
GROUP = 3
EPSILON = 1e-05
MASKED = -1e30
KERNEL_BITS = 4
ORDERS = ((0, 1, 2, 3), (1, 0, 2, 3))
VMEM_BYTES = 60 << 20
CHUNK = 512
BACK_CHUNK = 256
HEADS_STEP = 8
HEADS_BACK_STEP = 4
SUM_STEPS = (2, 3)
SHARE_BIT = 2
CONV_ORDERS = ((0, 1, 3), (1, 0, 3))
WINDOW_ORDER = (2, 0, 1, 3)
CONV_LAGS = (2, 4, 6)
EXTRA_STEPS = (2, 3, 5, 7)
VECTOR_STEPS = (1, 2, 3, 4, 5)
WEIGHTS_AHEAD = 3
WIDE_GROUP = 9


def to_low(values):
    return values.astype(jnp.bfloat16)


def to_wide(values):
    return values.astype(jnp.float32)


def product(left, right, left_dim, right_dim):
    dims = (((left_dim,), (right_dim,)), ((), ()))
    return lax.dot_general(left, right, dims, preferred_element_type=jnp.float32)


def layer_norm(values):
    row_mean = jnp.mean(values, axis=-1, keepdims=True)
    centred = values - row_mean
    inverse = lax.rsqrt(jnp.mean(centred * centred, axis=-1, keepdims=True) + EPSILON)
    return centred * inverse, inverse


def norm_back(upstream, normal_part, inverse, norm_gain):
    scaled = upstream * norm_gain
    across = (
        scaled
        - jnp.mean(scaled, axis=-1, keepdims=True)
        - normal_part * jnp.mean(scaled * normal_part, axis=-1, keepdims=True)
    )
    return across * inverse


def column_sum(values):
    return jnp.sum(values, axis=0, keepdims=True)


def nested_picks(channels, order):
    me = lax.axis_index("pts")
    order = order + tuple(range(KERNEL_BITS, patch_bits()))
    depth = channels >> len(order)
    lanes = 128
    place = lax.broadcasted_iota(jnp.int32, (channels, lanes), 0)
    picked = place & (depth - 1)
    for stage, bit in enumerate(order):
        kept = (place >> (channels.bit_length() - 2 - stage)) & 1
        picked = picked + (1 - ((kept + me // (1 << bit)) & 1)) * (depth << bit)
    column = lax.broadcasted_iota(jnp.int32, (channels, lanes), 1)
    return to_low(
        jnp.concatenate(
            [
                jnp.where(picked == column + low, 1.0, 0.0)
                for low in range(0, channels, lanes)
            ],
            axis=1,
        )
    )


class Copies:
    def __init__(self, send_sem, arrive_sem):
        self.send_sem, self.arrive_sem = send_sem, arrive_sem

    def to(self, device, source, target, send, arrive=None):
        return pltpu.make_async_remote_copy(
            src_ref=source,
            dst_ref=target,
            send_sem=self.send_sem.at[send],
            recv_sem=self.arrive_sem.at[send if arrive is None else arrive],
            device_id=device,
            device_id_type=MESH,
        )


def copy_sems(count):
    return [pltpu.SemaphoreType.DMA((count,))] * 2


def patch_bits():
    return lax.axis_size("pts").bit_length() - 1


def sibling():
    return {"tp": 1 - lax.axis_index("tp")}


def greet_sibling():
    barrier = pltpu.get_barrier_semaphore()
    pl.semaphore_signal(barrier, inc=1, device_id=sibling(), device_id_type=MESH)
    pl.semaphore_wait(barrier, 1)


def vmem():
    return pl.BlockSpec(memory_space=pltpu.VMEM)


def whole(array):
    zeros = (0,) * array.ndim
    return pl.BlockSpec(array.shape, lambda i: zeros, pipeline_mode=pl.Buffered(1))


def staged(units, begin, finish):
    ready = begin(units[0])
    for index, unit in enumerate(units):
        later = begin(units[index + 1]) if index + 1 < len(units) else None
        finish(unit, ready)
        ready = later


def forward_kernel(
    near_ref,
    points_ref,
    encode_gain_ref,
    encode_shift_ref,
    attend_gain_ref,
    attend_shift_ref,
    valid_ref,
    weight_hbm,
    encode_hbm,
    heads_hbm,
    output_hbm,
    expand_hbm,
    reduce_hbm,
    bias_hbm,
    mixed_ref,
    log_ref,
    mask_ref,
    turned_hbm,
    near_hbm,
    conved_hbm,
    linear_hbm,
    first_hbm,
    attend_hbm,
    projected_hbm,
    output_other,
    expand_other,
    reduce_other,
    bias_other,
    turned_ref,
    near_columns_ref,
    conved_ref,
    linear_ref,
    first_ref,
    attend_ref,
    projected_ref,
    window,
    total,
    rows,
    weight_own,
    weight_other,
    encode_ref,
    encode_other,
    conved_away,
    conved_other,
    attend_other,
    heads_ref,
    heads_turned,
    near_wide,
    near_tall,
    picks,
    load_sem,
    store_sem,
    send_sem,
    arrive_sem,
):
    local, channels = points_ref.shape
    offsets, _, width = weight_own.shape
    groups = offsets // GROUP
    points = 2 * local
    patches = lax.axis_size("pts")
    me, side = lax.axis_index("pts"), lax.axis_index("tp")
    copies = Copies(send_sem, arrive_sem)
    own_place = pl.ds(pl.multiple_of(HALO + side * local, HALO), local)
    other_place = pl.ds(pl.multiple_of(HALO + (1 - side) * local, HALO), local)
    low_rim, high_rim = slice(0, HALO), slice(HALO + points, 2 * HALO + points)
    points_copy = copies.to(sibling(), points_ref, window.at[own_place], 0)
    low_copies = [
        copies.to(
            {"pts": (me + 1) % patches, "tp": core},
            points_ref.at[local - HALO :],
            window.at[low_rim],
            3 + core,
            1,
        )
        for core in range(2)
    ]
    high_copies = [
        copies.to(
            {"pts": (me + patches - 1) % patches, "tp": core}, points_ref.at[0:HALO], window.at[high_rim], 3 + core, 2
        )
        for core in range(2)
    ]
    small_copies = [
        copies.to(sibling(), encode_hbm, encode_other, 5),
        copies.to(sibling(), output_hbm, output_other, 6),
        copies.to(sibling(), expand_hbm, expand_other, 7),
        copies.to(sibling(), reduce_hbm, reduce_other, 8),
        copies.to(sibling(), bias_hbm, bias_other, 9),
    ]
    small_loads = [
        pltpu.make_async_copy(encode_hbm, encode_ref, load_sem.at[groups]),
        pltpu.make_async_copy(heads_hbm, heads_ref, load_sem.at[groups + 1]),
    ]
    stores = [
        pltpu.make_async_copy(source, target, store_sem.at[index])
        for index, (source, target) in enumerate(
            (
                (turned_ref, turned_hbm),
                (near_columns_ref, near_hbm),
                (conved_ref, conved_hbm),
                (linear_ref, linear_hbm),
                (first_ref, first_hbm),
                (attend_ref, attend_hbm),
                (projected_ref, projected_hbm),
            )
        )
    ]
    up = (side == 1) & (me < patches - 1)
    down = (side == 0) & (me > 0)

    def weight_copy(group):
        part = pl.ds(group * GROUP, GROUP)
        return copies.to(sibling(), weight_hbm.at[part], weight_other.at[part], 12 + group)

    def weight_load(group):
        part = pl.ds(group * GROUP, GROUP)
        return pltpu.make_async_copy(
            weight_hbm.at[part], weight_own.at[part], load_sem.at[group]
        )

    def turn(place):
        return to_low(product(picks[...], window[place, :], 1, 1))

    for group in range(WEIGHTS_AHEAD):
        weight_load(group).start()
    for load in small_loads:
        load.start()
    barrier = pltpu.get_barrier_semaphore()
    pl.semaphore_signal(barrier, inc=1, device_id=sibling(), device_id_type=MESH)

    @pl.when(me > 0)
    def _():
        pl.semaphore_signal(
            barrier, inc=1, device_id={"pts": (me + patches - 1) % patches, "tp": 1}, device_id_type=MESH
        )

    @pl.when(me < patches - 1)
    def _():
        pl.semaphore_signal(
            barrier, inc=1, device_id={"pts": (me + 1) % patches, "tp": 0}, device_id_type=MESH
        )

    pl.semaphore_wait(barrier, jnp.where(up | down, 3, 1))
    points_copy.start()

    @pl.when(up)
    def _():
        for copy in low_copies:
            copy.start()

    @pl.when(down)
    def _():
        for copy in high_copies:
            copy.start()

    for group in range(WEIGHTS_AHEAD):
        weight_copy(group).start()
    window[own_place, :] = points_ref[...]

    @pl.when(me == 0)
    def _():
        window[low_rim, :] = jnp.zeros((HALO, channels), jnp.bfloat16)

    @pl.when(me == patches - 1)
    def _():
        window[high_rim, :] = jnp.zeros((HALO, channels), jnp.bfloat16)

    near_tall[...] = jnp.zeros_like(near_tall)
    near_tall[: near_ref.shape[0]] = to_wide(near_ref[...])
    near_columns_ref[...] = near_tall[: near_columns_ref.shape[0]]
    near_wide[...] = near_tall[...].T
    picks[...] = nested_picks(channels, WINDOW_ORDER)
    turned_ref[:, own_place] = turn(own_place)
    stores[1].start()
    points_copy.wait()

    lane = lax.broadcasted_iota(jnp.int32, (BLOCK, near_wide.shape[1]), 1)
    slots = to_wide(lax.broadcasted_iota(jnp.int32, (BLOCK, 2 * BLOCK), 1))
    places = [pl.ds(pl.multiple_of(block * BLOCK, BLOCK), BLOCK) for block in (1 - side, side)]

    def gather(index, group):
        low = pl.multiple_of(side * local + (1 - side, side)[index] * BLOCK, BLOCK)
        part = window[pl.ds(low, 2 * BLOCK), :]
        near = near_wide[pl.ds(low, BLOCK), :] - low.astype(jnp.float32)
        for offset in range(GROUP):
            chosen = jnp.where(lane == group * GROUP + offset, near, 0.0)
            column = jnp.sum(chosen, axis=1, keepdims=True)
            select = to_low(jnp.where(column == slots, 1.0, 0.0))
            rows[places[index], offset * channels : (offset + 1) * channels] = to_low(
                product(select, part, 1, 0)
            )

    def apply(place, group):
        picked = rows[place, :]
        part = pl.ds(group * GROUP, GROUP)
        flat = (GROUP * channels, width)
        return (
            product(picked, weight_own[part].reshape(flat), 1, 0),
            product(picked, weight_other[part].reshape(flat), 1, 0),
        )

    def both_blocks(group):
        gather(0, group)
        gather(1, group)
        own, other = apply(slice(None), group)
        total[:, :width] += own
        total[:, width:] += other

    def next_weights(group):
        later = group + WEIGHTS_AHEAD

        @pl.when(later < groups)
        def _():
            weight_load(later).start()
            weight_copy(later).start()

        weight_load(group).wait()
        weight_copy(group).wait()

    next_weights(0)
    gather(0, 0)
    total[places[0], :width], total[places[0], width:] = apply(places[0], 0)
    next_weights(1)
    gather(0, 1)
    own, other = apply(places[0], 1)
    total[places[0], :width] += own
    total[places[0], width:] += other

    @pl.when(me > 0)
    def _():
        low_copies[0].wait_recv()

    @pl.when(me < patches - 1)
    def _():
        high_copies[0].wait_recv()

    gather(1, 0)
    total[places[1], :width], total[places[1], width:] = apply(places[1], 0)
    gather(1, 1)
    own, other = apply(places[1], 1)
    total[places[1], :width] += own
    total[places[1], width:] += other

    @pl.when(up)
    def _():
        for copy in low_copies:
            copy.wait_send()

    @pl.when(down)
    def _():
        for copy in high_copies:
            copy.wait_send()

    for copy in small_copies:
        copy.start()
    for load in small_loads:
        load.wait()
    for place in (other_place, low_rim, high_rim):
        turned_ref[:, place] = turn(place)
    stores[0].start()
    for index in range(3):
        heads_turned[index] = heads_ref[index].T

    def group_step(group, _):
        next_weights(group)
        both_blocks(group)
        return 0

    lax.fori_loop(2, groups, group_step, 0)

    mine = pl.ds(pl.multiple_of(side * local, local), local)
    theirs = pl.ds(pl.multiple_of((1 - side) * local, local), local)
    conved_own = to_low(total[:, :width])
    conved_away[...] = to_low(total[:, width:])
    conved_ref[mine] = conved_own
    conved_copy = copies.to(sibling(), conved_away, conved_other, 10)
    conved_copy.start()
    small_copies[0].wait()
    linear = product(conved_own, encode_ref[...], 1, 0)
    linear += product(conved_away[...], encode_other[...], 1, 0)
    linear_ref[...] = linear
    first = layer_norm(linear)[0] * encode_gain_ref[...] + encode_shift_ref[...]
    first += to_wide(points_ref[...])
    first_ref[...] = first
    attend_out = layer_norm(first)[0] * attend_gain_ref[...] + attend_shift_ref[...]
    attend_ref[0] = to_low(attend_out)
    attend_copy = copies.to(sibling(), attend_ref.at[0], attend_other, 11)
    attend_copy.start()
    for index in range(3):
        projected_ref[index, :, :local] = to_low(
            product(heads_turned[index], attend_ref[0], 1, 1)
        )
    attend_copy.wait()
    attend_ref[1] = attend_other[...]
    for index in range(3):
        projected_ref[index, :, local:] = to_low(
            product(heads_turned[index], attend_other[...], 1, 1)
        )
    conved_copy.wait()
    conved_ref[theirs] = conved_other[...]
    for store in stores[2:]:
        store.start()

    row = lax.broadcasted_iota(jnp.int32, (HEAD_DIM, points), 0)
    ones = to_low(jnp.where(row == 0, 1.0, 0.0))
    place = (lax.broadcasted_iota(jnp.int32, (HEAD_DIM, points), 1) + side * local) & (points - 1)
    excluded = jnp.where(place < valid_ref[0], 0.0, MASKED)
    mask_ref[...] = to_low(jnp.where(row == 0, excluded, 0.0))

    def heads_step(step, _):
        operands, heads = [], []
        for offset in range(HEADS_STEP):
            head = step * HEADS_STEP + offset
            place = pl.ds(pl.multiple_of(head * HEAD_DIM, HEAD_DIM), HEAD_DIM)
            query, key, value = (projected_ref[index, place] for index in range(3))
            scaled = to_low(to_wide(query) * HEAD_DIM**-0.5)
            heads.append((head, place))
            operands.append(
                (
                    jnp.concatenate([scaled, ones], axis=0),
                    jnp.concatenate([key, mask_ref[...]], axis=0),
                    jnp.concatenate([value, ones], axis=0),
                )
            )

        def begin(unit):
            offset, start = unit
            queries, keys, _ = operands[offset]
            return product(keys, queries[:, start : start + CHUNK], 0, 0)

        def finish(unit, scores):
            offset, start = unit
            head, place = heads[offset]
            top = jnp.max(scores, axis=0, keepdims=True)
            mixed = product(operands[offset][2], to_low(jnp.exp(scores - top)), 1, 0)
            total = mixed[HEAD_DIM : HEAD_DIM + 1, :]
            now = slice(start, start + CHUNK)
            mixed_ref[place, now] = to_low(mixed[:HEAD_DIM] / total)
            log_ref[head, :, now] = top + jnp.log(total)

        units = [(h, c) for c in range(0, points, CHUNK) for h in range(HEADS_STEP)]
        staged(units, begin, finish)
        return 0

    lax.fori_loop(0, width // HEAD_DIM // HEADS_STEP, heads_step, 0)
    for copy in small_copies[1:]:
        copy.wait()
    for store in stores:
        store.wait()


def forward_start(
    near, points, conv_weight, encode_weight, norms, heads_weight, output_weight, expand_weight,
    reduce_weight, expand_bias, valid_count
):
    offsets, channels, width = conv_weight.shape
    local = points.shape[0]
    rows = 2 * local
    wide = rows + 2 * HALO
    groups = offsets // GROUP
    low, full = jnp.bfloat16, jnp.float32
    shape = jax.ShapeDtypeStruct
    anywhere = pl.BlockSpec(memory_space=pl.ANY)
    stored = [
        shape((channels, wide), low),
        shape((32, rows), full),
        shape((rows, width), low),
        shape((local, channels), full),
        shape((local, channels), full),
        shape((2, local, channels), low),
        shape((3, width, rows), low),
    ]
    away = [
        shape(array.shape, array.dtype)
        for array in (output_weight, expand_weight, reduce_weight, expand_bias)
    ]
    return pl.pallas_call(
        forward_kernel,
        in_specs=[vmem()] * 6 + [pl.BlockSpec(memory_space=pltpu.SMEM)] + [anywhere] * 7,
        out_specs=[vmem()] * 3 + [anywhere] * 11,
        out_shape=[
            shape((width, rows), low),
            shape((width // HEAD_DIM, 1, rows), full),
            shape((HEAD_DIM, rows), low),
        ]
        + stored
        + away,
        scratch_shapes=[
            *[pltpu.VMEM(each.shape, each.dtype) for each in stored],
            pltpu.VMEM((wide, channels), low),
            pltpu.VMEM((local, channels), full),
            pltpu.VMEM((local, GROUP * channels), low),
            pltpu.VMEM(conv_weight.shape, low),
            pltpu.VMEM(conv_weight.shape, low),
            pltpu.VMEM(encode_weight.shape, low),
            pltpu.VMEM(encode_weight.shape, low),
            pltpu.VMEM((local, width), low),
            pltpu.VMEM((local, width), low),
            pltpu.VMEM((local, channels), low),
            pltpu.VMEM(heads_weight.shape, low),
            pltpu.VMEM((3, width, channels), low),
            pltpu.VMEM((rows, 128), full),
            pltpu.VMEM((128, rows), full),
            pltpu.VMEM((channels, channels), low),
            pltpu.SemaphoreType.DMA((groups + 2,)),
            pltpu.SemaphoreType.DMA((len(stored),)),
            *copy_sems(12 + groups),
        ],
        compiler_params=pltpu.CompilerParams(
            vmem_limit_bytes=VMEM_BYTES, collective_id=2, has_side_effects=True
        ),
        cost_estimate=pl.CostEstimate(
            flops=60 * 10**9, bytes_accessed=20 * 10**6, transcendentals=0
        ),
    )(
        near, points, *norms, valid_count, conv_weight, encode_weight, heads_weight, output_weight,
        expand_weight, reduce_weight, expand_bias
    )


def partner_of(bit):
    me = lax.axis_index("pts")
    return me + (1 - 2 * ((me // (1 << bit)) % 2)) * (1 << bit)


def greet_partners():
    barrier = pltpu.get_barrier_semaphore()
    for bit in range(KERNEL_BITS):
        pl.semaphore_signal(
            barrier, inc=1, device_id={"pts": partner_of(bit)}, device_id_type=MESH
        )
    return barrier


class PairSums:
    def __init__(self, keep, sends, arrivals, send_sem, arrive_sem):
        self.keep, self.sends, self.arrivals = keep, sends, arrivals
        self.send_sem, self.arrive_sem = send_sem, arrive_sem

    def copy(self, stage, chunk, bit):
        return pltpu.make_async_remote_copy(
            src_ref=self.sends[stage].at[chunk],
            dst_ref=self.arrivals[stage].at[chunk],
            send_sem=self.send_sem.at[stage, chunk],
            recv_sem=self.arrive_sem.at[stage, chunk],
            device_id={"pts": partner_of(bit)},
            device_id_type=MESH,
        )

    def start(self, stage, chunk, kinds):
        for holds, order in kinds:
            if holds is True:
                self.copy(stage, chunk, order[stage]).start()
            else:

                @pl.when(holds)
                def _(order=order):
                    self.copy(stage, chunk, order[stage]).start()

    def advance(self, stage, chunk, kinds, finish):
        self.copy(stage, chunk, 0).wait()
        rows = self.keep.shape[2]
        low = rows - (rows >> stage)
        half = (rows - low) // 2
        arrived = self.arrivals[stage]
        if stage == len(self.sends) - 1:
            finish(self.keep[chunk, :, low:] + to_wide(arrived[chunk]))
            return
        self.sends[stage + 1][chunk] = to_low(
            self.keep[chunk, :, low : low + half] + to_wide(arrived[chunk, :, :half])
        )
        self.start(stage + 1, chunk, kinds)
        self.keep[chunk, :, low + half :] += to_wide(arrived[chunk, :, half:])


def pair_scratch(chunks, lead, rows, width, stages):
    halves = [(chunks, lead, rows >> (stage + 1), width) for stage in range(stages)]
    return (
        [pltpu.VMEM(halves[0], jnp.float32)]
        + [pltpu.VMEM(shape, jnp.bfloat16) for shape in halves]
        + [pltpu.VMEM(shape, jnp.bfloat16) for shape in halves]
        + [pltpu.SemaphoreType.DMA((stages, chunks))] * 2
    )


def pair_sums(scratch):
    stages = (len(scratch) - 3) // 2
    keep, rest = scratch[0], scratch[1:]
    return PairSums(keep, rest[:stages], rest[stages : 2 * stages], *rest[-2:])


def middle_kernel(
    mixed_ref,
    first_ref,
    output_ref,
    output_other_ref,
    output_bias_ref,
    gain_ref,
    shift_ref,
    cotangent_ref,
    bias_ref,
    bias_other_ref,
    reduce_bias_ref,
    mask_ref,
    log_ref,
    attend_gain_ref,
    encode_gain_ref,
    expand_hbm,
    expand_other_hbm,
    reduce_hbm,
    reduce_other_hbm,
    projected_hbm,
    heads_hbm,
    attend_hbm,
    linear_hbm,
    encode_hbm,
    conved_hbm,
    turned_hbm,
    near_hbm,
    conved_grad_ref,
    vectors_ref,
    reduce_sum_ref,
    expand_sum_ref,
    output_sum_ref,
    result_hbm,
    first_grad_hbm,
    extra_hbm,
    turned_other,
    near_other,
    first_grad_ref,
    extra_ref,
    expand_ref,
    expand_other_ref,
    reduce_ref,
    reduce_other_ref,
    projected_ref,
    heads_ref,
    attend_ref,
    linear_ref,
    encode_ref,
    conved_ref,
    result_ref,
    second_grad_ref,
    mixed_grad_ref,
    grad_ref,
    mixed_other,
    second_own,
    second_other,
    picks,
    top,
    away,
    arrived,
    attend_away,
    attend_arrived,
    linear_own,
    linear_other,
    load_sem,
    send_sem,
    arrive_sem,
    *scratch,
):
    local, channels = first_ref.shape
    width, points = mixed_ref.shape
    hidden_width = bias_ref.shape[1]
    columns = hidden_width // 2
    heads = width // HEAD_DIM
    half = channels // 2
    side = lax.axis_index("tp")
    mine = pl.ds(pl.multiple_of(side * local, local), local)
    theirs = pl.ds(pl.multiple_of((1 - side) * local, local), local)
    sums = pair_sums(scratch)
    copies = Copies(send_sem, arrive_sem)
    partner = {"pts": partner_of(SHARE_BIT)}
    share_copies = [
        copies.to(partner, turned_hbm.at[:half], turned_other, 0),
        copies.to(partner, near_hbm, near_other, 1),
    ]
    loads = [
        pltpu.make_async_copy(source, target, load_sem.at[index])
        for index, (source, target) in enumerate(
            (
                (expand_other_hbm, expand_other_ref),
                (reduce_other_hbm, reduce_other_ref),
                (expand_hbm, expand_ref),
                (reduce_hbm, reduce_ref),
                (projected_hbm, projected_ref),
                (heads_hbm, heads_ref),
                (attend_hbm, attend_ref),
                (linear_hbm, linear_ref),
                (encode_hbm, encode_ref),
                (conved_hbm, conved_ref),
            )
        )
    ]
    result_copy = pltpu.make_async_copy(result_ref, result_hbm, load_sem.at[len(loads)])
    first_store = pltpu.make_async_copy(first_grad_ref, first_grad_hbm, load_sem.at[len(loads) + 1])
    extra_stores = [
        pltpu.make_async_copy(
            extra_ref.at[kind], extra_hbm.at[kind], load_sem.at[len(loads) + 2 + kind]
        )
        for kind in range(2)
    ]

    for load in loads:
        load.start()
    barrier = greet_partners()
    pl.semaphore_signal(barrier, inc=1, device_id=sibling(), device_id_type=MESH)
    pl.semaphore_wait(barrier, KERNEL_BITS + 1)
    mixed_copy = copies.to(sibling(), mixed_ref.at[:, local:], mixed_other, 2)
    mixed_copy.start()
    for copy in share_copies:
        copy.start()

    cotangent = cotangent_ref[...]
    for kind in range(2):
        picks[kind] = nested_picks(channels, ORDERS[kind])
    cotangent_turned = to_low(product(picks[0], cotangent, 1, 1))
    second = first_ref[...] + output_bias_ref[...]
    second += product(mixed_ref[:, :local], output_ref[...], 0, 0)
    mixed_copy.wait()
    second += product(mixed_other[...], output_other_ref[...], 0, 0)
    normal, inverse = layer_norm(second)
    feed_low = to_low(normal * gain_ref[...] + shift_ref[...])
    feed_turned = to_low(product(picks[1], feed_low, 1, 1))
    result = second + reduce_bias_ref[...]
    feed_grad = jnp.zeros_like(second)
    for load in loads[:4]:
        load.wait()
    weight_copies = []
    for index, (up_ref, up_bias_ref, down_ref) in enumerate(
        (
            (expand_other_ref, bias_other_ref, reduce_other_ref),
            (expand_ref, bias_ref, reduce_ref),
        )
    ):
        bias_grads = []
        for start in range(0, hidden_width, columns):
            now = slice(start, start + columns)
            hidden = product(feed_low, up_ref[:, now], 1, 0) + up_bias_ref[:, now]
            below = 0.5 + 0.5 * lax.erf(hidden * 0.5**0.5)
            slope = below + hidden * (jnp.exp(-0.5 * hidden * hidden) * (0.5 / jnp.pi) ** 0.5)
            active = to_low(hidden * below)
            hidden_grad = to_low(product(cotangent, down_ref[now, :], 1, 1) * slope)
            result += product(active, down_ref[now, :], 1, 0)
            feed_grad += product(hidden_grad, up_ref[:, now], 1, 1)
            bias_grads.append(column_sum(to_wide(hidden_grad)))
            weight_grads = (
                product(cotangent_turned, active, 1, 0),
                product(feed_turned, hidden_grad, 1, 0),
            )
            for kind, weight_grad in enumerate(weight_grads):
                if index == 0:
                    away[kind, :, now] = weight_grad
                    copy = copies.to(
                        sibling(),
                        away.at[kind, :, now],
                        arrived.at[kind, :, now],
                        4 + len(weight_copies),
                    )
                    copy.start()
                    weight_copies.append(copy)
                else:
                    top[kind, :, now] = weight_grad[:half]
                    sums.keep[kind, 0, :, now] = weight_grad[half:]
        owner = (1 - side) if index == 0 else side
        for part, grads in enumerate(bias_grads):
            vectors_ref[pl.ds(8 + 2 * owner + part, 1), :] = grads
    result_ref[...] = to_low(result)
    result_copy.start()
    upstream = to_wide(cotangent)
    second_grad = upstream + norm_back(feed_grad, normal, inverse, gain_ref[...])
    second_grad_ref[...] = second_grad
    second_own[...] = to_low(second_grad)
    second_copy = copies.to(sibling(), second_own, second_other, 3)
    second_copy.start()
    vectors_ref[0:1] = column_sum(second_grad)
    vectors_ref[1:2] = column_sum(feed_grad * normal)
    vectors_ref[2:3] = column_sum(feed_grad)
    vectors_ref[3:4] = column_sum(upstream)
    mixed_grad_ref[:, :local] = to_low(product(output_ref[...], second_own[...], 1, 1))
    part = width // 2
    output_grads = [
        product(
            to_low(product(picks[kind], second_own[...], 1, 1)),
            mixed_ref[kind * part : (kind + 1) * part, :local],
            1,
            1,
        )
        for kind in range(2)
    ]
    second_copy.wait()
    mixed_grad_ref[:, local:] = to_low(product(output_ref[...], second_other[...], 1, 1))
    for kind in range(2):
        output_grad = output_grads[kind] + product(
            to_low(product(picks[kind], second_other[...], 1, 1)),
            mixed_ref[kind * part : (kind + 1) * part, local:],
            1,
            1,
        )
        sums.sends[0][kind, 0, :, hidden_width:] = to_low(output_grad[:half])
        sums.keep[kind, 0, :, hidden_width:] = output_grad[half:]
    for copy in weight_copies:
        copy.wait()
    for kind in range(2):
        sums.sends[0][kind, 0, :, :hidden_width] = to_low(top[kind] + arrived[kind, :half])
        sums.start(0, kind, ((True, ORDERS[kind]),))
        sums.keep[kind, 0, :, :hidden_width] += arrived[kind, half:]

    scale = HEAD_DIM**-0.5
    row = lax.broadcasted_iota(jnp.int32, (HEAD_DIM, points), 0)
    ones = to_low(jnp.where((row > 0) & (row < 4), 1.0, 0.0))
    for load in loads[4:]:
        load.wait()

    def three_parts(values, lead):
        upper = to_wide(to_low(values))
        middle = to_wide(to_low(values - upper))
        lower = values - upper - middle
        tail = jnp.where(row == 1, -upper, jnp.where(row == 2, -middle, 0.0))
        tail = jnp.where(row == 3, -lower, tail)
        return to_low(jnp.where(row == 0, lead, tail))

    def finish_sum(index, total):
        if index == 0:
            reduce_sum_ref[...] = total[0, :, :hidden_width]
        else:
            expand_sum_ref[...] = total[0, :, :hidden_width]
        output_sum_ref[:, index * part : (index + 1) * part] = total[0, :, hidden_width:]

    def heads_step(step, _):
        for stage, due in enumerate(SUM_STEPS):

            @pl.when(step == due)
            def _(stage=stage):
                for index in range(2):
                    sums.advance(
                        stage, index, ((True, ORDERS[index]),), functools.partial(finish_sum, index)
                    )

        operands, places = [], []
        for offset in range(HEADS_BACK_STEP):
            head = step * HEADS_BACK_STEP + offset
            place = pl.ds(pl.multiple_of(head * HEAD_DIM, HEAD_DIM), HEAD_DIM)
            places.append(place)
            query, key, value = (projected_ref[index, place] for index in range(3))
            grad = mixed_grad_ref[place]
            row_dot = column_sum(to_wide(grad) * to_wide(mixed_ref[place]))
            scaled = to_low(to_wide(query) * scale)
            operands.append(
                (
                    jnp.concatenate([scaled, three_parts(log_ref[head], 1.0)], axis=0),
                    jnp.concatenate([key, mask_ref[...] + ones], axis=0),
                    jnp.concatenate([value, ones], axis=0),
                    jnp.concatenate([grad, three_parts(row_dot, 0.0)], axis=0),
                    query,
                    key,
                    grad,
                )
            )
        totals = [None] * HEADS_BACK_STEP

        def begin(unit):
            offset, start = unit
            queries, keys, values, grads = operands[offset][:4]
            return (
                product(keys, queries[:, start : start + BACK_CHUNK], 0, 0),
                product(values, grads[:, start : start + BACK_CHUNK], 0, 0),
            )

        def finish(unit, ready):
            offset, start = unit
            scores, prob_grad = ready
            query, key, grad = operands[offset][4:]
            now = slice(start, start + BACK_CHUNK)
            probs = jnp.exp(scores)
            score_grad = to_low(probs * prob_grad)
            grad_ref[0, places[offset], now] = to_low(product(key, score_grad, 1, 0) * scale)
            value_part = product(grad[:, now], to_low(probs), 1, 1)
            key_part = product(query[:, now], score_grad, 1, 1)
            if totals[offset] is not None:
                key_part, value_part = key_part + totals[offset][0], value_part + totals[offset][1]
            totals[offset] = (key_part, value_part)

        units = [(h, c) for c in range(0, points, BACK_CHUNK) for h in range(HEADS_BACK_STEP)]
        staged(units, begin, finish)
        for offset in range(HEADS_BACK_STEP):
            grad_ref[1, places[offset]] = to_low(totals[offset][0] * scale)
            grad_ref[2, places[offset]] = to_low(totals[offset][1])
        return 0

    lax.fori_loop(0, heads // HEADS_BACK_STEP, heads_step, 0)

    def last_sums(stage):
        for index in range(2):
            sums.advance(
                stage, index, ((True, ORDERS[index]),), functools.partial(finish_sum, index)
            )

    def attend_grad(start):
        return sum(
            product(grad_ref[index, :, start : start + local].T, heads_ref[index], 1, 1)
            for index in range(3)
        )

    attend_away[...] = attend_grad(local)
    attend_copy = copies.to(sibling(), attend_away, attend_arrived, 8)
    attend_copy.start()
    last_sums(KERNEL_BITS - 2)
    upstream = attend_grad(0)
    for kind in range(2):
        turned = [to_low(product(picks[kind], attend_ref[i], 1, 1)) for i in range(2)]
        for index in (0, 1) if kind == 0 else (2,):
            extra_ref[kind, index % 2] = product(
                turned[0], grad_ref[index, :, :local], 1, 1
            ) + product(turned[1], grad_ref[index, :, local:], 1, 1)
    extra_stores[0].start()
    normal, inverse = layer_norm(first_ref[...])
    attend_copy.wait()
    upstream += attend_arrived[...]
    first_grad = second_grad_ref[...] + norm_back(upstream, normal, inverse, attend_gain_ref[...])
    first_grad_ref[...] = first_grad
    first_store.start()
    vectors_ref[4:5] = column_sum(upstream * normal)
    vectors_ref[5:6] = column_sum(upstream)
    normal, inverse = layer_norm(linear_ref[...])
    linear_own[...] = to_low(norm_back(first_grad, normal, inverse, encode_gain_ref[...]))
    linear_copy = copies.to(sibling(), linear_own, linear_other, 9)
    linear_copy.start()
    vectors_ref[6:7] = column_sum(first_grad * normal)
    vectors_ref[7:8] = column_sum(first_grad)
    conved_grad_ref[mine] = to_low(product(linear_own[...], encode_ref[...], 1, 1))
    encode_grad = product(
        to_low(product(picks[1], linear_own[...], 1, 1)), conved_ref[mine], 1, 0
    )
    linear_copy.wait()
    conved_grad_ref[theirs] = to_low(product(linear_other[...], encode_ref[...], 1, 1))
    extra_ref[1, 1] = encode_grad + product(
        to_low(product(picks[1], linear_other[...], 1, 1)), conved_ref[theirs], 1, 0
    )
    extra_stores[1].start()
    last_sums(KERNEL_BITS - 1)
    for store in (result_copy, first_store, *extra_stores):
        store.wait()
    for copy in share_copies:
        copy.wait()


def middle(near_operands, far_operands):
    local, channels = near_operands[1].shape
    width, rows = near_operands[0].shape
    hidden = near_operands[8].shape[1]
    turned, near = far_operands[-2:]
    kept = channels >> KERNEL_BITS
    low, full = jnp.bfloat16, jnp.float32
    shape = jax.ShapeDtypeStruct
    anywhere = pl.BlockSpec(memory_space=pl.ANY)
    loaded = far_operands[:-2]
    square = (local, channels)
    return pl.pallas_call(
        middle_kernel,
        in_specs=[vmem()] * len(near_operands) + [anywhere] * len(far_operands),
        out_specs=[vmem()] * 5 + [anywhere] * 5,
        out_shape=[
            shape((rows, width), low),
            shape((8 + 2 * hidden // channels, channels), full),
            shape((kept, hidden), full),
            shape((kept, hidden), full),
            shape((kept, width), full),
            shape(square, low),
            shape(square, full),
            shape((2, 2, channels, width), full),
            shape((channels // 2, turned.shape[1]), low),
            shape(near.shape, full),
        ],
        scratch_shapes=[
            pltpu.VMEM(square, full),
            pltpu.VMEM((2, 2, channels, width), full),
            *[pltpu.VMEM(each.shape, each.dtype) for each in loaded],
            pltpu.VMEM(square, low),
            pltpu.VMEM(square, full),
            pltpu.VMEM((width, rows), low),
            pltpu.VMEM((3, width, rows), low),
            pltpu.VMEM((width, local), low),
            pltpu.VMEM(square, low),
            pltpu.VMEM(square, low),
            pltpu.VMEM((2, channels, channels), low),
            pltpu.VMEM((2, channels // 2, hidden), full),
            pltpu.VMEM((2, channels, hidden), full),
            pltpu.VMEM((2, channels, hidden), full),
            pltpu.VMEM(square, full),
            pltpu.VMEM(square, full),
            pltpu.VMEM(square, low),
            pltpu.VMEM(square, low),
            pltpu.SemaphoreType.DMA((len(loaded) + 4,)),
            *copy_sems(10),
            *pair_scratch(2, 1, channels, hidden + width // 2, KERNEL_BITS),
        ],
        compiler_params=pltpu.CompilerParams(
            vmem_limit_bytes=VMEM_BYTES, collective_id=3, has_side_effects=True
        ),
        cost_estimate=pl.CostEstimate(
            flops=70 * 10**9, bytes_accessed=20 * 10**6, transcendentals=0
        ),
    )(*near_operands, *far_operands)


def conv_backward_kernel(
    near_ref,
    near_other_ref,
    turned_hbm,
    turned_other_hbm,
    grad_ref,
    weight_hbm,
    extra_hbm,
    vector_ref,
    first_grad_hbm,
    conv_sum_ref,
    heads_sum_ref,
    encode_sum_ref,
    points_grad_ref,
    *refs,
):
    vector_refs, refs = refs[:9], refs[9:]
    (
        spread,
        windows,
        gathered,
        grad_other,
        input_grad,
        input_arrived,
        rim_away,
        rim_arrived,
        vector_away,
        vector_arrived,
        send_sem,
        arrive_sem,
        weight_ref,
        first_grad_ref,
        turned_ref,
        turned_other_ref,
        extra_ref,
        load_sem,
    ) = refs[:18]
    sums, extra_sums = pair_sums(refs[18:27]), pair_sums(refs[27:])
    rows, width = grad_ref.shape
    local, channels = first_grad_ref.shape
    half = channels // 2
    quarter = half // 4
    blocks = rows // BLOCK
    extras = extra_hbm.shape[0]
    chunks = conv_sum_ref.shape[0]
    patches = lax.axis_size("pts")
    me, side = lax.axis_index("pts"), lax.axis_index("tp")
    copies = Copies(send_sem, arrive_sem)
    loads = [
        pltpu.make_async_copy(weight_hbm, weight_ref, load_sem.at[0]),
        pltpu.make_async_copy(first_grad_hbm, first_grad_ref, load_sem.at[1]),
    ]
    early_loads = [
        pltpu.make_async_copy(extra_hbm, extra_ref, load_sem.at[2]),
        pltpu.make_async_copy(turned_hbm.at[half:], turned_ref, load_sem.at[3]),
        pltpu.make_async_copy(turned_other_hbm, turned_other_ref, load_sem.at[4]),
    ]
    mine = pl.ds(pl.multiple_of(HALO + side * local, HALO), local)
    theirs = pl.ds(pl.multiple_of(HALO + (1 - side) * local, HALO), local)
    grad_copy = copies.to({"pts": partner_of(SHARE_BIT)}, grad_ref, grad_other, 0)
    input_copy = copies.to(sibling(), input_grad.at[theirs], input_arrived, 1)
    rims = (
        (me > 0, {"pts": (me + patches - 1) % patches, "tp": 1}, slice(0, HALO)),
        (me < patches - 1, {"pts": (me + 1) % patches, "tp": 0}, slice(HALO + rows, rows + 2 * HALO)),
    )
    rim_copies = [
        [copies.to(rim[1], rim_away.at[i], rim_arrived.at[core], 2 + i, 4 + core) for core in (0, 1)]
        for i, rim in enumerate(rims)
    ]
    has_rim = ((side == 0) & (me > 0)) | ((side == 1) & (me < patches - 1))
    first_sum = chunks // GROUP
    first_input = first_sum + chunks
    input_steps = chunks // GROUP

    def vector_copy(stage):
        device = sibling() if stage == 0 else {"pts": partner_of(stage - 1)}
        return copies.to(device, vector_away.at[stage], vector_arrived.at[stage], 6 + stage)

    def kinds(chunk):
        return ((chunk % 2 == 0, CONV_ORDERS[0]), (chunk % 2 == 1, CONV_ORDERS[1]))

    steps = first_input + 2 * input_steps

    def begin():
        for load in early_loads:
            load.start()
        barrier = greet_partners()
        pl.semaphore_signal(barrier, inc=1, device_id=sibling(), device_id_type=MESH)
        for core in range(2):

            @pl.when((side == 0) & (me > 0))
            def _(core=core):
                device = {"pts": (me + patches - 1) % patches, "tp": core}
                pl.semaphore_signal(barrier, inc=1, device_id=device, device_id_type=MESH)

            @pl.when((side == 1) & (me < patches - 1))
            def _(core=core):
                device = {"pts": (me + 1) % patches, "tp": core}
                pl.semaphore_signal(barrier, inc=1, device_id=device, device_id_type=MESH)

        sent = jnp.where(me > 0, 1, 0) + jnp.where(me < patches - 1, 1, 0)
        pl.semaphore_wait(barrier, KERNEL_BITS + 1 + sent)
        grad_copy.start()
        for load in loads:
            load.start()
        early_loads[0].wait()
        for index in range(extras):
            extra_sums.sends[0][index] = to_low(extra_ref[index, :, :half])
            extra_sums.start(0, index, ((True, ORDERS[index]),))
            extra_sums.keep[index] = extra_ref[index, :, half:]
        vector_away[0] = vector_ref[...]
        vector_copy(0).start()
        for load in early_loads[1:]:
            load.wait()
        for kind, places in enumerate(((0, 1, 2, 3), (0, 2, 1, 3))):
            for place, source in enumerate(places):
                now = slice(place * quarter, (place + 1) * quarter)
                low = source * quarter
                windows[kind, 0, now] = turned_ref[low : low + quarter, :]
                windows[kind, 1, now] = turned_other_ref[low : low + quarter, :]
        input_grad[...] = jnp.zeros_like(input_grad)

    def one_step(step, _):
        @pl.when(step < first_sum)
        def _():
            slots = to_wide(lax.broadcasted_iota(jnp.int32, (BLOCK, 1), 0))

            def spread_group(group, _):
                for offset in range(GROUP):
                    index = (step * GROUP + group) * GROUP + offset
                    near = near_ref[pl.ds(index, 1), :]
                    for part in range(blocks + 1):
                        low = max(part - 1, 0) * BLOCK
                        high = min(part + 1, blocks) * BLOCK
                        select = to_low(
                            jnp.where(near[:, low:high] - float(part * BLOCK) == slots, 1.0, 0.0)
                        )
                        spread[index, part * BLOCK : (part + 1) * BLOCK] = to_low(
                            product(select, grad_ref[low:high, :], 1, 0)
                        )
                return 0

            lax.fori_loop(0, GROUP, spread_group, 0, unroll=True)

        @pl.when((step >= first_sum) & (step < first_input))
        def _():
            chunk = step - first_sum
            pl.when(chunk == 0)(grad_copy.wait)
            slots = to_wide(lax.broadcasted_iota(jnp.int32, (2 * BLOCK, 1), 0))
            for offset in range(GROUP):
                near = near_other_ref[pl.ds(chunk * GROUP + offset, 1), :]
                for block in range(blocks):
                    low = block * BLOCK
                    select = to_low(
                        jnp.where(near[:, low : low + BLOCK] - float(low) == slots, 1.0, 0.0)
                    )
                    gathered[offset, :, low : low + BLOCK] = to_low(
                        product(windows[chunk % 2, 1, :, low : low + 2 * BLOCK], select, 1, 0)
                    )
            for offset in range(GROUP):
                weight_grad = product(windows[chunk % 2, 0], spread[chunk * GROUP + offset], 1, 0)
                weight_grad += product(gathered[offset], grad_other[...], 1, 0)
                sums.sends[0][chunk, offset] = to_low(weight_grad[: half // 2])
                sums.keep[chunk, offset] = weight_grad[half // 2 :]
            sums.start(0, chunk, kinds(chunk))

        @pl.when(step == first_input)
        def _():
            for load in loads:
                load.wait()

        beside = pl.ds(pl.multiple_of((1 - side) * (local + HALO), HALO), local + HALO)
        apart = pl.ds(pl.multiple_of(side * (2 * local + HALO), HALO), HALO)
        for phase, parts in enumerate(((beside, apart), (mine,))):
            start = first_input + phase * input_steps

            @pl.when((step >= start) & (step < start + input_steps))
            def _(start=start, parts=parts):
                def input_group(group, _):
                    for part in parts:
                        total = input_grad[part, :]
                        for offset in range(GROUP):
                            index = group * GROUP + offset
                            total += product(
                                spread[(step - start) * WIDE_GROUP + index, part, :],
                                weight_ref[(step - start) * WIDE_GROUP + index],
                                1,
                                1,
                            )
                        input_grad[part, :] = total
                    return 0

                lax.fori_loop(0, GROUP, input_group, 0, unroll=True)

        @pl.when(step == first_input + input_steps - 1)
        def _():
            input_copy.start()
            for index, (has, _, part) in enumerate(rims):
                rim_away[index] = to_low(input_grad[part, :])

                @pl.when(has)
                def _(index=index):
                    for core in range(2):

                        @pl.when(side == core)
                        def _(core=core):
                            rim_copies[index][core].start()

        @pl.when(step == steps - 1)
        def _():
            input_copy.wait()
            points_grad_ref[...] = first_grad_ref[...] + input_grad[mine, :] + input_arrived[...]

            @pl.when(has_rim)
            def _():
                edge = pl.ds(pl.multiple_of(side * (local - HALO), HALO), HALO)
                for core in range(2):
                    rim_copies[0][core].wait_recv()
                    points_grad_ref[edge, :] += to_wide(rim_arrived[core])

            for index, (has, _, part) in enumerate(rims):
                pl.when(has)(rim_copies[index][0].wait_send)

        for stage, due in enumerate(VECTOR_STEPS):

            @pl.when(step == due)
            def _(stage=stage):
                vector_copy(stage).wait()
                summed = vector_away[stage] + vector_arrived[stage]
                if stage < KERNEL_BITS:
                    vector_away[stage + 1] = summed
                    vector_copy(stage + 1).start()
                    return
                for index in range(8):
                    vector_refs[index][...] = summed[index : index + 1]
                for index in range(8, summed.shape[0]):
                    low = (index - 8) * channels
                    vector_refs[8][:, low : low + channels] = summed[index : index + 1]

        for stage in range(len(CONV_LAGS)):
            chunk = step - first_sum - CONV_LAGS[stage]

            @pl.when((chunk >= 0) & (chunk < chunks))
            def _(stage=stage, chunk=chunk):
                def finish(total):
                    conv_sum_ref[chunk] = total

                sums.advance(stage, chunk, kinds(chunk), finish)

        def finish_extra(index, total):
            if index == 0:
                heads_sum_ref[0:2] = total
            else:
                heads_sum_ref[2] = total[0]
                encode_sum_ref[...] = total[1]

        for stage, due in enumerate(EXTRA_STEPS):

            @pl.when(step == due)
            def _(stage=stage):
                for index in range(extras):
                    extra_sums.advance(
                        stage,
                        index,
                        ((True, ORDERS[index]),),
                        functools.partial(finish_extra, index),
                    )
        return 0

    begin()
    lax.fori_loop(0, steps, one_step, 0)


def conv_backward(
    near, near_other, turned, turned_other, grad, weight, extra, vector, first_grad
):
    offsets, channels, width = weight.shape
    wide = turned.shape[1]
    rows = grad.shape[0]
    local = first_grad.shape[0]
    chunks = offsets // GROUP
    low, full = jnp.bfloat16, jnp.float32
    kept = channels >> KERNEL_BITS
    shape = jax.ShapeDtypeStruct
    outs = [
        shape((chunks, GROUP, kept, width), full),
        shape((3, kept, width), full),
        shape((kept, width), full),
        shape(first_grad.shape, full),
        *[shape((1, channels), full)] * 8,
        shape((1, (vector.shape[0] - 8) * channels), full),
    ]

    anywhere = pl.BlockSpec(memory_space=pl.ANY)
    return pl.pallas_call(
        conv_backward_kernel,
        in_specs=[vmem()] * 2 + [anywhere] * 2 + [vmem()] + [anywhere] * 2 + [vmem(), anywhere],
        out_specs=[vmem()] * len(outs),
        out_shape=outs,
        scratch_shapes=[
            pltpu.VMEM((offsets, wide, width), low),
            pltpu.VMEM((2, 2, channels // 2, wide), low),
            pltpu.VMEM((GROUP, channels // 2, rows), low),
            pltpu.VMEM((rows, width), low),
            pltpu.VMEM((wide, channels), full),
            pltpu.VMEM((local, channels), full),
            pltpu.VMEM((2, HALO, channels), low),
            pltpu.VMEM((2, HALO, channels), low),
            pltpu.VMEM((KERNEL_BITS + 1, *vector.shape), full),
            pltpu.VMEM((KERNEL_BITS + 1, *vector.shape), full),
            *copy_sems(7 + KERNEL_BITS),
            pltpu.VMEM(weight.shape, low),
            pltpu.VMEM(first_grad.shape, full),
            pltpu.VMEM(turned_other.shape, low),
            pltpu.VMEM(turned_other.shape, low),
            pltpu.VMEM(extra.shape, full),
            pltpu.SemaphoreType.DMA((5,)),
            *pair_scratch(chunks, GROUP, channels // 2, width, len(CONV_LAGS)),
            *pair_scratch(*extra.shape, KERNEL_BITS),
        ],
        compiler_params=pltpu.CompilerParams(
            vmem_limit_bytes=VMEM_BYTES, collective_id=1, has_side_effects=True
        ),
        cost_estimate=pl.CostEstimate(
            flops=80 * 10**9, bytes_accessed=16 * 10**6, transcendentals=0
        ),
    )(near, near_other, turned, turned_other, grad, weight, extra, vector, first_grad)


def hand_over_kernel(*refs):
    count = (len(refs) - 1) // 3
    sem = refs[-1]
    inward = [
        pltpu.make_async_copy(refs[i], refs[2 * count + i], sem.at[i]) for i in range(count)
    ]
    outward = [
        pltpu.make_async_copy(refs[2 * count + i], refs[count + i], sem.at[count + i])
        for i in range(count)
    ]
    for copy in inward:
        copy.start()
    for arrive, leave in zip(inward, outward):
        arrive.wait()
        leave.start()
    for copy in outward:
        copy.wait()


def hand_over(arrays):
    anywhere = pl.BlockSpec(memory_space=pl.ANY)
    return pl.pallas_call(
        hand_over_kernel,
        in_specs=[anywhere] * len(arrays),
        out_specs=[anywhere] * len(arrays),
        out_shape=[jax.ShapeDtypeStruct(each.shape, each.dtype) for each in arrays],
        scratch_shapes=[pltpu.VMEM(each.shape, each.dtype) for each in arrays]
        + [pltpu.SemaphoreType.DMA((2 * len(arrays),))],
        compiler_params=pltpu.CompilerParams(vmem_limit_bytes=VMEM_BYTES),
    )(*arrays)


def exchange(values, bit):
    count = lax.axis_size("pts")
    return lax.ppermute(values, "pts", [(i, i ^ (1 << bit)) for i in range(count)])


def sum_rest(keep, axis):
    for bit in range(KERNEL_BITS, patch_bits()):
        half = keep.shape[axis] // 2
        away = lax.slice_in_dim(keep, 0, half, axis=axis)
        keep = lax.slice_in_dim(keep, half, 2 * half, axis=axis)
        keep = keep + to_wide(exchange(to_low(away), bit))
    return keep


def per_device(
    points,
    neighbours,
    valid_count,
    conv_weight,
    encode_weight,
    encode_gain,
    encode_shift,
    attend_gain,
    attend_shift,
    heads_weight,
    output_weight,
    output_bias,
    feed_gain,
    feed_shift,
    expand_weight,
    expand_bias,
    reduce_weight,
    reduce_bias,
    cotangent,
):
    local, channels = points.shape
    norms = [v[None, :] for v in (encode_gain, encode_shift, attend_gain, attend_shift)]
    (
        mixed, logs, mask, turned, near_columns, conved, linear, first, attend_in, projected,
        output_other, expand_other, reduce_other, bias_other,
    ) = forward_start(
        neighbours.T, points, conv_weight, encode_weight, norms, heads_weight, output_weight,
        expand_weight, reduce_weight, expand_bias[None, :], valid_count
    )
    (
        conved_grad, vector, reduce_sum, expand_sum, output_sum, result, first_grad, extra,
        turned_other, near_other,
    ) = middle(
        [
            mixed, first, output_weight, output_other, output_bias[None, :], feed_gain[None, :],
            feed_shift[None, :], cotangent, expand_bias[None, :], bias_other,
            reduce_bias[None, :], mask, logs, norms[2], norms[0],
        ],
        [
            expand_weight, expand_other, reduce_weight, reduce_other, projected, heads_weight,
            attend_in, linear, encode_weight, conved, turned, near_columns,
        ],
    )
    conv_sum, heads_sum, encode_sum, points_gradient, *vectors = conv_backward(
        near_columns, near_other, turned, turned_other, conved_grad, conv_weight, extra, vector,
        first_grad
    )
    for bit in range(KERNEL_BITS, patch_bits()):
        vectors = [each + exchange(each, bit) for each in vectors]
    parts = hand_over(
        [
            result,
            points_gradient,
            sum_rest(conv_sum, 2),
            sum_rest(encode_sum, 0),
            sum_rest(heads_sum, 1),
            sum_rest(output_sum, 0),
            sum_rest(expand_sum, 0),
            sum_rest(reduce_sum, 0),
            *vectors,
        ]
    )
    vectors = [each.reshape(-1) for each in parts[8:]]
    return (
        parts[0],
        parts[1],
        parts[2].reshape(-1, *parts[2].shape[2:]),
        parts[3].T,
        vectors[6],
        vectors[7],
        vectors[4],
        vectors[5],
        parts[4],
        parts[5].T,
        vectors[0],
        vectors[1],
        vectors[2],
        parts[6],
        vectors[8],
        parts[7].T,
        vectors[3],
    )


def solution(mesh):
    placed = (
        P(("pts", "tp"), None),
        P("pts", None),
        P("pts"),
        P(None, None, "tp"),
        P("tp", None),
        P(),
        P(),
        P(),
        P(),
        P(None, None, "tp"),
        P("tp", None),
        P(),
        P(),
        P(),
        P(None, "tp"),
        P("tp"),
        P("tp", None),
        P(),
        P(("pts", "tp"), None),
    )
    return jax.shard_map(
        per_device,
        mesh=mesh,
        in_specs=placed,
        out_specs=(
            P(("pts", "tp"), None),
            P(("pts", "tp"), None),
            P(None, "pts", "tp"),
            P("tp", "pts"),
            P(),
            P(),
            P(),
            P(),
            P(None, "pts", "tp"),
            P("tp", "pts"),
            P(),
            P(),
            P(),
            P("pts", "tp"),
            P(),
            P("tp", "pts"),
            P(),
        ),
        check_vma=False,
    )
```
